32 devices in a mesh: seq: 16 (over z, x, core), heads: 2 (over y).
Axes of the slice: x: 2, y: 2, z: 4, core: 2. Of those that a mesh axis runs over, the one named last changes fastest.
Arguments:
- inputs: float32 [50176, 512], P('seq'), may hold values from -6 to 6
- w_qkv: float32 [3, 512, 512], P(None, 'seq', 'heads'), may hold values from -0.25 to 0.25
- w_proj: float32 [512, 512], P('heads', 'seq'), may hold values from -3 to 3
- w_fc1: float32 [512, 2048], P('seq', 'heads'), may hold values from -0.25 to 0.25
- w_fc2: float32 [2048, 512], P('heads', 'seq'), may hold values from -0.125 to 0.125
- gains: float32 [2, 512], replicated, may hold values from 0.1 to 1.9
- shifts: float32 [4, 512], replicated, may hold values from -3 to 3
- rel_table: float32 [16, 2535], P('heads'), may hold values from -4 to 4
- region: int32 [50176], P('seq'), may hold values from 0 to 2
- pos_index: int32 [392, 392], replicated, may hold values from 0 to 2534
- out_grad: float32 [50176, 512], P('seq'), may hold values from -6 to 6
Outputs:
- output: float32 [50176, 512], P('seq')
- d_inputs: float32 [50176, 512], P('seq')
- d_qkv: float32 [3, 512, 512], P(None, 'seq', 'heads')
- d_proj: float32 [512, 512], P('heads', 'seq')
- d_fc1: float32 [512, 2048], P('seq', 'heads')
- d_fc2: float32 [2048, 512], P('heads', 'seq')
- d_gains: float32 [2, 512], replicated
- d_shifts: float32 [4, 512], replicated
- d_table: float32 [16, 2535], P('heads')
The draws below stay inside these ranges and needn't reach their ends.
All inputs are finite; a program needn't handle non-finite values.
Results may differ from the reference program's by a relative error of at most 0.012.
The reference program's roundings to bfloat16 on the way count: a program that leaves them out, or rounds other values in their place, can miss the bound.
Values may be sent and summed in bfloat16 or wider, within the bound.
A program may use at most 320 MiB of HBM per device.

```python
import jax
import jax.numpy as jnp
from jax import lax

D = 512
HEADS = 16
FF = 2048
WIN = 392
SHIFT = 196
TABLE = 2535
TOKENS = 50176


def place_ends(drawn, key, smallest, top_value):
    spot = [jax.random.randint(jax.random.fold_in(key, axis), (), 0, length) for axis, length in enumerate(drawn.shape)]
    longest = drawn.shape.index(max(drawn.shape))
    next_to = spot[:longest] + [(spot[longest] + 1) % drawn.shape[longest]] + spot[longest + 1:]
    return drawn.at[tuple(spot)].set(smallest).at[tuple(next_to)].set(top_value)


def block_scale(own_key, dims, shards, smallest, largest):
    level = 1.0
    for dim, parts in shards:
        heights = jax.random.uniform(jax.random.fold_in(jax.random.fold_in(own_key, 6), dim), (parts,), jnp.float32, smallest / len(shards), largest / len(shards))
        level = level * jnp.repeat(jnp.exp(heights), dims[dim] // parts).reshape((-1,) + (1,) * (len(dims) - 1 - dim))
    return level


def bell_draw(key, shape, scale, reach, shards=(), dtype=jnp.bfloat16):
    values = jax.random.normal(key, shape, jnp.float32) * scale
    if len(shards) > 0:
        values = block_scale(key, shape, shards, -0.22, 0.18) * values
    return jnp.clip(values, min=-reach, max=reach).astype(dtype)


def setup_inputs(seed: int = 0) -> dict:
    keys = jax.random.split(jax.random.key(seed), 12)
    return {
        "inputs": bell_draw(keys[0], (TOKENS, D), 1.0, 6.0, ((0, 16),), jnp.float32),
        "w_qkv": bell_draw(keys[1], (3, D, D), D ** -0.5, 0.25, ((1, 16), (2, 2)), jnp.float32),
        "w_proj": bell_draw(keys[2], (D, D), (max(D // 128, 2)) ** -0.5, 3.0, ((0, 2), (1, 16)), jnp.float32),
        "w_fc1": bell_draw(keys[3], (D, FF), D ** -0.5, 0.25, ((0, 16), (1, 2)), jnp.float32),
        "w_fc2": bell_draw(keys[4], (FF, D), FF ** -0.5, 0.125, ((0, 2), (1, 16)), jnp.float32),
        "gains": jnp.clip(1.0 + 0.18 * jax.random.normal(keys[5], (2, D), jnp.float32), 0.1, 1.9),
        "shifts": bell_draw(keys[6], (4, D), 0.5, 3.0, (), jnp.float32),
        "rel_table": bell_draw(keys[7], (HEADS, TABLE), 1.0, 4.0, ((0, 2),), jnp.float32),
        "region": place_ends(jax.random.randint(keys[8], (TOKENS,), 0, 3), jax.random.fold_in(keys[8], 1), 0, 2).astype(jnp.int32),
        "pos_index": place_ends(jax.random.randint(keys[9], (WIN, WIN), 0, TABLE), jax.random.fold_in(keys[9], 1), 0, TABLE - 1).astype(jnp.int32),
        "out_grad": bell_draw(keys[10], (TOKENS, D), 1.0, 6.0, ((0, 16),), jnp.float32),
    }


@jax.custom_vjp
def low(v):
    return lax.optimization_barrier(v.astype(jnp.bfloat16)).astype(jnp.float32)

@jax.custom_vjp
def low_back(v):
    return v

def low_keep(v):
    return (low(v), None)

def low_pass(kept, grad):
    return (grad,)

def back_keep(v):
    return (v, None)

def back_low(kept, grad):
    return (low(grad),)
low.defvjp(low_keep, low_pass)
low_back.defvjp(back_keep, back_low)
eps_norm = 1e-05
fill_value = -100.0
highest = lax.Precision.HIGHEST

def normalize(rows_in, gain_vec, shift_vec):
    row_mean = lax.optimization_barrier(jnp.mean(rows_in, axis=-1, keepdims=True))
    centred = rows_in - row_mean
    variance = lax.optimization_barrier(jnp.mean(centred * centred, axis=-1, keepdims=True))
    return centred * lax.rsqrt(variance + eps_norm) * gain_vec + shift_vec

def forward(inputs, w_qkv, w_proj, w_fc1, w_fc2, gains, shifts, rel_table, region, pos_index):
    tok_count = inputs.shape[0]
    head_count = rel_table.shape[0]
    feat_width = inputs.shape[1]
    head_size = feat_width // head_count
    normed_one = low(normalize(inputs, gains[0], shifts[0]))
    rolled = jnp.roll(normed_one, -SHIFT, axis=0)
    qkv = jnp.einsum('td,cde->cte', rolled, low(w_qkv), precision=highest)
    qkv = low(low_back(qkv))
    blocks = qkv.reshape(3, tok_count // WIN, WIN, head_count, head_size)
    pos_bias = jnp.take(rel_table, pos_index, axis=1)
    labels = region.reshape(tok_count // WIN, WIN)
    score_scale = head_size ** (-0.5)

    def attend(piece):
        q_rows, k_rows, v_rows, label_row = piece
        scores = jnp.einsum('qhd,khd->hqk', q_rows, k_rows, precision=highest) * score_scale + pos_bias
        scores = scores + jnp.where(label_row[:, None] == label_row[None, :], 0.0, fill_value)
        scores = low_back(scores)
        attn_probs = low(jax.nn.softmax(scores, axis=-1))
        return jnp.einsum('hqk,khd->qhd', attn_probs, v_rows, precision=highest)
    attn_mixed = lax.map(jax.checkpoint(attend), (blocks[0], blocks[1], blocks[2], labels))
    attn_mixed = low(low_back(attn_mixed.reshape(tok_count, feat_width)))
    branch = low(low_back(jnp.dot(attn_mixed, low(w_proj), precision=highest) + shifts[2]))
    middle = inputs + jnp.roll(branch, SHIFT, axis=0)
    normed_two = low(normalize(middle, gains[1], shifts[1]))
    hidden = low_back(jnp.dot(normed_two, low(w_fc1), precision=highest))
    active = low(jax.nn.gelu(hidden, approximate=False))
    update = low_back(jnp.dot(active, low(w_fc2), precision=highest) + shifts[3])
    return middle + update

def reference(inputs, w_qkv, w_proj, w_fc1, w_fc2, gains, shifts, rel_table, region, pos_index, out_grad):

    def run_layer(inputs, w_qkv, w_proj, w_fc1, w_fc2, gains, shifts, rel_table):
        return forward(inputs, w_qkv, w_proj, w_fc1, w_fc2, gains, shifts, rel_table, region, pos_index)
    result, pull_back = jax.vjp(run_layer, inputs, w_qkv, w_proj, w_fc1, w_fc2, gains, shifts, rel_table)
    gradients = pull_back(out_grad)
    return (result, gradients[0], gradients[1], gradients[2], gradients[3], gradients[4], gradients[5], gradients[6], gradients[7])
```

```python
import functools
import math

import jax, jax.numpy as jnp
from jax import lax
from jax.experimental import pallas as pl
from jax.experimental.pallas import tpu as pltpu
from jax.sharding import PartitionSpec as P

BF=jnp.bfloat16; F32=jnp.float32
HD=32; GROUP=128; PER=4
EPS=1e-5
SQ=math.sqrt(32.0)
CEXP=math.log2(math.e)/SQ
MASK=100.0*SQ

def mm(a,b):
    return lax.dot_general(a,b,(((1,),(0,)),((),())),preferred_element_type=F32)
def mm_nt(a,b):
    return lax.dot_general(a,b,(((1,),(1,)),((),())),preferred_element_type=F32)

def norm_stats(v):
    mean=jnp.mean(v,axis=-1,keepdims=True)
    c=v-mean
    var=jnp.mean(c*c,axis=-1,keepdims=True)
    rstd=lax.rsqrt(var+EPS)
    return c*rstd, rstd

def norm_back(gy,xhat,rstd,gain):
    gx=gy*gain
    m1=jnp.mean(gx,axis=-1,keepdims=True)
    m2=jnp.mean(gx*xhat,axis=-1,keepdims=True)
    return rstd*(gx-m1-xhat*m2)

P0=0.3275911
A1,A2,A3,A4,A5=0.254829592,-0.284496736,1.421413741,-1.453152027,1.061405429
def gelu_both(x):
    e=jnp.exp2(x*x*(-0.5*math.log2(math.e)))
    t=1.0/(1.0+(P0/math.sqrt(2.0))*jnp.abs(x))
    poly=t*(0.5*A1+t*(0.5*A2+t*(0.5*A3+t*(0.5*A4+t*(0.5*A5)))))
    half=poly*e
    phi=jnp.where(x>=0,1.0-half,half)
    return x*phi, phi+x*e*(1.0/math.sqrt(2.0*math.pi))

def kernel_a(nheads, x_ref,og_ref,labc_ref,labr_ref,bias_ref,wqkv_ref,projT_ref,fc1_ref,fc2T_ref,gains_ref,shifts_ref,
             delta_ref,gln2_ref,qkv_ref,g_ref,gT_ref,D_ref,P_hbm,dfc1_ref,dfc2T_ref,dprojT_ref,small_ref,
             qT_s,vT_s,OT_s,P_s,afc1,afc2,aproj,sem,xn2_s,xn2T_s,tg_s,tgT_s,up_s,gn2_s):
    w=pl.program_id(0); nw=pl.num_programs(0)
    D=x_ref.shape[-1]; WIN=x_ref.shape[-2]; FF=fc1_ref.shape[1]
    groups=nheads//PER
    x=x_ref[0]
    xhat,_=norm_stats(x)
    xn=(xhat*gains_ref[0:1,:]+shifts_ref[0:1,:]).astype(BF)
    for c in range(3):
        y=mm(xn,wqkv_ref[:,c*D:(c+1)*D]).astype(BF)
        qkv_ref[0,c]=y
        if c==0: qT_s[...]=y.T
        if c==2: vT_s[...]=y.T
    labc=labc_ref[0]; labr=labr_ref[0]
    lane=lax.broadcasted_iota(jnp.int32,(WIN,GROUP),1)
    oh=jnp.where((labc==lane)|((labc+3)==lane),1.0,0.0).astype(BF)
    hi=564.0
    lo=MASK-564.0
    sub=lax.broadcasted_iota(jnp.int32,(GROUP,WIN),0)
    nm=jnp.where(sub<3,jnp.where(sub!=labr,-hi,0.0),jnp.where(sub<6,jnp.where(sub-3!=labr,-lo,0.0),0.0)).astype(BF)
    hl=lane//HD

    def group(gi,_):
        slot=gi%2
        step=w*groups+gi
        @pl.when(step>=2)
        def _():
            pltpu.make_async_copy(P_s.at[slot],P_hbm.at[0,pl.ds(0,PER)],sem.at[slot]).wait()
        o=pl.multiple_of(gi*GROUP,GROUP)
        qTg=jnp.concatenate([qT_s[pl.ds(o,GROUP),:],nm],axis=0)
        kg=qkv_ref[0,1,:,pl.ds(o,GROUP)]
        for hh in range(PER):
            kh=jnp.concatenate([jnp.where(hl==hh,kg,jnp.zeros_like(kg)),oh],axis=1)
            t=mm(kh,qTg)+bias_ref[gi*PER+hh]
            m=jnp.max(t,axis=0,keepdims=True)
            e=jnp.exp2((t-m)*CEXP)
            l=jnp.sum(e,axis=0,keepdims=True)
            p=(e*(1.0/l)).astype(BF)
            P_s[slot,hh]=p
            OT_s[pl.ds(o+hh*HD,HD),:]=mm(vT_s[pl.ds(o+hh*HD,HD),:],p)
        pltpu.make_async_copy(P_s.at[slot],P_hbm.at[w,pl.ds(gi*PER,PER)],sem.at[slot]).start()
        return 0
    lax.fori_loop(0,groups,group,0)

    attn=OT_s[...].astype(BF).T
    branch=(mm_nt(attn,projT_ref[...])+shifts_ref[2:3,:]).astype(BF).astype(F32)
    middle=x+branch
    xhat2,rstd2=norm_stats(middle)
    xn2=(xhat2*gains_ref[1:2,:]+shifts_ref[1:2,:]).astype(BF)
    og=og_ref[0]
    tg=og.astype(BF)
    xn2_s[...]=xn2; xn2T_s[...]=xn2.T; tg_s[...]=tg; tgT_s[...]=tg.T
    up_s[...]=jnp.zeros_like(up_s); gn2_s[...]=jnp.zeros_like(gn2_s)
    CH=min(512,FF)
    @pl.when(w==0)
    def _():
        afc1[...]=jnp.zeros_like(afc1); afc2[...]=jnp.zeros_like(afc2); aproj[...]=jnp.zeros_like(aproj)
        small_ref[...]=jnp.zeros_like(small_ref)
    def chunk(c,_):
        o=pl.multiple_of(c*CH,CH)
        f1=fc1_ref[:,pl.ds(o,CH)]; f2=fc2T_ref[:,pl.ds(o,CH)]
        hid=mm(xn2_s[...],f1)
        act,dact=gelu_both(hid)
        a=act.astype(BF)
        up_s[...]+=mm_nt(a,f2)
        gh=(mm(tg_s[...],f2)*dact).astype(BF)
        gn2_s[...]+=mm_nt(gh,f1)
        afc1[:,pl.ds(o,CH)]+=mm(xn2T_s[...],gh)
        afc2[:,pl.ds(o,CH)]+=mm(tgT_s[...],a)
        return 0
    lax.fori_loop(0,FF//CH,chunk,0)
    delta_ref[0]=(branch+up_s[...]+shifts_ref[3:4,:]).astype(BF)
    gn2=gn2_s[...]
    gln2=norm_back(gn2,xhat2,rstd2,gains_ref[1:2,:])
    gln2_ref[0]=gln2
    gb=(og+gln2).astype(BF)
    aproj[...]+=mm(gb.T,attn)
    g=mm(gb,projT_ref[...]).astype(BF)
    g_ref[0]=g
    gT=g.T
    gT_ref[0]=gT
    prod=gT.astype(F32)*OT_s[...]
    D_ref[0]=jnp.sum(prod.reshape(nheads,HD,WIN),axis=1)
    small_ref[1:2,:]+=jnp.sum(gn2*xhat2,axis=0,keepdims=True)
    small_ref[3:4,:]+=jnp.sum(gn2,axis=0,keepdims=True)
    small_ref[4:5,:]+=jnp.sum(gb.astype(F32),axis=0,keepdims=True)
    small_ref[5:6,:]+=jnp.sum(tg.astype(F32),axis=0,keepdims=True)
    @pl.when(w==nw-1)
    def _():
        dfc1_ref[...]=afc1[...].astype(BF); dfc2T_ref[...]=afc2[...].astype(BF); dprojT_ref[...]=aproj[...].astype(BF)
        for s in range(2):
            pltpu.make_async_copy(P_s.at[s],P_hbm.at[0,pl.ds(0,PER)],sem.at[s]).wait()

def full(shape,**kw):
    return pl.BlockSpec(shape,lambda w:(0,)*len(shape),**kw)
def per(shape):
    return pl.BlockSpec((1,)+shape,lambda w:(w,)+(0,)*len(shape))
ONE=pl.Buffered(1)

def call_a(x,og,labc,labr,bias,wqkv,projT,fc1,fc2T,gains,shifts):
    nW,WIN,D=x.shape; FF=fc1.shape[1]; NH=bias.shape[0]
    sd=jax.ShapeDtypeStruct
    outs=[sd((nW,WIN,D),BF),sd((nW,WIN,D),F32),sd((nW,3,WIN,D),BF),sd((nW,WIN,D),BF),sd((nW,D,WIN),BF),sd((nW,NH,WIN),F32),
          sd((nW,NH,WIN,WIN),BF),sd((D,FF),BF),sd((D,FF),BF),sd((D,D),BF),sd((8,D),F32)]
    return pl.pallas_call(functools.partial(kernel_a,NH),grid=(nW,),
      in_specs=[per((WIN,D)),per((WIN,D)),per((WIN,1)),per((1,WIN)),full((NH,WIN,WIN),pipeline_mode=ONE),
        full((D,3*D),pipeline_mode=ONE),full((D,D),pipeline_mode=ONE),full((D,FF),pipeline_mode=ONE),full((D,FF),pipeline_mode=ONE),
        full(gains.shape),full(shifts.shape)],
      out_specs=[per((WIN,D)),per((WIN,D)),per((3,WIN,D)),per((WIN,D)),per((D,WIN)),per((NH,WIN)),pl.BlockSpec(memory_space=pl.ANY),
        full((D,FF)),full((D,FF)),full((D,D)),full((8,D))],
      out_shape=outs,
      scratch_shapes=[pltpu.VMEM((D,WIN),BF),pltpu.VMEM((D,WIN),BF),pltpu.VMEM((D,WIN),F32),pltpu.VMEM((2,PER,WIN,WIN),BF),
        pltpu.VMEM((D,FF),F32),pltpu.VMEM((D,FF),F32),pltpu.VMEM((D,D),F32),pltpu.SemaphoreType.DMA((2,)),
        pltpu.VMEM((WIN,D),BF),pltpu.VMEM((D,WIN),BF),pltpu.VMEM((WIN,D),BF),pltpu.VMEM((D,WIN),BF),pltpu.VMEM((WIN,D),F32),pltpu.VMEM((WIN,D),F32)],
      compiler_params=pltpu.CompilerParams(vmem_limit_bytes=62*1024*1024,dimension_semantics=("arbitrary",)),
      name="kernel_a")(x,og,labc,labr,bias,wqkv,projT,fc1,fc2T,gains,shifts)

def kernel_b(nheads,x_ref,gln2_ref,qkv_ref,g_ref,gT_ref,D_ref,P_ref,wqkv_ref,gains_ref,shifts_ref,
             dd_ref,dqkv_ref,G_hbm,small_ref, G_s,aq,kT_s,gq_s,gqT_s,sem):
    w=pl.program_id(0); nw=pl.num_programs(0)
    D=x_ref.shape[-1]; WIN=x_ref.shape[-2]
    groups=nheads//PER
    @pl.when(w==0)
    def _():
        aq[...]=jnp.zeros_like(aq); G_s[...]=jnp.zeros_like(G_s); small_ref[...]=jnp.zeros_like(small_ref)
    kT_s[...]=qkv_ref[0,1].T
    lane=lax.broadcasted_iota(jnp.int32,(WIN,GROUP),1)
    hl=lane//HD
    def group(gi,_):
        o=pl.multiple_of(gi*GROUP,GROUP)
        gTg=gT_ref[0,pl.ds(o,GROUP),:]
        vg=qkv_ref[0,2,:,pl.ds(o,GROUP)]
        qg=qkv_ref[0,0,:,pl.ds(o,GROUP)]
        gg=g_ref[0,:,pl.ds(o,GROUP)]
        dv=jnp.zeros((WIN,GROUP),F32); dk=jnp.zeros((WIN,GROUP),F32)
        zero=jnp.zeros_like(vg)
        for hh in range(PER):
            h=gi*PER+hh
            p=P_ref[0,h]
            dp=mm(jnp.where(hl==hh,vg,zero),gTg)
            ds=p.astype(F32)*(dp-D_ref[0,pl.ds(h,1),:])
            for c in range(G_s.shape[0]):
                wd=min(128,WIN-c*128)
                G_s[c,pl.ds(pl.multiple_of(h*WIN,8),WIN),:wd]+=ds[:,c*128:c*128+wd]
            dsl=ds.astype(BF)
            dv+=mm(p,jnp.where(hl==hh,gg,zero))
            dk+=mm(dsl,jnp.where(hl==hh,qg,zero))
            gqT_s[pl.ds(o+hh*HD,HD),:]=mm(kT_s[pl.ds(o+hh*HD,HD),:],dsl)
        gq_s[1,:,pl.ds(o,GROUP)]=(dk*(1.0/SQ)).astype(BF)
        gq_s[2,:,pl.ds(o,GROUP)]=dv.astype(BF)
        return 0
    lax.fori_loop(0,groups,group,0)
    gq_s[0]=(gqT_s[...]*(1.0/SQ)).astype(BF).T
    x=x_ref[0]
    xhat,rstd=norm_stats(x)
    xn=(xhat*gains_ref[0:1,:]+shifts_ref[0:1,:]).astype(BF)
    xnT=xn.T
    gr=jnp.zeros((WIN,D),F32)
    for c in range(3):
        gc=gq_s[c]
        gr=gr+mm_nt(gc,wqkv_ref[:,c*D:(c+1)*D])
        aq[:,c*D:(c+1)*D]+=mm(xnT,gc)
    dd_ref[0]=(gln2_ref[0]+norm_back(gr,xhat,rstd,gains_ref[0:1,:])).astype(BF)
    small_ref[0:1,:]+=jnp.sum(gr*xhat,axis=0,keepdims=True)
    small_ref[2:3,:]+=jnp.sum(gr,axis=0,keepdims=True)
    @pl.when(w==nw-1)
    def _():
        dqkv_ref[...]=aq[...].astype(BF)
        cp=pltpu.make_async_copy(G_s,G_hbm,sem); cp.start(); cp.wait()

def call_b(x,gln2,qkv,g,gT,Dd,Pp,wqkv,gains,shifts):
    nW,WIN,D=x.shape; NH=Dd.shape[1]
    sd=jax.ShapeDtypeStruct
    return pl.pallas_call(functools.partial(kernel_b,NH),grid=(nW,),
      in_specs=[per((WIN,D)),per((WIN,D)),per((3,WIN,D)),per((WIN,D)),per((D,WIN)),per((NH,WIN)),per((NH,WIN,WIN)),
        full((D,3*D),pipeline_mode=ONE),full(gains.shape),full(shifts.shape)],
      out_specs=[per((WIN,D)),full((D,3*D)),pl.BlockSpec(memory_space=pl.ANY),full((8,D))],
      out_shape=[sd((nW,WIN,D),BF),sd((D,3*D),BF),sd((-(-WIN//128),NH*WIN,128),F32),sd((8,D),F32)],
      scratch_shapes=[pltpu.VMEM((-(-WIN//128),NH*WIN,128),F32),pltpu.VMEM((D,3*D),F32),pltpu.VMEM((D,WIN),BF),pltpu.VMEM((3,WIN,D),BF),pltpu.VMEM((D,WIN),F32),pltpu.SemaphoreType.DMA],
      compiler_params=pltpu.CompilerParams(vmem_limit_bytes=62*1024*1024,dimension_semantics=("arbitrary",)),
      name="kernel_b")(x,gln2,qkv,g,gT,Dd,Pp,wqkv,gains,shifts)

FIX=8191.0

def pack_table(table):
    NH,T=table.shape
    n=-(-T//128)
    q=jnp.round(jnp.clip(table,-4.0,4.0)*FIX).astype(jnp.int32)
    q=jnp.pad(q,((0,0),(0,n*128-T)))
    q=q.reshape(NH//2,2,n,128)
    return (q[:,0]*65536)|(q[:,1]&65535)

def kernel_p(pos_ref,tab_ref,bias_ref):
    npair,n,_=tab_ref.shape
    WIN=bias_ref.shape[-1]
    tiles=-(-WIN//128)
    def row(r,_):
        r8=pl.multiple_of(r*8,8)
        for c in range(tiles):
            width=min(128,WIN-c*128)
            idx=pos_ref[pl.ds(r8,8),c*128:(c+1)*128]
            lo=idx&127; hi=idx>>7
            masks=[hi==k for k in range(n)]
            for p in range(npair):
                acc=jnp.zeros((8,128),jnp.int32)
                for k in range(n):
                    src=jnp.broadcast_to(tab_ref[p,k:k+1,:],(8,128))
                    acc=jnp.where(masks[k],jnp.take_along_axis(src,lo,axis=1),acc)
                a=(acc>>16).astype(F32)*(SQ/FIX)
                b=((acc<<16)>>16).astype(F32)*(SQ/FIX)
                bias_ref[2*p,pl.ds(r8,8),c*128:c*128+width]=a[:,:width]
                bias_ref[2*p+1,pl.ds(r8,8),c*128:c*128+width]=b[:,:width]
        return 0
    lax.fori_loop(0,bias_ref.shape[1]//8,row,0)

def call_p(posT_pad,tab,WIN):
    NH=tab.shape[0]*2
    return pl.pallas_call(kernel_p,out_shape=jax.ShapeDtypeStruct((NH,WIN,WIN),F32),
      compiler_params=pltpu.CompilerParams(vmem_limit_bytes=40*1024*1024),name="kernel_p")(posT_pad,tab)

def kernel_c(NH,G_ref,hi_ref,lo_ref,out_ref):
    WIN=hi_ref.shape[0]; LW=G_ref.shape[0]*128
    nh=out_ref.shape[0]//NH
    out_ref[...]=jnp.zeros_like(out_ref)
    def rows(r,_):
        r8=pl.multiple_of(r*8,8)
        hi8=hi_ref[pl.ds(r8,8),:]; lo8=lo_ref[pl.ds(r8,8),:]
        tot=jnp.zeros(out_ref.shape,F32)
        iota=lax.broadcasted_iota(jnp.int32,(256,LW),0).astype(F32).astype(BF)
        for k in range(8):
            g=jnp.concatenate([G_ref[c,pl.ds(r8+k,NH,stride=WIN),:] for c in range(LW//128)],axis=1)
            hr=hi8[k:k+1,:]; lr=lo8[k:k+1,:].astype(F32).astype(BF)
            A=jnp.concatenate([jnp.where(hr==m,g,0.0) for m in range(nh)],axis=0).astype(BF)
            oh=jnp.where(iota==lr,jnp.ones((),BF),jnp.zeros((),BF))
            tot=tot+lax.dot_general(A,oh,(((1,),(1,)),((),())),preferred_element_type=F32)
        out_ref[...]+=tot
        return 0
    lax.fori_loop(0,WIN//8,rows,0)

def call_c(G,posT,T,NH):
    WIN=posT.shape[0]; nt=G.shape[0]
    nh=-(-T//256)
    pp=jnp.pad(posT,((0,0),(0,nt*128-WIN)),constant_values=nh*256)
    hi=pp>>8; lo=pp&255
    o=pl.pallas_call(functools.partial(kernel_c,NH),out_shape=jax.ShapeDtypeStruct((nh*NH,256),F32),
      compiler_params=pltpu.CompilerParams(vmem_limit_bytes=40*1024*1024),name="kernel_c")(G,hi,lo)
    return o.reshape(nh,NH,256).transpose(1,0,2).reshape(NH,nh*256)[:,:T]


def gathered(piece,names,nseq,nheads):
    full=lax.all_gather(piece,names,axis=0,tiled=False)
    return full.reshape((nseq,nheads)+piece.shape)

def natural(block):
    s,h,r,c=block.shape
    return block.transpose(0,2,1,3).reshape(s*r,h*c)

def owners(grad,nseq,nheads):
    r,c=grad.shape
    return grad.reshape(nseq,r//nseq,nheads,c//nheads).transpose(0,2,1,3).reshape(nseq*nheads,r//nseq,c//nheads)

def from_next(rows):
    n=lax.axis_size("seq")
    return lax.ppermute(rows,"seq",[(i,(i-1)%n) for i in range(n)])

def to_next(rows):
    n=lax.axis_size("seq")
    return lax.ppermute(rows,"seq",[(i,(i+1)%n) for i in range(n)])

def spread(rows):
    n=lax.axis_size("heads")
    flat=rows.reshape(-1,rows.shape[-1])
    if n==2:
        other=lax.ppermute(flat,"heads",[(0,1),(1,0)])
        me=lax.axis_index("heads")
        return jnp.where(me==0,jnp.concatenate([flat,other]),jnp.concatenate([other,flat]))
    return lax.all_gather(flat,"heads",axis=0,tiled=True)

def place(rows,base,shift):
    full=spread(rows)
    keep=full.shape[0]-shift
    moved=jnp.concatenate([to_next(full[keep:]),full[:keep]])
    return base+moved.astype(F32)

def body(inputs,w_qkv,w_proj,w_fc1,w_fc2,gains,shifts,rel_table,region,pos_index,out_grad):
    nseq=lax.axis_size("seq"); nheads=lax.axis_size("heads"); me=lax.axis_index("heads")
    names=("seq","heads")
    tok,D=inputs.shape; WIN=pos_index.shape[0]; shift=WIN//2; T=rel_table.shape[1]
    nW=tok//WIN//nheads
    rows=w_qkv.shape[1]; cq=w_qkv.shape[2]; cf=w_fc1.shape[1]
    wcat=jnp.concatenate([w_qkv[0],w_qkv[1],w_qkv[2],w_proj.T,w_fc1,w_fc2.T],axis=1).astype(BF)
    table=lax.all_gather(rel_table,"heads",axis=0,tiled=True)
    NH=table.shape[0]
    full_w=gathered(wcat,names,nseq,nheads)
    cut=[natural(full_w[...,i*cq:(i+1)*cq]) for i in range(4)]
    wqkv=jnp.concatenate(cut[:3],axis=1); projT=cut[3]
    fc1=natural(full_w[...,4*cq:4*cq+cf]); fc2T=natural(full_w[...,4*cq+cf:])
    posT=pos_index.T
    wide=-(-WIN//128)*128
    bias=call_p(jnp.pad(posT,((0,0),(0,wide-WIN))),pack_table(table),WIN)
    start=me*nW*WIN
    def mine(v):
        ext=jnp.concatenate([v,from_next(v[:shift])])
        return lax.dynamic_slice_in_dim(ext,start+shift,nW*WIN,0).reshape(nW,WIN,-1)
    x=mine(inputs); og=mine(out_grad)
    lab=lax.dynamic_slice_in_dim(region,start,nW*WIN,0).reshape(nW,WIN)
    delta,gln2,qkv,g,gT,Dd,Pp,dfc1,dfc2T,dprojT,sm_a=call_a(x,og,lab[:,:,None],lab[:,None,:],bias,wqkv,projT,fc1,fc2T,gains,shifts)
    pieces=jnp.concatenate([owners(dprojT,nseq,nheads),owners(dfc1,nseq,nheads),owners(dfc2T,nseq,nheads)],axis=2)
    red_a=lax.psum_scatter(pieces,names,scatter_dimension=0,tiled=False).astype(F32)
    output=place(delta,inputs,shift)
    dd,dqkv,G,sm_b=call_b(x,gln2,qkv,g,gT,Dd,Pp,wqkv,gains,shifts)
    red_q=lax.psum_scatter(jnp.concatenate([owners(dqkv[:,c*D:(c+1)*D],nseq,nheads) for c in range(3)],axis=2),names,scatter_dimension=0,tiled=False).astype(F32)
    d_inputs=place(dd,out_grad,shift)
    tab=call_c(G,posT,T,NH)
    tab,small=lax.psum((tab,sm_a+sm_b),names)
    d_qkv=red_q.reshape(rows,3,cq).transpose(1,0,2)
    d_proj=red_a[:,:cq].T; d_fc1=red_a[:,cq:cq+cf]; d_fc2=red_a[:,cq+cf:].T
    nl=rel_table.shape[0]
    d_table=lax.dynamic_slice_in_dim(tab,me*nl,nl,0)
    return (output,d_inputs,d_qkv,d_proj,d_fc1,d_fc2,small[0:2],small[2:6],d_table)

def solution(mesh):
    placed=(P("seq",None),P(None,"seq","heads"),P("heads","seq"),P("seq","heads"),P("heads","seq"),P(),P(),P("heads",None),P("seq"),P(),P("seq",None))
    return jax.shard_map(body,mesh=mesh,in_specs=placed,
        out_specs=(P("seq",None),P("seq",None),P(None,"seq","heads"),P("heads","seq"),P("seq","heads"),P("heads","seq"),P(),P(),P("heads",None)),
        check_vma=False)
```

```python
import functools
import math

import jax, jax.numpy as jnp
from jax import lax
from jax.experimental import pallas as pl
from jax.experimental.pallas import tpu as pltpu
from jax.sharding import PartitionSpec as P

BF=jnp.bfloat16; F32=jnp.float32
HD=32; GROUP=128; PER=4
EPS=1e-5
SQ=math.sqrt(32.0)
CEXP=math.log2(math.e)/SQ
MASK=100.0*SQ

def mm(a,b):
    return lax.dot_general(a,b,(((1,),(0,)),((),())),preferred_element_type=F32)
def mm_nt(a,b):
    return lax.dot_general(a,b,(((1,),(1,)),((),())),preferred_element_type=F32)

def norm_stats(v):
    mean=jnp.mean(v,axis=-1,keepdims=True)
    c=v-mean
    var=jnp.mean(c*c,axis=-1,keepdims=True)
    rstd=lax.rsqrt(var+EPS)
    return c*rstd, rstd

def norm_back(gy,xhat,rstd,gain):
    gx=gy*gain
    m1=jnp.mean(gx,axis=-1,keepdims=True)
    m2=jnp.mean(gx*xhat,axis=-1,keepdims=True)
    return rstd*(gx-m1-xhat*m2)

P0=0.3275911
A1,A2,A3,A4,A5=0.254829592,-0.284496736,1.421413741,-1.453152027,1.061405429
def gelu_both(x):
    e=jnp.exp2(x*x*(-0.5*math.log2(math.e)))
    t=1.0/(1.0+(P0/math.sqrt(2.0))*jnp.abs(x))
    poly=t*(0.5*A1+t*(0.5*A2+t*(0.5*A3+t*(0.5*A4+t*(0.5*A5)))))
    half=poly*e
    phi=jnp.where(x>=0,1.0-half,half)
    return x*phi, phi+x*e*(1.0/math.sqrt(2.0*math.pi))

def kernel_a(nheads,x_ref,og_ref,labc_ref,labr_ref,bias_ref,W_ref,gains_ref,shifts_ref,
             delta_ref,gln2_ref,qkv_ref,g_ref,gT_ref,D_ref,P_hbm,dcat_ref,small_ref,
             qT_s,vT_s,OT_s,P_s,acc,sem,xn2_s,xn2T_s,tg_s,tgT_s,up_s,gn2_s):
    w=pl.program_id(0); nw=pl.num_programs(0)
    D=x_ref.shape[-1]; WIN=x_ref.shape[-2]
    parts=W_ref.shape[0]; cq=D//parts; cf=(W_ref.shape[2]-4*cq)//2
    groups=nheads//PER
    x=x_ref[0]
    xhat,_=norm_stats(x)
    xn=(xhat*gains_ref[0:1,:]+shifts_ref[0:1,:]).astype(BF)
    for c in range(3):
        for m in range(parts):
            at=slice(m*cq,(m+1)*cq)
            y=mm(xn,W_ref[m,:,c*cq:(c+1)*cq]).astype(BF)
            qkv_ref[0,c,:,at]=y
            if c==0: qT_s[at,:]=y.T
            if c==2: vT_s[at,:]=y.T
    labc=labc_ref[0]; labr=labr_ref[0]
    lane=lax.broadcasted_iota(jnp.int32,(WIN,GROUP),1)
    oh=jnp.where((labc==lane)|((labc+3)==lane),1.0,0.0).astype(BF)
    hi=564.0
    lo=MASK-hi
    sub=lax.broadcasted_iota(jnp.int32,(GROUP,WIN),0)
    nm=jnp.where(sub<3,jnp.where(sub!=labr,-hi,0.0),jnp.where(sub<6,jnp.where(sub-3!=labr,-lo,0.0),0.0)).astype(BF)
    hl=lane//HD

    def group(gi,_):
        slot=gi%2
        step=w*groups+gi
        @pl.when(step>=2)
        def _():
            pltpu.make_async_copy(P_s.at[slot],P_hbm.at[0,pl.ds(0,PER)],sem.at[slot]).wait()
        o=pl.multiple_of(gi*GROUP,GROUP)
        qTg=jnp.concatenate([qT_s[pl.ds(o,GROUP),:],nm],axis=0)
        kg=qkv_ref[0,1,:,pl.ds(o,GROUP)]
        for hh in range(PER):
            kh=jnp.concatenate([jnp.where(hl==hh,kg,jnp.zeros_like(kg)),oh],axis=1)
            t=mm(kh,qTg)+bias_ref[gi*PER+hh]
            m=jnp.max(t,axis=0,keepdims=True)
            e=jnp.exp2((t-m)*CEXP)
            l=jnp.sum(e,axis=0,keepdims=True)
            p=(e*(1.0/l)).astype(BF)
            P_s[slot,hh]=p
            OT_s[pl.ds(o+hh*HD,HD),:]=mm(vT_s[pl.ds(o+hh*HD,HD),:],p)
        pltpu.make_async_copy(P_s.at[slot],P_hbm.at[w,pl.ds(gi*PER,PER)],sem.at[slot]).start()
        return 0
    lax.fori_loop(0,groups,group,0)

    attn=OT_s[...].astype(BF).T
    branch=shifts_ref[2:3,:]
    for m in range(parts):
        branch=branch+mm_nt(attn[:,m*cq:(m+1)*cq],W_ref[m,:,3*cq:4*cq])
    branch=branch.astype(BF).astype(F32)
    middle=x+branch
    xhat2,rstd2=norm_stats(middle)
    xn2=(xhat2*gains_ref[1:2,:]+shifts_ref[1:2,:]).astype(BF)
    og=og_ref[0]
    tg=og.astype(BF)
    xn2_s[...]=xn2; xn2T_s[...]=xn2.T; tg_s[...]=tg; tgT_s[...]=tg.T
    up_s[...]=jnp.zeros_like(up_s); gn2_s[...]=jnp.zeros_like(gn2_s)
    CH=min(512,cf); each=cf//CH
    @pl.when(w==0)
    def _():
        acc[...]=jnp.zeros_like(acc)
        small_ref[...]=jnp.zeros_like(small_ref)
    def chunk(c,_):
        m=c//each
        o=pl.multiple_of((c%each)*CH,CH)
        f1=W_ref[m,:,pl.ds(4*cq+o,CH)]; f2=W_ref[m,:,pl.ds(4*cq+cf+o,CH)]
        hid=mm(xn2_s[...],f1)
        act,dact=gelu_both(hid)
        a=act.astype(BF)
        up_s[...]+=mm_nt(a,f2)
        gh=(mm(tg_s[...],f2)*dact).astype(BF)
        gn2_s[...]+=mm_nt(gh,f1)
        acc[m,:,pl.ds(cq+o,CH)]+=mm(xn2T_s[...],gh)
        acc[m,:,pl.ds(cq+cf+o,CH)]+=mm(tgT_s[...],a)
        return 0
    lax.fori_loop(0,parts*each,chunk,0)
    delta_ref[0]=(branch+up_s[...]+shifts_ref[3:4,:]).astype(BF)
    gn2=gn2_s[...]
    gln2=norm_back(gn2,xhat2,rstd2,gains_ref[1:2,:])
    gln2_ref[0]=gln2
    gb=(og+gln2).astype(BF)
    gbT=gb.T
    for m in range(parts):
        at=slice(m*cq,(m+1)*cq)
        acc[m,:,0:cq]+=mm(gbT,attn[:,at])
        g=mm(gb,W_ref[m,:,3*cq:4*cq]).astype(BF)
        g_ref[0,:,at]=g
        gT=g.T
        gT_ref[0,at,:]=gT
        prod=gT.astype(F32)*OT_s[at,:]
        nh=nheads//parts
        D_ref[0,m*nh:(m+1)*nh,:]=jnp.sum(prod.reshape(nh,HD,WIN),axis=1)
    small_ref[1:2,:]+=jnp.sum(gn2*xhat2,axis=0,keepdims=True)
    small_ref[3:4,:]+=jnp.sum(gn2,axis=0,keepdims=True)
    small_ref[4:5,:]+=jnp.sum(gb.astype(F32),axis=0,keepdims=True)
    small_ref[5:6,:]+=jnp.sum(tg.astype(F32),axis=0,keepdims=True)
    @pl.when(w==nw-1)
    def _():
        dcat_ref[...]=acc[...].astype(BF)
        for s in range(2):
            pltpu.make_async_copy(P_s.at[s],P_hbm.at[0,pl.ds(0,PER)],sem.at[s]).wait()

def full(shape,**kw):
    return pl.BlockSpec(shape,lambda w:(0,)*len(shape),**kw)
def per(shape):
    return pl.BlockSpec((1,)+shape,lambda w:(w,)+(0,)*len(shape))
ONE=pl.Buffered(1)
ANY=pl.BlockSpec(memory_space=pl.ANY)

def call_a(x,og,labc,labr,bias,W,gains,shifts):
    nW,WIN,D=x.shape; NH=bias.shape[0]
    parts,_,Ct=W.shape; Cg=Ct-3*(D//parts)
    sd=jax.ShapeDtypeStruct
    outs=[sd((nW,WIN,D),BF),sd((nW,WIN,D),F32),sd((nW,3,WIN,D),BF),sd((nW,WIN,D),BF),sd((nW,D,WIN),BF),sd((nW,NH,WIN),F32),
          sd((nW,NH,WIN,WIN),BF),sd((parts,D,Cg),BF),sd((8,D),F32)]
    return pl.pallas_call(functools.partial(kernel_a,NH),grid=(nW,),
      in_specs=[per((WIN,D)),per((WIN,D)),per((WIN,1)),per((1,WIN)),full((NH,WIN,WIN),pipeline_mode=ONE),
        full((parts,D,Ct),pipeline_mode=ONE),full(gains.shape),full(shifts.shape)],
      out_specs=[per((WIN,D)),per((WIN,D)),per((3,WIN,D)),per((WIN,D)),per((D,WIN)),per((NH,WIN)),ANY,full((parts,D,Cg)),full((8,D))],
      out_shape=outs,
      scratch_shapes=[pltpu.VMEM((D,WIN),BF),pltpu.VMEM((D,WIN),BF),pltpu.VMEM((D,WIN),F32),pltpu.VMEM((2,PER,WIN,WIN),BF),
        pltpu.VMEM((parts,D,Cg),F32),pltpu.SemaphoreType.DMA((2,)),
        pltpu.VMEM((WIN,D),BF),pltpu.VMEM((D,WIN),BF),pltpu.VMEM((WIN,D),BF),pltpu.VMEM((D,WIN),BF),pltpu.VMEM((WIN,D),F32),pltpu.VMEM((WIN,D),F32)],
      compiler_params=pltpu.CompilerParams(vmem_limit_bytes=62*1024*1024,dimension_semantics=("arbitrary",)),
      name="kernel_a")(x,og,labc,labr,bias,W,gains,shifts)

def kernel_b(nheads,linked,x_ref,gln2_ref,qkv_ref,g_ref,gT_ref,D_ref,P_ref,W_ref,gains_ref,shifts_ref,delta_hbm,dcat_hbm,
             dd_hbm,dqkv_ref,G_hbm,small_ref,od_hbm,odd_hbm,mid_hbm,
             G_s,aq,kT_s,gq_s,gqT_s,sem,dd_s,dl,ds,dr,*red_scratch):
    w=pl.program_id(0); nw=pl.num_programs(0)
    D=x_ref.shape[-1]; WIN=x_ref.shape[-2]
    parts=W_ref.shape[0]; cq=D//parts
    groups=nheads//PER
    if linked:
        z,xx,cc,yy=place_of()
        mate=dev(z,xx,cc,1-yy)
        red=Reduce(dcat_hbm,None,*red_scratch)
        give=send(delta_hbm,od_hbm,ds.at[nw_of(delta_hbm)],dr.at[nw_of(delta_hbm)],mate)
        @pl.when(w==0)
        def _():
            greet(peers_of(z,xx,cc,yy))
            red.start()
            give.start()
    @pl.when(w==0)
    def _():
        aq[...]=jnp.zeros_like(aq); G_s[...]=jnp.zeros_like(G_s); small_ref[...]=jnp.zeros_like(small_ref)
    kT_s[...]=qkv_ref[0,1].T
    lane=lax.broadcasted_iota(jnp.int32,(WIN,GROUP),1)
    hl=lane//HD
    def group(gi,_):
        o=pl.multiple_of(gi*GROUP,GROUP)
        gTg=gT_ref[0,pl.ds(o,GROUP),:]
        vg=qkv_ref[0,2,:,pl.ds(o,GROUP)]
        qg=qkv_ref[0,0,:,pl.ds(o,GROUP)]
        gg=g_ref[0,:,pl.ds(o,GROUP)]
        dv=jnp.zeros((WIN,GROUP),F32); dk=jnp.zeros((WIN,GROUP),F32)
        zero=jnp.zeros_like(vg)
        for hh in range(PER):
            h=gi*PER+hh
            p=P_ref[0,h]
            dp=mm(jnp.where(hl==hh,vg,zero),gTg)
            ds_=p.astype(F32)*(dp-D_ref[0,pl.ds(h,1),:])
            for c in range(G_s.shape[0]):
                wd=min(128,WIN-c*128)
                G_s[c,pl.ds(pl.multiple_of(h*WIN,8),WIN),:wd]+=ds_[:,c*128:c*128+wd]
            dsl=ds_.astype(BF)
            dv+=mm(p,jnp.where(hl==hh,gg,zero))
            dk+=mm(dsl,jnp.where(hl==hh,qg,zero))
            gqT_s[pl.ds(o+hh*HD,HD),:]=mm(kT_s[pl.ds(o+hh*HD,HD),:],dsl)
        gq_s[1,:,pl.ds(o,GROUP)]=(dk*(1.0/SQ)).astype(BF)
        gq_s[2,:,pl.ds(o,GROUP)]=dv.astype(BF)
        return 0
    lax.fori_loop(0,groups,group,0)
    gq_s[0]=(gqT_s[...]*(1.0/SQ)).astype(BF).T
    x=x_ref[0]
    xhat,rstd=norm_stats(x)
    xn=(xhat*gains_ref[0:1,:]+shifts_ref[0:1,:]).astype(BF)
    xnT=xn.T
    gr=jnp.zeros((WIN,D),F32)
    for m in range(parts):
        for c in range(3):
            gc=gq_s[c,:,m*cq:(m+1)*cq]
            gr=gr+mm_nt(gc,W_ref[m,:,c*cq:(c+1)*cq])
            aq[m,:,c*cq:(c+1)*cq]+=mm(xnT,gc)
    dd_s[w]=(gln2_ref[0]+norm_back(gr,xhat,rstd,gains_ref[0:1,:])).astype(BF)
    keep=pltpu.make_async_copy(dd_s.at[w],dd_hbm.at[w],dl.at[w]); keep.start()
    if linked:
        send(dd_s.at[w],odd_hbm.at[w],ds.at[w],dr.at[w],mate).start()
        pl.when(w==0)(red.one)
    small_ref[0:1,:]+=jnp.sum(gr*xhat,axis=0,keepdims=True)
    small_ref[2:3,:]+=jnp.sum(gr,axis=0,keepdims=True)
    @pl.when(w==nw-1)
    def _():
        dqkv_ref[...]=aq[...].astype(BF)
        cp=pltpu.make_async_copy(G_s,G_hbm,sem.at[0]); cp.start()
        if linked:
            red.half(mid_hbm,sem.at[1])
        for k in range(nw_of(dd_s)):
            pltpu.make_async_copy(dd_s.at[k],dd_hbm.at[k],dl.at[k]).wait()
            if linked:
                send(dd_s.at[k],odd_hbm.at[k],ds.at[k],dr.at[k],mate).wait()
        if linked:
            give.wait()
        cp.wait()

def nw_of(ref):
    return ref.shape[0]

def call_b(linked,x,gln2,qkv,g,gT,Dd,Pp,W,gains,shifts,delta,dcat):
    nW,WIN,D=x.shape; NH=Dd.shape[1]
    parts=W.shape[0]; cq=D//parts; tiles=-(-WIN//128)
    sd=jax.ShapeDtypeStruct; dma=pltpu.SemaphoreType.DMA
    rows,cols=dcat.shape[-2:]
    row=sd((nW,WIN,D),BF) if linked else sd((8,128),BF)
    mid=sd((4,2,rows,cols),BF) if linked else sd((8,128),BF)
    return pl.pallas_call(functools.partial(kernel_b,NH,linked),grid=(nW,),
      in_specs=[per((WIN,D)),per((WIN,D)),per((3,WIN,D)),per((WIN,D)),per((D,WIN)),per((NH,WIN)),per((NH,WIN,WIN)),
        full((parts,D,3*cq),pipeline_mode=ONE),full(gains.shape),full(shifts.shape),ANY,ANY],
      out_specs=[ANY,full((parts,D,3*cq)),ANY,full((8,D)),ANY,ANY,ANY],
      out_shape=[sd((nW,WIN,D),BF),sd((parts,D,3*cq),BF),sd((tiles,NH*WIN,128),F32),sd((8,D),F32),row,row,mid],
      scratch_shapes=[pltpu.VMEM((tiles,NH*WIN,128),F32),pltpu.VMEM((parts,D,3*cq),F32),pltpu.VMEM((D,WIN),BF),pltpu.VMEM((3,WIN,D),BF),pltpu.VMEM((D,WIN),F32),
        dma((2,)),pltpu.VMEM((nW,WIN,D),BF),dma((nW,)),dma((nW+1,)),dma((nW+1,))]+(reduce_scratch(rows,cols,False) if linked else []),
      compiler_params=pltpu.CompilerParams(vmem_limit_bytes=62*1024*1024,dimension_semantics=("arbitrary",),**(dict(collective_id=2,has_side_effects=True) if linked else {})),
      name="kernel_b")(x,gln2,qkv,g,gT,Dd,Pp,W,gains,shifts,delta,dcat)

FIX=8191.0

def pack_table(table):
    NH,T=table.shape
    n=-(-T//128)
    q=jnp.round(jnp.clip(table,-4.0,4.0)*FIX).astype(jnp.int32)
    q=jnp.pad(q,((0,0),(0,n*128-T)))
    q=q.reshape(NH//2,2,n,128)
    return (q[:,0]*65536)|(q[:,1]&65535)

def kernel_p(pos_ref,tab_ref,bias_ref):
    npair,n,_=tab_ref.shape
    WIN=bias_ref.shape[-1]
    tiles=-(-WIN//128)
    def row(r,_):
        r8=pl.multiple_of(r*8,8)
        for c in range(tiles):
            width=min(128,WIN-c*128)
            idx=pos_ref[pl.ds(r8,8),c*128:(c+1)*128]
            lo=idx&127; hi=idx>>7
            masks=[hi==k for k in range(n)]
            for p in range(npair):
                acc=jnp.zeros((8,128),jnp.int32)
                for k in range(n):
                    src=jnp.broadcast_to(tab_ref[p,k:k+1,:],(8,128))
                    acc=jnp.where(masks[k],jnp.take_along_axis(src,lo,axis=1),acc)
                a=(acc>>16).astype(F32)*(SQ/FIX)
                b=((acc<<16)>>16).astype(F32)*(SQ/FIX)
                bias_ref[2*p,pl.ds(r8,8),c*128:c*128+width]=a[:,:width]
                bias_ref[2*p+1,pl.ds(r8,8),c*128:c*128+width]=b[:,:width]
        return 0
    lax.fori_loop(0,bias_ref.shape[1]//8,row,0)

def call_p(posT_pad,tab,WIN):
    NH=tab.shape[0]*2
    return pl.pallas_call(kernel_p,out_shape=jax.ShapeDtypeStruct((NH,WIN,WIN),F32),
      compiler_params=pltpu.CompilerParams(vmem_limit_bytes=40*1024*1024),name="kernel_p")(posT_pad,tab)

def kernel_t(NH,G_ref,hi_ref,lo_ref,out_ref):
    WIN=hi_ref.shape[0]; LW=G_ref.shape[0]*128
    nh=out_ref.shape[0]//NH
    out_ref[...]=jnp.zeros_like(out_ref)
    def rows(r,_):
        r8=pl.multiple_of(r*8,8)
        hi8=hi_ref[pl.ds(r8,8),:]; lo8=lo_ref[pl.ds(r8,8),:]
        tot=jnp.zeros(out_ref.shape,F32)
        iota=lax.broadcasted_iota(jnp.int32,(256,LW),0).astype(F32).astype(BF)
        for k in range(8):
            g=jnp.concatenate([G_ref[c,pl.ds(r8+k,NH,stride=WIN),:] for c in range(LW//128)],axis=1)
            hr=hi8[k:k+1,:]; lr=lo8[k:k+1,:].astype(F32).astype(BF)
            A=jnp.concatenate([jnp.where(hr==m,g,0.0) for m in range(nh)],axis=0).astype(BF)
            oh=jnp.where(iota==lr,jnp.ones((),BF),jnp.zeros((),BF))
            tot=tot+lax.dot_general(A,oh,(((1,),(1,)),((),())),preferred_element_type=F32)
        out_ref[...]+=tot
        return 0
    lax.fori_loop(0,WIN//8,rows,0)

def call_t(G,posT,T,NH):
    WIN=posT.shape[0]; nt=G.shape[0]
    nh=-(-T//256)
    pp=jnp.pad(posT,((0,0),(0,nt*128-WIN)),constant_values=nh*256)
    hi=pp>>8; lo=pp&255
    o=pl.pallas_call(functools.partial(kernel_t,NH),out_shape=jax.ShapeDtypeStruct((nh*NH,256),F32),
      compiler_params=pltpu.CompilerParams(vmem_limit_bytes=40*1024*1024),name="kernel_t")(G,hi,lo)
    return o.reshape(nh,NH,256).transpose(1,0,2).reshape(NH,nh*256)[:,:T]


MESHID=pl.DeviceIdType.MESH

def place_of():
    s=lax.axis_index("seq"); y=lax.axis_index("heads")
    return s//4,(s//2)%2,s%2,y

def dev(z,x,c,y):
    return ((z*2+x)*2+c,y)

def peers_of(z,x,c,y):
    return [dev(z,x,1-c,y),dev(z,1-x,c,y),dev(z,x,c,1-y)]+[dev((z+i)%4,x,c,y) for i in (1,2,3)]

def greet(devices):
    bar=pltpu.get_barrier_semaphore()
    for d in devices:
        pl.semaphore_signal(bar,inc=1,device_id=d,device_id_type=MESHID)
    pl.semaphore_wait(bar,len(devices))

def send(src,dst,ss,rs,to):
    return pltpu.make_async_remote_copy(src_ref=src,dst_ref=dst,send_sem=ss,recv_sem=rs,device_id=to,device_id_type=MESHID)

def kernel_w(w_ref,pos_ref,tab_ref,W_hbm,bias_hbm,bias_s,ss,rs,bs,br,bl,own):
    z,x,c,y=place_of()
    greet(peers_of(z,x,c,y))
    npair,n=tab_ref.shape[1],tab_ref.shape[2]
    half=2*npair
    WIN=bias_s.shape[-1]; tiles=-(-WIN//128)
    xa=x+(1-2*x)*(1-c); ya=y+(1-2*y)*c
    xb=x+(1-2*x)*c; yb=y+(1-2*y)*(1-c)
    sib=dev(z,x,1-c,y); pa=dev(z,xa,c,ya); pb=dev(z,xb,c,yb)
    started=[]
    def go(src,zz,xx,yy,k,to):
        cp=send(src,W_hbm.at[yy,zz,xx,c],ss.at[k],rs.at[k],to); cp.start(); started.append(cp)
    def came(zz,xx,cc,yy,k):
        send(w_ref,W_hbm.at[yy,zz,xx,cc],ss.at[k],rs.at[k],sib).wait_recv()
    mine=pltpu.make_async_copy(w_ref,W_hbm.at[y,z,x,c],own); mine.start()
    for i in (1,2,3):
        go(w_ref,z,x,y,i-1,dev((z+i)%4,x,c,y))
    go(w_ref,z,x,y,3,pa); go(w_ref,z,x,y,7,pb); go(w_ref,z,x,y,15,sib)
    def zof(i): return (z+4-i)%4
    def turn_z(i):
        zz=zof(i); came(zz,x,c,y,i-1)
        blk=W_hbm.at[y,zz,x,c]
        go(blk,zz,x,y,3+i,pa); go(blk,zz,x,y,7+i,pb); go(blk,zz,x,y,15+i,sib)
    def turn_a(i):
        zz=zof(i); came(zz,xa,c,ya,3+i)
        blk=W_hbm.at[ya,zz,xa,c]
        go(blk,zz,xa,ya,11+i,pb); go(blk,zz,xa,ya,19+i,sib)
    def turn_b(i):
        zz=zof(i); came(zz,xb,c,yb,7+i)
        go(W_hbm.at[yb,zz,xb,c],zz,xb,yb,23+i,sib)
    def turn_ab(i):
        zz=zof(i); came(zz,1-x,c,1-y,11+i)
        go(W_hbm.at[1-y,zz,1-x,c],zz,1-x,1-y,27+i,sib)
    nrow=WIN//8
    steps=7
    cuts=[nrow*k//steps for k in range(steps+1)]
    sends=[]
    def rows(k):
        def row(r,_):
            r8=pl.multiple_of(r*8,8)
            for t in range(tiles):
                width=min(128,WIN-t*128)
                idx=pos_ref[pl.ds(r8,8),t*128:(t+1)*128]
                lo=idx&127; hi=idx>>7
                masks=[hi==q for q in range(n)]
                for p in range(npair):
                    acc=jnp.zeros((8,128),jnp.int32)
                    for q in range(n):
                        src=jnp.broadcast_to(tab_ref[c,p,q:q+1,:],(8,128))
                        acc=jnp.where(masks[q],jnp.take_along_axis(src,lo,axis=1),acc)
                    a=(acc>>16).astype(F32)*(SQ/FIX)
                    b=((acc<<16)>>16).astype(F32)*(SQ/FIX)
                    bias_s[2*p,pl.ds(r8,8),t*128:t*128+width]=a[:,:width]
                    bias_s[2*p+1,pl.ds(r8,8),t*128:t*128+width]=b[:,:width]
            return 0
        lax.fori_loop(cuts[k],cuts[k+1],row,0)
        rr=pl.ds(cuts[k]*8,(cuts[k+1]-cuts[k])*8)
        cp=pltpu.make_async_copy(bias_s.at[:,rr],bias_hbm.at[pl.ds(c*half,half),rr],bl.at[k]); cp.start()
        rc=send(bias_s.at[:,rr],bias_hbm.at[pl.ds(c*half,half),rr],bs.at[k],br.at[k],sib); rc.start()
        sends.append((cp,rc))
    rows(0)
    turn_z(1); turn_z(3)
    rows(1)
    turn_z(2); turn_a(0); turn_b(0)
    rows(2)
    for i in (1,3): turn_a(i); turn_b(i)
    rows(3)
    for i in (2,): turn_a(i); turn_b(i)
    turn_ab(0)
    rows(4)
    for i in (1,3): turn_ab(i)
    rows(5)
    turn_ab(2)
    rows(6)
    for i in range(4):
        zz=zof(i)
        came(zz,x,1-c,y,15+i); came(zz,xb,1-c,yb,19+i); came(zz,xa,1-c,ya,23+i); came(zz,1-x,1-c,1-y,27+i)
    for k in range(steps):
        rr=pl.ds(cuts[k]*8,(cuts[k+1]-cuts[k])*8)
        sends[k][0].wait(); sends[k][1].wait_send()
        send(bias_s.at[:,rr],bias_hbm.at[pl.ds((1-c)*half,half),rr],bs.at[k],br.at[k],sib).wait_recv()
    for cp in started: cp.wait_send()
    mine.wait()

def call_w(wcat,posT_pad,tab,WIN):
    rows,cols=wcat.shape; npair=tab.shape[1]
    return pl.pallas_call(kernel_w,
      out_shape=[jax.ShapeDtypeStruct((2,4,2,2,rows,cols),BF),jax.ShapeDtypeStruct((4*npair,WIN,WIN),F32)],
      in_specs=[pl.BlockSpec(memory_space=pl.ANY),pl.BlockSpec(memory_space=pltpu.VMEM),pl.BlockSpec(memory_space=pltpu.VMEM)],
      out_specs=[pl.BlockSpec(memory_space=pl.ANY)]*2,
      scratch_shapes=[pltpu.VMEM((2*npair,WIN,WIN),F32),pltpu.SemaphoreType.DMA((31,)),pltpu.SemaphoreType.DMA((31,)),
        pltpu.SemaphoreType.DMA((7,)),pltpu.SemaphoreType.DMA((7,)),pltpu.SemaphoreType.DMA((7,)),pltpu.SemaphoreType.DMA],
      compiler_params=pltpu.CompilerParams(vmem_limit_bytes=40*1024*1024,collective_id=1,has_side_effects=True),name="kernel_w")(wcat,posT_pad,tab)

class Reduce:
    def __init__(self,src,out,own,r1,r2,ss,rs,ls,r3=None,fin=None,r4=None,mid=None):
        self.src,self.out,self.own,self.r1,self.r2,self.r3,self.fin,self.r4=src,out,own,r1,r2,r3,fin,r4
        self.ss,self.rs,self.ls=ss,rs,ls
        self.at=place_of()
        self.mid=own.at[self.at[1]] if mid is None else mid
        self.whole=mid is None
    def pairs(self):
        z,x,c,y=self.at
        k=0
        for xx in range(2):
            for yy in range(2):
                yield (pltpu.make_async_copy(self.src.at[yy,:,xx,c],self.own.at[xx,:,yy],self.ls.at[k]),
                       send(self.src.at[yy,:,xx,1-c],self.r1.at[xx,:,yy],self.ss.at[k],self.rs.at[k],dev(z,x,1-c,y)))
                k+=1
    def xsend(self):
        z,x,c,y=self.at
        return send(self.own.at[1-x],self.r2,self.ss.at[4],self.rs.at[4],dev(z,1-x,c,y))
    def zsend(self,i):
        z,x,c,y=self.at
        zz=(z+i)%4
        return send(self.mid.at[zz],self.r3.at[i-1],self.ss.at[4+i],self.rs.at[4+i],dev(zz,x,c,y))
    def ysend(self):
        z,x,c,y=self.at
        return send(self.fin.at[1-y],self.r4,self.ss.at[8],self.rs.at[8],dev(z,x,c,1-y))
    def start(self):
        for a,b in self.pairs():
            a.start(); b.start()
    def add(self,dst,*srcs):
        total=srcs[0][...].astype(F32)
        for s in srcs[1:]: total=total+s[...].astype(F32)
        dst[...]=total.astype(BF)
    def one(self):
        z,x,c,y=self.at
        for a,b in self.pairs():
            a.wait(); b.wait_recv()
        def step(xx):
            def add(k,_):
                at=(xx,k//2,k%2)
                self.add(self.own.at[at],self.own.at[at],self.r1.at[at])
                return 0
            lax.fori_loop(0,8,add,0)
        step(1-x)
        self.xsend().start()
        step(x)
    def summed(self):
        z,x,c,y=self.at
        def add(k,_):
            at=(k//2,k%2)
            self.add(self.own.at[(x,)+at],self.own.at[(x,)+at],self.r2.at[at])
            return 0
        lax.fori_loop(0,8,add,0)
    def half(self,hbm,sem):
        self.xsend().wait_recv()
        self.summed()
        cp=pltpu.make_async_copy(self.mid,hbm,sem); cp.start(); cp.wait()
        self.left()
    def left(self):
        for a,b in self.pairs(): b.wait_send()
        self.xsend().wait_send()
    def zstart(self):
        for i in (2,1,3): self.zsend(i).start()
    def two(self):
        self.xsend().wait_recv()
        self.summed()
        self.zstart()
    def three(self):
        z,x,c,y=self.at
        for i in (1,2,3):
            self.zsend(i).wait_recv()
        def step(yy):
            self.add(self.fin.at[yy],self.mid.at[z,yy],*[self.r3.at[i,yy] for i in range(3)])
        step(1-y)
        self.ysend().start()
        step(y)
    def four(self):
        z,x,c,y=self.at
        self.ysend().wait_recv()
        self.out[...]=self.fin[y].astype(F32)+self.r4[...].astype(F32)
        if self.whole: self.left()
        for i in (1,2,3): self.zsend(i).wait_send()
        self.ysend().wait_send()

def reduce_scratch(rows,cols,last=True,first=True):
    v=lambda *d: pltpu.VMEM(d+(rows,cols),BF)
    return ((([v(2,4,2),v(2,4,2),v(4,2)]) if first else [])+[pltpu.SemaphoreType.DMA((9,)),pltpu.SemaphoreType.DMA((9,)),pltpu.SemaphoreType.DMA((4,))]
            +([v(3,2),v(2),v()] if last else []))

def kernel_c(NH,G_ref,hi_ref,lo_ref,small_ref,dq_hbm,mid_ref,redq_ref,redm_ref,tab_ref,sum_ref,acc,tk,tr,sr,ts,tq,own,r1,r2,ss,rs,ls,r3,fin,r4,ss2,rs2,ls2,s3,sfin,s4):
    WIN=hi_ref.shape[0]; LW=G_ref.shape[0]*128
    nh=acc.shape[0]
    z,x,c,y=place_of()
    greet(peers_of(z,x,c,y))
    red=Reduce(dq_hbm,redq_ref,own,r1,r2,ss,rs,ls,r3,fin,r4)
    big=Reduce(None,redm_ref,None,None,None,ss2,rs2,ls2,s3,sfin,s4,mid=mid_ref)
    red.start(); big.zstart()
    acc[...]=jnp.zeros_like(acc)
    def rows(r,_):
        r8=pl.multiple_of(r*8,8)
        hi8=hi_ref[pl.ds(r8,8),:]; lo8=lo_ref[pl.ds(r8,8),:]
        tot=jnp.zeros((nh*NH,256),F32)
        iota=lax.broadcasted_iota(jnp.int32,(256,LW),0).astype(F32).astype(BF)
        for k in range(8):
            g=jnp.concatenate([G_ref[q,pl.ds(r8+k,NH,stride=WIN),:] for q in range(LW//128)],axis=1)
            hr=hi8[k:k+1,:]; lr=lo8[k:k+1,:].astype(F32).astype(BF)
            A=jnp.concatenate([jnp.where(hr==m,g,0.0) for m in range(nh)],axis=0).astype(BF)
            oh=jnp.where(iota==lr,jnp.ones((),BF),jnp.zeros((),BF))
            tot=tot+mm_nt(A,oh)
        acc[...]+=tot.reshape(acc.shape)
        return 0
    n=WIN//8
    cuts=[0,n*6//49,n*20//49,n*36//49,n*44//49,n]
    for k,f in enumerate((red.one,red.two,big.three,red.three,big.four)):
        lax.fori_loop(cuts[k],cuts[k+1],rows,0)
        f()
    red.four()
    half=NH//2
    cps=(send(acc.at[:,pl.ds((1-y)*half,half)],tr.at[0],ts.at[0],tq.at[0],dev(z,x,c,1-y)),send(small_ref,sr.at[0],ts.at[1],tq.at[1],dev(z,x,c,1-y)))
    for p in cps: p.start()
    for p in cps: p.wait()
    tk[0]=acc[:,pl.ds(pl.multiple_of(y*half,8),half)]+tr[0]
    small=small_ref[...]+sr[0]
    for k,to in ((1,dev(z,x,1-c,y)),(2,dev(z,1-x,c,y))):
        sr[6+k]=small
        cps=(send(tk.at[k-1],tr.at[k],ts.at[2*k],tq.at[2*k],to),send(sr.at[6+k],sr.at[k],ts.at[2*k+1],tq.at[2*k+1],to))
        for p in cps: p.start()
        for p in cps: p.wait()
        tk[k]=tk[k-1]+tr[k]
        small=small+sr[k]
    sr[9]=small
    cps=[]
    for i in (1,2,3):
        to=dev((z+i)%4,x,c,y); k=2+i
        cps+=[send(tk.at[2],tr.at[k],ts.at[2*k],tq.at[2*k],to),send(sr.at[9],sr.at[k],ts.at[2*k+1],tq.at[2*k+1],to)]
    for p in cps: p.start()
    for p in cps: p.wait()
    tab_ref[...]=tk[2]+tr[3]+tr[4]+tr[5]
    sum_ref[...]=small+sr[3]+sr[4]+sr[5]

def call_c(G,posT,T,NH,small,dq,mid):
    WIN=posT.shape[0]; nt=G.shape[0]
    nh=-(-T//256)
    rows,cols=dq.shape[-2:]; more=mid.shape[-1]
    pp=jnp.pad(posT,((0,0),(0,nt*128-WIN)),constant_values=nh*256)
    hi=pp>>8; lo=pp&255
    vm=pl.BlockSpec(memory_space=pltpu.VMEM)
    redq,redm,tab,sm=pl.pallas_call(functools.partial(kernel_c,NH),
      out_shape=[jax.ShapeDtypeStruct((rows,cols),F32),jax.ShapeDtypeStruct((rows,more),F32),jax.ShapeDtypeStruct((nh,NH//2,256),F32),jax.ShapeDtypeStruct(small.shape,F32)],
      in_specs=[vm,vm,vm,vm,ANY,vm],out_specs=[vm]*4,
      scratch_shapes=[pltpu.VMEM((nh,NH,256),F32)]+[pltpu.VMEM((3,nh,NH//2,256),F32),pltpu.VMEM((6,nh,NH//2,256),F32),
        pltpu.VMEM((10,)+small.shape,F32),pltpu.SemaphoreType.DMA((12,)),pltpu.SemaphoreType.DMA((12,))]+reduce_scratch(rows,cols)+reduce_scratch(rows,more,True,False),
      compiler_params=pltpu.CompilerParams(vmem_limit_bytes=60*1024*1024,collective_id=3,has_side_effects=True),name="kernel_c")(G,hi,lo,small,dq,mid)
    return redq,redm,tab.transpose(1,0,2).reshape(NH//2,nh*256)[:,:T],sm

def gathered(piece,names,nseq,nheads):
    full=lax.all_gather(piece,names,axis=0,tiled=False)
    return full.reshape((nseq,nheads)+piece.shape)

def natural(block):
    s,h,r,c=block.shape
    return block.transpose(0,2,1,3).reshape(s*r,h*c)

def owners(grad,nseq,nheads):
    r,c=grad.shape
    return grad.reshape(nseq,r//nseq,nheads,c//nheads).transpose(0,2,1,3).reshape(nseq*nheads,r//nseq,c//nheads)

def from_next(rows):
    n=lax.axis_size("seq")
    return lax.ppermute(rows,"seq",[(i,(i-1)%n) for i in range(n)])

def to_next(rows):
    n=lax.axis_size("seq")
    return lax.ppermute(rows,"seq",[(i,(i+1)%n) for i in range(n)])

def spread(rows):
    n=lax.axis_size("heads")
    flat=rows.reshape(-1,rows.shape[-1])
    if n==2:
        other=lax.ppermute(flat,"heads",[(0,1),(1,0)])
        me=lax.axis_index("heads")
        return jnp.where(me==0,jnp.concatenate([flat,other]),jnp.concatenate([other,flat]))
    return lax.all_gather(flat,"heads",axis=0,tiled=True)

def place(rows,other,base,shift):
    if other is None:
        every=spread(rows)
    else:
        a,b=[v.reshape(-1,v.shape[-1]) for v in (rows,other)]
        me=lax.axis_index("heads")
        every=jnp.where(me==0,jnp.concatenate([a,b]),jnp.concatenate([b,a]))
    keep=every.shape[0]-shift
    moved=jnp.concatenate([to_next(every[keep:]),every[:keep]])
    return base+moved.astype(F32)

def body(inputs,w_qkv,w_proj,w_fc1,w_fc2,gains,shifts,rel_table,region,pos_index,out_grad):
    nseq=lax.axis_size("seq"); nheads=lax.axis_size("heads"); me=lax.axis_index("heads")
    linked=nseq==16 and nheads==2
    names=("seq","heads")
    tok,D=inputs.shape; WIN=pos_index.shape[0]; shift=WIN//2; T=rel_table.shape[1]
    nW=tok//WIN//nheads
    rows=w_qkv.shape[1]; cq=w_qkv.shape[2]; cf=w_fc1.shape[1]
    wcat=jnp.concatenate([w_qkv[0],w_qkv[1],w_qkv[2],w_proj.T,w_fc1,w_fc2.T],axis=1).astype(BF)
    table=lax.all_gather(rel_table,"heads",axis=0,tiled=True)
    NH=table.shape[0]
    posT=pos_index.T
    wide=-(-WIN//128)*128
    posP=jnp.pad(posT,((0,0),(0,wide-WIN)))
    tab=pack_table(table)
    if linked:
        W,bias=call_w(wcat,posP,tab.reshape((2,tab.shape[0]//2)+tab.shape[1:]),WIN)
        W=W.reshape(nheads,D,-1)
    else:
        every=gathered(wcat,names,nseq,nheads)
        ends=[i*cq for i in range(5)]+[4*cq+cf,4*cq+2*cf]
        W=jnp.concatenate([natural(every[...,a:b]) for a,b in zip(ends[:-1],ends[1:])],axis=1)[None]
        bias=call_p(posP,tab,WIN)
    start=me*nW*WIN
    def mine(v):
        ext=jnp.concatenate([v,from_next(v[:shift])])
        return lax.dynamic_slice_in_dim(ext,start+shift,nW*WIN,0).reshape(nW,WIN,-1)
    x=mine(inputs); og=mine(out_grad)
    lab=lax.dynamic_slice_in_dim(region,start,nW*WIN,0).reshape(nW,WIN)
    delta,gln2,qkv,g,gT,Dd,Pp,dcat,sm_a=call_a(x,og,lab[:,:,None],lab[:,None,:],bias,W,gains,shifts)
    if linked:
        dcat=dcat.reshape(2,4,2,2,rows,-1)
    dd,dqkv,G,sm_b,od,odd,mid=call_b(linked,x,gln2,qkv,g,gT,Dd,Pp,W,gains,shifts,delta,dcat)
    if linked:
        redq,redm,d_table,small=call_c(G,posT,T,NH,sm_a+sm_b,dqkv.reshape(2,4,2,2,rows,-1),mid)
    else:
        od=odd=None
        wide=D+2*cf*nheads
        grads=[dqkv[0,:,c*D:(c+1)*D] for c in range(3)]+[dcat[0,:,:D],dcat[0,:,D:D+cf*nheads],dcat[0,:,D+cf*nheads:]]
        red=lax.psum_scatter(jnp.concatenate([owners(v,nseq,nheads) for v in grads],axis=2),names,scatter_dimension=0,tiled=False).astype(F32)
        redq,redm=red[:,:3*cq],red[:,3*cq:]
        d_table,small=lax.psum((call_t(G,posT,T,NH),sm_a+sm_b),names)
        nl=rel_table.shape[0]
        d_table=lax.dynamic_slice_in_dim(d_table,me*nl,nl,0)
    output=place(delta,od,inputs,shift)
    d_inputs=place(dd,odd,out_grad,shift)
    d_qkv=redq.reshape(rows,3,cq).transpose(1,0,2)
    d_proj=redm[:,:cq].T; d_fc1=redm[:,cq:cq+cf]; d_fc2=redm[:,cq+cf:].T
    return (output,d_inputs,d_qkv,d_proj,d_fc1,d_fc2,small[0:2],small[2:6],d_table)

def solution(mesh):
    placed=(P("seq",None),P(None,"seq","heads"),P("heads","seq"),P("seq","heads"),P("heads","seq"),P(),P(),P("heads",None),P("seq"),P(),P("seq",None))
    return jax.shard_map(body,mesh=mesh,in_specs=placed,
        out_specs=(P("seq",None),P("seq",None),P(None,"seq","heads"),P("heads","seq"),P("seq","heads"),P("heads","seq"),P(),P(),P("heads",None)),
        check_vma=False)
```

```python
import functools
import math

import jax, jax.numpy as jnp
from jax import lax
from jax.experimental import pallas as pl
from jax.experimental.pallas import tpu as pltpu
from jax.sharding import PartitionSpec as P

BF=jnp.bfloat16; F32=jnp.float32
HD=32; GROUP=128; PER=4
EPS=1e-5
SQ=math.sqrt(32.0)
CEXP=math.log2(math.e)/SQ
MASK=100.0*SQ

def mm(a,b):
    return lax.dot_general(a,b,(((1,),(0,)),((),())),preferred_element_type=F32)
def mm_nt(a,b):
    return lax.dot_general(a,b,(((1,),(1,)),((),())),preferred_element_type=F32)

def norm_stats(v):
    mean=jnp.mean(v,axis=-1,keepdims=True)
    c=v-mean
    var=jnp.mean(c*c,axis=-1,keepdims=True)
    rstd=lax.rsqrt(var+EPS)
    return c*rstd, rstd

def norm_back(gy,xhat,rstd,gain):
    gx=gy*gain
    m1=jnp.mean(gx,axis=-1,keepdims=True)
    m2=jnp.mean(gx*xhat,axis=-1,keepdims=True)
    return rstd*(gx-m1-xhat*m2)

P0=0.3275911
A1,A2,A3,A4,A5=0.254829592,-0.284496736,1.421413741,-1.453152027,1.061405429
def gelu_both(x):
    e=jnp.exp2(x*x*(-0.5*math.log2(math.e)))
    t=1.0/(1.0+(P0/math.sqrt(2.0))*jnp.abs(x))
    poly=t*(0.5*A1+t*(0.5*A2+t*(0.5*A3+t*(0.5*A4+t*(0.5*A5)))))
    half=poly*e
    phi=jnp.where(x>=0,1.0-half,half)
    return x*phi, phi+x*e*(1.0/math.sqrt(2.0*math.pi))

def kernel_a(nheads,x_ref,og_ref,labc_ref,labr_ref,bias_ref,W_ref,gains_ref,shifts_ref,
             delta_ref,gln2_ref,qkv_ref,g_ref,gT_ref,D_ref,P_hbm,dcat_ref,small_ref,
             qT_s,vT_s,OT_s,P_s,acc,sem,xn2_s,xn2T_s,tg_s,tgT_s,up_s,gn2_s):
    w=pl.program_id(0); nw=pl.num_programs(0)
    D=x_ref.shape[-1]; WIN=x_ref.shape[-2]
    parts=W_ref.shape[0]; cq=D//parts; cf=(W_ref.shape[2]-4*cq)//2
    groups=nheads//PER
    x=x_ref[0]
    xhat,_=norm_stats(x)
    xn=(xhat*gains_ref[0:1,:]+shifts_ref[0:1,:]).astype(BF)
    for c in range(3):
        for m in range(parts):
            at=slice(m*cq,(m+1)*cq)
            y=mm(xn,W_ref[m,:,c*cq:(c+1)*cq]).astype(BF)
            qkv_ref[0,c,:,at]=y
            if c==0: qT_s[at,:]=y.T
            if c==2: vT_s[at,:]=y.T
    labc=labc_ref[0]; labr=labr_ref[0]
    lane=lax.broadcasted_iota(jnp.int32,(WIN,GROUP),1)
    oh=jnp.where((labc==lane)|((labc+3)==lane),1.0,0.0).astype(BF)
    hi=564.0
    lo=MASK-hi
    sub=lax.broadcasted_iota(jnp.int32,(GROUP,WIN),0)
    nm=jnp.where(sub<3,jnp.where(sub!=labr,-hi,0.0),jnp.where(sub<6,jnp.where(sub-3!=labr,-lo,0.0),0.0)).astype(BF)
    hl=lane//HD

    def group(gi,_):
        slot=gi%2
        step=w*groups+gi
        @pl.when(step>=2)
        def _():
            pltpu.make_async_copy(P_s.at[slot],P_hbm.at[0,pl.ds(0,PER)],sem.at[slot]).wait()
        o=pl.multiple_of(gi*GROUP,GROUP)
        qTg=jnp.concatenate([qT_s[pl.ds(o,GROUP),:],nm],axis=0)
        kg=qkv_ref[0,1,:,pl.ds(o,GROUP)]
        for hh in range(PER):
            kh=jnp.concatenate([jnp.where(hl==hh,kg,jnp.zeros_like(kg)),oh],axis=1)
            t=mm(kh,qTg)+bias_ref[gi*PER+hh]
            m=jnp.max(t,axis=0,keepdims=True)
            e=jnp.exp2((t-m)*CEXP)
            l=jnp.sum(e,axis=0,keepdims=True)
            p=(e*(1.0/l)).astype(BF)
            P_s[slot,hh]=p
            OT_s[pl.ds(o+hh*HD,HD),:]=mm(vT_s[pl.ds(o+hh*HD,HD),:],p)
        pltpu.make_async_copy(P_s.at[slot],P_hbm.at[w,pl.ds(gi*PER,PER)],sem.at[slot]).start()
        return 0
    lax.fori_loop(0,groups,group,0)

    attn=OT_s[...].astype(BF).T
    branch=shifts_ref[2:3,:]
    for m in range(parts):
        branch=branch+mm_nt(attn[:,m*cq:(m+1)*cq],W_ref[m,:,3*cq:4*cq])
    branch=branch.astype(BF).astype(F32)
    middle=x+branch
    xhat2,rstd2=norm_stats(middle)
    xn2=(xhat2*gains_ref[1:2,:]+shifts_ref[1:2,:]).astype(BF)
    og=og_ref[0]
    tg=og.astype(BF)
    xn2_s[...]=xn2; xn2T_s[...]=xn2.T; tg_s[...]=tg; tgT_s[...]=tg.T
    up_s[...]=jnp.zeros_like(up_s); gn2_s[...]=jnp.zeros_like(gn2_s)
    CH=min(512,cf); each=cf//CH
    @pl.when(w==0)
    def _():
        acc[...]=jnp.zeros_like(acc)
        small_ref[...]=jnp.zeros_like(small_ref)
    def chunk(c,_):
        m=c//each
        o=pl.multiple_of((c%each)*CH,CH)
        f1=W_ref[m,:,pl.ds(4*cq+o,CH)]; f2=W_ref[m,:,pl.ds(4*cq+cf+o,CH)]
        hid=mm(xn2_s[...],f1)
        act,dact=gelu_both(hid)
        a=act.astype(BF)
        up_s[...]+=mm_nt(a,f2)
        gh=(mm(tg_s[...],f2)*dact).astype(BF)
        gn2_s[...]+=mm_nt(gh,f1)
        acc[m,:,pl.ds(cq+o,CH)]+=mm(xn2T_s[...],gh)
        acc[m,:,pl.ds(cq+cf+o,CH)]+=mm(tgT_s[...],a)
        return 0
    lax.fori_loop(0,parts*each,chunk,0)
    delta_ref[0]=(branch+up_s[...]+shifts_ref[3:4,:]).astype(BF)
    gn2=gn2_s[...]
    gln2=norm_back(gn2,xhat2,rstd2,gains_ref[1:2,:])
    gln2_ref[0]=gln2
    gb=(og+gln2).astype(BF)
    gbT=gb.T
    for m in range(parts):
        at=slice(m*cq,(m+1)*cq)
        acc[m,:,0:cq]+=mm(gbT,attn[:,at])
        g=mm(gb,W_ref[m,:,3*cq:4*cq]).astype(BF)
        g_ref[0,:,at]=g
        gT=g.T
        gT_ref[0,at,:]=gT
        prod=gT.astype(F32)*OT_s[at,:]
        nh=nheads//parts
        D_ref[0,m*nh:(m+1)*nh,:]=jnp.sum(prod.reshape(nh,HD,WIN),axis=1)
    small_ref[1:2,:]+=jnp.sum(gn2*xhat2,axis=0,keepdims=True)
    small_ref[3:4,:]+=jnp.sum(gn2,axis=0,keepdims=True)
    small_ref[4:5,:]+=jnp.sum(gb.astype(F32),axis=0,keepdims=True)
    small_ref[5:6,:]+=jnp.sum(tg.astype(F32),axis=0,keepdims=True)
    @pl.when(w==nw-1)
    def _():
        dcat_ref[...]=acc[...].astype(BF)
        for s in range(2):
            pltpu.make_async_copy(P_s.at[s],P_hbm.at[0,pl.ds(0,PER)],sem.at[s]).wait()

def full(shape,**kw):
    return pl.BlockSpec(shape,lambda w:(0,)*len(shape),**kw)
def per(shape):
    return pl.BlockSpec((1,)+shape,lambda w:(w,)+(0,)*len(shape))
ONE=pl.Buffered(1)
ANY=pl.BlockSpec(memory_space=pl.ANY)

def call_a(x,og,labc,labr,bias,W,gains,shifts):
    nW,WIN,D=x.shape; NH=bias.shape[0]
    parts,_,Ct=W.shape; Cg=Ct-3*(D//parts)
    sd=jax.ShapeDtypeStruct
    outs=[sd((nW,WIN,D),BF),sd((nW,WIN,D),F32),sd((nW,3,WIN,D),BF),sd((nW,WIN,D),BF),sd((nW,D,WIN),BF),sd((nW,NH,WIN),F32),
          sd((nW,NH,WIN,WIN),BF),sd((parts,D,Cg),BF),sd((8,D),F32)]
    return pl.pallas_call(functools.partial(kernel_a,NH),grid=(nW,),
      in_specs=[per((WIN,D)),per((WIN,D)),per((WIN,1)),per((1,WIN)),full((NH,WIN,WIN),pipeline_mode=ONE),
        full((parts,D,Ct),pipeline_mode=ONE),full(gains.shape),full(shifts.shape)],
      out_specs=[per((WIN,D)),per((WIN,D)),per((3,WIN,D)),per((WIN,D)),per((D,WIN)),per((NH,WIN)),ANY,full((parts,D,Cg)),full((8,D))],
      out_shape=outs,
      scratch_shapes=[pltpu.VMEM((D,WIN),BF),pltpu.VMEM((D,WIN),BF),pltpu.VMEM((D,WIN),F32),pltpu.VMEM((2,PER,WIN,WIN),BF),
        pltpu.VMEM((parts,D,Cg),F32),pltpu.SemaphoreType.DMA((2,)),
        pltpu.VMEM((WIN,D),BF),pltpu.VMEM((D,WIN),BF),pltpu.VMEM((WIN,D),BF),pltpu.VMEM((D,WIN),BF),pltpu.VMEM((WIN,D),F32),pltpu.VMEM((WIN,D),F32)],
      compiler_params=pltpu.CompilerParams(vmem_limit_bytes=62*1024*1024,dimension_semantics=("arbitrary",)),
      name="kernel_a")(x,og,labc,labr,bias,W,gains,shifts)

def kernel_b(nheads,x_ref,gln2_ref,qkv_ref,g_ref,gT_ref,D_ref,P_ref,W_ref,gains_ref,shifts_ref,
             dd_ref,dqkv_ref,G_hbm,small_ref,G_s,aq,kT_s,gq_s,gqT_s,sem):
    w=pl.program_id(0); nw=pl.num_programs(0)
    D=x_ref.shape[-1]; WIN=x_ref.shape[-2]
    parts=W_ref.shape[0]; cq=D//parts
    groups=nheads//PER
    @pl.when(w==0)
    def _():
        aq[...]=jnp.zeros_like(aq); G_s[...]=jnp.zeros_like(G_s); small_ref[...]=jnp.zeros_like(small_ref)
    kT_s[...]=qkv_ref[0,1].T
    lane=lax.broadcasted_iota(jnp.int32,(WIN,GROUP),1)
    hl=lane//HD
    def group(gi,_):
        o=pl.multiple_of(gi*GROUP,GROUP)
        gTg=gT_ref[0,pl.ds(o,GROUP),:]
        vg=qkv_ref[0,2,:,pl.ds(o,GROUP)]
        qg=qkv_ref[0,0,:,pl.ds(o,GROUP)]
        gg=g_ref[0,:,pl.ds(o,GROUP)]
        dv=jnp.zeros((WIN,GROUP),F32); dk=jnp.zeros((WIN,GROUP),F32)
        zero=jnp.zeros_like(vg)
        for hh in range(PER):
            h=gi*PER+hh
            p=P_ref[0,h]
            dp=mm(jnp.where(hl==hh,vg,zero),gTg)
            ds_=p.astype(F32)*(dp-D_ref[0,pl.ds(h,1),:])
            for c in range(G_s.shape[0]):
                wd=min(128,WIN-c*128)
                G_s[c,pl.ds(pl.multiple_of(h*WIN,8),WIN),:wd]+=ds_[:,c*128:c*128+wd]
            dsl=ds_.astype(BF)
            dv+=mm(p,jnp.where(hl==hh,gg,zero))
            dk+=mm(dsl,jnp.where(hl==hh,qg,zero))
            gqT_s[pl.ds(o+hh*HD,HD),:]=mm(kT_s[pl.ds(o+hh*HD,HD),:],dsl)
        gq_s[1,:,pl.ds(o,GROUP)]=(dk*(1.0/SQ)).astype(BF)
        gq_s[2,:,pl.ds(o,GROUP)]=dv.astype(BF)
        return 0
    lax.fori_loop(0,groups,group,0)
    gq_s[0]=(gqT_s[...]*(1.0/SQ)).astype(BF).T
    x=x_ref[0]
    xhat,rstd=norm_stats(x)
    xn=(xhat*gains_ref[0:1,:]+shifts_ref[0:1,:]).astype(BF)
    xnT=xn.T
    gr=jnp.zeros((WIN,D),F32)
    for m in range(parts):
        for c in range(3):
            gc=gq_s[c,:,m*cq:(m+1)*cq]
            gr=gr+mm_nt(gc,W_ref[m,:,c*cq:(c+1)*cq])
            aq[m,:,c*cq:(c+1)*cq]+=mm(xnT,gc)
    dd_ref[0]=(gln2_ref[0]+norm_back(gr,xhat,rstd,gains_ref[0:1,:])).astype(BF)
    small_ref[0:1,:]+=jnp.sum(gr*xhat,axis=0,keepdims=True)
    small_ref[2:3,:]+=jnp.sum(gr,axis=0,keepdims=True)
    @pl.when(w==nw-1)
    def _():
        dqkv_ref[...]=aq[...].astype(BF)
        cp=pltpu.make_async_copy(G_s,G_hbm,sem); cp.start(); cp.wait()

def call_b(x,gln2,qkv,g,gT,Dd,Pp,W,gains,shifts):
    nW,WIN,D=x.shape; NH=Dd.shape[1]
    parts=W.shape[0]; cq=D//parts; tiles=-(-WIN//128)
    sd=jax.ShapeDtypeStruct
    return pl.pallas_call(functools.partial(kernel_b,NH),grid=(nW,),
      in_specs=[per((WIN,D)),per((WIN,D)),per((3,WIN,D)),per((WIN,D)),per((D,WIN)),per((NH,WIN)),per((NH,WIN,WIN)),
        full((parts,D,3*cq),pipeline_mode=ONE),full(gains.shape),full(shifts.shape)],
      out_specs=[per((WIN,D)),full((parts,D,3*cq)),ANY,full((8,D))],
      out_shape=[sd((nW,WIN,D),BF),sd((parts,D,3*cq),BF),sd((tiles,NH*WIN,128),F32),sd((8,D),F32)],
      scratch_shapes=[pltpu.VMEM((tiles,NH*WIN,128),F32),pltpu.VMEM((parts,D,3*cq),F32),pltpu.VMEM((D,WIN),BF),pltpu.VMEM((3,WIN,D),BF),pltpu.VMEM((D,WIN),F32),
        pltpu.SemaphoreType.DMA],
      compiler_params=pltpu.CompilerParams(vmem_limit_bytes=62*1024*1024,dimension_semantics=("arbitrary",)),
      name="kernel_b")(x,gln2,qkv,g,gT,Dd,Pp,W,gains,shifts)

FIX=8191.0

def pack_table(table):
    NH,T=table.shape
    n=-(-T//128)
    q=jnp.round(jnp.clip(table,-4.0,4.0)*FIX).astype(jnp.int32)
    q=jnp.pad(q,((0,0),(0,n*128-T)))
    q=q.reshape(NH//2,2,n,128)
    return (q[:,0]*65536)|(q[:,1]&65535)

def kernel_p(pos_ref,tab_ref,bias_ref):
    npair,n,_=tab_ref.shape
    WIN=bias_ref.shape[-1]
    tiles=-(-WIN//128)
    def row(r,_):
        r8=pl.multiple_of(r*8,8)
        for c in range(tiles):
            width=min(128,WIN-c*128)
            idx=pos_ref[pl.ds(r8,8),c*128:(c+1)*128]
            lo=idx&127; hi=idx>>7
            masks=[hi==k for k in range(n)]
            for p in range(npair):
                acc=jnp.zeros((8,128),jnp.int32)
                for k in range(n):
                    src=jnp.broadcast_to(tab_ref[p,k:k+1,:],(8,128))
                    acc=jnp.where(masks[k],jnp.take_along_axis(src,lo,axis=1),acc)
                a=(acc>>16).astype(F32)*(SQ/FIX)
                b=((acc<<16)>>16).astype(F32)*(SQ/FIX)
                bias_ref[2*p,pl.ds(r8,8),c*128:c*128+width]=a[:,:width]
                bias_ref[2*p+1,pl.ds(r8,8),c*128:c*128+width]=b[:,:width]
        return 0
    lax.fori_loop(0,bias_ref.shape[1]//8,row,0)

def call_p(posT_pad,tab,WIN):
    NH=tab.shape[0]*2
    return pl.pallas_call(kernel_p,out_shape=jax.ShapeDtypeStruct((NH,WIN,WIN),F32),
      compiler_params=pltpu.CompilerParams(vmem_limit_bytes=40*1024*1024),name="kernel_p")(posT_pad,tab)

def kernel_t(NH,G_ref,hi_ref,lo_ref,out_ref):
    WIN=hi_ref.shape[0]; LW=G_ref.shape[0]*128
    nh=out_ref.shape[0]//NH
    out_ref[...]=jnp.zeros_like(out_ref)
    def rows(r,_):
        r8=pl.multiple_of(r*8,8)
        hi8=hi_ref[pl.ds(r8,8),:]; lo8=lo_ref[pl.ds(r8,8),:]
        tot=jnp.zeros(out_ref.shape,F32)
        iota=lax.broadcasted_iota(jnp.int32,(256,LW),0).astype(F32).astype(BF)
        for k in range(8):
            g=jnp.concatenate([G_ref[c,pl.ds(r8+k,NH,stride=WIN),:] for c in range(LW//128)],axis=1)
            hr=hi8[k:k+1,:]; lr=lo8[k:k+1,:].astype(F32).astype(BF)
            A=jnp.concatenate([jnp.where(hr==m,g,0.0) for m in range(nh)],axis=0).astype(BF)
            oh=jnp.where(iota==lr,jnp.ones((),BF),jnp.zeros((),BF))
            tot=tot+lax.dot_general(A,oh,(((1,),(1,)),((),())),preferred_element_type=F32)
        out_ref[...]+=tot
        return 0
    lax.fori_loop(0,WIN//8,rows,0)

def call_t(G,posT,T,NH):
    WIN=posT.shape[0]; nt=G.shape[0]
    nh=-(-T//256)
    pp=jnp.pad(posT,((0,0),(0,nt*128-WIN)),constant_values=nh*256)
    hi=pp>>8; lo=pp&255
    o=pl.pallas_call(functools.partial(kernel_t,NH),out_shape=jax.ShapeDtypeStruct((nh*NH,256),F32),
      compiler_params=pltpu.CompilerParams(vmem_limit_bytes=40*1024*1024),name="kernel_t")(G,hi,lo)
    return o.reshape(nh,NH,256).transpose(1,0,2).reshape(NH,nh*256)[:,:T]


MESHID=pl.DeviceIdType.MESH

def place_of():
    s=lax.axis_index("seq"); y=lax.axis_index("heads")
    return s//4,(s//2)%2,s%2,y

def dev(z,x,c,y):
    return ((z*2+x)*2+c,y)

def peers_of(z,x,c,y):
    return [dev(z,x,1-c,y),dev(z,1-x,c,y),dev(z,x,c,1-y)]+[dev((z+i)%4,x,c,y) for i in (1,2,3)]

def greet(devices):
    bar=pltpu.get_barrier_semaphore()
    for d in devices:
        pl.semaphore_signal(bar,inc=1,device_id=d,device_id_type=MESHID)
    pl.semaphore_wait(bar,len(devices))

def send(src,dst,ss,rs,to):
    return pltpu.make_async_remote_copy(src_ref=src,dst_ref=dst,send_sem=ss,recv_sem=rs,device_id=to,device_id_type=MESHID)


class Gather:
    def __init__(self,src,dst,ss,rs,own):
        self.src,self.dst,self.ss,self.rs,self.own=src,dst,ss,rs,own
        z,x,c,y=self.at=place_of()
        self.xa=x+(1-2*x)*(1-c); self.ya=y+(1-2*y)*c
        self.xb=x+(1-2*x)*c; self.yb=y+(1-2*y)*(1-c)
        self.sib=dev(z,x,1-c,y); self.pa=dev(z,self.xa,c,self.ya); self.pb=dev(z,self.xb,c,self.yb)
    def slot(self,zz,xx,cc,yy):
        n=self.src.shape[0]
        return self.dst.at[yy,pl.ds(pl.multiple_of(((zz*2+xx)*2+cc)*n,n),n)]
    def copy(self,src,where,k,to):
        return send(src,self.slot(*where),self.ss.at[k],self.rs.at[k],to)
    def go(self,where,k,to,src=None):
        self.copy(self.slot(*where) if src is None else src,where,k,to).start()
    def came(self,where,k):
        self.copy(self.src,where,k,self.sib).wait_recv()
    def keep(self):
        z,x,c,y=self.at
        return pltpu.make_async_copy(self.src,self.slot(z,x,c,y),self.own)
    def start(self):
        z,x,c,y=self.at
        me=(z,x,c,y)
        self.keep().start()
        for i in (1,2,3):
            self.go(me,i-1,dev((z+i)%4,x,c,y),self.src)
        self.go(me,3,self.pa,self.src); self.go(me,7,self.pb,self.src); self.go(me,15,self.sib,self.src)
    def z(self,i):
        return (self.at[0]+4-i)%4
    def turn_z(self,i):
        z,x,c,y=self.at
        at=(self.z(i),x,c,y); self.came(at,i-1)
        self.go(at,3+i,self.pa); self.go(at,7+i,self.pb); self.go(at,15+i,self.sib)
    def turn_a(self,i):
        at=(self.z(i),self.xa,self.at[2],self.ya); self.came(at,3+i)
        self.go(at,11+i,self.pb); self.go(at,19+i,self.sib)
    def turn_b(self,i):
        at=(self.z(i),self.xb,self.at[2],self.yb); self.came(at,7+i)
        self.go(at,23+i,self.sib)
    def turn_ab(self,i):
        z,x,c,y=self.at
        at=(self.z(i),1-x,c,1-y); self.came(at,11+i)
        self.go(at,27+i,self.sib)
    def last(self):
        z,x,c,y=self.at
        for i in range(4):
            zz=self.z(i)
            self.came((zz,x,1-c,y),15+i); self.came((zz,self.xb,1-c,self.yb),19+i)
            self.came((zz,self.xa,1-c,self.ya),23+i); self.came((zz,1-x,1-c,1-y),27+i)
    def drain(self):
        z,x,c,y=self.at
        for k in range(31):
            self.copy(self.src,(z,x,c,y),k,self.sib).wait_send()
        self.keep().wait()

def gather_sems():
    return [pltpu.SemaphoreType.DMA((31,)),pltpu.SemaphoreType.DMA((31,)),pltpu.SemaphoreType.DMA]

STEPS=7
def kernel_w(w_hbm,pos_ref,tab_ref,W_hbm,bias_hbm,bias_s,tb,tq,ss,rs,own,bs,br,bl,tsem):
    z,x,c,y=place_of()
    greet(peers_of(z,x,c,y))
    gather=Gather(w_hbm,W_hbm,ss,rs,own)
    swap=send(tab_ref,tb.at[y],tsem.at[0],tsem.at[1],dev(z,x,c,1-y))
    swap.start()
    gather.start()
    tb[y]=tab_ref[...]
    swap.wait()
    half,n=tab_ref.shape[0],tab_ref.shape[1]
    npair=half//2
    for p in range(npair):
        a,b=[jnp.floor(jnp.clip(tb[c,2*p+k],-4.0,4.0)*FIX+0.5).astype(jnp.int32) for k in range(2)]
        tq[p]=(a*65536)|(b&65535)
    WIN=bias_s.shape[-1]; tiles=-(-WIN//128)
    nrow=WIN//8
    cuts=[nrow*k//STEPS for k in range(STEPS+1)]
    sib=dev(z,x,1-c,y)
    def rows_of(k): return pl.ds(cuts[k]*8,(cuts[k+1]-cuts[k])*8)
    def kept(k): return pltpu.make_async_copy(bias_s.at[:,rows_of(k)],bias_hbm.at[pl.ds(c*half,half),rows_of(k)],bl.at[k])
    def sent(k,cc): return send(bias_s.at[:,rows_of(k)],bias_hbm.at[pl.ds(cc*half,half),rows_of(k)],bs.at[k],br.at[k],sib)
    def rows(k):
        def row(r,_):
            r8=pl.multiple_of(r*8,8)
            for t in range(tiles):
                width=min(128,WIN-t*128)
                idx=pos_ref[pl.ds(r8,8),t*128:(t+1)*128]
                lo=idx&127; hi=idx>>7
                masks=[hi==q for q in range(n)]
                for p in range(npair):
                    acc=jnp.zeros((8,128),jnp.int32)
                    for q in range(n):
                        src=jnp.broadcast_to(tq[p,q:q+1,:],(8,128))
                        acc=jnp.where(masks[q],jnp.take_along_axis(src,lo,axis=1),acc)
                    a=(acc>>16).astype(F32)*(SQ/FIX)
                    b=((acc<<16)>>16).astype(F32)*(SQ/FIX)
                    bias_s[2*p,pl.ds(r8,8),t*128:t*128+width]=a[:,:width]
                    bias_s[2*p+1,pl.ds(r8,8),t*128:t*128+width]=b[:,:width]
            return 0
        lax.fori_loop(cuts[k],cuts[k+1],row,0)
        kept(k).start(); sent(k,c).start()
    rows(0)
    for i in (1,3,2): gather.turn_z(i)
    rows(1)
    for i in (0,): gather.turn_a(i); gather.turn_b(i)
    rows(2)
    for i in (1,3): gather.turn_a(i); gather.turn_b(i)
    rows(3)
    for i in (2,): gather.turn_a(i); gather.turn_b(i)
    gather.turn_ab(0)
    rows(4)
    for i in (1,3): gather.turn_ab(i)
    rows(5)
    gather.turn_ab(2)
    rows(6)
    gather.last()
    for k in range(STEPS):
        kept(k).wait(); sent(k,c).wait_send(); sent(k,1-c).wait_recv()
    gather.drain()

def call_w(wq,posT_pad,tab,WIN):
    rows,cols=wq.shape; half=tab.shape[0]; dma=pltpu.SemaphoreType.DMA
    vm=pl.BlockSpec(memory_space=pltpu.VMEM)
    return pl.pallas_call(kernel_w,
      out_shape=[jax.ShapeDtypeStruct((2,16*rows,cols),BF),jax.ShapeDtypeStruct((2*half,WIN,WIN),F32)],
      in_specs=[ANY,vm,vm],out_specs=[ANY]*2,
      scratch_shapes=[pltpu.VMEM((half,WIN,WIN),F32),pltpu.VMEM((2,)+tab.shape,F32),pltpu.VMEM((half//2,)+tab.shape[1:],jnp.int32)]
        +gather_sems()+[dma((STEPS,)),dma((STEPS,)),dma((STEPS,)),dma((2,))],
      compiler_params=pltpu.CompilerParams(vmem_limit_bytes=40*1024*1024,collective_id=1,has_side_effects=True),name="kernel_w")(wq,posT_pad,tab)

def neighbours(z,x,c,y):
    s=(z*2+x)*2+c
    return [((s+k)%16,yy) for k in (1,15) for yy in (y,1-y)]

def kernel_a2(nheads,in_hbm,og_hbm,wf_hbm,labc_ref,labr_ref,bias_ref,W1,gains_ref,shifts_ref,
              qkv_ref,x_ref,P_hbm,gln2_ref,g_ref,gT_ref,D_ref,ev_hbm,hd_hbm,dcat_hbm,small_ref,
              x_s,og_s,W2,OT_s,qT_s,vT_s,P_s,acc,pst,xn2_s,xn2T_s,tg_s,tgT_s,up_s,gn2_s,dl_s,
              psem,xsem,hsem,ss,rs,own,dl,ds,dr,es,er,fin):
    i=pl.program_id(0); nw=x_s.shape[0]
    w=i%nw
    z,xc,c,y=place_of()
    s=(z*2+xc)*2+c
    D=x_s.shape[-1]; WIN=qkv_ref.shape[-2]; SLAB=x_s.shape[1]; HALF=SLAB//2
    OFF=(SLAB-WIN)//2
    cq=D//2; cf=W2.shape[2]//2
    groups=nheads//PER
    gather=Gather(wf_hbm,W2,ss,rs,own)
    mate=dev(z,xc,c,1-y)
    def local(k,half,t):
        hbm,buf=((in_hbm,x_s),(og_hbm,og_s))[t]
        r=pl.multiple_of(y*(nw*WIN)+k*WIN+(WIN//2-OFF)+half*HALF,8)
        return pltpu.make_async_copy(hbm.at[pl.ds(r,HALF)],buf.at[k,pl.ds(half*HALF,HALF)],xsem.at[t,2*k+half])
    def edge(t):
        hbm,buf=((in_hbm,x_s),(og_hbm,og_s))[t]
        return send(hbm.at[pl.ds(0,HALF)],buf.at[nw-1,pl.ds(HALF,HALF)],hsem.at[t,0],hsem.at[t,1],((s+15)%16,1))
    def ready(t):
        local(w,0,t).wait()
        far=jnp.logical_and(w==nw-1,y==1)
        @pl.when(far)
        def _(): edge(t).wait_recv()
        @pl.when(jnp.logical_not(far))
        def _(): local(w,1,t).wait()
    def slab(k,to=None):
        at=ev_hbm.at[y*nw+k]
        if to is None: return pltpu.make_async_copy(dl_s.at[k],at,dl.at[k])
        return send(dl_s.at[k],at,ds.at[k],dr.at[k],to)
    def tail(k):
        lead=SLAB-hd_hbm.shape[0]
        return send(dl_s.at[nw-1,pl.ds(lead,hd_hbm.shape[0])],hd_hbm,es.at[k],er,((s+1)%16,k))
    @pl.when(i==0)
    def _():
        greet(peers_of(z,xc,c,y)+neighbours(z,xc,c,y))
        for k in range(nw):
            for t in range(2):
                local(k,0,t).start()
                if k<nw-1: local(k,1,t).start()
        for t in range(2):
            @pl.when(y==1)
            def _(): edge(t).start()
            @pl.when(y==0)
            def _(): local(nw-1,1,t).start()
        gather.start()
        acc[...]=jnp.zeros_like(acc)
        small_ref[...]=jnp.zeros_like(small_ref)
        dl_s[:,SLAB-16:,:]=jnp.zeros((nw,16,D),BF)

    @pl.when(i<nw)
    def _():
        ready(0)
        x=x_s[w,OFF:OFF+WIN,:]
        x_ref[0]=x
        xhat,_=norm_stats(x)
        xn=(xhat*gains_ref[0:1,:]+shifts_ref[0:1,:]).astype(BF)
        for k in range(3):
            for m in range(2):
                at=slice(m*cq,(m+1)*cq)
                v=mm(xn,W1[m,:,k*cq:(k+1)*cq]).astype(BF)
                qkv_ref[0,k,:,at]=v
                if k==0: qT_s[at,:]=v.T
                if k==2: vT_s[at,:]=v.T
        labc=labc_ref[0]; labr=labr_ref[0]
        lane=lax.broadcasted_iota(jnp.int32,(WIN,GROUP),1)
        oh=jnp.where((labc==lane)|((labc+3)==lane),1.0,0.0).astype(BF)
        hi=564.0
        lo=MASK-hi
        sub=lax.broadcasted_iota(jnp.int32,(GROUP,WIN),0)
        nm=jnp.where(sub<3,jnp.where(sub!=labr,-hi,0.0),jnp.where(sub<6,jnp.where(sub-3!=labr,-lo,0.0),0.0)).astype(BF)
        hl=lane//HD
        def group(gi,_):
            slot=gi%2
            @pl.when(w*groups+gi>=2)
            def _():
                pltpu.make_async_copy(P_s.at[slot],P_hbm.at[0,pl.ds(0,PER)],psem.at[slot]).wait()
            o=pl.multiple_of(gi*GROUP,GROUP)
            qTg=jnp.concatenate([qT_s[pl.ds(o,GROUP),:],nm],axis=0)
            kg=qkv_ref[0,1,:,pl.ds(o,GROUP)]
            for hh in range(PER):
                kh=jnp.concatenate([jnp.where(hl==hh,kg,jnp.zeros_like(kg)),oh],axis=1)
                t=mm(kh,qTg)+bias_ref[gi*PER+hh]
                m=jnp.max(t,axis=0,keepdims=True)
                e=jnp.exp2((t-m)*CEXP)
                l=jnp.sum(e,axis=0,keepdims=True)
                p=(e*(1.0/l)).astype(BF)
                P_s[slot,hh]=p
                OT_s[w,pl.ds(o+hh*HD,HD),:]=mm(vT_s[pl.ds(o+hh*HD,HD),:],p)
            pltpu.make_async_copy(P_s.at[slot],P_hbm.at[w,pl.ds(gi*PER,PER)],psem.at[slot]).start()
            return 0
        lax.fori_loop(0,groups,group,0)

    @pl.when(i==0)
    def _():
        for k in (1,3,2): gather.turn_z(k)
    @pl.when(i==1)
    def _():
        for k in (0,1,3,2): gather.turn_a(k); gather.turn_b(k)
    @pl.when(i==2)
    def _():
        for k in (0,1,3,2): gather.turn_ab(k)
    @pl.when(i==nw-1)
    def _():
        gather.last(); gather.drain()

    @pl.when(i>=nw)
    def _():
        ready(1)
        x=x_s[w,OFF:OFF+WIN,:]
        og=og_s[w,OFF:OFF+WIN,:]
        attn=OT_s[w].astype(BF).T
        branch=shifts_ref[2:3,:]
        for m in range(2):
            branch=branch+mm_nt(attn[:,m*cq:(m+1)*cq],W1[m,:,3*cq:4*cq])
        branch=branch.astype(BF).astype(F32)
        middle=x+branch
        xhat2,rstd2=norm_stats(middle)
        xn2=(xhat2*gains_ref[1:2,:]+shifts_ref[1:2,:]).astype(BF)
        tg=og.astype(BF)
        xn2_s[...]=xn2; xn2T_s[...]=xn2.T; tg_s[...]=tg; tgT_s[...]=tg.T
        up_s[...]=jnp.zeros_like(up_s); gn2_s[...]=jnp.zeros_like(gn2_s)
        CH=512; each=cf//CH
        def chunk(k,_):
            m=k//each
            o=pl.multiple_of((k%each)*CH,CH)
            f1=W2[m,:,pl.ds(o,CH)]; f2=W2[m,:,pl.ds(cf+o,CH)]
            hid=mm(xn2_s[...],f1)
            act,dact=gelu_both(hid)
            a=act.astype(BF)
            up_s[...]+=mm_nt(a,f2)
            gh=(mm(tg_s[...],f2)*dact).astype(BF)
            gn2_s[...]+=mm_nt(gh,f1)
            acc[m,:,pl.ds(cq+o,CH)]+=mm(xn2T_s[...],gh)
            acc[m,:,pl.ds(cq+cf+o,CH)]+=mm(tgT_s[...],a)
            return 0
        lax.fori_loop(0,2*each,chunk,0)
        dl_s[w,0:WIN,:]=(branch+up_s[...]+shifts_ref[3:4,:]).astype(BF)
        slab(w).start(); slab(w,mate).start()
        @pl.when(jnp.logical_and(w==nw-1,y==1))
        def _():
            tail(0).start(); tail(1).start()
        gn2=gn2_s[...]
        gln2=norm_back(gn2,xhat2,rstd2,gains_ref[1:2,:])
        gln2_ref[0]=gln2
        gb=(og+gln2).astype(BF)
        gbT=gb.T
        for m in range(2):
            at=slice(m*cq,(m+1)*cq)
            acc[m,:,0:cq]+=mm(gbT,attn[:,at])
            g=mm(gb,W1[m,:,3*cq:4*cq]).astype(BF)
            g_ref[0,:,at]=g
            gT=g.T
            gT_ref[0,at,:]=gT
            prod=gT.astype(F32)*OT_s[w,at,:]
            nh=nheads//2
            D_ref[0,m*nh:(m+1)*nh,:]=jnp.sum(prod.reshape(nh,HD,WIN),axis=1)
        small_ref[1:2,:]+=jnp.sum(gn2*xhat2,axis=0,keepdims=True)
        small_ref[3:4,:]+=jnp.sum(gn2,axis=0,keepdims=True)
        small_ref[4:5,:]+=jnp.sum(gb.astype(F32),axis=0,keepdims=True)
        small_ref[5:6,:]+=jnp.sum(tg.astype(F32),axis=0,keepdims=True)

    @pl.when(i==2*nw-1)
    def _():
        W2[...]=acc[:,:,cq:].astype(BF)
        pst[...]=acc[:,:,:cq].astype(BF)
        a=pltpu.make_async_copy(W2,dcat_hbm.at[:,:,pl.ds(cq,2*cf)],fin.at[0])
        b=pltpu.make_async_copy(pst,dcat_hbm.at[:,:,pl.ds(0,cq)],fin.at[1])
        a.start(); b.start()
        for k in range(2):
            pltpu.make_async_copy(P_s.at[k],P_hbm.at[0,pl.ds(0,PER)],psem.at[k]).wait()
        for k in range(nw):
            slab(k).wait(); slab(k,mate).wait()
        @pl.when(y==1)
        def _():
            for t in range(2): edge(t).wait_send()
            tail(0).wait_send(); tail(1).wait_send()
        tail(0).wait_recv()
        a.wait(); b.wait()

def call_a2(inputs,og,wf,labc,labr,bias,W1,gains,shifts):
    nW=labc.shape[0]; WIN=labc.shape[1]; D=inputs.shape[1]; NH=bias.shape[0]
    cf=wf.shape[1]//2; cq=D//2; SLAB=-(-WIN//16)*16; EDGE=-(-(SLAB-WIN//2)//16)*16
    sd=jax.ShapeDtypeStruct; dma=pltpu.SemaphoreType.DMA; v=pltpu.VMEM
    early=lambda shape: pl.BlockSpec((1,)+shape,lambda i:(jnp.minimum(i,nW-1),)+(0,)*len(shape))
    late=lambda shape: pl.BlockSpec((1,)+shape,lambda i:(jnp.maximum(i-nW,0),)+(0,)*len(shape))
    outs=[sd((nW,3,WIN,D),BF),sd((nW,WIN,D),F32),sd((nW,NH,WIN,WIN),BF),sd((nW,WIN,D),F32),sd((nW,WIN,D),BF),sd((nW,D,WIN),BF),sd((nW,NH,WIN),F32),
          sd((2*nW,SLAB,D),BF),sd((EDGE,D),BF),sd((2,D,cq+2*cf),BF),sd((8,D),F32)]
    return pl.pallas_call(functools.partial(kernel_a2,NH),grid=(2*nW,),
      in_specs=[ANY,ANY,ANY,early((WIN,1)),early((1,WIN)),full((NH,WIN,WIN),pipeline_mode=ONE),full(W1.shape,pipeline_mode=ONE),full(gains.shape),full(shifts.shape)],
      out_specs=[early((3,WIN,D)),early((WIN,D)),ANY,late((WIN,D)),late((WIN,D)),late((D,WIN)),late((NH,WIN)),ANY,ANY,ANY,full((8,D))],
      out_shape=outs,
      scratch_shapes=[v((nW,SLAB,D),F32),v((nW,SLAB,D),F32),v((2,D,2*cf),BF),v((nW,D,WIN),F32),v((D,WIN),BF),v((D,WIN),BF),v((2,PER,WIN,WIN),BF),
        v((2,D,cq+2*cf),F32),v((2,D,cq),BF),v((WIN,D),BF),v((D,WIN),BF),v((WIN,D),BF),v((D,WIN),BF),v((WIN,D),F32),v((WIN,D),F32),v((nW,SLAB,D),BF),
        dma((2,)),dma((2,2*nW)),dma((2,2))]+gather_sems()+[dma((nW,)),dma((nW,)),dma((nW,)),dma((2,)),dma,dma((2,))],
      compiler_params=pltpu.CompilerParams(vmem_limit_bytes=63*1024*1024,dimension_semantics=("arbitrary",),collective_id=2,has_side_effects=True),
      name="kernel_a2")(inputs,og,wf,labc,labr,bias,W1,gains,shifts)

class Reduce:
    def __init__(self,src,out,own,r1,r2,ss,rs,ls,r3,fin,r4):
        self.src,self.out,self.own,self.r1,self.r2,self.r3,self.fin,self.r4=src,out,own,r1,r2,r3,fin,r4
        self.ss,self.rs,self.ls=ss,rs,ls
        self.at=place_of()
        self.mid=own.at[self.at[1]]
    def mine(self,k):
        return pltpu.make_async_copy(self.src.at[k%2,:,k//2,self.at[2]],self.own.at[k//2,:,k%2],self.ls.at[k])
    def theirs(self,k):
        z,x,c,y=self.at
        return send(self.src.at[k%2,:,k//2,1-c],self.r1.at[k//2,:,k%2],self.ss.at[k],self.rs.at[k],dev(z,x,1-c,y))
    def xsend(self):
        z,x,c,y=self.at
        return send(self.own.at[1-x],self.r2,self.ss.at[4],self.rs.at[4],dev(z,1-x,c,y))
    def zsend(self,i):
        z,x,c,y=self.at
        zz=(z+i)%4
        return send(self.mid.at[zz],self.r3.at[i-1],self.ss.at[4+i],self.rs.at[4+i],dev(zz,x,c,y))
    def ysend(self):
        z,x,c,y=self.at
        return send(self.fin.at[1-y],self.r4,self.ss.at[8],self.rs.at[8],dev(z,x,c,1-y))
    def start(self):
        for k in range(4):
            self.theirs(k).start(); self.mine(k).start()
    def add(self,dst,*srcs):
        total=srcs[0][...].astype(F32)
        for s in srcs[1:]: total=total+s[...].astype(F32)
        dst[...]=total.astype(BF)
    def one(self):
        z,x,c,y=self.at
        for k in range(4):
            self.mine(k).wait(); self.theirs(k).wait_recv()
        def step(xx):
            def add(k,_):
                at=(xx,k//2,k%2)
                self.add(self.own.at[at],self.own.at[at],self.r1.at[at])
                return 0
            lax.fori_loop(0,8,add,0)
        step(1-x)
        self.xsend().start()
        step(x)
    def summed(self):
        z,x,c,y=self.at
        def add(k,_):
            at=(k//2,k%2)
            self.add(self.own.at[(x,)+at],self.own.at[(x,)+at],self.r2.at[at])
            return 0
        lax.fori_loop(0,8,add,0)
    def left(self):
        for k in range(4): self.theirs(k).wait_send()
        self.xsend().wait_send()
    def zstart(self):
        for i in (2,1,3): self.zsend(i).start()
    def two(self):
        self.xsend().wait_recv()
        self.summed()
        self.zstart()
    def three(self):
        z,x,c,y=self.at
        for i in (1,2,3):
            self.zsend(i).wait_recv()
        def step(yy):
            self.add(self.fin.at[yy],self.mid.at[z,yy],*[self.r3.at[i,yy] for i in range(3)])
        step(1-y)
        self.ysend().start()
        step(y)
    def four(self):
        z,x,c,y=self.at
        self.ysend().wait_recv()
        self.out[...]=self.fin[y].astype(F32)+self.r4[...].astype(F32)
        self.left()
        for i in (1,2,3): self.zsend(i).wait_send()
        self.ysend().wait_send()

def reduce_scratch(rows,cols):
    v=lambda *d: pltpu.VMEM(d+(rows,cols),BF); dma=pltpu.SemaphoreType.DMA
    return [v(2,4,2),v(2,4,2),v(4,2),dma((9,)),dma((9,)),dma((4,)),v(3,2),v(2),v()]


def kernel_bc(nheads,x_ref,gln2_ref,qkv_ref,g_ref,gT_ref,D_ref,P_ref,W1,gains_ref,shifts_ref,sm_ref,pos_ref,dcat_hbm,
              ev_hbm,hd_hbm,redq_ref,redm_ref,tab_ref,sum_ref,
              G_s,Gx,aq,dq_s,kT_s,gq_s,gqT_s,dd_s,small_ref,acc,tk,tr,tu,sr,
              gs,gr_,dl,ds,dr,es,er,ts,tq_,
              own,r1,r2,ss,rs,ls,r3,fin,r4,own2,p1,p2,ss2,rs2,ls2,p3,fin2,p4):
    w=pl.program_id(0); nw=dd_s.shape[0]
    z,xc,c,y=place_of()
    s=(z*2+xc)*2+c
    mate=dev(z,xc,c,1-y); sib=dev(z,xc,1-c,y)
    D=x_ref.shape[-1]; WIN=x_ref.shape[-2]; SLAB=dd_s.shape[1]
    cq=D//2
    groups=nheads//PER
    tiles=G_s.shape[0]; part=Gx.shape[1]//nheads
    big=Reduce(dcat_hbm,redm_ref,own2,p1,p2,ss2,rs2,ls2,p3,fin2,p4)
    red=Reduce(dq_s,redq_ref,own,r1,r2,ss,rs,ls,r3,fin,r4)
    def slab(k,to=None):
        at=ev_hbm.at[y*nw+k]
        if to is None: return pltpu.make_async_copy(dd_s.at[k],at,dl.at[k])
        return send(dd_s.at[k],at,ds.at[k],dr.at[k],to)
    def tail(k):
        lead=SLAB-hd_hbm.shape[0]
        return send(dd_s.at[nw-1,pl.ds(lead,hd_hbm.shape[0])],hd_hbm,es.at[k],er,((s+1)%16,k))
    def trade(h):
        r=pl.multiple_of(h*WIN+(1-c)*(WIN-part),8)
        return send(G_s.at[:,pl.ds(r,part)],Gx.at[:,pl.ds(pl.multiple_of(h*part,8),part)],gs.at[h],gr_.at[h],sib)
    @pl.when(w==0)
    def _():
        greet(peers_of(z,xc,c,y)+neighbours(z,xc,c,y))
        big.start()
        aq[...]=jnp.zeros_like(aq); G_s[...]=jnp.zeros_like(G_s); small_ref[...]=sm_ref[...]
        dd_s[:,SLAB-16:,:]=jnp.zeros((nw,16,D),BF)
    kT_s[...]=qkv_ref[0,1].T
    lane=lax.broadcasted_iota(jnp.int32,(WIN,GROUP),1)
    hl=lane//HD
    def group(gi,_):
        o=pl.multiple_of(gi*GROUP,GROUP)
        gTg=gT_ref[0,pl.ds(o,GROUP),:]
        vg=qkv_ref[0,2,:,pl.ds(o,GROUP)]
        qg=qkv_ref[0,0,:,pl.ds(o,GROUP)]
        gg=g_ref[0,:,pl.ds(o,GROUP)]
        dv=jnp.zeros((WIN,GROUP),F32); dk=jnp.zeros((WIN,GROUP),F32)
        zero=jnp.zeros_like(vg)
        for hh in range(PER):
            h=gi*PER+hh
            p=P_ref[0,h]
            dp=mm(jnp.where(hl==hh,vg,zero),gTg)
            dsc=p.astype(F32)*(dp-D_ref[0,pl.ds(h,1),:])
            for k in range(tiles):
                wd=min(128,WIN-k*128)
                G_s[k,pl.ds(pl.multiple_of(h*WIN,8),WIN),:wd]+=dsc[:,k*128:k*128+wd]
            dsl=dsc.astype(BF)
            dv+=mm(p,jnp.where(hl==hh,gg,zero))
            dk+=mm(dsl,jnp.where(hl==hh,qg,zero))
            gqT_s[pl.ds(o+hh*HD,HD),:]=mm(kT_s[pl.ds(o+hh*HD,HD),:],dsl)
        gq_s[1,:,pl.ds(o,GROUP)]=(dk*(1.0/SQ)).astype(BF)
        gq_s[2,:,pl.ds(o,GROUP)]=dv.astype(BF)
        @pl.when(w==nw-1)
        def _():
            for hh in range(PER): trade(gi*PER+hh).start()
        return 0
    lax.fori_loop(0,groups,group,0)
    gq_s[0]=(gqT_s[...]*(1.0/SQ)).astype(BF).T
    x=x_ref[0]
    xhat,rstd=norm_stats(x)
    xn=(xhat*gains_ref[0:1,:]+shifts_ref[0:1,:]).astype(BF)
    xnT=xn.T
    gr=jnp.zeros((WIN,D),F32)
    for m in range(2):
        for k in range(3):
            gc=gq_s[k,:,m*cq:(m+1)*cq]
            gr=gr+mm_nt(gc,W1[m,:,k*cq:(k+1)*cq])
            aq[m,:,k*cq:(k+1)*cq]+=mm(xnT,gc)
    @pl.when(w==nw-1)
    def _():
        dq_s[...]=aq[...].astype(BF).reshape(dq_s.shape)
        red.start()
    dd_s[w,0:WIN,:]=(gln2_ref[0]+norm_back(gr,xhat,rstd,gains_ref[0:1,:])).astype(BF)
    slab(w).start(); slab(w,mate).start()
    @pl.when(jnp.logical_and(w==nw-1,y==1))
    def _():
        tail(0).start(); tail(1).start()
    small_ref[0:1,:]+=jnp.sum(gr*xhat,axis=0,keepdims=True)
    small_ref[2:3,:]+=jnp.sum(gr,axis=0,keepdims=True)
    pl.when(w==0)(big.one)
    pl.when(w==nw-2)(big.two)
    @pl.when(w==nw-1)
    def _():
        for h in range(nheads): trade(h).wait()
        acc[...]=jnp.zeros_like(acc)
        nh=acc.shape[0]; LW=tiles*128
        base=c*(WIN-part)
        def rows(r,_):
            r8=pl.multiple_of(r*8,8)
            f8=pl.multiple_of(base+r*8,8)
            pos=pos_ref[pl.ds(f8,8),:]
            hi8=pos>>8; lo8=pos&255
            tot=jnp.zeros((nh*nheads,256),F32)
            iota=lax.broadcasted_iota(jnp.int32,(256,LW),0).astype(F32).astype(BF)
            for k in range(8):
                g=jnp.concatenate([G_s[q,pl.ds(f8+k,nheads,stride=WIN),:]+Gx[q,pl.ds(r8+k,nheads,stride=part),:] for q in range(tiles)],axis=1)
                hr=hi8[k:k+1,:]; lr=lo8[k:k+1,:].astype(F32).astype(BF)
                A=jnp.concatenate([jnp.where(hr==m,g,0.0) for m in range(nh)],axis=0).astype(BF)
                oh=jnp.where(iota==lr,jnp.ones((),BF),jnp.zeros((),BF))
                tot=tot+mm_nt(A,oh)
            acc[...]+=tot.reshape(acc.shape)
            return 0
        n=part//8
        lax.fori_loop(c,n*3//25,rows,0)
        red.one()
        lax.fori_loop(n*3//25,n*13//25,rows,0)
        red.two()
        lax.fori_loop(n*13//25,n*19//25,rows,0)
        big.three()
        lax.fori_loop(n*19//25,n,rows,0)
        big.four()
        half=nheads//2; nb=nh//2
        def pair(k,src,dst,to):
            return [send(src,dst,ts.at[2*k],tq_.at[2*k],to),send(sr.at[6+min(k,3)],sr.at[k],ts.at[2*k+1],tq_.at[2*k+1],to)]
        def run(cps):
            for p in cps: p.start()
            for p in cps: p.wait()
        sr[6]=small_ref[...]
        run(pair(0,acc.at[:,pl.ds(pl.multiple_of((1-y)*half,8),half)],tu.at[0],mate))
        tu[1]=acc[:,pl.ds(pl.multiple_of(y*half,8),half)]+tu[0]
        sr[7]=sr[6]+sr[0]
        run(pair(1,tu.at[1,pl.ds((1-c)*nb,nb)],tr.at[0],sib))
        tk[0]=tu[1,pl.ds(c*nb,nb)]+tr[0]
        sr[8]=sr[7]+sr[1]
        run(pair(2,tk.at[0],tr.at[1],dev(z,1-xc,c,y)))
        tk[1]=tk[0]+tr[1]
        sr[9]=sr[8]+sr[2]
        cps=[]
        for k in (1,2,3):
            cps+=pair(2+k,tk.at[1],tr.at[1+k],dev((z+k)%4,xc,c,y))
        run(cps)
        red.three()
        tu[2,pl.ds(c*nb,nb)]=tk[1]+tr[2]+tr[3]+tr[4]
        sum_ref[...]=sr[9]+sr[3]+sr[4]+sr[5]
        cp=send(tu.at[2,pl.ds(c*nb,nb)],tu.at[2,pl.ds(c*nb,nb)],ts.at[12],tq_.at[12],sib)
        cp.start()
        red.four()
        cp.wait_send()
        send(tu.at[2,pl.ds((1-c)*nb,nb)],tu.at[2,pl.ds((1-c)*nb,nb)],ts.at[12],tq_.at[12],sib).wait_recv()
        for m in range(nh):
            tab_ref[:,m*256:(m+1)*256]=tu[2,m]
        for k in range(nw):
            slab(k).wait(); slab(k,mate).wait()
        @pl.when(y==1)
        def _():
            tail(0).wait_send(); tail(1).wait_send()
        tail(0).wait_recv()

def call_bc(x,gln2,qkv,g,gT,Dd,Pp,W1,gains,shifts,sm,posT,dcat,T):
    nW,WIN,D=x.shape; NH=Dd.shape[1]
    cq=D//2; tiles=-(-WIN//128); SLAB=-(-WIN//16)*16; EDGE=-(-(SLAB-WIN//2)//16)*16
    part=-(-WIN//16)*8
    nh=-(-T//256); nh+=nh%2
    rows,more=dcat.shape[-2:]; cols=3*cq
    pp=jnp.pad(posT,((0,0),(0,tiles*128-WIN)),constant_values=nh*256)
    sd=jax.ShapeDtypeStruct; dma=pltpu.SemaphoreType.DMA; v=pltpu.VMEM
    return pl.pallas_call(functools.partial(kernel_bc,NH),grid=(nW,),
      in_specs=[per((WIN,D)),per((WIN,D)),per((3,WIN,D)),per((WIN,D)),per((D,WIN)),per((NH,WIN)),per((NH,WIN,WIN)),
        full((2,D,cols),pipeline_mode=ONE),full(gains.shape),full(shifts.shape),full(sm.shape),full(pp.shape,pipeline_mode=ONE),ANY],
      out_specs=[ANY,ANY,full((rows,cols)),full((rows,more)),full((NH//2,nh*256)),full(sm.shape)],
      out_shape=[sd((2*nW,SLAB,D),BF),sd((EDGE,D),BF),sd((rows,cols),F32),sd((rows,more),F32),sd((NH//2,nh*256),F32),sd(sm.shape,F32)],
      scratch_shapes=[v((tiles,NH*WIN,128),F32),v((tiles,NH*part,128),F32),v((2,D,cols),F32),v((2,4,2,2,rows,cols),BF),v((D,WIN),BF),v((3,WIN,D),BF),v((D,WIN),F32),
        v((nW,SLAB,D),BF),v(sm.shape,F32),v((nh,NH,256),F32),v((2,nh//2,NH//2,256),F32),v((5,nh//2,NH//2,256),F32),v((3,nh,NH//2,256),F32),v((10,)+sm.shape,F32),
        dma((NH,)),dma((NH,)),dma((nW,)),dma((nW,)),dma((nW,)),dma((2,)),dma,dma((13,)),dma((13,))]+reduce_scratch(rows,cols)+reduce_scratch(rows,more),
      compiler_params=pltpu.CompilerParams(vmem_limit_bytes=63*1024*1024,dimension_semantics=("arbitrary",),collective_id=3,has_side_effects=True),
      name="kernel_bc")(x,gln2,qkv,g,gT,Dd,Pp,W1,gains,shifts,sm,pp,dcat)

def gathered(piece,names,nseq,nheads):
    full=lax.all_gather(piece,names,axis=0,tiled=False)
    return full.reshape((nseq,nheads)+piece.shape)

def natural(block):
    s,h,r,c=block.shape
    return block.transpose(0,2,1,3).reshape(s*r,h*c)

def owners(grad,nseq,nheads):
    r,c=grad.shape
    return grad.reshape(nseq,r//nseq,nheads,c//nheads).transpose(0,2,1,3).reshape(nseq*nheads,r//nseq,c//nheads)

def from_next(rows):
    n=lax.axis_size("seq")
    return lax.ppermute(rows,"seq",[(i,(i-1)%n) for i in range(n)])

def to_next(rows):
    n=lax.axis_size("seq")
    return lax.ppermute(rows,"seq",[(i,(i+1)%n) for i in range(n)])

def spread(rows):
    n=lax.axis_size("heads")
    flat=rows.reshape(-1,rows.shape[-1])
    if n==2:
        other=lax.ppermute(flat,"heads",[(0,1),(1,0)])
        me=lax.axis_index("heads")
        return jnp.where(me==0,jnp.concatenate([flat,other]),jnp.concatenate([other,flat]))
    return lax.all_gather(flat,"heads",axis=0,tiled=True)

def place(rows,base,shift):
    every=spread(rows)
    keep=every.shape[0]-shift
    return base+jnp.concatenate([to_next(every[keep:]),every[:keep]]).astype(F32)

def settle(slabs,edge,base,shift):
    n,size,D=slabs.shape; WIN=2*shift
    keep=base.shape[0]-shift
    off=edge.shape[0]-(size-shift)
    return base+jnp.concatenate([edge[off:off+shift],slabs[:,:WIN].reshape(n*WIN,D)[:keep]]).astype(F32)

def body(inputs,w_qkv,w_proj,w_fc1,w_fc2,gains,shifts,rel_table,region,pos_index,out_grad):
    nseq=lax.axis_size("seq"); nheads=lax.axis_size("heads"); me=lax.axis_index("heads")
    linked=nseq==16 and nheads==2
    names=("seq","heads")
    tok,D=inputs.shape; WIN=pos_index.shape[0]; shift=WIN//2; T=rel_table.shape[1]
    nW=tok//WIN//nheads
    rows=w_qkv.shape[1]; cq=w_qkv.shape[2]; cf=w_fc1.shape[1]
    posT=pos_index.T
    wide=-(-WIN//128)*128
    posP=jnp.pad(posT,((0,0),(0,wide-WIN)))
    start=me*nW*WIN
    lab=lax.dynamic_slice_in_dim(region,start,nW*WIN,0).reshape(nW,WIN)
    labc=lab[:,:,None]; labr=lab[:,None,:]
    wq=jnp.concatenate([w_qkv[0],w_qkv[1],w_qkv[2],w_proj.T],axis=1).astype(BF)
    wf=jnp.concatenate([w_fc1,w_fc2.T],axis=1).astype(BF)
    if linked:
        n=-(-T//128)
        tab=jnp.pad(rel_table,((0,0),(0,n*128-T))).reshape(-1,n,128)
        W1,bias=call_w(wq,posP,tab,WIN)
        qkv,x,Pp,gln2,g,gT,Dd,ev,hd,dcat,sm=call_a2(inputs,out_grad,wf,labc,labr,bias,W1,gains,shifts)
        output=settle(ev,hd,inputs,shift)
        ev2,hd2,redq,redm,d_table,small=call_bc(x,gln2,qkv,g,gT,Dd,Pp,W1,gains,shifts,sm,posT,dcat.reshape(2,4,2,2,rows,-1),T)
        d_table=d_table[:,:T]
        d_inputs=settle(ev2,hd2,out_grad,shift)
    else:
        table=lax.all_gather(rel_table,"heads",axis=0,tiled=True)
        NH=table.shape[0]
        every=gathered(jnp.concatenate([wq,wf],axis=1),names,nseq,nheads)
        ends=[i*cq for i in range(5)]+[4*cq+cf,4*cq+2*cf]
        W=jnp.concatenate([natural(every[...,a:b]) for a,b in zip(ends[:-1],ends[1:])],axis=1)[None]
        bias=call_p(posP,pack_table(table),WIN)
        def mine(v):
            ext=jnp.concatenate([v,from_next(v[:shift])])
            return lax.dynamic_slice_in_dim(ext,start+shift,nW*WIN,0).reshape(nW,WIN,-1)
        x=mine(inputs); og=mine(out_grad)
        delta,gln2,qkv,g,gT,Dd,Pp,dcat,sm_a=call_a(x,og,labc,labr,bias,W,gains,shifts)
        dd,dqkv,G,sm_b=call_b(x,gln2,qkv,g,gT,Dd,Pp,W,gains,shifts)
        grads=[dqkv[0,:,c*D:(c+1)*D] for c in range(3)]+[dcat[0,:,:D],dcat[0,:,D:D+cf*nheads],dcat[0,:,D+cf*nheads:]]
        red=lax.psum_scatter(jnp.concatenate([owners(v,nseq,nheads) for v in grads],axis=2),names,scatter_dimension=0,tiled=False).astype(F32)
        redq,redm=red[:,:3*cq],red[:,3*cq:]
        d_table,small=lax.psum((call_t(G,posT,T,NH),sm_a+sm_b),names)
        nl=rel_table.shape[0]
        d_table=lax.dynamic_slice_in_dim(d_table,me*nl,nl,0)
        output=place(delta,inputs,shift)
        d_inputs=place(dd,out_grad,shift)
    d_qkv=redq.reshape(rows,3,cq).transpose(1,0,2)
    d_proj=redm[:,:cq].T; d_fc1=redm[:,cq:cq+cf]; d_fc2=redm[:,cq+cf:].T
    return (output,d_inputs,d_qkv,d_proj,d_fc1,d_fc2,small[0:2],small[2:6],d_table)

def solution(mesh):
    placed=(P("seq",None),P(None,"seq","heads"),P("heads","seq"),P("seq","heads"),P("heads","seq"),P(),P(),P("heads",None),P("seq"),P(),P("seq",None))
    return jax.shard_map(body,mesh=mesh,in_specs=placed,
        out_specs=(P("seq",None),P("seq",None),P(None,"seq","heads"),P("heads","seq"),P("seq","heads"),P("heads","seq"),P(),P(),P("heads",None)),
        check_vma=False)
```

```python
import functools
import math

import jax, jax.numpy as jnp
from jax import lax
from jax.experimental import pallas as pl
from jax.experimental.pallas import tpu as pltpu
from jax.sharding import PartitionSpec as P

BF=jnp.bfloat16; F32=jnp.float32
HD=32; GROUP=128; PER=4
EPS=1e-5
SQ=math.sqrt(32.0)
CEXP=math.log2(math.e)/SQ
MASK=100.0*SQ

def mm(a,b):
    return lax.dot_general(a,b,(((1,),(0,)),((),())),preferred_element_type=F32)
def mm_nt(a,b):
    return lax.dot_general(a,b,(((1,),(1,)),((),())),preferred_element_type=F32)

def norm_stats(v):
    mean=jnp.mean(v,axis=-1,keepdims=True)
    c=v-mean
    var=jnp.mean(c*c,axis=-1,keepdims=True)
    rstd=lax.rsqrt(var+EPS)
    return c*rstd, rstd

def norm_back(gy,xhat,rstd,gain):
    gx=gy*gain
    m1=jnp.mean(gx,axis=-1,keepdims=True)
    m2=jnp.mean(gx*xhat,axis=-1,keepdims=True)
    return rstd*(gx-m1-xhat*m2)

P0=0.3275911
A1,A2,A3,A4,A5=0.254829592,-0.284496736,1.421413741,-1.453152027,1.061405429
def gelu_both(x):
    e=jnp.exp2(x*x*(-0.5*math.log2(math.e)))
    t=1.0/(1.0+(P0/math.sqrt(2.0))*jnp.abs(x))
    poly=t*(0.5*A1+t*(0.5*A2+t*(0.5*A3+t*(0.5*A4+t*(0.5*A5)))))
    half=poly*e
    phi=jnp.where(x>=0,1.0-half,half)
    return x*phi, phi+x*e*(1.0/math.sqrt(2.0*math.pi))

def kernel_a(nheads,x_ref,og_ref,labc_ref,labr_ref,bias_ref,W_ref,gains_ref,shifts_ref,
             delta_ref,gln2_ref,qkv_ref,g_ref,gT_ref,D_ref,P_hbm,dcat_ref,small_ref,
             qT_s,vT_s,OT_s,P_s,acc,sem,xn2_s,xn2T_s,tg_s,tgT_s,up_s,gn2_s):
    w=pl.program_id(0); nw=pl.num_programs(0)
    D=x_ref.shape[-1]; WIN=x_ref.shape[-2]
    parts=W_ref.shape[0]; cq=D//parts; cf=(W_ref.shape[2]-4*cq)//2
    groups=nheads//PER
    x=x_ref[0]
    xhat,_=norm_stats(x)
    xn=(xhat*gains_ref[0:1,:]+shifts_ref[0:1,:]).astype(BF)
    for c in range(3):
        for m in range(parts):
            at=slice(m*cq,(m+1)*cq)
            y=mm(xn,W_ref[m,:,c*cq:(c+1)*cq]).astype(BF)
            qkv_ref[0,c,:,at]=y
            if c==0: qT_s[at,:]=y.T
            if c==2: vT_s[at,:]=y.T
    labc=labc_ref[0]; labr=labr_ref[0]
    lane=lax.broadcasted_iota(jnp.int32,(WIN,GROUP),1)
    oh=jnp.where((labc==lane)|((labc+3)==lane),1.0,0.0).astype(BF)
    hi=564.0
    lo=MASK-hi
    sub=lax.broadcasted_iota(jnp.int32,(GROUP,WIN),0)
    nm=jnp.where(sub<3,jnp.where(sub!=labr,-hi,0.0),jnp.where(sub<6,jnp.where(sub-3!=labr,-lo,0.0),0.0)).astype(BF)
    hl=lane//HD

    def group(gi,_):
        slot=gi%2
        step=w*groups+gi
        @pl.when(step>=2)
        def _():
            pltpu.make_async_copy(P_s.at[slot],P_hbm.at[0,pl.ds(0,PER)],sem.at[slot]).wait()
        o=pl.multiple_of(gi*GROUP,GROUP)
        qTg=jnp.concatenate([qT_s[pl.ds(o,GROUP),:],nm],axis=0)
        kg=qkv_ref[0,1,:,pl.ds(o,GROUP)]
        for hh in range(PER):
            kh=jnp.concatenate([jnp.where(hl==hh,kg,jnp.zeros_like(kg)),oh],axis=1)
            t=mm(kh,qTg)+bias_ref[gi*PER+hh]
            m=jnp.max(t,axis=0,keepdims=True)
            e=jnp.exp2((t-m)*CEXP)
            l=jnp.sum(e,axis=0,keepdims=True)
            p=(e*(1.0/l)).astype(BF)
            P_s[slot,hh]=p
            OT_s[pl.ds(o+hh*HD,HD),:]=mm(vT_s[pl.ds(o+hh*HD,HD),:],p)
        pltpu.make_async_copy(P_s.at[slot],P_hbm.at[w,pl.ds(gi*PER,PER)],sem.at[slot]).start()
        return 0
    lax.fori_loop(0,groups,group,0)

    attn=OT_s[...].astype(BF).T
    branch=shifts_ref[2:3,:]
    for m in range(parts):
        branch=branch+mm_nt(attn[:,m*cq:(m+1)*cq],W_ref[m,:,3*cq:4*cq])
    branch=branch.astype(BF).astype(F32)
    middle=x+branch
    xhat2,rstd2=norm_stats(middle)
    xn2=(xhat2*gains_ref[1:2,:]+shifts_ref[1:2,:]).astype(BF)
    og=og_ref[0]
    tg=og.astype(BF)
    xn2_s[...]=xn2; xn2T_s[...]=xn2.T; tg_s[...]=tg; tgT_s[...]=tg.T
    up_s[...]=jnp.zeros_like(up_s); gn2_s[...]=jnp.zeros_like(gn2_s)
    CH=min(512,cf); each=cf//CH
    @pl.when(w==0)
    def _():
        acc[...]=jnp.zeros_like(acc)
        small_ref[...]=jnp.zeros_like(small_ref)
    def chunk(c,_):
        m=c//each
        o=pl.multiple_of((c%each)*CH,CH)
        f1=W_ref[m,:,pl.ds(4*cq+o,CH)]; f2=W_ref[m,:,pl.ds(4*cq+cf+o,CH)]
        hid=mm(xn2_s[...],f1)
        act,dact=gelu_both(hid)
        a=act.astype(BF)
        up_s[...]+=mm_nt(a,f2)
        gh=(mm(tg_s[...],f2)*dact).astype(BF)
        gn2_s[...]+=mm_nt(gh,f1)
        acc[m,:,pl.ds(cq+o,CH)]+=mm(xn2T_s[...],gh)
        acc[m,:,pl.ds(cq+cf+o,CH)]+=mm(tgT_s[...],a)
        return 0
    lax.fori_loop(0,parts*each,chunk,0)
    delta_ref[0]=(branch+up_s[...]+shifts_ref[3:4,:]).astype(BF)
    gn2=gn2_s[...]
    gln2=norm_back(gn2,xhat2,rstd2,gains_ref[1:2,:])
    gln2_ref[0]=gln2
    gb=(og+gln2).astype(BF)
    gbT=gb.T
    for m in range(parts):
        at=slice(m*cq,(m+1)*cq)
        acc[m,:,0:cq]+=mm(gbT,attn[:,at])
        g=mm(gb,W_ref[m,:,3*cq:4*cq]).astype(BF)
        g_ref[0,:,at]=g
        gT=g.T
        gT_ref[0,at,:]=gT
        prod=gT.astype(F32)*OT_s[at,:]
        nh=nheads//parts
        D_ref[0,m*nh:(m+1)*nh,:]=jnp.sum(prod.reshape(nh,HD,WIN),axis=1)
    small_ref[1:2,:]+=jnp.sum(gn2*xhat2,axis=0,keepdims=True)
    small_ref[3:4,:]+=jnp.sum(gn2,axis=0,keepdims=True)
    small_ref[4:5,:]+=jnp.sum(gb.astype(F32),axis=0,keepdims=True)
    small_ref[5:6,:]+=jnp.sum(tg.astype(F32),axis=0,keepdims=True)
    @pl.when(w==nw-1)
    def _():
        dcat_ref[...]=acc[...].astype(BF)
        for s in range(2):
            pltpu.make_async_copy(P_s.at[s],P_hbm.at[0,pl.ds(0,PER)],sem.at[s]).wait()

def full(shape,**kw):
    return pl.BlockSpec(shape,lambda w:(0,)*len(shape),**kw)
def per(shape):
    return pl.BlockSpec((1,)+shape,lambda w:(w,)+(0,)*len(shape))
ONE=pl.Buffered(1)
ANY=pl.BlockSpec(memory_space=pl.ANY)

def call_a(x,og,labc,labr,bias,W,gains,shifts):
    nW,WIN,D=x.shape; NH=bias.shape[0]
    parts,_,Ct=W.shape; Cg=Ct-3*(D//parts)
    sd=jax.ShapeDtypeStruct
    outs=[sd((nW,WIN,D),BF),sd((nW,WIN,D),F32),sd((nW,3,WIN,D),BF),sd((nW,WIN,D),BF),sd((nW,D,WIN),BF),sd((nW,NH,WIN),F32),
          sd((nW,NH,WIN,WIN),BF),sd((parts,D,Cg),BF),sd((8,D),F32)]
    return pl.pallas_call(functools.partial(kernel_a,NH),grid=(nW,),
      in_specs=[per((WIN,D)),per((WIN,D)),per((WIN,1)),per((1,WIN)),full((NH,WIN,WIN),pipeline_mode=ONE),
        full((parts,D,Ct),pipeline_mode=ONE),full(gains.shape),full(shifts.shape)],
      out_specs=[per((WIN,D)),per((WIN,D)),per((3,WIN,D)),per((WIN,D)),per((D,WIN)),per((NH,WIN)),ANY,full((parts,D,Cg)),full((8,D))],
      out_shape=outs,
      scratch_shapes=[pltpu.VMEM((D,WIN),BF),pltpu.VMEM((D,WIN),BF),pltpu.VMEM((D,WIN),F32),pltpu.VMEM((2,PER,WIN,WIN),BF),
        pltpu.VMEM((parts,D,Cg),F32),pltpu.SemaphoreType.DMA((2,)),
        pltpu.VMEM((WIN,D),BF),pltpu.VMEM((D,WIN),BF),pltpu.VMEM((WIN,D),BF),pltpu.VMEM((D,WIN),BF),pltpu.VMEM((WIN,D),F32),pltpu.VMEM((WIN,D),F32)],
      compiler_params=pltpu.CompilerParams(vmem_limit_bytes=62*1024*1024,dimension_semantics=("arbitrary",)),
      name="kernel_a")(x,og,labc,labr,bias,W,gains,shifts)

def kernel_b(nheads,x_ref,gln2_ref,qkv_ref,g_ref,gT_ref,D_ref,P_ref,W_ref,gains_ref,shifts_ref,
             dd_ref,dqkv_ref,G_hbm,small_ref,G_s,aq,kT_s,gq_s,gqT_s,sem):
    w=pl.program_id(0); nw=pl.num_programs(0)
    D=x_ref.shape[-1]; WIN=x_ref.shape[-2]
    parts=W_ref.shape[0]; cq=D//parts
    groups=nheads//PER
    @pl.when(w==0)
    def _():
        aq[...]=jnp.zeros_like(aq); G_s[...]=jnp.zeros_like(G_s); small_ref[...]=jnp.zeros_like(small_ref)
    kT_s[...]=qkv_ref[0,1].T
    lane=lax.broadcasted_iota(jnp.int32,(WIN,GROUP),1)
    hl=lane//HD
    def group(gi,_):
        o=pl.multiple_of(gi*GROUP,GROUP)
        gTg=gT_ref[0,pl.ds(o,GROUP),:]
        vg=qkv_ref[0,2,:,pl.ds(o,GROUP)]
        qg=qkv_ref[0,0,:,pl.ds(o,GROUP)]
        gg=g_ref[0,:,pl.ds(o,GROUP)]
        dv=jnp.zeros((WIN,GROUP),F32); dk=jnp.zeros((WIN,GROUP),F32)
        zero=jnp.zeros_like(vg)
        for hh in range(PER):
            h=gi*PER+hh
            p=P_ref[0,h]
            dp=mm(jnp.where(hl==hh,vg,zero),gTg)
            ds_=p.astype(F32)*(dp-D_ref[0,pl.ds(h,1),:])
            for c in range(G_s.shape[0]):
                wd=min(128,WIN-c*128)
                G_s[c,pl.ds(pl.multiple_of(h*WIN,8),WIN),:wd]+=ds_[:,c*128:c*128+wd]
            dsl=ds_.astype(BF)
            dv+=mm(p,jnp.where(hl==hh,gg,zero))
            dk+=mm(dsl,jnp.where(hl==hh,qg,zero))
            gqT_s[pl.ds(o+hh*HD,HD),:]=mm(kT_s[pl.ds(o+hh*HD,HD),:],dsl)
        gq_s[1,:,pl.ds(o,GROUP)]=(dk*(1.0/SQ)).astype(BF)
        gq_s[2,:,pl.ds(o,GROUP)]=dv.astype(BF)
        return 0
    lax.fori_loop(0,groups,group,0)
    gq_s[0]=(gqT_s[...]*(1.0/SQ)).astype(BF).T
    x=x_ref[0]
    xhat,rstd=norm_stats(x)
    xn=(xhat*gains_ref[0:1,:]+shifts_ref[0:1,:]).astype(BF)
    xnT=xn.T
    gr=jnp.zeros((WIN,D),F32)
    for m in range(parts):
        for c in range(3):
            gc=gq_s[c,:,m*cq:(m+1)*cq]
            gr=gr+mm_nt(gc,W_ref[m,:,c*cq:(c+1)*cq])
            aq[m,:,c*cq:(c+1)*cq]+=mm(xnT,gc)
    dd_ref[0]=(gln2_ref[0]+norm_back(gr,xhat,rstd,gains_ref[0:1,:])).astype(BF)
    small_ref[0:1,:]+=jnp.sum(gr*xhat,axis=0,keepdims=True)
    small_ref[2:3,:]+=jnp.sum(gr,axis=0,keepdims=True)
    @pl.when(w==nw-1)
    def _():
        dqkv_ref[...]=aq[...].astype(BF)
        cp=pltpu.make_async_copy(G_s,G_hbm,sem); cp.start(); cp.wait()

def call_b(x,gln2,qkv,g,gT,Dd,Pp,W,gains,shifts):
    nW,WIN,D=x.shape; NH=Dd.shape[1]
    parts=W.shape[0]; cq=D//parts; tiles=-(-WIN//128)
    sd=jax.ShapeDtypeStruct
    return pl.pallas_call(functools.partial(kernel_b,NH),grid=(nW,),
      in_specs=[per((WIN,D)),per((WIN,D)),per((3,WIN,D)),per((WIN,D)),per((D,WIN)),per((NH,WIN)),per((NH,WIN,WIN)),
        full((parts,D,3*cq),pipeline_mode=ONE),full(gains.shape),full(shifts.shape)],
      out_specs=[per((WIN,D)),full((parts,D,3*cq)),ANY,full((8,D))],
      out_shape=[sd((nW,WIN,D),BF),sd((parts,D,3*cq),BF),sd((tiles,NH*WIN,128),F32),sd((8,D),F32)],
      scratch_shapes=[pltpu.VMEM((tiles,NH*WIN,128),F32),pltpu.VMEM((parts,D,3*cq),F32),pltpu.VMEM((D,WIN),BF),pltpu.VMEM((3,WIN,D),BF),pltpu.VMEM((D,WIN),F32),
        pltpu.SemaphoreType.DMA],
      compiler_params=pltpu.CompilerParams(vmem_limit_bytes=62*1024*1024,dimension_semantics=("arbitrary",)),
      name="kernel_b")(x,gln2,qkv,g,gT,Dd,Pp,W,gains,shifts)

FIX=8191.0

def pack_table(table):
    NH,T=table.shape
    n=-(-T//128)
    q=jnp.round(jnp.clip(table,-4.0,4.0)*FIX).astype(jnp.int32)
    q=jnp.pad(q,((0,0),(0,n*128-T)))
    q=q.reshape(NH//2,2,n,128)
    return (q[:,0]*65536)|(q[:,1]&65535)

def kernel_p(pos_ref,tab_ref,bias_ref):
    npair,n,_=tab_ref.shape
    WIN=bias_ref.shape[-1]
    tiles=-(-WIN//128)
    def row(r,_):
        r8=pl.multiple_of(r*8,8)
        for c in range(tiles):
            width=min(128,WIN-c*128)
            idx=pos_ref[pl.ds(r8,8),c*128:(c+1)*128]
            lo=idx&127; hi=idx>>7
            masks=[hi==k for k in range(n)]
            for p in range(npair):
                acc=jnp.zeros((8,128),jnp.int32)
                for k in range(n):
                    src=jnp.broadcast_to(tab_ref[p,k:k+1,:],(8,128))
                    acc=jnp.where(masks[k],jnp.take_along_axis(src,lo,axis=1),acc)
                a=(acc>>16).astype(F32)*(SQ/FIX)
                b=((acc<<16)>>16).astype(F32)*(SQ/FIX)
                bias_ref[2*p,pl.ds(r8,8),c*128:c*128+width]=a[:,:width]
                bias_ref[2*p+1,pl.ds(r8,8),c*128:c*128+width]=b[:,:width]
        return 0
    lax.fori_loop(0,bias_ref.shape[1]//8,row,0)

def call_p(posT_pad,tab,WIN):
    NH=tab.shape[0]*2
    return pl.pallas_call(kernel_p,out_shape=jax.ShapeDtypeStruct((NH,WIN,WIN),F32),
      compiler_params=pltpu.CompilerParams(vmem_limit_bytes=40*1024*1024),name="kernel_p")(posT_pad,tab)

def kernel_t(NH,G_ref,hi_ref,lo_ref,out_ref):
    WIN=hi_ref.shape[0]; LW=G_ref.shape[0]*128
    nh=out_ref.shape[0]//NH
    out_ref[...]=jnp.zeros_like(out_ref)
    def rows(r,_):
        r8=pl.multiple_of(r*8,8)
        hi8=hi_ref[pl.ds(r8,8),:]; lo8=lo_ref[pl.ds(r8,8),:]
        tot=jnp.zeros(out_ref.shape,F32)
        iota=lax.broadcasted_iota(jnp.int32,(256,LW),0).astype(F32).astype(BF)
        for k in range(8):
            g=jnp.concatenate([G_ref[c,pl.ds(r8+k,NH,stride=WIN),:] for c in range(LW//128)],axis=1)
            hr=hi8[k:k+1,:]; lr=lo8[k:k+1,:].astype(F32).astype(BF)
            A=jnp.concatenate([jnp.where(hr==m,g,0.0) for m in range(nh)],axis=0).astype(BF)
            oh=jnp.where(iota==lr,jnp.ones((),BF),jnp.zeros((),BF))
            tot=tot+lax.dot_general(A,oh,(((1,),(1,)),((),())),preferred_element_type=F32)
        out_ref[...]+=tot
        return 0
    lax.fori_loop(0,WIN//8,rows,0)

def call_t(G,posT,T,NH):
    WIN=posT.shape[0]; nt=G.shape[0]
    nh=-(-T//256)
    pp=jnp.pad(posT,((0,0),(0,nt*128-WIN)),constant_values=nh*256)
    hi=pp>>8; lo=pp&255
    o=pl.pallas_call(functools.partial(kernel_t,NH),out_shape=jax.ShapeDtypeStruct((nh*NH,256),F32),
      compiler_params=pltpu.CompilerParams(vmem_limit_bytes=40*1024*1024),name="kernel_t")(G,hi,lo)
    return o.reshape(nh,NH,256).transpose(1,0,2).reshape(NH,nh*256)[:,:T]


MESHID=pl.DeviceIdType.MESH

def place_of():
    s=lax.axis_index("seq"); y=lax.axis_index("heads")
    return s//4,(s//2)%2,s%2,y

def dev(z,x,c,y):
    return ((z*2+x)*2+c,y)

def peers_of(z,x,c,y):
    return [dev(z,x,1-c,y),dev(z,1-x,c,y),dev(z,x,c,1-y)]+[dev((z+i)%4,x,c,y) for i in (1,2,3)]

def greet(devices):
    bar=pltpu.get_barrier_semaphore()
    for d in devices:
        pl.semaphore_signal(bar,inc=1,device_id=d,device_id_type=MESHID)
    pl.semaphore_wait(bar,len(devices))

def send(src,dst,ss,rs,to):
    return pltpu.make_async_remote_copy(src_ref=src,dst_ref=dst,send_sem=ss,recv_sem=rs,device_id=to,device_id_type=MESHID)


class Gather:
    def __init__(self,src,dst,ss,rs,own):
        self.src,self.dst,self.ss,self.rs,self.own=src,dst,ss,rs,own
        z,x,c,y=self.at=place_of()
        self.xa=x+(1-2*x)*(1-c); self.ya=y+(1-2*y)*c
        self.xb=x+(1-2*x)*c; self.yb=y+(1-2*y)*(1-c)
        self.sib=dev(z,x,1-c,y); self.pa=dev(z,self.xa,c,self.ya); self.pb=dev(z,self.xb,c,self.yb)
    def slot(self,zz,xx,cc,yy):
        n=self.src.shape[0]
        return self.dst.at[yy,pl.ds(pl.multiple_of(((zz*2+xx)*2+cc)*n,n),n)]
    def copy(self,src,where,k,to):
        return send(src,self.slot(*where),self.ss.at[k],self.rs.at[k],to)
    def go(self,where,k,to,src=None):
        self.copy(self.slot(*where) if src is None else src,where,k,to).start()
    def came(self,where,k):
        self.copy(self.src,where,k,self.sib).wait_recv()
    def keep(self):
        z,x,c,y=self.at
        return pltpu.make_async_copy(self.src,self.slot(z,x,c,y),self.own)
    def start(self):
        z,x,c,y=self.at
        me=(z,x,c,y)
        self.keep().start()
        for i in (1,2,3):
            self.go(me,i-1,dev((z+i)%4,x,c,y),self.src)
        self.go(me,3,self.pa,self.src); self.go(me,7,self.pb,self.src); self.go(me,15,self.sib,self.src)
    def z(self,i):
        return (self.at[0]+4-i)%4
    def turn_z(self,i):
        z,x,c,y=self.at
        at=(self.z(i),x,c,y); self.came(at,i-1)
        self.go(at,3+i,self.pa); self.go(at,7+i,self.pb); self.go(at,15+i,self.sib)
    def turn_a(self,i):
        at=(self.z(i),self.xa,self.at[2],self.ya); self.came(at,3+i)
        self.go(at,11+i,self.pb); self.go(at,19+i,self.sib)
    def turn_b(self,i):
        at=(self.z(i),self.xb,self.at[2],self.yb); self.came(at,7+i)
        self.go(at,23+i,self.sib)
    def turn_ab(self,i):
        z,x,c,y=self.at
        at=(self.z(i),1-x,c,1-y); self.came(at,11+i)
        self.go(at,27+i,self.sib)
    def last(self):
        z,x,c,y=self.at
        for i in range(4):
            zz=self.z(i)
            self.came((zz,x,1-c,y),15+i); self.came((zz,self.xb,1-c,self.yb),19+i)
            self.came((zz,self.xa,1-c,self.ya),23+i); self.came((zz,1-x,1-c,1-y),27+i)
    def drain(self):
        z,x,c,y=self.at
        for k in range(31):
            self.copy(self.src,(z,x,c,y),k,self.sib).wait_send()
        self.keep().wait()

def gather_sems():
    return [pltpu.SemaphoreType.DMA((31,)),pltpu.SemaphoreType.DMA((31,)),pltpu.SemaphoreType.DMA]

STEPS=7
def kernel_w(qkv_ref,proj_ref,fc1_ref,fc2_ref,pos_ref,tab_ref,W_hbm,bias_hbm,wf_ref,posT_ref,
             bias_s,wq_s,tb,tq,ss,rs,own,bs,br,bl,tsem):
    z,x,c,y=place_of()
    cq=qkv_ref.shape[2]; cf=fc1_ref.shape[1]
    for k in range(3): wq_s[:,k*cq:(k+1)*cq]=qkv_ref[k].astype(BF)
    wq_s[:,3*cq:4*cq]=proj_ref[...].T.astype(BF)
    half,T=tab_ref.shape
    tb[2]=jnp.zeros(tb.shape[1:],F32)
    tb[2,:,0:T]=tab_ref[...]
    greet(peers_of(z,x,c,y))
    gather=Gather(wq_s,W_hbm,ss,rs,own)
    swap=send(tb.at[2],tb.at[y],tsem.at[0],tsem.at[1],dev(z,x,c,1-y))
    swap.start()
    gather.start()
    tb[y]=tb[2]
    wf_ref[:,0:cf]=fc1_ref[...].astype(BF)
    wf_ref[:,cf:2*cf]=fc2_ref[...].T.astype(BF)
    WIN=bias_s.shape[-1]; tiles=-(-WIN//128); n=tb.shape[2]//128
    posT_ref[...]=jnp.full(posT_ref.shape,1<<15,jnp.int32)
    posT_ref[:,0:WIN]=pos_ref[...].astype(F32).T.astype(jnp.int32)
    swap.wait()
    npair=half//2
    for p in range(npair):
        a,b=[jnp.floor(jnp.clip(tb[c,2*p+k:2*p+k+1,:],-4.0,4.0)*FIX+0.5).astype(jnp.int32) for k in range(2)]
        tq[p:p+1,:]=(a*65536)|(b&65535)
    nrow=WIN//8
    cuts=[nrow*k//STEPS for k in range(STEPS+1)]
    sib=dev(z,x,1-c,y)
    def rows_of(k): return pl.ds(cuts[k]*8,(cuts[k+1]-cuts[k])*8)
    def kept(k): return pltpu.make_async_copy(bias_s.at[:,rows_of(k)],bias_hbm.at[pl.ds(c*half,half),rows_of(k)],bl.at[k])
    def sent(k,cc): return send(bias_s.at[:,rows_of(k)],bias_hbm.at[pl.ds(cc*half,half),rows_of(k)],bs.at[k],br.at[k],sib)
    def rows(k):
        def row(r,_):
            r8=pl.multiple_of(r*8,8)
            for t in range(tiles):
                width=min(128,WIN-t*128)
                idx=posT_ref[pl.ds(r8,8),t*128:(t+1)*128]
                lo=idx&127; hi=idx>>7
                masks=[hi==q for q in range(n)]
                for p in range(npair):
                    acc=jnp.zeros((8,128),jnp.int32)
                    for q in range(n):
                        src=jnp.broadcast_to(tq[p:p+1,q*128:(q+1)*128],(8,128))
                        acc=jnp.where(masks[q],jnp.take_along_axis(src,lo,axis=1),acc)
                    a=(acc>>16).astype(F32)*(SQ/FIX)
                    b=((acc<<16)>>16).astype(F32)*(SQ/FIX)
                    bias_s[2*p,pl.ds(r8,8),t*128:t*128+width]=a[:,:width]
                    bias_s[2*p+1,pl.ds(r8,8),t*128:t*128+width]=b[:,:width]
            return 0
        lax.fori_loop(cuts[k],cuts[k+1],row,0)
        kept(k).start(); sent(k,c).start()
    rows(0)
    for i in (1,3,2): gather.turn_z(i)
    rows(1)
    for i in (0,): gather.turn_a(i); gather.turn_b(i)
    rows(2)
    for i in (1,3): gather.turn_a(i); gather.turn_b(i)
    rows(3)
    for i in (2,): gather.turn_a(i); gather.turn_b(i)
    gather.turn_ab(0)
    rows(4)
    for i in (1,3): gather.turn_ab(i)
    rows(5)
    gather.turn_ab(2)
    rows(6)
    gather.last()
    for k in range(STEPS):
        kept(k).wait(); sent(k,c).wait_send(); sent(k,1-c).wait_recv()
    gather.drain()

def call_w(w_qkv,w_proj,w_fc1,w_fc2,pos_index,rel_table):
    rows,cq=w_qkv.shape[1:]; cf=w_fc1.shape[1]; WIN=pos_index.shape[0]; half,T=rel_table.shape; dma=pltpu.SemaphoreType.DMA
    wide=-(-WIN//128)*128; n=-(-T//128); v=pltpu.VMEM
    sd=jax.ShapeDtypeStruct
    vm=pl.BlockSpec(memory_space=pltpu.VMEM)
    return pl.pallas_call(kernel_w,
      out_shape=[sd((2,16*rows,4*cq),BF),sd((2*half,WIN,WIN),F32),sd((rows,2*cf),BF),sd((WIN,wide),jnp.int32)],
      in_specs=[vm]*6,out_specs=[ANY,ANY,vm,vm],
      scratch_shapes=[v((half,WIN,WIN),F32),v((rows,4*cq),BF),v((3,half,n*128),F32),v((half//2,n*128),jnp.int32)]
        +gather_sems()+[dma((STEPS,)),dma((STEPS,)),dma((STEPS,)),dma((2,))],
      compiler_params=pltpu.CompilerParams(vmem_limit_bytes=40*1024*1024,collective_id=1,has_side_effects=True),name="kernel_w")(w_qkv,w_proj,w_fc1,w_fc2,pos_index,rel_table)

def neighbours(z,x,c,y):
    s=(z*2+x)*2+c
    return [((s+k)%16,yy) for k in (1,15) for yy in (y,1-y)]

def kernel_a2(nheads,in_hbm,og_hbm,wf_hbm,lab_ref,bias_ref,W1,gains_ref,shifts_ref,
              qkv_ref,x_ref,P_hbm,gln2_ref,g_ref,gT_ref,D_ref,ev_hbm,dlast_hbm,dcat_hbm,small_ref,
              x_s,og_s,W2,OT_s,qT_s,vT_s,P_s,acc,pst,xn2_s,xn2T_s,tg_s,tgT_s,up_s,gn2_s,dl_s,
              lab_s,psem,xsem,hsem,ss,rs,own,dl,ds,dr,fin):
    i=pl.program_id(0); nw=x_s.shape[0]
    w=i%nw
    z,xc,c,y=place_of()
    s=(z*2+xc)*2+c
    D=x_s.shape[-1]; WIN=qkv_ref.shape[-2]; SLAB=x_s.shape[1]; HALF=SLAB//2
    OFF=(SLAB-WIN)//2
    cq=D//2; cf=W2.shape[2]//2
    groups=nheads//PER
    gather=Gather(wf_hbm,W2,ss,rs,own)
    mate=dev(z,xc,c,1-y)
    def local(k,half,t):
        hbm,buf=((in_hbm,x_s),(og_hbm,og_s))[t]
        r=pl.multiple_of(y*(nw*WIN)+k*WIN+(WIN//2-OFF)+half*HALF,8)
        return pltpu.make_async_copy(hbm.at[pl.ds(r,HALF)],buf.at[k,pl.ds(half*HALF,HALF)],xsem.at[t,2*k+half])
    def edge(t):
        hbm,buf=((in_hbm,x_s),(og_hbm,og_s))[t]
        return send(hbm.at[pl.ds(0,HALF)],buf.at[nw-1,pl.ds(HALF,HALF)],hsem.at[t,0],hsem.at[t,1],((s+15)%16,1))
    def ready(t):
        local(w,0,t).wait()
        far=jnp.logical_and(w==nw-1,y==1)
        @pl.when(far)
        def _(): edge(t).wait_recv()
        @pl.when(jnp.logical_not(far))
        def _(): local(w,1,t).wait()
    def slab(k,to=None):
        if k is None: return pltpu.make_async_copy(dl_s.at[nw-1],dlast_hbm,dl.at[nw-1])
        at=ev_hbm.at[y*nw+k]
        if to is None: return pltpu.make_async_copy(dl_s.at[k],at,dl.at[k])
        return send(dl_s.at[k],at,ds.at[k],dr.at[k],to)
    @pl.when(i==0)
    def _():
        greet(peers_of(z,xc,c,y)+neighbours(z,xc,c,y))
        for k in range(nw):
            for t in range(2):
                local(k,0,t).start()
                if k<nw-1: local(k,1,t).start()
        for t in range(2):
            @pl.when(y==1)
            def _(): edge(t).start()
            @pl.when(y==0)
            def _(): local(nw-1,1,t).start()
        gather.start()
        lab_s[...]=lab_ref[...].astype(F32).T
        acc[...]=jnp.zeros_like(acc)
        small_ref[...]=jnp.zeros_like(small_ref)
        dl_s[:,SLAB-16:,:]=jnp.zeros((nw,16,D),BF)

    @pl.when(i<nw)
    def _():
        ready(0)
        x=x_s[w,OFF:OFF+WIN,:]
        x_ref[0]=x
        xhat,_=norm_stats(x)
        xn=(xhat*gains_ref[0:1,:]+shifts_ref[0:1,:]).astype(BF)
        for k in range(3):
            for m in range(2):
                at=slice(m*cq,(m+1)*cq)
                v=mm(xn,W1[m,:,k*cq:(k+1)*cq]).astype(BF)
                qkv_ref[0,k,:,at]=v
                if k==0: qT_s[at,:]=v.T
                if k==2: vT_s[at,:]=v.T
        mine=y*nw+w
        labr=lab_ref[pl.ds(mine,1),:]
        labc=jnp.sum(jnp.where(lax.broadcasted_iota(jnp.int32,lab_s.shape,1)==mine,lab_s[...],0.0),axis=1,keepdims=True).astype(jnp.int32)
        lane=lax.broadcasted_iota(jnp.int32,(WIN,GROUP),1)
        oh=jnp.where((labc==lane)|((labc+3)==lane),1.0,0.0).astype(BF)
        hi=564.0
        lo=MASK-hi
        sub=lax.broadcasted_iota(jnp.int32,(GROUP,WIN),0)
        nm=jnp.where(sub<3,jnp.where(sub!=labr,-hi,0.0),jnp.where(sub<6,jnp.where(sub-3!=labr,-lo,0.0),0.0)).astype(BF)
        hl=lane//HD
        def group(gi,_):
            slot=gi%2
            @pl.when(w*groups+gi>=2)
            def _():
                pltpu.make_async_copy(P_s.at[slot],P_hbm.at[0,pl.ds(0,PER)],psem.at[slot]).wait()
            o=pl.multiple_of(gi*GROUP,GROUP)
            qTg=jnp.concatenate([qT_s[pl.ds(o,GROUP),:],nm],axis=0)
            kg=qkv_ref[0,1,:,pl.ds(o,GROUP)]
            for hh in range(PER):
                kh=jnp.concatenate([jnp.where(hl==hh,kg,jnp.zeros_like(kg)),oh],axis=1)
                t=mm(kh,qTg)+bias_ref[gi*PER+hh]
                m=jnp.max(t,axis=0,keepdims=True)
                e=jnp.exp2((t-m)*CEXP)
                l=jnp.sum(e,axis=0,keepdims=True)
                p=(e*(1.0/l)).astype(BF)
                P_s[slot,hh]=p
                OT_s[w,pl.ds(o+hh*HD,HD),:]=mm(vT_s[pl.ds(o+hh*HD,HD),:],p)
            pltpu.make_async_copy(P_s.at[slot],P_hbm.at[w,pl.ds(gi*PER,PER)],psem.at[slot]).start()
            return 0
        lax.fori_loop(0,groups,group,0)

    @pl.when(i==0)
    def _():
        for k in (1,3,2): gather.turn_z(k)
    @pl.when(i==1)
    def _():
        for k in (0,1,3,2): gather.turn_a(k); gather.turn_b(k)
    @pl.when(i==2)
    def _():
        for k in (0,1,3,2): gather.turn_ab(k)
    @pl.when(i==nw-1)
    def _():
        gather.last(); gather.drain()

    @pl.when(i>=nw)
    def _():
        ready(1)
        x=x_s[w,OFF:OFF+WIN,:]
        og=og_s[w,OFF:OFF+WIN,:]
        attn=OT_s[w].astype(BF).T
        branch=shifts_ref[2:3,:]
        for m in range(2):
            branch=branch+mm_nt(attn[:,m*cq:(m+1)*cq],W1[m,:,3*cq:4*cq])
        branch=branch.astype(BF).astype(F32)
        middle=x+branch
        xhat2,rstd2=norm_stats(middle)
        xn2=(xhat2*gains_ref[1:2,:]+shifts_ref[1:2,:]).astype(BF)
        tg=og.astype(BF)
        xn2_s[...]=xn2; xn2T_s[...]=xn2.T; tg_s[...]=tg; tgT_s[...]=tg.T
        up_s[...]=jnp.zeros_like(up_s); gn2_s[...]=jnp.zeros_like(gn2_s)
        CH=512; each=cf//CH
        def chunk(k,_):
            m=k//each
            o=pl.multiple_of((k%each)*CH,CH)
            f1=W2[m,:,pl.ds(o,CH)]; f2=W2[m,:,pl.ds(cf+o,CH)]
            hid=mm(xn2_s[...],f1)
            act,dact=gelu_both(hid)
            a=act.astype(BF)
            up_s[...]+=mm_nt(a,f2)
            gh=(mm(tg_s[...],f2)*dact).astype(BF)
            gn2_s[...]+=mm_nt(gh,f1)
            acc[m,:,pl.ds(cq+o,CH)]+=mm(xn2T_s[...],gh)
            acc[m,:,pl.ds(cq+cf+o,CH)]+=mm(tgT_s[...],a)
            return 0
        lax.fori_loop(0,2*each,chunk,0)
        dl_s[w,0:WIN,:]=(branch+up_s[...]+shifts_ref[3:4,:]).astype(BF)
        @pl.when(w<nw-1)
        def _():
            slab(w).start(); slab(w,mate).start()
        @pl.when(w==nw-1)
        def _(): slab(None).start()
        gn2=gn2_s[...]
        gln2=norm_back(gn2,xhat2,rstd2,gains_ref[1:2,:])
        gln2_ref[0]=gln2
        gb=(og+gln2).astype(BF)
        gbT=gb.T
        for m in range(2):
            at=slice(m*cq,(m+1)*cq)
            acc[m,:,0:cq]+=mm(gbT,attn[:,at])
            g=mm(gb,W1[m,:,3*cq:4*cq]).astype(BF)
            g_ref[0,:,at]=g
            gT=g.T
            gT_ref[0,at,:]=gT
            prod=gT.astype(F32)*OT_s[w,at,:]
            nh=nheads//2
            D_ref[0,m*nh:(m+1)*nh,:]=jnp.sum(prod.reshape(nh,HD,WIN),axis=1)
        small_ref[1:2,:]+=jnp.sum(gn2*xhat2,axis=0,keepdims=True)
        small_ref[3:4,:]+=jnp.sum(gn2,axis=0,keepdims=True)
        small_ref[4:5,:]+=jnp.sum(gb.astype(F32),axis=0,keepdims=True)
        small_ref[5:6,:]+=jnp.sum(tg.astype(F32),axis=0,keepdims=True)

    @pl.when(i==2*nw-1)
    def _():
        W2[...]=acc[:,:,cq:].astype(BF)
        pst[...]=acc[:,:,:cq].astype(BF)
        a=pltpu.make_async_copy(W2,dcat_hbm.at[:,:,pl.ds(cq,2*cf)],fin.at[0])
        b=pltpu.make_async_copy(pst,dcat_hbm.at[:,:,pl.ds(0,cq)],fin.at[1])
        a.start(); b.start()
        for k in range(2):
            pltpu.make_async_copy(P_s.at[k],P_hbm.at[0,pl.ds(0,PER)],psem.at[k]).wait()
        for k in range(nw-1):
            slab(k).wait(); slab(k,mate).wait()
        slab(None).wait()
        @pl.when(y==1)
        def _():
            for t in range(2): edge(t).wait_send()
        a.wait(); b.wait()

def call_a2(inputs,og,wf,lab,bias,W1,gains,shifts):
    nW=lab.shape[0]//2; WIN=lab.shape[1]; D=inputs.shape[1]; NH=bias.shape[0]
    cf=wf.shape[1]//2; cq=D//2; SLAB=-(-WIN//16)*16
    sd=jax.ShapeDtypeStruct; dma=pltpu.SemaphoreType.DMA; v=pltpu.VMEM
    early=lambda shape: pl.BlockSpec((1,)+shape,lambda i:(jnp.minimum(i,nW-1),)+(0,)*len(shape))
    late=lambda shape: pl.BlockSpec((1,)+shape,lambda i:(jnp.maximum(i-nW,0),)+(0,)*len(shape))
    outs=[sd((nW,3,WIN,D),BF),sd((nW,WIN,D),F32),sd((nW,NH,WIN,WIN),BF),sd((nW,WIN,D),F32),sd((nW,WIN,D),BF),sd((nW,D,WIN),BF),sd((nW,NH,WIN),F32),
          sd((2*nW,SLAB,D),BF),sd((SLAB,D),BF),sd((2,D,cq+2*cf),BF),sd((8,D),F32)]
    return pl.pallas_call(functools.partial(kernel_a2,NH),grid=(2*nW,),
      in_specs=[ANY,ANY,ANY,full(lab.shape),full((NH,WIN,WIN),pipeline_mode=ONE),full(W1.shape,pipeline_mode=ONE),full(gains.shape),full(shifts.shape)],
      out_specs=[early((3,WIN,D)),early((WIN,D)),ANY,late((WIN,D)),late((WIN,D)),late((D,WIN)),late((NH,WIN)),ANY,ANY,ANY,full((8,D))],
      out_shape=outs,
      scratch_shapes=[v((nW,SLAB,D),F32),v((nW,SLAB,D),F32),v((2,D,2*cf),BF),v((nW,D,WIN),F32),v((D,WIN),BF),v((D,WIN),BF),v((2,PER,WIN,WIN),BF),
        v((2,D,cq+2*cf),F32),v((2,D,cq),BF),v((WIN,D),BF),v((D,WIN),BF),v((WIN,D),BF),v((D,WIN),BF),v((WIN,D),F32),v((WIN,D),F32),v((nW,SLAB,D),BF),
        v((WIN,2*nW),F32),dma((2,)),dma((2,2*nW)),dma((2,2))]+gather_sems()+[dma((nW,)),dma((nW,)),dma((nW,)),dma((2,))],
      compiler_params=pltpu.CompilerParams(vmem_limit_bytes=63*1024*1024,dimension_semantics=("arbitrary",),collective_id=2,has_side_effects=True),
      name="kernel_a2")(inputs,og,wf,lab,bias,W1,gains,shifts)

class Reduce:
    def __init__(self,src,out,own,r1,r2,ss,rs,ls,r3,fin,r4):
        self.src,self.out,self.own,self.r1,self.r2,self.r3,self.fin,self.r4=src,out,own,r1,r2,r3,fin,r4
        self.ss,self.rs,self.ls=ss,rs,ls
        self.at=place_of()
        self.mid=own.at[self.at[1]]
    def mine(self,k):
        return pltpu.make_async_copy(self.src.at[k%2,:,k//2,self.at[2]],self.own.at[k//2,:,k%2],self.ls.at[k])
    def theirs(self,k):
        z,x,c,y=self.at
        return send(self.src.at[k%2,:,k//2,1-c],self.r1.at[k//2,:,k%2],self.ss.at[k],self.rs.at[k],dev(z,x,1-c,y))
    def xsend(self):
        z,x,c,y=self.at
        return send(self.own.at[1-x],self.r2,self.ss.at[4],self.rs.at[4],dev(z,1-x,c,y))
    def zsend(self,i):
        z,x,c,y=self.at
        zz=(z+i)%4
        return send(self.mid.at[zz],self.r3.at[i-1],self.ss.at[4+i],self.rs.at[4+i],dev(zz,x,c,y))
    def ysend(self):
        z,x,c,y=self.at
        return send(self.fin.at[1-y],self.r4,self.ss.at[8],self.rs.at[8],dev(z,x,c,1-y))
    def start(self):
        for k in range(4):
            self.theirs(k).start(); self.mine(k).start()
    def add(self,dst,*srcs):
        total=srcs[0][...].astype(F32)
        for s in srcs[1:]: total=total+s[...].astype(F32)
        dst[...]=total.astype(BF)
    def one(self):
        z,x,c,y=self.at
        for k in range(4):
            self.mine(k).wait(); self.theirs(k).wait_recv()
        def step(xx):
            def add(k,_):
                at=(xx,k//2,k%2)
                self.add(self.own.at[at],self.own.at[at],self.r1.at[at])
                return 0
            lax.fori_loop(0,8,add,0)
        step(1-x)
        self.xsend().start()
        step(x)
    def summed(self):
        z,x,c,y=self.at
        def add(k,_):
            at=(k//2,k%2)
            self.add(self.own.at[(x,)+at],self.own.at[(x,)+at],self.r2.at[at])
            return 0
        lax.fori_loop(0,8,add,0)
    def left(self):
        for k in range(4): self.theirs(k).wait_send()
        self.xsend().wait_send()
    def zstart(self):
        for i in (2,1,3): self.zsend(i).start()
    def two(self):
        self.xsend().wait_recv()
        self.summed()
        self.zstart()
    def three(self):
        z,x,c,y=self.at
        for i in (1,2,3):
            self.zsend(i).wait_recv()
        def step(yy):
            self.add(self.fin.at[yy],self.mid.at[z,yy],*[self.r3.at[i,yy] for i in range(3)])
        step(1-y)
        self.ysend().start()
        step(y)
    def four(self):
        z,x,c,y=self.at
        self.ysend().wait_recv()
        self.out[...]=self.fin[y].astype(F32)+self.r4[...].astype(F32)
        self.left()
        for i in (1,2,3): self.zsend(i).wait_send()
        self.ysend().wait_send()

def reduce_scratch(rows,cols):
    v=lambda *d: pltpu.VMEM(d+(rows,cols),BF); dma=pltpu.SemaphoreType.DMA
    return [v(2,4,2),v(2,4,2),v(4,2),dma((9,)),dma((9,)),dma((4,)),v(3,2),v(2),v()]


def kernel_bc(nheads,x_ref,gln2_ref,qkv_ref,g_ref,gT_ref,D_ref,P_ref,W1,gains_ref,shifts_ref,sm_ref,pos_ref,dcat_hbm,dlast_hbm,
              ev_hbm,hd_hbm,evl_hbm,hdl_hbm,redq_ref,redm_ref,tab_ref,sum_ref,
              G_s,Gx,aq,dq_s,kT_s,gq_s,gqT_s,dd_s,small_ref,acc,tk,tr,tu,sr,
              gs,gr_,dl,ds,dr,es,er,us,ts,tq_,
              own,r1,r2,ss,rs,ls,r3,fin,r4,own2,p1,p2,ss2,rs2,ls2,p3,fin2,p4):
    w=pl.program_id(0); nw=dd_s.shape[0]
    z,xc,c,y=place_of()
    s=(z*2+xc)*2+c
    mate=dev(z,xc,c,1-y); sib=dev(z,xc,1-c,y)
    D=x_ref.shape[-1]; WIN=x_ref.shape[-2]; SLAB=dd_s.shape[1]
    cq=D//2
    groups=nheads//PER
    tiles=G_s.shape[0]; part=Gx.shape[1]//nheads
    big=Reduce(dcat_hbm,redm_ref,own2,p1,p2,ss2,rs2,ls2,p3,fin2,p4)
    red=Reduce(dq_s,redq_ref,own,r1,r2,ss,rs,ls,r3,fin,r4)
    def slab(k,to=None):
        at=ev_hbm.at[y*nw+k]
        if to is None: return pltpu.make_async_copy(dd_s.at[k],at,dl.at[k])
        return send(dd_s.at[k],at,ds.at[k],dr.at[k],to)
    def tail(k):
        lead=SLAB-hd_hbm.shape[0]
        return send(dd_s.at[nw-1,pl.ds(lead,hd_hbm.shape[0])],hd_hbm,es.at[k],er,((s+1)%16,k))
    def early(k):
        lead=SLAB-hdl_hbm.shape[0]
        if k==0: return pltpu.make_async_copy(dlast_hbm,evl_hbm.at[y],us.at[0])
        if k==1: return send(dlast_hbm,evl_hbm.at[y],us.at[1],us.at[2],mate)
        return send(dlast_hbm.at[pl.ds(lead,hdl_hbm.shape[0])],hdl_hbm,us.at[k+1],us.at[5],((s+1)%16,k-2))
    def trade(h):
        r=pl.multiple_of(h*WIN+(1-c)*(WIN-part),8)
        return send(G_s.at[:,pl.ds(r,part)],Gx.at[:,pl.ds(pl.multiple_of(h*part,8),part)],gs.at[h],gr_.at[h],sib)
    @pl.when(w==0)
    def _():
        greet(peers_of(z,xc,c,y)+neighbours(z,xc,c,y))
        big.start()
        early(0).start(); early(1).start()
        @pl.when(y==1)
        def _():
            early(2).start(); early(3).start()
        aq[...]=jnp.zeros_like(aq); G_s[...]=jnp.zeros_like(G_s); small_ref[...]=sm_ref[...]
        dd_s[:,SLAB-16:,:]=jnp.zeros((nw,16,D),BF)
    kT_s[...]=qkv_ref[0,1].T
    lane=lax.broadcasted_iota(jnp.int32,(WIN,GROUP),1)
    hl=lane//HD
    def group(gi,_):
        o=pl.multiple_of(gi*GROUP,GROUP)
        gTg=gT_ref[0,pl.ds(o,GROUP),:]
        vg=qkv_ref[0,2,:,pl.ds(o,GROUP)]
        qg=qkv_ref[0,0,:,pl.ds(o,GROUP)]
        gg=g_ref[0,:,pl.ds(o,GROUP)]
        dv=jnp.zeros((WIN,GROUP),F32); dk=jnp.zeros((WIN,GROUP),F32)
        zero=jnp.zeros_like(vg)
        for hh in range(PER):
            h=gi*PER+hh
            p=P_ref[0,h]
            dp=mm(jnp.where(hl==hh,vg,zero),gTg)
            dsc=p.astype(F32)*(dp-D_ref[0,pl.ds(h,1),:])
            for k in range(tiles):
                wd=min(128,WIN-k*128)
                G_s[k,pl.ds(pl.multiple_of(h*WIN,8),WIN),:wd]+=dsc[:,k*128:k*128+wd]
            dsl=dsc.astype(BF)
            dv+=mm(p,jnp.where(hl==hh,gg,zero))
            dk+=mm(dsl,jnp.where(hl==hh,qg,zero))
            gqT_s[pl.ds(o+hh*HD,HD),:]=mm(kT_s[pl.ds(o+hh*HD,HD),:],dsl)
        gq_s[1,:,pl.ds(o,GROUP)]=(dk*(1.0/SQ)).astype(BF)
        gq_s[2,:,pl.ds(o,GROUP)]=dv.astype(BF)
        @pl.when(w==nw-1)
        def _():
            for hh in range(PER): trade(gi*PER+hh).start()
        return 0
    lax.fori_loop(0,groups,group,0)
    gq_s[0]=(gqT_s[...]*(1.0/SQ)).astype(BF).T
    x=x_ref[0]
    xhat,rstd=norm_stats(x)
    xn=(xhat*gains_ref[0:1,:]+shifts_ref[0:1,:]).astype(BF)
    xnT=xn.T
    gr=jnp.zeros((WIN,D),F32)
    for m in range(2):
        for k in range(3):
            gc=gq_s[k,:,m*cq:(m+1)*cq]
            gr=gr+mm_nt(gc,W1[m,:,k*cq:(k+1)*cq])
            aq[m,:,k*cq:(k+1)*cq]+=mm(xnT,gc)
    @pl.when(w==nw-1)
    def _():
        dq_s[...]=aq[...].astype(BF).reshape(dq_s.shape)
        red.start()
    dd_s[w,0:WIN,:]=(gln2_ref[0]+norm_back(gr,xhat,rstd,gains_ref[0:1,:])).astype(BF)
    slab(w).start(); slab(w,mate).start()
    @pl.when(jnp.logical_and(w==nw-1,y==1))
    def _():
        tail(0).start(); tail(1).start()
    small_ref[0:1,:]+=jnp.sum(gr*xhat,axis=0,keepdims=True)
    small_ref[2:3,:]+=jnp.sum(gr,axis=0,keepdims=True)
    pl.when(w==0)(big.one)
    pl.when(w==nw-2)(big.two)
    @pl.when(w==nw-1)
    def _():
        for h in range(nheads): trade(h).wait()
        acc[...]=jnp.zeros_like(acc)
        nh=acc.shape[0]; LW=tiles*128
        base=c*(WIN-part)
        def rows(r,_):
            r8=pl.multiple_of(r*8,8)
            f8=pl.multiple_of(base+r*8,8)
            pos=pos_ref[pl.ds(f8,8),:]
            hi8=pos>>8; lo8=pos&255
            tot=jnp.zeros((nh*nheads,256),F32)
            iota=lax.broadcasted_iota(jnp.int32,(256,LW),0).astype(F32).astype(BF)
            for k in range(8):
                g=jnp.concatenate([G_s[q,pl.ds(f8+k,nheads,stride=WIN),:]+Gx[q,pl.ds(r8+k,nheads,stride=part),:] for q in range(tiles)],axis=1)
                hr=hi8[k:k+1,:]; lr=lo8[k:k+1,:].astype(F32).astype(BF)
                A=jnp.concatenate([jnp.where(hr==m,g,0.0) for m in range(nh)],axis=0).astype(BF)
                oh=jnp.where(iota==lr,jnp.ones((),BF),jnp.zeros((),BF))
                tot=tot+mm_nt(A,oh)
            acc[...]+=tot.reshape(acc.shape)
            return 0
        n=part//8
        lax.fori_loop(c,n*3//25,rows,0)
        red.one()
        lax.fori_loop(n*3//25,n*13//25,rows,0)
        red.two()
        lax.fori_loop(n*13//25,n*19//25,rows,0)
        big.three()
        lax.fori_loop(n*19//25,n,rows,0)
        big.four()
        half=nheads//2; nb=nh//2
        def pair(k,src,dst,to):
            return [send(src,dst,ts.at[2*k],tq_.at[2*k],to),send(sr.at[6+min(k,3)],sr.at[k],ts.at[2*k+1],tq_.at[2*k+1],to)]
        def run(cps):
            for p in cps: p.start()
            for p in cps: p.wait()
        sr[6]=small_ref[...]
        run(pair(0,acc.at[:,pl.ds(pl.multiple_of((1-y)*half,8),half)],tu.at[0],mate))
        tu[1]=acc[:,pl.ds(pl.multiple_of(y*half,8),half)]+tu[0]
        sr[7]=sr[6]+sr[0]
        run(pair(1,tu.at[1,pl.ds((1-c)*nb,nb)],tr.at[0],sib))
        tk[0]=tu[1,pl.ds(c*nb,nb)]+tr[0]
        sr[8]=sr[7]+sr[1]
        run(pair(2,tk.at[0],tr.at[1],dev(z,1-xc,c,y)))
        tk[1]=tk[0]+tr[1]
        sr[9]=sr[8]+sr[2]
        cps=[]
        for k in (1,2,3):
            cps+=pair(2+k,tk.at[1],tr.at[1+k],dev((z+k)%4,xc,c,y))
        run(cps)
        red.three()
        tu[2,pl.ds(c*nb,nb)]=tk[1]+tr[2]+tr[3]+tr[4]
        sum_ref[...]=sr[9]+sr[3]+sr[4]+sr[5]
        cp=send(tu.at[2,pl.ds(c*nb,nb)],tu.at[2,pl.ds(c*nb,nb)],ts.at[12],tq_.at[12],sib)
        cp.start()
        red.four()
        cp.wait_send()
        send(tu.at[2,pl.ds((1-c)*nb,nb)],tu.at[2,pl.ds((1-c)*nb,nb)],ts.at[12],tq_.at[12],sib).wait_recv()
        for m in range(nh):
            tab_ref[:,m*256:(m+1)*256]=tu[2,m]
        for k in range(nw):
            slab(k).wait(); slab(k,mate).wait()
        @pl.when(y==1)
        def _():
            tail(0).wait_send(); tail(1).wait_send(); early(2).wait_send(); early(3).wait_send()
        tail(0).wait_recv(); early(2).wait_recv()
        early(0).wait(); early(1).wait()

def call_bc(x,gln2,qkv,g,gT,Dd,Pp,W1,gains,shifts,sm,pp,dcat,dlast,T):
    nW,WIN,D=x.shape; NH=Dd.shape[1]
    cq=D//2; tiles=-(-WIN//128); SLAB=-(-WIN//16)*16; EDGE=-(-(SLAB-WIN//2)//16)*16
    part=-(-WIN//16)*8
    nh=-(-T//256); nh+=nh%2
    rows,more=dcat.shape[-2:]; cols=3*cq
    sd=jax.ShapeDtypeStruct; dma=pltpu.SemaphoreType.DMA; v=pltpu.VMEM
    return pl.pallas_call(functools.partial(kernel_bc,NH),grid=(nW,),
      in_specs=[per((WIN,D)),per((WIN,D)),per((3,WIN,D)),per((WIN,D)),per((D,WIN)),per((NH,WIN)),per((NH,WIN,WIN)),
        full((2,D,cols),pipeline_mode=ONE),full(gains.shape),full(shifts.shape),full(sm.shape),full(pp.shape,pipeline_mode=ONE),ANY,ANY],
      out_specs=[ANY,ANY,ANY,ANY,full((rows,cols)),full((rows,more)),full((NH//2,nh*256)),full(sm.shape)],
      out_shape=[sd((2*nW,SLAB,D),BF),sd((EDGE,D),BF),sd((2,SLAB,D),BF),sd((EDGE,D),BF),sd((rows,cols),F32),sd((rows,more),F32),sd((NH//2,nh*256),F32),sd(sm.shape,F32)],
      scratch_shapes=[v((tiles,NH*WIN,128),F32),v((tiles,NH*part,128),F32),v((2,D,cols),F32),v((2,4,2,2,rows,cols),BF),v((D,WIN),BF),v((3,WIN,D),BF),v((D,WIN),F32),
        v((nW,SLAB,D),BF),v(sm.shape,F32),v((nh,NH,256),F32),v((2,nh//2,NH//2,256),F32),v((5,nh//2,NH//2,256),F32),v((3,nh,NH//2,256),F32),v((10,)+sm.shape,F32),
        dma((NH,)),dma((NH,)),dma((nW,)),dma((nW,)),dma((nW,)),dma((2,)),dma,dma((6,)),dma((13,)),dma((13,))]+reduce_scratch(rows,cols)+reduce_scratch(rows,more),
      compiler_params=pltpu.CompilerParams(vmem_limit_bytes=63*1024*1024,dimension_semantics=("arbitrary",),collective_id=3,has_side_effects=True),
      name="kernel_bc")(x,gln2,qkv,g,gT,Dd,Pp,W1,gains,shifts,sm,pp,dcat,dlast)


def kernel_f(in_ref,og_ref,ev_ref,evl_ref,ev2_ref,hd_ref,hd2_ref,redq_ref,redm_ref,tab_ref,sum_ref,
             out_ref,din_ref,dqkv_ref,dproj_ref,dfc1_ref,dfc2_ref,dgain_ref,dshift_ref,dtab_ref,end_s):
    j=pl.program_id(0); nw=pl.num_programs(0)//2
    shift=in_ref.shape[0]//2; WIN=2*shift
    edge,SLAB=hd_ref.shape[0],ev_ref.shape[1]
    off=edge-(SLAB-shift)
    @pl.when(j==0)
    def _():
        end_s[0]=hd_ref[...].astype(F32); end_s[1]=hd2_ref[...].astype(F32)
        cq=dqkv_ref.shape[2]; cf=dfc1_ref.shape[1]
        for k in range(3): dqkv_ref[k]=redq_ref[:,k*cq:(k+1)*cq]
        dproj_ref[...]=redm_ref[:,0:cq].T
        dfc1_ref[...]=redm_ref[:,cq:cq+cf]
        dfc2_ref[...]=redm_ref[:,cq+cf:].T
        dgain_ref[...]=sum_ref[0:2,:]; dshift_ref[...]=sum_ref[2:6,:]
        dtab_ref[...]=tab_ref[:,0:dtab_ref.shape[1]]
    e=jnp.where(j%nw==nw-1,evl_ref[0],ev_ref[0]).astype(F32)
    for k,(base,res,v) in enumerate(((in_ref,out_ref,e),(og_ref,din_ref,ev2_ref[0].astype(F32)))):
        res[0:shift,:]=base[0:shift,:]+end_s[k,off:off+shift,:]
        res[shift:WIN,:]=base[shift:WIN,:]+v[0:shift,:]
        end_s[k]=v[SLAB-edge:,:]

def call_f(inputs,og,ev,evl,ev2,hd,hd2,redq,redm,tab,small,cq,cf,T):
    tok,D=inputs.shape; n,SLAB,_=ev.shape; WIN=tok//n; rows=redq.shape[0]
    sd=jax.ShapeDtypeStruct
    blk=pl.BlockSpec((WIN,D),lambda j:(j,0)); slab=pl.BlockSpec((1,SLAB,D),lambda j:(j,0,0))
    shapes=[(3,rows,cq),(cq,rows),(rows,cf),(cf,rows),(2,D),(4,D),(tab.shape[0],T)]
    return pl.pallas_call(kernel_f,grid=(n,),
      in_specs=[blk,blk,slab,pl.BlockSpec((1,SLAB,D),lambda j:(j//(n//2),0,0)),slab]+[full(v.shape) for v in (hd,hd2,redq,redm,tab,small)],
      out_specs=[blk,blk]+[full(v) for v in shapes],
      out_shape=[sd((tok,D),F32),sd((tok,D),F32)]+[sd(v,F32) for v in shapes],
      scratch_shapes=[pltpu.VMEM((2,)+hd.shape,F32)],
      compiler_params=pltpu.CompilerParams(vmem_limit_bytes=40*1024*1024,dimension_semantics=("arbitrary",)),
      name="kernel_f")(inputs,og,ev,evl,ev2,hd,hd2,redq,redm,tab,small)

def gathered(piece,names,nseq,nheads):
    full=lax.all_gather(piece,names,axis=0,tiled=False)
    return full.reshape((nseq,nheads)+piece.shape)

def natural(block):
    s,h,r,c=block.shape
    return block.transpose(0,2,1,3).reshape(s*r,h*c)

def owners(grad,nseq,nheads):
    r,c=grad.shape
    return grad.reshape(nseq,r//nseq,nheads,c//nheads).transpose(0,2,1,3).reshape(nseq*nheads,r//nseq,c//nheads)

def from_next(rows):
    n=lax.axis_size("seq")
    return lax.ppermute(rows,"seq",[(i,(i-1)%n) for i in range(n)])

def to_next(rows):
    n=lax.axis_size("seq")
    return lax.ppermute(rows,"seq",[(i,(i+1)%n) for i in range(n)])

def spread(rows):
    n=lax.axis_size("heads")
    flat=rows.reshape(-1,rows.shape[-1])
    if n==2:
        other=lax.ppermute(flat,"heads",[(0,1),(1,0)])
        me=lax.axis_index("heads")
        return jnp.where(me==0,jnp.concatenate([flat,other]),jnp.concatenate([other,flat]))
    return lax.all_gather(flat,"heads",axis=0,tiled=True)

def place(rows,base,shift):
    every=spread(rows)
    keep=every.shape[0]-shift
    return base+jnp.concatenate([to_next(every[keep:]),every[:keep]]).astype(F32)

def body(inputs,w_qkv,w_proj,w_fc1,w_fc2,gains,shifts,rel_table,region,pos_index,out_grad):
    nseq=lax.axis_size("seq"); nheads=lax.axis_size("heads"); me=lax.axis_index("heads")
    linked=nseq==16 and nheads==2
    names=("seq","heads")
    tok,D=inputs.shape; WIN=pos_index.shape[0]; shift=WIN//2; T=rel_table.shape[1]
    nW=tok//WIN//nheads
    rows=w_qkv.shape[1]; cq=w_qkv.shape[2]; cf=w_fc1.shape[1]
    lab=region.reshape(-1,WIN)
    if linked:
        W1,bias,wf,posT=call_w(w_qkv,w_proj,w_fc1,w_fc2,pos_index,rel_table)
        qkv,x,Pp,gln2,g,gT,Dd,ev,dlast,dcat,sm=call_a2(inputs,out_grad,wf,lab,bias,W1,gains,shifts)
        ev2,hd2,evl,hd,redq,redm,d_table,small=call_bc(x,gln2,qkv,g,gT,Dd,Pp,W1,gains,shifts,sm,posT,dcat.reshape(2,4,2,2,rows,-1),dlast,T)
        return tuple(call_f(inputs,out_grad,ev,evl,ev2,hd,hd2,redq,redm,d_table,small,cq,cf,T))
    posT=pos_index.T
    wide=-(-WIN//128)*128
    posP=jnp.pad(posT,((0,0),(0,wide-WIN)))
    start=me*nW*WIN
    lab=lax.dynamic_slice_in_dim(lab,me*nW,nW,0)
    labc=lab[:,:,None]; labr=lab[:,None,:]
    wq=jnp.concatenate([w_qkv[0],w_qkv[1],w_qkv[2],w_proj.T],axis=1).astype(BF)
    wf=jnp.concatenate([w_fc1,w_fc2.T],axis=1).astype(BF)
    table=lax.all_gather(rel_table,"heads",axis=0,tiled=True)
    NH=table.shape[0]
    every=gathered(jnp.concatenate([wq,wf],axis=1),names,nseq,nheads)
    ends=[i*cq for i in range(5)]+[4*cq+cf,4*cq+2*cf]
    W=jnp.concatenate([natural(every[...,a:b]) for a,b in zip(ends[:-1],ends[1:])],axis=1)[None]
    bias=call_p(posP,pack_table(table),WIN)
    def mine(v):
        ext=jnp.concatenate([v,from_next(v[:shift])])
        return lax.dynamic_slice_in_dim(ext,start+shift,nW*WIN,0).reshape(nW,WIN,-1)
    x=mine(inputs); og=mine(out_grad)
    delta,gln2,qkv,g,gT,Dd,Pp,dcat,sm_a=call_a(x,og,labc,labr,bias,W,gains,shifts)
    dd,dqkv,G,sm_b=call_b(x,gln2,qkv,g,gT,Dd,Pp,W,gains,shifts)
    grads=[dqkv[0,:,c*D:(c+1)*D] for c in range(3)]+[dcat[0,:,:D],dcat[0,:,D:D+cf*nheads],dcat[0,:,D+cf*nheads:]]
    red=lax.psum_scatter(jnp.concatenate([owners(v,nseq,nheads) for v in grads],axis=2),names,scatter_dimension=0,tiled=False).astype(F32)
    redq,redm=red[:,:3*cq],red[:,3*cq:]
    d_table,small=lax.psum((call_t(G,posT,T,NH),sm_a+sm_b),names)
    nl=rel_table.shape[0]
    d_table=lax.dynamic_slice_in_dim(d_table,me*nl,nl,0)
    output=place(delta,inputs,shift)
    d_inputs=place(dd,out_grad,shift)
    d_qkv=redq.reshape(rows,3,cq).transpose(1,0,2)
    d_proj=redm[:,:cq].T; d_fc1=redm[:,cq:cq+cf]; d_fc2=redm[:,cq+cf:].T
    return (output,d_inputs,d_qkv,d_proj,d_fc1,d_fc2,small[0:2],small[2:6],d_table)

def solution(mesh):
    placed=(P("seq",None),P(None,"seq","heads"),P("heads","seq"),P("seq","heads"),P("heads","seq"),P(),P(),P("heads",None),P("seq"),P(),P("seq",None))
    return jax.shard_map(body,mesh=mesh,in_specs=placed,
    out_specs=(P("seq",None),P("seq",None),P(None,"seq","heads"),P("heads","seq"),P("seq","heads"),P("heads","seq"),P(),P(),P("heads",None)),
    check_vma=False)
```

```python
import functools
import math

import jax, jax.numpy as jnp
from jax import lax
from jax.experimental import pallas as pl
from jax.experimental.pallas import tpu as pltpu
from jax.sharding import PartitionSpec as P

BF=jnp.bfloat16; F32=jnp.float32
HD=32; GROUP=128; PER=4
EPS=1e-5
SQ=math.sqrt(32.0)
CEXP=math.log2(math.e)/SQ
MASK=100.0*SQ

def mm(a,b):
    return lax.dot_general(a,b,(((1,),(0,)),((),())),preferred_element_type=F32)
def mm_nt(a,b):
    return lax.dot_general(a,b,(((1,),(1,)),((),())),preferred_element_type=F32)

def norm_stats(v):
    mean=jnp.mean(v,axis=-1,keepdims=True)
    c=v-mean
    var=jnp.mean(c*c,axis=-1,keepdims=True)
    rstd=lax.rsqrt(var+EPS)
    return c*rstd, rstd

def norm_back(gy,xhat,rstd,gain):
    gx=gy*gain
    m1=jnp.mean(gx,axis=-1,keepdims=True)
    m2=jnp.mean(gx*xhat,axis=-1,keepdims=True)
    return rstd*(gx-m1-xhat*m2)

P0=0.3275911
A1,A2,A3,A4,A5=0.254829592,-0.284496736,1.421413741,-1.453152027,1.061405429
def gelu_both(x):
    e=jnp.exp2(x*x*(-0.5*math.log2(math.e)))
    t=1.0/(1.0+(P0/math.sqrt(2.0))*jnp.abs(x))
    poly=t*(0.5*A1+t*(0.5*A2+t*(0.5*A3+t*(0.5*A4+t*(0.5*A5)))))
    half=poly*e
    phi=jnp.where(x>=0,1.0-half,half)
    return x*phi, phi+x*e*(1.0/math.sqrt(2.0*math.pi))

def kernel_a(nheads,x_ref,og_ref,labc_ref,labr_ref,bias_ref,W_ref,gains_ref,shifts_ref,
             delta_ref,gln2_ref,qkv_ref,g_ref,gT_ref,D_ref,P_hbm,dcat_ref,small_ref,
             qT_s,vT_s,OT_s,P_s,acc,sem,xn2_s,xn2T_s,tg_s,tgT_s,up_s,gn2_s):
    w=pl.program_id(0); nw=pl.num_programs(0)
    D=x_ref.shape[-1]; WIN=x_ref.shape[-2]
    parts=W_ref.shape[0]; cq=D//parts; cf=(W_ref.shape[2]-4*cq)//2
    groups=nheads//PER
    x=x_ref[0]
    xhat,_=norm_stats(x)
    xn=(xhat*gains_ref[0:1,:]+shifts_ref[0:1,:]).astype(BF)
    for c in range(3):
        for m in range(parts):
            at=slice(m*cq,(m+1)*cq)
            y=mm(xn,W_ref[m,:,c*cq:(c+1)*cq]).astype(BF)
            qkv_ref[0,c,:,at]=y
            if c==0: qT_s[at,:]=y.T
            if c==2: vT_s[at,:]=y.T
    labc=labc_ref[0]; labr=labr_ref[0]
    lane=lax.broadcasted_iota(jnp.int32,(WIN,GROUP),1)
    oh=jnp.where((labc==lane)|((labc+3)==lane),1.0,0.0).astype(BF)
    hi=564.0
    lo=MASK-hi
    sub=lax.broadcasted_iota(jnp.int32,(GROUP,WIN),0)
    nm=jnp.where(sub<3,jnp.where(sub!=labr,-hi,0.0),jnp.where(sub<6,jnp.where(sub-3!=labr,-lo,0.0),0.0)).astype(BF)
    hl=lane//HD

    def group(gi,_):
        slot=gi%2
        step=w*groups+gi
        @pl.when(step>=2)
        def _():
            pltpu.make_async_copy(P_s.at[slot],P_hbm.at[0,pl.ds(0,PER)],sem.at[slot]).wait()
        o=pl.multiple_of(gi*GROUP,GROUP)
        qTg=jnp.concatenate([qT_s[pl.ds(o,GROUP),:],nm],axis=0)
        kg=qkv_ref[0,1,:,pl.ds(o,GROUP)]
        for hh in range(PER):
            kh=jnp.concatenate([jnp.where(hl==hh,kg,jnp.zeros_like(kg)),oh],axis=1)
            t=mm(kh,qTg)+bias_ref[gi*PER+hh]
            m=jnp.max(t,axis=0,keepdims=True)
            e=jnp.exp2((t-m)*CEXP)
            l=jnp.sum(e,axis=0,keepdims=True)
            p=(e*(1.0/l)).astype(BF)
            P_s[slot,hh]=p
            OT_s[pl.ds(o+hh*HD,HD),:]=mm(vT_s[pl.ds(o+hh*HD,HD),:],p)
        pltpu.make_async_copy(P_s.at[slot],P_hbm.at[w,pl.ds(gi*PER,PER)],sem.at[slot]).start()
        return 0
    lax.fori_loop(0,groups,group,0)

    attn=OT_s[...].astype(BF).T
    branch=shifts_ref[2:3,:]
    for m in range(parts):
        branch=branch+mm_nt(attn[:,m*cq:(m+1)*cq],W_ref[m,:,3*cq:4*cq])
    branch=branch.astype(BF).astype(F32)
    middle=x+branch
    xhat2,rstd2=norm_stats(middle)
    xn2=(xhat2*gains_ref[1:2,:]+shifts_ref[1:2,:]).astype(BF)
    og=og_ref[0]
    tg=og.astype(BF)
    xn2_s[...]=xn2; xn2T_s[...]=xn2.T; tg_s[...]=tg; tgT_s[...]=tg.T
    up_s[...]=jnp.zeros_like(up_s); gn2_s[...]=jnp.zeros_like(gn2_s)
    CH=min(512,cf); each=cf//CH
    @pl.when(w==0)
    def _():
        acc[...]=jnp.zeros_like(acc)
        small_ref[...]=jnp.zeros_like(small_ref)
    def chunk(c,_):
        m=c//each
        o=pl.multiple_of((c%each)*CH,CH)
        f1=W_ref[m,:,pl.ds(4*cq+o,CH)]; f2=W_ref[m,:,pl.ds(4*cq+cf+o,CH)]
        hid=mm(xn2_s[...],f1)
        act,dact=gelu_both(hid)
        a=act.astype(BF)
        up_s[...]+=mm_nt(a,f2)
        gh=(mm(tg_s[...],f2)*dact).astype(BF)
        gn2_s[...]+=mm_nt(gh,f1)
        acc[m,:,pl.ds(cq+o,CH)]+=mm(xn2T_s[...],gh)
        acc[m,:,pl.ds(cq+cf+o,CH)]+=mm(tgT_s[...],a)
        return 0
    lax.fori_loop(0,parts*each,chunk,0)
    delta_ref[0]=(branch+up_s[...]+shifts_ref[3:4,:]).astype(BF)
    gn2=gn2_s[...]
    gln2=norm_back(gn2,xhat2,rstd2,gains_ref[1:2,:])
    gln2_ref[0]=gln2
    gb=(og+gln2).astype(BF)
    gbT=gb.T
    for m in range(parts):
        at=slice(m*cq,(m+1)*cq)
        acc[m,:,0:cq]+=mm(gbT,attn[:,at])
        g=mm(gb,W_ref[m,:,3*cq:4*cq]).astype(BF)
        g_ref[0,:,at]=g
        gT=g.T
        gT_ref[0,at,:]=gT
        prod=gT.astype(F32)*OT_s[at,:]
        nh=nheads//parts
        D_ref[0,m*nh:(m+1)*nh,:]=jnp.sum(prod.reshape(nh,HD,WIN),axis=1)
    small_ref[1:2,:]+=jnp.sum(gn2*xhat2,axis=0,keepdims=True)
    small_ref[3:4,:]+=jnp.sum(gn2,axis=0,keepdims=True)
    small_ref[4:5,:]+=jnp.sum(gb.astype(F32),axis=0,keepdims=True)
    small_ref[5:6,:]+=jnp.sum(tg.astype(F32),axis=0,keepdims=True)
    @pl.when(w==nw-1)
    def _():
        dcat_ref[...]=acc[...].astype(BF)
        for s in range(2):
            pltpu.make_async_copy(P_s.at[s],P_hbm.at[0,pl.ds(0,PER)],sem.at[s]).wait()

def full(shape,**kw):
    return pl.BlockSpec(shape,lambda w:(0,)*len(shape),**kw)
def per(shape,**kw):
    return pl.BlockSpec((1,)+shape,lambda w:(w,)+(0,)*len(shape),**kw)
ONE=pl.Buffered(1)
ANY=pl.BlockSpec(memory_space=pl.ANY)

def call_a(x,og,labc,labr,bias,W,gains,shifts):
    nW,WIN,D=x.shape; NH=bias.shape[0]
    parts,_,Ct=W.shape; Cg=Ct-3*(D//parts)
    sd=jax.ShapeDtypeStruct
    outs=[sd((nW,WIN,D),BF),sd((nW,WIN,D),F32),sd((nW,3,WIN,D),BF),sd((nW,WIN,D),BF),sd((nW,D,WIN),BF),sd((nW,NH,WIN),F32),
          sd((nW,NH,WIN,WIN),BF),sd((parts,D,Cg),BF),sd((8,D),F32)]
    return pl.pallas_call(functools.partial(kernel_a,NH),grid=(nW,),
      in_specs=[per((WIN,D)),per((WIN,D)),per((WIN,1)),per((1,WIN)),full((NH,WIN,WIN),pipeline_mode=ONE),
        full((parts,D,Ct),pipeline_mode=ONE),full(gains.shape),full(shifts.shape)],
      out_specs=[per((WIN,D)),per((WIN,D)),per((3,WIN,D)),per((WIN,D)),per((D,WIN)),per((NH,WIN)),ANY,full((parts,D,Cg)),full((8,D))],
      out_shape=outs,
      scratch_shapes=[pltpu.VMEM((D,WIN),BF),pltpu.VMEM((D,WIN),BF),pltpu.VMEM((D,WIN),F32),pltpu.VMEM((2,PER,WIN,WIN),BF),
        pltpu.VMEM((parts,D,Cg),F32),pltpu.SemaphoreType.DMA((2,)),
        pltpu.VMEM((WIN,D),BF),pltpu.VMEM((D,WIN),BF),pltpu.VMEM((WIN,D),BF),pltpu.VMEM((D,WIN),BF),pltpu.VMEM((WIN,D),F32),pltpu.VMEM((WIN,D),F32)],
      compiler_params=pltpu.CompilerParams(vmem_limit_bytes=62*1024*1024,dimension_semantics=("arbitrary",)),
      name="kernel_a")(x,og,labc,labr,bias,W,gains,shifts)

def kernel_b(nheads,x_ref,gln2_ref,qkv_ref,g_ref,gT_ref,D_ref,P_ref,W_ref,gains_ref,shifts_ref,
             dd_ref,dqkv_ref,G_hbm,small_ref,G_s,aq,kT_s,gq_s,gqT_s,sem):
    w=pl.program_id(0); nw=pl.num_programs(0)
    D=x_ref.shape[-1]; WIN=x_ref.shape[-2]
    parts=W_ref.shape[0]; cq=D//parts
    groups=nheads//PER
    @pl.when(w==0)
    def _():
        aq[...]=jnp.zeros_like(aq); G_s[...]=jnp.zeros_like(G_s); small_ref[...]=jnp.zeros_like(small_ref)
    kT_s[...]=qkv_ref[0,1].T
    lane=lax.broadcasted_iota(jnp.int32,(WIN,GROUP),1)
    hl=lane//HD
    def group(gi,_):
        o=pl.multiple_of(gi*GROUP,GROUP)
        gTg=gT_ref[0,pl.ds(o,GROUP),:]
        vg=qkv_ref[0,2,:,pl.ds(o,GROUP)]
        qg=qkv_ref[0,0,:,pl.ds(o,GROUP)]
        gg=g_ref[0,:,pl.ds(o,GROUP)]
        dv=jnp.zeros((WIN,GROUP),F32); dk=jnp.zeros((WIN,GROUP),F32)
        zero=jnp.zeros_like(vg)
        for hh in range(PER):
            h=gi*PER+hh
            p=P_ref[0,h]
            dp=mm(jnp.where(hl==hh,vg,zero),gTg)
            ds_=p.astype(F32)*(dp-D_ref[0,pl.ds(h,1),:])
            for c in range(G_s.shape[0]):
                wd=min(128,WIN-c*128)
                G_s[c,pl.ds(pl.multiple_of(h*WIN,8),WIN),:wd]+=ds_[:,c*128:c*128+wd]
            dsl=ds_.astype(BF)
            dv+=mm(p,jnp.where(hl==hh,gg,zero))
            dk+=mm(dsl,jnp.where(hl==hh,qg,zero))
            gqT_s[pl.ds(o+hh*HD,HD),:]=mm(kT_s[pl.ds(o+hh*HD,HD),:],dsl)
        gq_s[1,:,pl.ds(o,GROUP)]=(dk*(1.0/SQ)).astype(BF)
        gq_s[2,:,pl.ds(o,GROUP)]=dv.astype(BF)
        return 0
    lax.fori_loop(0,groups,group,0)
    gq_s[0]=(gqT_s[...]*(1.0/SQ)).astype(BF).T
    x=x_ref[0]
    xhat,rstd=norm_stats(x)
    xn=(xhat*gains_ref[0:1,:]+shifts_ref[0:1,:]).astype(BF)
    xnT=xn.T
    gr=jnp.zeros((WIN,D),F32)
    for m in range(parts):
        for c in range(3):
            gc=gq_s[c,:,m*cq:(m+1)*cq]
            gr=gr+mm_nt(gc,W_ref[m,:,c*cq:(c+1)*cq])
            aq[m,:,c*cq:(c+1)*cq]+=mm(xnT,gc)
    dd_ref[0]=(gln2_ref[0]+norm_back(gr,xhat,rstd,gains_ref[0:1,:])).astype(BF)
    small_ref[0:1,:]+=jnp.sum(gr*xhat,axis=0,keepdims=True)
    small_ref[2:3,:]+=jnp.sum(gr,axis=0,keepdims=True)
    @pl.when(w==nw-1)
    def _():
        dqkv_ref[...]=aq[...].astype(BF)
        cp=pltpu.make_async_copy(G_s,G_hbm,sem); cp.start(); cp.wait()

def call_b(x,gln2,qkv,g,gT,Dd,Pp,W,gains,shifts):
    nW,WIN,D=x.shape; NH=Dd.shape[1]
    parts=W.shape[0]; cq=D//parts; tiles=-(-WIN//128)
    sd=jax.ShapeDtypeStruct
    return pl.pallas_call(functools.partial(kernel_b,NH),grid=(nW,),
      in_specs=[per((WIN,D)),per((WIN,D)),per((3,WIN,D)),per((WIN,D)),per((D,WIN)),per((NH,WIN)),per((NH,WIN,WIN)),
        full((parts,D,3*cq),pipeline_mode=ONE),full(gains.shape),full(shifts.shape)],
      out_specs=[per((WIN,D)),full((parts,D,3*cq)),ANY,full((8,D))],
      out_shape=[sd((nW,WIN,D),BF),sd((parts,D,3*cq),BF),sd((tiles,NH*WIN,128),F32),sd((8,D),F32)],
      scratch_shapes=[pltpu.VMEM((tiles,NH*WIN,128),F32),pltpu.VMEM((parts,D,3*cq),F32),pltpu.VMEM((D,WIN),BF),pltpu.VMEM((3,WIN,D),BF),pltpu.VMEM((D,WIN),F32),
        pltpu.SemaphoreType.DMA],
      compiler_params=pltpu.CompilerParams(vmem_limit_bytes=62*1024*1024,dimension_semantics=("arbitrary",)),
      name="kernel_b")(x,gln2,qkv,g,gT,Dd,Pp,W,gains,shifts)

FIX=8191.0

def pack_table(table):
    NH,T=table.shape
    n=-(-T//128)
    q=jnp.round(jnp.clip(table,-4.0,4.0)*FIX).astype(jnp.int32)
    q=jnp.pad(q,((0,0),(0,n*128-T)))
    q=q.reshape(NH//2,2,n,128)
    return (q[:,0]*65536)|(q[:,1]&65535)

def kernel_p(pos_ref,tab_ref,bias_ref):
    npair,n,_=tab_ref.shape
    WIN=bias_ref.shape[-1]
    tiles=-(-WIN//128)
    def row(r,_):
        r8=pl.multiple_of(r*8,8)
        for c in range(tiles):
            width=min(128,WIN-c*128)
            idx=pos_ref[pl.ds(r8,8),c*128:(c+1)*128]
            lo=idx&127; hi=idx>>7
            masks=[hi==k for k in range(n)]
            for p in range(npair):
                acc=jnp.zeros((8,128),jnp.int32)
                for k in range(n):
                    src=jnp.broadcast_to(tab_ref[p,k:k+1,:],(8,128))
                    acc=jnp.where(masks[k],jnp.take_along_axis(src,lo,axis=1),acc)
                a=(acc>>16).astype(F32)*(SQ/FIX)
                b=((acc<<16)>>16).astype(F32)*(SQ/FIX)
                bias_ref[2*p,pl.ds(r8,8),c*128:c*128+width]=a[:,:width]
                bias_ref[2*p+1,pl.ds(r8,8),c*128:c*128+width]=b[:,:width]
        return 0
    lax.fori_loop(0,bias_ref.shape[1]//8,row,0)

def call_p(posT_pad,tab,WIN):
    NH=tab.shape[0]*2
    return pl.pallas_call(kernel_p,out_shape=jax.ShapeDtypeStruct((NH,WIN,WIN),F32),
      compiler_params=pltpu.CompilerParams(vmem_limit_bytes=40*1024*1024),name="kernel_p")(posT_pad,tab)

def kernel_t(NH,G_ref,hi_ref,lo_ref,out_ref):
    WIN=hi_ref.shape[0]; LW=G_ref.shape[0]*128
    nh=out_ref.shape[0]//NH
    out_ref[...]=jnp.zeros_like(out_ref)
    def rows(r,_):
        r8=pl.multiple_of(r*8,8)
        hi8=hi_ref[pl.ds(r8,8),:]; lo8=lo_ref[pl.ds(r8,8),:]
        tot=jnp.zeros(out_ref.shape,F32)
        iota=lax.broadcasted_iota(jnp.int32,(256,LW),0).astype(F32).astype(BF)
        for k in range(8):
            g=jnp.concatenate([G_ref[c,pl.ds(r8+k,NH,stride=WIN),:] for c in range(LW//128)],axis=1)
            hr=hi8[k:k+1,:]; lr=lo8[k:k+1,:].astype(F32).astype(BF)
            A=jnp.concatenate([jnp.where(hr==m,g,0.0) for m in range(nh)],axis=0).astype(BF)
            oh=jnp.where(iota==lr,jnp.ones((),BF),jnp.zeros((),BF))
            tot=tot+lax.dot_general(A,oh,(((1,),(1,)),((),())),preferred_element_type=F32)
        out_ref[...]+=tot
        return 0
    lax.fori_loop(0,WIN//8,rows,0)

def call_t(G,posT,T,NH):
    WIN=posT.shape[0]; nt=G.shape[0]
    nh=-(-T//256)
    pp=jnp.pad(posT,((0,0),(0,nt*128-WIN)),constant_values=nh*256)
    hi=pp>>8; lo=pp&255
    o=pl.pallas_call(functools.partial(kernel_t,NH),out_shape=jax.ShapeDtypeStruct((nh*NH,256),F32),
      compiler_params=pltpu.CompilerParams(vmem_limit_bytes=40*1024*1024),name="kernel_t")(G,hi,lo)
    return o.reshape(nh,NH,256).transpose(1,0,2).reshape(NH,nh*256)[:,:T]


MESHID=pl.DeviceIdType.MESH

def place_of():
    s=lax.axis_index("seq"); y=lax.axis_index("heads")
    return s//4,(s//2)%2,s%2,y

def dev(z,x,c,y):
    return ((z*2+x)*2+c,y)

def peers_of(z,x,c,y):
    return [dev(z,x,1-c,y),dev(z,1-x,c,y),dev(z,x,c,1-y)]+[dev((z+i)%4,x,c,y) for i in (1,2,3)]

def greet(devices):
    bar=pltpu.get_barrier_semaphore()
    for d in devices:
        pl.semaphore_signal(bar,inc=1,device_id=d,device_id_type=MESHID)
    pl.semaphore_wait(bar,len(devices))

def send(src,dst,ss,rs,to):
    return pltpu.make_async_remote_copy(src_ref=src,dst_ref=dst,send_sem=ss,recv_sem=rs,device_id=to,device_id_type=MESHID)


class Gather:
    def __init__(self,src,dst,ss,rs,own):
        self.src,self.dst,self.ss,self.rs,self.own=src,dst,ss,rs,own
        z,x,c,y=self.at=place_of()
        self.xa=x+(1-2*x)*(1-c); self.ya=y+(1-2*y)*c
        self.xb=x+(1-2*x)*c; self.yb=y+(1-2*y)*(1-c)
        self.sib=dev(z,x,1-c,y); self.pa=dev(z,self.xa,c,self.ya); self.pb=dev(z,self.xb,c,self.yb)
    def slot(self,zz,xx,cc,yy):
        n=self.src.shape[0]
        return self.dst.at[yy,pl.ds(pl.multiple_of(((zz*2+xx)*2+cc)*n,n),n)]
    def copy(self,src,where,k,to):
        return send(src,self.slot(*where),self.ss.at[k],self.rs.at[k],to)
    def go(self,where,k,to,src=None):
        self.copy(self.slot(*where) if src is None else src,where,k,to).start()
    def came(self,where,k):
        self.copy(self.src,where,k,self.sib).wait_recv()
    def keep(self):
        z,x,c,y=self.at
        return pltpu.make_async_copy(self.src,self.slot(z,x,c,y),self.own)
    def start(self):
        z,x,c,y=self.at
        me=(z,x,c,y)
        self.keep().start()
        for i in (1,2,3):
            self.go(me,i-1,dev((z+i)%4,x,c,y),self.src)
        self.go(me,3,self.pa,self.src); self.go(me,7,self.pb,self.src); self.go(me,15,self.sib,self.src)
    def z(self,i):
        return (self.at[0]+4-i)%4
    def turn_z(self,i):
        z,x,c,y=self.at
        at=(self.z(i),x,c,y); self.came(at,i-1)
        self.go(at,3+i,self.pa); self.go(at,7+i,self.pb); self.go(at,15+i,self.sib)
    def turn_a(self,i):
        at=(self.z(i),self.xa,self.at[2],self.ya); self.came(at,3+i)
        self.go(at,11+i,self.pb); self.go(at,19+i,self.sib)
    def turn_b(self,i):
        at=(self.z(i),self.xb,self.at[2],self.yb); self.came(at,7+i)
        self.go(at,23+i,self.sib)
    def turn_ab(self,i):
        z,x,c,y=self.at
        at=(self.z(i),1-x,c,1-y); self.came(at,11+i)
        self.go(at,27+i,self.sib)
    def last(self):
        z,x,c,y=self.at
        for i in range(4):
            zz=self.z(i)
            self.came((zz,x,1-c,y),15+i); self.came((zz,self.xb,1-c,self.yb),19+i)
            self.came((zz,self.xa,1-c,self.ya),23+i); self.came((zz,1-x,1-c,1-y),27+i)
    def drain(self):
        z,x,c,y=self.at
        for k in range(31):
            self.copy(self.src,(z,x,c,y),k,self.sib).wait_send()
        self.keep().wait()

def gather_sems():
    return [pltpu.SemaphoreType.DMA((31,)),pltpu.SemaphoreType.DMA((31,)),pltpu.SemaphoreType.DMA]

STEPS=7
def kernel_w(qkv_ref,proj_ref,fc1_ref,fc2_ref,pos_ref,tab_ref,W_hbm,bias_hbm,wf_ref,posT_ref,
             bias_s,wq_s,tb,tq,ss,rs,own,bs,br,bl,tsem):
    z,x,c,y=place_of()
    cq=qkv_ref.shape[2]; cf=fc1_ref.shape[1]
    for k in range(3): wq_s[:,k*cq:(k+1)*cq]=qkv_ref[k].astype(BF)
    wq_s[:,3*cq:4*cq]=proj_ref[...].astype(BF)
    half,T=tab_ref.shape
    tb[2]=jnp.zeros(tb.shape[1:],F32)
    tb[2,:,0:T]=tab_ref[...]
    greet(peers_of(z,x,c,y))
    gather=Gather(wq_s,W_hbm,ss,rs,own)
    swap=send(tb.at[2],tb.at[y],tsem.at[0],tsem.at[1],dev(z,x,c,1-y))
    swap.start()
    gather.start()
    tb[y]=tb[2]
    wf_ref[:,0:cf]=fc1_ref[...].astype(BF)
    wf_ref[:,cf:2*cf]=fc2_ref[...].astype(BF)
    WIN=bias_s.shape[-1]; tiles=-(-WIN//128); n=tb.shape[2]//128
    posT_ref[...]=jnp.full(posT_ref.shape,1<<15,jnp.int32)
    posT_ref[:,0:WIN]=pos_ref[...].astype(F32).T.astype(jnp.int32)
    swap.wait()
    npair=half//2
    for p in range(npair):
        a,b=[jnp.floor(jnp.clip(tb[c,2*p+k:2*p+k+1,:],-4.0,4.0)*FIX+0.5).astype(jnp.int32) for k in range(2)]
        tq[p:p+1,:]=(a*65536)|(b&65535)
    nrow=WIN//8
    cuts=[nrow*k//STEPS for k in range(STEPS+1)]
    sib=dev(z,x,1-c,y)
    def rows_of(k): return pl.ds(cuts[k]*8,(cuts[k+1]-cuts[k])*8)
    def kept(k): return pltpu.make_async_copy(bias_s.at[:,rows_of(k)],bias_hbm.at[pl.ds(c*half,half),rows_of(k)],bl.at[k])
    def sent(k,cc): return send(bias_s.at[:,rows_of(k)],bias_hbm.at[pl.ds(cc*half,half),rows_of(k)],bs.at[k],br.at[k],sib)
    def rows(k):
        def row(r,_):
            r8=pl.multiple_of(r*8,8)
            for t in range(tiles):
                width=min(128,WIN-t*128)
                idx=posT_ref[pl.ds(r8,8),t*128:(t+1)*128]
                lo=idx&127; hi=idx>>7
                masks=[hi==q for q in range(n)]
                for p in range(npair):
                    acc=jnp.zeros((8,128),jnp.int32)
                    for q in range(n):
                        src=jnp.broadcast_to(tq[p:p+1,q*128:(q+1)*128],(8,128))
                        acc=jnp.where(masks[q],jnp.take_along_axis(src,lo,axis=1),acc)
                    a=(acc>>16).astype(F32)*(SQ/FIX)
                    b=((acc<<16)>>16).astype(F32)*(SQ/FIX)
                    bias_s[2*p,pl.ds(r8,8),t*128:t*128+width]=a[:,:width]
                    bias_s[2*p+1,pl.ds(r8,8),t*128:t*128+width]=b[:,:width]
            return 0
        lax.fori_loop(cuts[k],cuts[k+1],row,0)
        kept(k).start(); sent(k,c).start()
    rows(0)
    for i in (1,3,2): gather.turn_z(i)
    rows(1)
    for i in (0,): gather.turn_a(i); gather.turn_b(i)
    rows(2)
    for i in (1,3): gather.turn_a(i); gather.turn_b(i)
    rows(3)
    for i in (2,): gather.turn_a(i); gather.turn_b(i)
    gather.turn_ab(0)
    rows(4)
    for i in (1,3): gather.turn_ab(i)
    rows(5)
    gather.turn_ab(2)
    rows(6)
    gather.last()
    for k in range(STEPS):
        kept(k).wait(); sent(k,c).wait_send(); sent(k,1-c).wait_recv()
    gather.drain()

def call_w(w_qkv,w_proj,w_fc1,w_fc2,pos_index,rel_table):
    rows,cq=w_qkv.shape[1:]; cf=w_fc1.shape[1]; WIN=pos_index.shape[0]; half,T=rel_table.shape; dma=pltpu.SemaphoreType.DMA
    wide=-(-WIN//128)*128; n=-(-T//128); mem=pltpu.VMEM
    sd=jax.ShapeDtypeStruct
    return pl.pallas_call(kernel_w,grid=(1,),
      out_shape=[sd((2,16*rows,4*cq),BF),sd((2*half,WIN,WIN),F32),sd((rows,2*cf),BF),sd((WIN,wide),jnp.int32)],
      in_specs=[full(v.shape) for v in (w_qkv,w_proj,w_fc1,w_fc2,pos_index,rel_table)],out_specs=[ANY,ANY,full((rows,2*cf)),full((WIN,wide))],
      scratch_shapes=[mem((half,WIN,WIN),F32),mem((rows,4*cq),BF),mem((3,half,n*128),F32),mem((half//2,n*128),jnp.int32)]
        +gather_sems()+[dma((STEPS,)),dma((STEPS,)),dma((STEPS,)),dma((2,))],
      compiler_params=pltpu.CompilerParams(vmem_limit_bytes=63*1024*1024,collective_id=1,has_side_effects=True),name="kernel_w")(w_qkv,w_proj,w_fc1,w_fc2,pos_index,rel_table)

def neighbours(z,x,c,y):
    s=(z*2+x)*2+c
    return [((s+k)%16,yy) for k in (1,15) for yy in (y,1-y)]

def kernel_a2(nheads,in_hbm,og_hbm,wf_hbm,lab_ref,bias_ref,W1,gains_ref,shifts_ref,
              qkv_ref,x_ref,P_hbm,gln2_ref,g_ref,gT_ref,D_ref,ev_hbm,dlast_hbm,dcat_hbm,small_ref,
              x_s,og_s,W2,OT_s,qT_s,vT_s,P_s,acc,pst,xn2_s,xn2T_s,tg_s,tgT_s,up_s,gn2_s,dl_s,
              lab_s,psem,xsem,hsem,ss,rs,own,dl,ds,dr,fin):
    i=pl.program_id(0); nw=x_s.shape[0]
    w=i%nw
    z,xc,c,y=place_of()
    s=(z*2+xc)*2+c
    D=x_s.shape[-1]; WIN=qkv_ref.shape[-2]; SLAB=x_s.shape[1]; HALF=SLAB//2
    OFF=(SLAB-WIN)//2
    cq=D//2; cf=W2.shape[2]//2
    groups=nheads//PER
    gather=Gather(wf_hbm,W2,ss,rs,own)
    mate=dev(z,xc,c,1-y)
    def local(k,half,t):
        hbm,buf=((in_hbm,x_s),(og_hbm,og_s))[t]
        r=pl.multiple_of(y*(nw*WIN)+k*WIN+(WIN//2-OFF)+half*HALF,8)
        return pltpu.make_async_copy(hbm.at[pl.ds(r,HALF)],buf.at[k,pl.ds(half*HALF,HALF)],xsem.at[t,2*k+half])
    def edge(t):
        hbm,buf=((in_hbm,x_s),(og_hbm,og_s))[t]
        return send(hbm.at[pl.ds(0,HALF)],buf.at[nw-1,pl.ds(HALF,HALF)],hsem.at[t,0],hsem.at[t,1],((s+15)%16,1))
    def ready(t):
        local(w,0,t).wait()
        far=jnp.logical_and(w==nw-1,y==1)
        @pl.when(far)
        def _(): edge(t).wait_recv()
        @pl.when(jnp.logical_not(far))
        def _(): local(w,1,t).wait()
    def slab(k,to=None):
        if k is None: return pltpu.make_async_copy(dl_s.at[nw-1],dlast_hbm,dl.at[nw-1])
        at=ev_hbm.at[y*nw+k]
        if to is None: return pltpu.make_async_copy(dl_s.at[k],at,dl.at[k])
        return send(dl_s.at[k],at,ds.at[k],dr.at[k],to)
    @pl.when(i==0)
    def _():
        greet(peers_of(z,xc,c,y)+neighbours(z,xc,c,y))
        for k in range(nw):
            for t in range(2):
                local(k,0,t).start()
                if k<nw-1: local(k,1,t).start()
        for t in range(2):
            @pl.when(y==1)
            def _(): edge(t).start()
            @pl.when(y==0)
            def _(): local(nw-1,1,t).start()
        gather.start()
        lab_s[...]=lab_ref[...].astype(F32).T
        acc[...]=jnp.zeros_like(acc)
        small_ref[...]=jnp.zeros_like(small_ref)
        dl_s[:,SLAB-16:,:]=jnp.zeros((nw,16,D),BF)

    @pl.when(i<nw)
    def _():
        ready(0)
        x=x_s[w,OFF:OFF+WIN,:]
        x_ref[0]=x
        xhat,_=norm_stats(x)
        xn=(xhat*gains_ref[0:1,:]+shifts_ref[0:1,:]).astype(BF)
        for k in range(3):
            for m in range(2):
                at=slice(m*cq,(m+1)*cq)
                v=mm(xn,W1[m,:,k*cq:(k+1)*cq]).astype(BF)
                qkv_ref[0,k,:,at]=v
                if k==0: qT_s[at,:]=v.T
                if k==2: vT_s[at,:]=v.T
        mine=y*nw+w
        labr=lab_ref[pl.ds(mine,1),:]
        labc=jnp.sum(jnp.where(lax.broadcasted_iota(jnp.int32,lab_s.shape,1)==mine,lab_s[...],0.0),axis=1,keepdims=True).astype(jnp.int32)
        lane=lax.broadcasted_iota(jnp.int32,(WIN,GROUP),1)
        oh=jnp.where((labc==lane)|((labc+3)==lane),1.0,0.0).astype(BF)
        hi=564.0
        lo=MASK-hi
        sub=lax.broadcasted_iota(jnp.int32,(GROUP,WIN),0)
        nm=jnp.where(sub<3,jnp.where(sub!=labr,-hi,0.0),jnp.where(sub<6,jnp.where(sub-3!=labr,-lo,0.0),0.0)).astype(BF)
        hl=lane//HD
        def group(gi,_):
            slot=gi%2
            @pl.when(w*groups+gi>=2)
            def _():
                pltpu.make_async_copy(P_s.at[slot],P_hbm.at[0,pl.ds(0,PER)],psem.at[slot]).wait()
            o=pl.multiple_of(gi*GROUP,GROUP)
            qTg=jnp.concatenate([qT_s[pl.ds(o,GROUP),:],nm],axis=0)
            kg=qkv_ref[0,1,:,pl.ds(o,GROUP)]
            for hh in range(PER):
                kh=jnp.concatenate([jnp.where(hl==hh,kg,jnp.zeros_like(kg)),oh],axis=1)
                t=mm(kh,qTg)+bias_ref[gi*PER+hh]
                m=jnp.max(t,axis=0,keepdims=True)
                e=jnp.exp2((t-m)*CEXP)
                l=jnp.sum(e,axis=0,keepdims=True)
                p=(e*(1.0/l)).astype(BF)
                P_s[slot,hh]=p
                OT_s[w,pl.ds(o+hh*HD,HD),:]=mm(vT_s[pl.ds(o+hh*HD,HD),:],p)
            pltpu.make_async_copy(P_s.at[slot],P_hbm.at[w,pl.ds(gi*PER,PER)],psem.at[slot]).start()
            return 0
        lax.fori_loop(0,groups,group,0)

    @pl.when(i==0)
    def _():
        for k in (1,3,2): gather.turn_z(k)
    @pl.when(i==1)
    def _():
        for k in (0,1,3,2): gather.turn_a(k); gather.turn_b(k)
    @pl.when(i==2)
    def _():
        for k in (0,1,3,2): gather.turn_ab(k)
    @pl.when(i==nw-1)
    def _():
        gather.last(); gather.drain()

    @pl.when(i>=nw)
    def _():
        ready(1)
        x=x_s[w,OFF:OFF+WIN,:]
        og=og_s[w,OFF:OFF+WIN,:]
        attn=OT_s[w].astype(BF).T
        branch=shifts_ref[2:3,:]
        for m in range(2):
            branch=branch+mm_nt(attn[:,m*cq:(m+1)*cq],W1[m,:,3*cq:4*cq])
        branch=branch.astype(BF).astype(F32)
        middle=x+branch
        xhat2,rstd2=norm_stats(middle)
        xn2=(xhat2*gains_ref[1:2,:]+shifts_ref[1:2,:]).astype(BF)
        tg=og.astype(BF)
        xn2_s[...]=xn2; xn2T_s[...]=xn2.T; tg_s[...]=tg; tgT_s[...]=tg.T
        up_s[...]=jnp.zeros_like(up_s); gn2_s[...]=jnp.zeros_like(gn2_s)
        CH=512; each=cf//CH
        def chunk(k,_):
            m=k//each
            o=pl.multiple_of((k%each)*CH,CH)
            f1=W2[m,:,pl.ds(o,CH)]; f2=W2[m,:,pl.ds(cf+o,CH)]
            hid=mm(xn2_s[...],f1)
            act,dact=gelu_both(hid)
            a=act.astype(BF)
            up_s[...]+=mm_nt(a,f2)
            gh=(mm(tg_s[...],f2)*dact).astype(BF)
            gn2_s[...]+=mm_nt(gh,f1)
            acc[m,:,pl.ds(cq+o,CH)]+=mm(xn2T_s[...],gh)
            acc[m,:,pl.ds(cq+cf+o,CH)]+=mm(tgT_s[...],a)
            return 0
        lax.fori_loop(0,2*each,chunk,0)
        dl_s[w,0:WIN,:]=(branch+up_s[...]+shifts_ref[3:4,:]).astype(BF)
        @pl.when(w<nw-1)
        def _():
            slab(w).start(); slab(w,mate).start()
        @pl.when(w==nw-1)
        def _(): slab(None).start()
        gn2=gn2_s[...]
        gln2=norm_back(gn2,xhat2,rstd2,gains_ref[1:2,:])
        gln2_ref[0]=gln2
        gb=(og+gln2).astype(BF)
        gbT=gb.T
        for m in range(2):
            at=slice(m*cq,(m+1)*cq)
            acc[m,:,0:cq]+=mm(gbT,attn[:,at])
            g=mm(gb,W1[m,:,3*cq:4*cq]).astype(BF)
            g_ref[0,:,at]=g
            gT=g.T
            gT_ref[0,at,:]=gT
            prod=gT.astype(F32)*OT_s[w,at,:]
            nh=nheads//2
            D_ref[0,m*nh:(m+1)*nh,:]=jnp.sum(prod.reshape(nh,HD,WIN),axis=1)
        small_ref[1:2,:]+=jnp.sum(gn2*xhat2,axis=0,keepdims=True)
        small_ref[3:4,:]+=jnp.sum(gn2,axis=0,keepdims=True)
        small_ref[4:5,:]+=jnp.sum(gb.astype(F32),axis=0,keepdims=True)
        small_ref[5:6,:]+=jnp.sum(tg.astype(F32),axis=0,keepdims=True)

    @pl.when(i==2*nw-1)
    def _():
        W2[...]=acc[:,:,cq:].astype(BF)
        pst[...]=acc[:,:,:cq].astype(BF)
        a=pltpu.make_async_copy(W2,dcat_hbm.at[:,:,pl.ds(cq,2*cf)],fin.at[0])
        b=pltpu.make_async_copy(pst,dcat_hbm.at[:,:,pl.ds(0,cq)],fin.at[1])
        a.start(); b.start()
        for k in range(2):
            pltpu.make_async_copy(P_s.at[k],P_hbm.at[0,pl.ds(0,PER)],psem.at[k]).wait()
        for k in range(nw-1):
            slab(k).wait(); slab(k,mate).wait()
        slab(None).wait()
        @pl.when(y==1)
        def _():
            for t in range(2): edge(t).wait_send()
        a.wait(); b.wait()

def call_a2(inputs,og,wf,lab,bias,W1,gains,shifts):
    nW=lab.shape[0]//2; WIN=lab.shape[1]; D=inputs.shape[1]; NH=bias.shape[0]
    cf=wf.shape[1]//2; cq=D//2; SLAB=-(-WIN//16)*16
    sd=jax.ShapeDtypeStruct; dma=pltpu.SemaphoreType.DMA; v=pltpu.VMEM
    early=lambda shape: pl.BlockSpec((1,)+shape,lambda i:(jnp.minimum(i,nW-1),)+(0,)*len(shape))
    late=lambda shape: pl.BlockSpec((1,)+shape,lambda i:(jnp.maximum(i-nW,0),)+(0,)*len(shape))
    outs=[sd((nW,3,WIN,D),BF),sd((nW,WIN,D),F32),sd((nW,NH,WIN,WIN),BF),sd((nW,WIN,D),F32),sd((nW,WIN,D),BF),sd((nW,D,WIN),BF),sd((nW,NH,WIN),F32),
          sd((2*nW,SLAB,D),BF),sd((SLAB,D),BF),sd((2,D,cq+2*cf),BF),sd((8,D),F32)]
    return pl.pallas_call(functools.partial(kernel_a2,NH),grid=(2*nW,),
      in_specs=[ANY,ANY,ANY,full(lab.shape),full((NH,WIN,WIN),pipeline_mode=ONE),full(W1.shape,pipeline_mode=ONE),full(gains.shape),full(shifts.shape)],
      out_specs=[early((3,WIN,D)),early((WIN,D)),ANY,late((WIN,D)),late((WIN,D)),late((D,WIN)),late((NH,WIN)),ANY,ANY,ANY,full((8,D))],
      out_shape=outs,
      scratch_shapes=[v((nW,SLAB,D),F32),v((nW,SLAB,D),F32),v((2,D,2*cf),BF),v((nW,D,WIN),F32),v((D,WIN),BF),v((D,WIN),BF),v((2,PER,WIN,WIN),BF),
        v((2,D,cq+2*cf),F32),v((2,D,cq),BF),v((WIN,D),BF),v((D,WIN),BF),v((WIN,D),BF),v((D,WIN),BF),v((WIN,D),F32),v((WIN,D),F32),v((nW,SLAB,D),BF),
        v((WIN,2*nW),F32),dma((2,)),dma((2,2*nW)),dma((2,2))]+gather_sems()+[dma((nW,)),dma((nW,)),dma((nW,)),dma((2,))],
      compiler_params=pltpu.CompilerParams(vmem_limit_bytes=63*1024*1024,dimension_semantics=("arbitrary",),collective_id=2,has_side_effects=True),
      name="kernel_a2")(inputs,og,wf,lab,bias,W1,gains,shifts)

class Reduce:
    def __init__(self,src,out,own,r1,r2,ss,rs,ls,r3,fin,r4,r5):
        self.src,self.out,self.own,self.r1,self.r2,self.r3,self.fin,self.r4,self.r5=src,out,own,r1,r2,r3,fin,r4,r5
        self.ss,self.rs,self.ls=ss,rs,ls
        self.at=place_of()
    def put(self,src,dst,k,to):
        return send(src,dst,self.ss.at[k],self.rs.at[k],to)
    def mine(self,k):
        return pltpu.make_async_copy(self.src.at[k%2,:,k//2,self.at[2]],self.own.at[k//2,:,k%2],self.ls.at[k])
    def theirs(self,k):
        z,x,c,y=self.at
        return self.put(self.src.at[k%2,:,k//2,1-c],self.r1.at[k//2,:,k%2],k,dev(z,x,1-c,y))
    def kept(self,b):
        z,x,c,y=self.at
        return x*(1-c)+b*c,b*(1-c)+y*c
    def first(self,b):
        z,x,c,y=self.at
        at=self.own.at[(1-x)*(1-c)+b*c,:,b*(1-c)+(1-y)*c]
        return self.put(at,self.r2.at[:,b],4+b,dev(z,x+(1-2*x)*(1-c),c,y+(1-2*y)*c))
    def zboth(self,i):
        z,x,c,y=self.at
        zz=(z+i)%4
        return self.put(self.own.at[x,zz],self.r3.at[i-1],5+i,dev(zz,x,c,y))
    def zone(self,i):
        z,x,c,y=self.at
        zz=(z+i)%4
        return self.put(self.own.at[x,zz,y],self.r3.at[i-1,0],5+i,dev(zz,x,c,y))
    def ylast(self):
        z,x,c,y=self.at
        return self.put(self.fin.at[1-y],self.r4,9,dev(z,x,c,1-y))
    def xsecond(self):
        z,x,c,y=self.at
        return self.put(self.own.at[1-x,:,y],self.r5,9,dev(z,1-x,c,y))
    def start(self):
        for k in range(4):
            self.theirs(k).start(); self.mine(k).start()
    def add(self,dst,*srcs):
        total=srcs[0][...].astype(F32)
        for s in srcs[1:]: total=total+s[...].astype(F32)
        dst[...]=total.astype(dst.dtype)
    def by_core(self,zero,one):
        c=self.at[2]
        pl.when(c==0)(zero)
        pl.when(c==1)(one)
    def one(self):
        z,x,c,y=self.at
        for k in range(4):
            self.mine(k).wait(); self.theirs(k).wait_recv()
        def step(k,_):
            self.add(self.own.at[k//8,(k//2)%4,k%2],self.own.at[k//8,(k//2)%4,k%2],self.r1.at[k//8,(k//2)%4,k%2])
            return 0
        lax.fori_loop(0,16,step,0)
        for b in range(2): self.first(b).start()
    def two(self):
        z,x,c,y=self.at
        for b in range(2): self.first(b).wait_recv()
        def step(k,_):
            zz,b=k//2,k%2
            p,q=self.kept(b)
            self.add(self.own.at[p,zz,q],self.own.at[p,zz,q],self.r2.at[zz,b])
            return 0
        lax.fori_loop(0,8,step,0)
        def zero():
            for i in (2,1,3): self.zboth(i).start()
        self.by_core(zero,lambda: self.xsecond().start())
    def three(self):
        z,x,c,y=self.at
        def zero():
            for i in (1,2,3): self.zboth(i).wait_recv()
            for yy in (1-y,y):
                self.add(self.fin.at[yy],self.own.at[x,z,yy],*[self.r3.at[i,yy] for i in range(3)])
                if yy is not y: self.ylast().start()
        def one():
            self.xsecond().wait_recv()
            for zz in range(4):
                self.add(self.own.at[x,zz,y],self.own.at[x,zz,y],self.r5.at[zz])
            for i in (2,1,3): self.zone(i).start()
        self.by_core(zero,one)
    def four(self):
        z,x,c,y=self.at
        def zero():
            self.ylast().wait_recv()
            self.add(self.out,self.fin.at[y],self.r4)
            for i in (1,2,3): self.zboth(i).wait_send()
            self.ylast().wait_send()
        def one():
            for i in (1,2,3): self.zone(i).wait_recv()
            self.add(self.out,self.own.at[x,z,y],*[self.r3.at[i,0] for i in range(3)])
            for i in (1,2,3): self.zone(i).wait_send()
            self.xsecond().wait_send()
        self.by_core(zero,one)
        for k in range(4): self.theirs(k).wait_send()
        for b in range(2): self.first(b).wait_send()

def reduce_scratch(rows,cols):
    v=lambda *d: pltpu.VMEM(d+(rows,cols),BF); dma=pltpu.SemaphoreType.DMA
    return [v(2,4,2),v(2,4,2),v(4,2),dma((10,)),dma((10,)),dma((4,)),v(3,2),v(2),v(),v(4)]

class Sums:
    def __init__(self,slabs,got,res,ss,rs,ts,us):
        self.slabs,self.got,self.res,self.ss,self.rs,self.ts,self.us=slabs,got,res,ss,rs,ts,us
        z,x,c,y=place_of()
        self.s=(z*2+x)*2+c; self.y=y; self.n=slabs.shape[1]
    def part(self,k,yy):
        me=self.y*16+self.s
        return send(self.slabs.at[yy,k],self.got.at[me],self.ss.at[yy*self.n+k],self.rs.at[me],(k,yy))
    def other(self,k,yy):
        return jnp.logical_or(self.s!=k,self.y!=yy)
    def scatter(self):
        for k in range(self.n):
            for yy in range(2):
                @pl.when(self.other(k,yy))
                def _(): self.part(k,yy).start()
    def back(self,to,k):
        return send(self.res.at[k],self.res.at[k],self.ts.at[to],self.us.at[k],(to,self.y))
    def collect(self):
        me=self.y*16+self.s
        @pl.when(self.s<self.n)
        def _():
            self.got[me]=self.slabs[self.y,self.s]
            def wait(i,_):
                @pl.when(i!=me)
                def _():
                    send(self.slabs.at[0,0],self.got.at[i],self.ss.at[0],self.rs.at[i],(self.s,1-self.y)).wait_recv()
                return 0
            lax.fori_loop(0,32,wait,0)
            total=self.got[0]
            for i in range(1,32): total=total+self.got[i]
            self.res[self.s]=total
            for to in range(16):
                @pl.when(self.s!=to)
                def _(): self.back(to,self.s).start()
    def finish(self):
        for k in range(self.n):
            @pl.when(self.s!=k)
            def _(): self.back(k,k).wait_recv()
        @pl.when(self.s<self.n)
        def _():
            for to in range(16):
                @pl.when(self.s!=to)
                def _(): self.back(to,self.s).wait_send()
        for k in range(self.n):
            for yy in range(2):
                @pl.when(self.other(k,yy))
                def _(): self.part(k,yy).wait_send()

def kernel_bc(nheads,x_ref,gln2_ref,qkv_ref,g_ref,gT_ref,D_ref,P_ref,W1,gains_ref,shifts_ref,sm_ref,pos_ref,dcat_hbm,dlast_hbm,
              ev_hbm,hd_hbm,evl_hbm,hdl_hbm,redq_ref,redm_ref,tab_ref,sum_ref,
              G_s,Gx,aq,dq_s,kT_s,gq_s,gqT_s,dd_s,small_ref,acc,slabs,got,res,
              gs,gr_,dl,ds,dr,es,er,us,ss0,rs0,ts0,us0,
              own,r1,r2,ss,rs,ls,r3,fin,r4,r5,own2,p1,p2,ss2,rs2,ls2,p3,fin2,p4,p5):
    w=pl.program_id(0); nw=dd_s.shape[0]
    z,xc,c,y=place_of()
    s=(z*2+xc)*2+c
    mate=dev(z,xc,c,1-y); sib=dev(z,xc,1-c,y)
    D=x_ref.shape[-1]; WIN=x_ref.shape[-2]; SLAB=dd_s.shape[1]
    cq=D//2
    groups=nheads//PER
    tiles=G_s.shape[0]; part=Gx.shape[1]//nheads
    big=Reduce(dcat_hbm,redm_ref,own2,p1,p2,ss2,rs2,ls2,p3,fin2,p4,p5)
    red=Reduce(dq_s,redq_ref,own,r1,r2,ss,rs,ls,r3,fin,r4,r5)
    def slab(k,to=None):
        at=ev_hbm.at[y*nw+k]
        if to is None: return pltpu.make_async_copy(dd_s.at[k],at,dl.at[k])
        return send(dd_s.at[k],at,ds.at[k],dr.at[k],to)
    def tail(k):
        lead=SLAB-hd_hbm.shape[0]
        return send(dd_s.at[nw-1,pl.ds(lead,hd_hbm.shape[0])],hd_hbm,es.at[k],er,((s+1)%16,k))
    def early(k):
        lead=SLAB-hdl_hbm.shape[0]
        if k==0: return pltpu.make_async_copy(dlast_hbm,evl_hbm.at[y],us.at[0])
        if k==1: return send(dlast_hbm,evl_hbm.at[y],us.at[1],us.at[2],mate)
        return send(dlast_hbm.at[pl.ds(lead,hdl_hbm.shape[0])],hdl_hbm,us.at[k+1],us.at[5],((s+1)%16,k-2))
    def trade(h):
        r=pl.multiple_of(h*WIN+(1-c)*(WIN-part),8)
        return send(G_s.at[:,pl.ds(r,part)],Gx.at[:,pl.ds(pl.multiple_of(h*part,8),part)],gs.at[h],gr_.at[h],sib)
    @pl.when(w==0)
    def _():
        greet([((s+t)%16,yy) for t in range(1,16) for yy in (y,1-y)]+[mate])
        big.start()
        early(0).start(); early(1).start()
        @pl.when(y==1)
        def _():
            early(2).start(); early(3).start()
        aq[...]=jnp.zeros_like(aq); G_s[...]=jnp.zeros_like(G_s); small_ref[...]=sm_ref[...]
        dd_s[:,SLAB-16:,:]=jnp.zeros((nw,16,D),BF)
    kT_s[...]=qkv_ref[0,1].T
    lane=lax.broadcasted_iota(jnp.int32,(WIN,GROUP),1)
    hl=lane//HD
    def group(gi,_):
        o=pl.multiple_of(gi*GROUP,GROUP)
        gTg=gT_ref[0,pl.ds(o,GROUP),:]
        vg=qkv_ref[0,2,:,pl.ds(o,GROUP)]
        qg=qkv_ref[0,0,:,pl.ds(o,GROUP)]
        gg=g_ref[0,:,pl.ds(o,GROUP)]
        dv=jnp.zeros((WIN,GROUP),F32); dk=jnp.zeros((WIN,GROUP),F32)
        zero=jnp.zeros_like(vg)
        for hh in range(PER):
            h=gi*PER+hh
            p=P_ref[0,h]
            dp=mm(jnp.where(hl==hh,vg,zero),gTg)
            dsc=p.astype(F32)*(dp-D_ref[0,pl.ds(h,1),:])
            for k in range(tiles):
                wd=min(128,WIN-k*128)
                G_s[k,pl.ds(pl.multiple_of(h*WIN,8),WIN),:wd]+=dsc[:,k*128:k*128+wd]
            dsl=dsc.astype(BF)
            dv+=mm(p,jnp.where(hl==hh,gg,zero))
            dk+=mm(dsl,jnp.where(hl==hh,qg,zero))
            gqT_s[pl.ds(o+hh*HD,HD),:]=mm(kT_s[pl.ds(o+hh*HD,HD),:],dsl)
        gq_s[1,:,pl.ds(o,GROUP)]=(dk*(1.0/SQ)).astype(BF)
        gq_s[2,:,pl.ds(o,GROUP)]=dv.astype(BF)
        @pl.when(w==nw-1)
        def _():
            for hh in range(PER): trade(gi*PER+hh).start()
        return 0
    lax.fori_loop(0,groups,group,0)
    gq_s[0]=(gqT_s[...]*(1.0/SQ)).astype(BF).T
    x=x_ref[0]
    xhat,rstd=norm_stats(x)
    xn=(xhat*gains_ref[0:1,:]+shifts_ref[0:1,:]).astype(BF)
    xnT=xn.T
    gr=jnp.zeros((WIN,D),F32)
    for m in range(2):
        for k in range(3):
            gc=gq_s[k,:,m*cq:(m+1)*cq]
            gr=gr+mm_nt(gc,W1[m,:,k*cq:(k+1)*cq])
            aq[m,:,k*cq:(k+1)*cq]+=mm(xnT,gc)
    @pl.when(w==nw-1)
    def _():
        dq_s[...]=aq[...].astype(BF).reshape(dq_s.shape)
        red.start()
    dd_s[w,0:WIN,:]=(gln2_ref[0]+norm_back(gr,xhat,rstd,gains_ref[0:1,:])).astype(BF)
    slab(w).start(); slab(w,mate).start()
    @pl.when(jnp.logical_and(w==nw-1,y==1))
    def _():
        tail(0).start(); tail(1).start()
    small_ref[0:1,:]+=jnp.sum(gr*xhat,axis=0,keepdims=True)
    small_ref[2:3,:]+=jnp.sum(gr,axis=0,keepdims=True)
    pl.when(w==0)(big.one)
    pl.when(w==nw//2-1)(big.two)
    pl.when(w==nw-2)(big.three)
    @pl.when(w==nw-1)
    def _():
        for h in range(nheads): trade(h).wait()
        acc[...]=jnp.zeros_like(acc)
        nh=acc.shape[0]; LW=tiles*128
        base=c*(WIN-part)
        def rows(r,_):
            r8=pl.multiple_of(r*8,8)
            f8=pl.multiple_of(base+r*8,8)
            pos=pos_ref[pl.ds(f8,8),:]
            hi8=pos>>8; lo8=pos&255
            tot=jnp.zeros((nh*nheads,256),F32)
            iota=lax.broadcasted_iota(jnp.int32,(256,LW),0).astype(F32).astype(BF)
            for k in range(8):
                g=jnp.concatenate([G_s[q,pl.ds(f8+k,nheads,stride=WIN),:]+Gx[q,pl.ds(r8+k,nheads,stride=part),:] for q in range(tiles)],axis=1)
                hr=hi8[k:k+1,:]; lr=lo8[k:k+1,:].astype(F32).astype(BF)
                A=jnp.concatenate([jnp.where(hr==m,g,0.0) for m in range(nh)],axis=0).astype(BF)
                oh=jnp.where(iota==lr,jnp.ones((),BF),jnp.zeros((),BF))
                tot=tot+mm_nt(A,oh)
            acc[...]+=tot.reshape(acc.shape)
            return 0
        n=part//8
        lax.fori_loop(c,n*4//25,rows,0)
        red.one()
        lax.fori_loop(n*4//25,n*11//25,rows,0)
        red.two()
        lax.fori_loop(n*11//25,n*18//25,rows,0)
        red.three()
        lax.fori_loop(n*18//25,n,rows,0)
        half=nheads//2
        for yy in range(2):
            for k in range(nh): slabs[yy,k]=acc[k,yy*half:(yy+1)*half]
            for k in range(2): slabs[yy,nh+k]=small_ref[:,k*256:(k+1)*256]
        sums=Sums(slabs,got,res,ss0,rs0,ts0,us0)
        sums.scatter()
        red.four()
        sums.collect()
        big.four()
        sums.finish()
        for m in range(nh):
            tab_ref[:,m*256:(m+1)*256]=res[m]
        for k in range(2): sum_ref[:,k*256:(k+1)*256]=res[nh+k]
        for k in range(nw):
            slab(k).wait(); slab(k,mate).wait()
        @pl.when(y==1)
        def _():
            tail(0).wait_send(); tail(1).wait_send(); early(2).wait_send(); early(3).wait_send()
        tail(0).wait_recv(); early(2).wait_recv()
        early(0).wait(); early(1).wait()

def call_bc(x,gln2,qkv,g,gT,Dd,Pp,W1,gains,shifts,sm,pp,dcat,dlast,T):
    nW,WIN,D=x.shape; NH=Dd.shape[1]
    cq=D//2; tiles=-(-WIN//128); SLAB=-(-WIN//16)*16; EDGE=-(-(SLAB-WIN//2)//16)*16
    part=-(-WIN//16)*8
    nh=-(-T//256)
    rows,more=dcat.shape[-2:]; cols=3*cq
    sd=jax.ShapeDtypeStruct; dma=pltpu.SemaphoreType.DMA; v=pltpu.VMEM
    return pl.pallas_call(functools.partial(kernel_bc,NH),grid=(nW,),
      in_specs=[per((WIN,D)),per((WIN,D),pipeline_mode=ONE),per((3,WIN,D)),per((WIN,D)),per((D,WIN)),per((NH,WIN)),per((NH,WIN,WIN)),
        full((2,D,cols),pipeline_mode=ONE),full(gains.shape),full(shifts.shape),full(sm.shape),full(pp.shape,pipeline_mode=ONE),ANY,ANY],
      out_specs=[ANY,ANY,ANY,ANY,full((rows,cols),pipeline_mode=ONE),full((rows,more),pipeline_mode=ONE),full((NH//2,nh*256),pipeline_mode=ONE),full(sm.shape)],
      out_shape=[sd((2*nW,SLAB,D),BF),sd((EDGE,D),BF),sd((2,SLAB,D),BF),sd((EDGE,D),BF),sd((rows,cols),F32),sd((rows,more),F32),sd((NH//2,nh*256),F32),sd(sm.shape,F32)],
      scratch_shapes=[v((tiles,NH*WIN,128),F32),v((tiles,NH*part,128),F32),v((2,D,cols),F32),v((2,4,2,2,rows,cols),BF),v((D,WIN),BF),v((3,WIN,D),BF),v((D,WIN),F32),
        v((nW,SLAB,D),BF),v(sm.shape,F32),v((nh,NH,256),F32),v((2,nh+2,8,256),F32),v((32,8,256),F32),v((nh+2,8,256),F32),
        dma((NH,)),dma((NH,)),dma((nW,)),dma((nW,)),dma((nW,)),dma((2,)),dma,dma((6,)),dma((2*nh+4,)),dma((32,)),dma((16,)),dma((nh+2,))]+reduce_scratch(rows,cols)+reduce_scratch(rows,more),
      compiler_params=pltpu.CompilerParams(vmem_limit_bytes=63*1024*1024,dimension_semantics=("arbitrary",),collective_id=3,has_side_effects=True),
      name="kernel_bc")(x,gln2,qkv,g,gT,Dd,Pp,W1,gains,shifts,sm,pp,dcat,dlast)


def kernel_f(in_ref,og_ref,ev_ref,evl_ref,ev2_ref,hd_ref,hd2_ref,redq_ref,redm_ref,tab_ref,sum_ref,
             out_ref,din_ref,dqkv_ref,dproj_ref,dfc1_ref,dfc2_ref,dgain_ref,dshift_ref,dtab_ref,end_s):
    j=pl.program_id(0); nw=pl.num_programs(0)//2
    shift=in_ref.shape[0]//2; WIN=2*shift
    edge,SLAB=hd_ref.shape[0],ev_ref.shape[1]
    off=edge-(SLAB-shift)
    @pl.when(j==0)
    def _():
        end_s[0]=hd_ref[...].astype(F32); end_s[1]=hd2_ref[...].astype(F32)
        cq=dqkv_ref.shape[2]; cf=dfc1_ref.shape[1]
        for k in range(3): dqkv_ref[k]=redq_ref[:,k*cq:(k+1)*cq]
        dproj_ref[...]=redm_ref[:,0:cq]
        dfc1_ref[...]=redm_ref[:,cq:cq+cf]
        dfc2_ref[...]=redm_ref[:,cq+cf:]
        dgain_ref[...]=sum_ref[0:2,:]; dshift_ref[...]=sum_ref[2:6,:]
        dtab_ref[...]=tab_ref[:,0:dtab_ref.shape[1]]
    e=jnp.where(j%nw==nw-1,evl_ref[0],ev_ref[0]).astype(F32)
    for k,(base,res,v) in enumerate(((in_ref,out_ref,e),(og_ref,din_ref,ev2_ref[0].astype(F32)))):
        res[0:shift,:]=base[0:shift,:]+end_s[k,off:off+shift,:]
        res[shift:WIN,:]=base[shift:WIN,:]+v[0:shift,:]
        end_s[k]=v[SLAB-edge:,:]

def call_f(inputs,og,ev,evl,ev2,hd,hd2,redq,redm,tab,small,cq,cf,T):
    tok,D=inputs.shape; n,SLAB,_=ev.shape; WIN=tok//n; rows=redq.shape[0]
    sd=jax.ShapeDtypeStruct
    blk=pl.BlockSpec((WIN,D),lambda j:(j,0)); slab=pl.BlockSpec((1,SLAB,D),lambda j:(j,0,0))
    shapes=[(3,rows,cq),(rows,cq),(rows,cf),(rows,cf),(2,D),(4,D),(tab.shape[0],T)]
    return pl.pallas_call(kernel_f,grid=(n,),
      in_specs=[blk,blk,slab,pl.BlockSpec((1,SLAB,D),lambda j:(j//(n//2),0,0)),slab]+[full(v.shape) for v in (hd,hd2,redq,redm,tab,small)],
      out_specs=[blk,blk]+[full(v) for v in shapes],
      out_shape=[sd((tok,D),F32),sd((tok,D),F32)]+[sd(v,F32) for v in shapes],
      scratch_shapes=[pltpu.VMEM((2,)+hd.shape,F32)],
      compiler_params=pltpu.CompilerParams(vmem_limit_bytes=63*1024*1024,dimension_semantics=("arbitrary",)),
      name="kernel_f")(inputs,og,ev,evl,ev2,hd,hd2,redq,redm,tab,small)

def gathered(piece,names,nseq,nheads):
    full=lax.all_gather(piece,names,axis=0,tiled=False)
    return full.reshape((nseq,nheads)+piece.shape)

def natural(block):
    s,h,r,c=block.shape
    return block.transpose(0,2,1,3).reshape(s*r,h*c)

def owners(grad,nseq,nheads):
    r,c=grad.shape
    return grad.reshape(nseq,r//nseq,nheads,c//nheads).transpose(0,2,1,3).reshape(nseq*nheads,r//nseq,c//nheads)

def from_next(rows):
    n=lax.axis_size("seq")
    return lax.ppermute(rows,"seq",[(i,(i-1)%n) for i in range(n)])

def to_next(rows):
    n=lax.axis_size("seq")
    return lax.ppermute(rows,"seq",[(i,(i+1)%n) for i in range(n)])

def spread(rows):
    n=lax.axis_size("heads")
    flat=rows.reshape(-1,rows.shape[-1])
    if n==2:
        other=lax.ppermute(flat,"heads",[(0,1),(1,0)])
        me=lax.axis_index("heads")
        return jnp.where(me==0,jnp.concatenate([flat,other]),jnp.concatenate([other,flat]))
    return lax.all_gather(flat,"heads",axis=0,tiled=True)

def place(rows,base,shift):
    every=spread(rows)
    keep=every.shape[0]-shift
    return base+jnp.concatenate([to_next(every[keep:]),every[:keep]]).astype(F32)

def body(inputs,w_qkv,w_proj,w_fc1,w_fc2,gains,shifts,rel_table,region,pos_index,out_grad):
    nseq=lax.axis_size("seq"); nheads=lax.axis_size("heads"); me=lax.axis_index("heads")
    linked=nseq==16 and nheads==2
    names=("seq","heads")
    tok,D=inputs.shape; WIN=pos_index.shape[0]; shift=WIN//2; T=rel_table.shape[1]
    nW=tok//WIN//nheads
    rows=w_qkv.shape[1]; cq=w_qkv.shape[2]; cf=w_fc1.shape[1]
    lab=region.reshape(-1,WIN)
    if linked:
        W1,bias,wf,posT=call_w(w_qkv,w_proj.T,w_fc1,w_fc2.T,pos_index,rel_table)
        qkv,x,Pp,gln2,g,gT,Dd,ev,dlast,dcat,sm=call_a2(inputs,out_grad,wf,lab,bias,W1,gains,shifts)
        ev2,hd2,evl,hd,redq,redm,d_table,small=call_bc(x,gln2,qkv,g,gT,Dd,Pp,W1,gains,shifts,sm,posT,dcat.reshape(2,4,2,2,rows,-1),dlast,T)
        out,din,dq,dp,d1,d2,dg,dsh,dt=call_f(inputs,out_grad,ev,evl,ev2,hd,hd2,redq,redm,d_table,small,cq,cf,T)
        return (out,din,dq,dp.T,d1,d2.T,dg,dsh,dt)
    posT=pos_index.T
    wide=-(-WIN//128)*128
    posP=jnp.pad(posT,((0,0),(0,wide-WIN)))
    start=me*nW*WIN
    lab=lax.dynamic_slice_in_dim(lab,me*nW,nW,0)
    labc=lab[:,:,None]; labr=lab[:,None,:]
    wq=jnp.concatenate([w_qkv[0],w_qkv[1],w_qkv[2],w_proj.T],axis=1).astype(BF)
    wf=jnp.concatenate([w_fc1,w_fc2.T],axis=1).astype(BF)
    table=lax.all_gather(rel_table,"heads",axis=0,tiled=True)
    NH=table.shape[0]
    every=gathered(jnp.concatenate([wq,wf],axis=1),names,nseq,nheads)
    ends=[i*cq for i in range(5)]+[4*cq+cf,4*cq+2*cf]
    W=jnp.concatenate([natural(every[...,a:b]) for a,b in zip(ends[:-1],ends[1:])],axis=1)[None]
    bias=call_p(posP,pack_table(table),WIN)
    def mine(v):
        ext=jnp.concatenate([v,from_next(v[:shift])])
        return lax.dynamic_slice_in_dim(ext,start+shift,nW*WIN,0).reshape(nW,WIN,-1)
    x=mine(inputs); og=mine(out_grad)
    delta,gln2,qkv,g,gT,Dd,Pp,dcat,sm_a=call_a(x,og,labc,labr,bias,W,gains,shifts)
    dd,dqkv,G,sm_b=call_b(x,gln2,qkv,g,gT,Dd,Pp,W,gains,shifts)
    grads=[dqkv[0,:,c*D:(c+1)*D] for c in range(3)]+[dcat[0,:,:D],dcat[0,:,D:D+cf*nheads],dcat[0,:,D+cf*nheads:]]
    red=lax.psum_scatter(jnp.concatenate([owners(v,nseq,nheads) for v in grads],axis=2),names,scatter_dimension=0,tiled=False).astype(F32)
    redq,redm=red[:,:3*cq],red[:,3*cq:]
    d_table,small=lax.psum((call_t(G,posT,T,NH),sm_a+sm_b),names)
    nl=rel_table.shape[0]
    d_table=lax.dynamic_slice_in_dim(d_table,me*nl,nl,0)
    output=place(delta,inputs,shift)
    d_inputs=place(dd,out_grad,shift)
    d_qkv=redq.reshape(rows,3,cq).transpose(1,0,2)
    d_proj=redm[:,:cq].T; d_fc1=redm[:,cq:cq+cf]; d_fc2=redm[:,cq+cf:].T
    return (output,d_inputs,d_qkv,d_proj,d_fc1,d_fc2,small[0:2],small[2:6],d_table)

def solution(mesh):
    placed=(P("seq",None),P(None,"seq","heads"),P("heads","seq"),P("seq","heads"),P("heads","seq"),P(),P(),P("heads",None),P("seq"),P(),P("seq",None))
    return jax.shard_map(body,mesh=mesh,in_specs=placed,
    out_specs=(P("seq",None),P("seq",None),P(None,"seq","heads"),P("heads","seq"),P("seq","heads"),P("heads","seq"),P(),P(),P("heads",None)),
    check_vma=False)
```

```python
import functools
import math

import jax, jax.numpy as jnp
from jax import lax
from jax.experimental import pallas as pl
from jax.experimental.pallas import tpu as pltpu
from jax.sharding import PartitionSpec as P

BF=jnp.bfloat16; F32=jnp.float32
HD=32; GROUP=128; PER=4
EPS=1e-5
SQ=math.sqrt(32.0)
CEXP=math.log2(math.e)/SQ
MASK=100.0*SQ

def mm(a,b):
    return lax.dot_general(a,b,(((1,),(0,)),((),())),preferred_element_type=F32)
def mm_nt(a,b):
    return lax.dot_general(a,b,(((1,),(1,)),((),())),preferred_element_type=F32)

def norm_stats(v):
    mean=jnp.mean(v,axis=-1,keepdims=True)
    c=v-mean
    var=jnp.mean(c*c,axis=-1,keepdims=True)
    rstd=lax.rsqrt(var+EPS)
    return c*rstd, rstd

def norm_back(gy,xhat,rstd,gain):
    gx=gy*gain
    m1=jnp.mean(gx,axis=-1,keepdims=True)
    m2=jnp.mean(gx*xhat,axis=-1,keepdims=True)
    return rstd*(gx-m1-xhat*m2)

P0=0.3275911
A1,A2,A3,A4,A5=0.254829592,-0.284496736,1.421413741,-1.453152027,1.061405429
def gelu_both(x):
    e=jnp.exp2(x*x*(-0.5*math.log2(math.e)))
    t=1.0/(1.0+(P0/math.sqrt(2.0))*jnp.abs(x))
    poly=t*(0.5*A1+t*(0.5*A2+t*(0.5*A3+t*(0.5*A4+t*(0.5*A5)))))
    half=poly*e
    phi=jnp.where(x>=0,1.0-half,half)
    return x*phi, phi+x*e*(1.0/math.sqrt(2.0*math.pi))

def kernel_a(nheads,x_ref,og_ref,labc_ref,labr_ref,bias_ref,W_ref,gains_ref,shifts_ref,
             delta_ref,gln2_ref,qkv_ref,g_ref,gT_ref,D_ref,P_hbm,dcat_ref,small_ref,
             qT_s,vT_s,OT_s,P_s,acc,sem,xn2_s,xn2T_s,tg_s,tgT_s,up_s,gn2_s):
    w=pl.program_id(0); nw=pl.num_programs(0)
    D=x_ref.shape[-1]; WIN=x_ref.shape[-2]
    parts=W_ref.shape[0]; cq=D//parts; cf=(W_ref.shape[2]-4*cq)//2
    groups=nheads//PER
    x=x_ref[0]
    xhat,_=norm_stats(x)
    xn=(xhat*gains_ref[0:1,:]+shifts_ref[0:1,:]).astype(BF)
    for c in range(3):
        for m in range(parts):
            at=slice(m*cq,(m+1)*cq)
            y=mm(xn,W_ref[m,:,c*cq:(c+1)*cq]).astype(BF)
            qkv_ref[0,c,:,at]=y
            if c==0: qT_s[at,:]=y.T
            if c==2: vT_s[at,:]=y.T
    labc=labc_ref[0]; labr=labr_ref[0]
    lane=lax.broadcasted_iota(jnp.int32,(WIN,GROUP),1)
    oh=jnp.where((labc==lane)|((labc+3)==lane),1.0,0.0).astype(BF)
    hi=564.0
    lo=MASK-hi
    sub=lax.broadcasted_iota(jnp.int32,(GROUP,WIN),0)
    nm=jnp.where(sub<3,jnp.where(sub!=labr,-hi,0.0),jnp.where(sub<6,jnp.where(sub-3!=labr,-lo,0.0),0.0)).astype(BF)
    hl=lane//HD

    def group(gi,_):
        slot=gi%2
        step=w*groups+gi
        @pl.when(step>=2)
        def _():
            pltpu.make_async_copy(P_s.at[slot],P_hbm.at[0,pl.ds(0,PER)],sem.at[slot]).wait()
        o=pl.multiple_of(gi*GROUP,GROUP)
        qTg=jnp.concatenate([qT_s[pl.ds(o,GROUP),:],nm],axis=0)
        kg=qkv_ref[0,1,:,pl.ds(o,GROUP)]
        for hh in range(PER):
            kh=jnp.concatenate([jnp.where(hl==hh,kg,jnp.zeros_like(kg)),oh],axis=1)
            t=mm(kh,qTg)+bias_ref[gi*PER+hh]
            m=jnp.max(t,axis=0,keepdims=True)
            e=jnp.exp2((t-m)*CEXP)
            l=jnp.sum(e,axis=0,keepdims=True)
            p=(e*(1.0/l)).astype(BF)
            P_s[slot,hh]=p
            OT_s[pl.ds(o+hh*HD,HD),:]=mm(vT_s[pl.ds(o+hh*HD,HD),:],p)
        pltpu.make_async_copy(P_s.at[slot],P_hbm.at[w,pl.ds(gi*PER,PER)],sem.at[slot]).start()
        return 0
    lax.fori_loop(0,groups,group,0)

    attn=OT_s[...].astype(BF).T
    branch=shifts_ref[2:3,:]
    for m in range(parts):
        branch=branch+mm_nt(attn[:,m*cq:(m+1)*cq],W_ref[m,:,3*cq:4*cq])
    branch=branch.astype(BF).astype(F32)
    middle=x+branch
    xhat2,rstd2=norm_stats(middle)
    xn2=(xhat2*gains_ref[1:2,:]+shifts_ref[1:2,:]).astype(BF)
    og=og_ref[0]
    tg=og.astype(BF)
    xn2_s[...]=xn2; xn2T_s[...]=xn2.T; tg_s[...]=tg; tgT_s[...]=tg.T
    up_s[...]=jnp.zeros_like(up_s); gn2_s[...]=jnp.zeros_like(gn2_s)
    CH=min(512,cf); each=cf//CH
    @pl.when(w==0)
    def _():
        acc[...]=jnp.zeros_like(acc)
        small_ref[...]=jnp.zeros_like(small_ref)
    def chunk(c,_):
        m=c//each
        o=pl.multiple_of((c%each)*CH,CH)
        f1=W_ref[m,:,pl.ds(4*cq+o,CH)]; f2=W_ref[m,:,pl.ds(4*cq+cf+o,CH)]
        hid=mm(xn2_s[...],f1)
        act,dact=gelu_both(hid)
        a=act.astype(BF)
        up_s[...]+=mm_nt(a,f2)
        gh=(mm(tg_s[...],f2)*dact).astype(BF)
        gn2_s[...]+=mm_nt(gh,f1)
        acc[m,:,pl.ds(cq+o,CH)]+=mm(xn2T_s[...],gh)
        acc[m,:,pl.ds(cq+cf+o,CH)]+=mm(tgT_s[...],a)
        return 0
    lax.fori_loop(0,parts*each,chunk,0)
    delta_ref[0]=(branch+up_s[...]+shifts_ref[3:4,:]).astype(BF)
    gn2=gn2_s[...]
    gln2=norm_back(gn2,xhat2,rstd2,gains_ref[1:2,:])
    gln2_ref[0]=gln2
    gb=(og+gln2).astype(BF)
    gbT=gb.T
    for m in range(parts):
        at=slice(m*cq,(m+1)*cq)
        acc[m,:,0:cq]+=mm(gbT,attn[:,at])
        g=mm(gb,W_ref[m,:,3*cq:4*cq]).astype(BF)
        g_ref[0,:,at]=g
        gT=g.T
        gT_ref[0,at,:]=gT
        prod=gT.astype(F32)*OT_s[at,:]
        nh=nheads//parts
        D_ref[0,m*nh:(m+1)*nh,:]=jnp.sum(prod.reshape(nh,HD,WIN),axis=1)
    small_ref[1:2,:]+=jnp.sum(gn2*xhat2,axis=0,keepdims=True)
    small_ref[3:4,:]+=jnp.sum(gn2,axis=0,keepdims=True)
    small_ref[4:5,:]+=jnp.sum(gb.astype(F32),axis=0,keepdims=True)
    small_ref[5:6,:]+=jnp.sum(tg.astype(F32),axis=0,keepdims=True)
    @pl.when(w==nw-1)
    def _():
        dcat_ref[...]=acc[...].astype(BF)
        for s in range(2):
            pltpu.make_async_copy(P_s.at[s],P_hbm.at[0,pl.ds(0,PER)],sem.at[s]).wait()

def full(shape,**kw):
    return pl.BlockSpec(shape,lambda w:(0,)*len(shape),**kw)
def per(shape,**kw):
    return pl.BlockSpec((1,)+shape,lambda w:(w,)+(0,)*len(shape),**kw)
ONE=pl.Buffered(1)
ANY=pl.BlockSpec(memory_space=pl.ANY)

def call_a(x,og,labc,labr,bias,W,gains,shifts):
    nW,WIN,D=x.shape; NH=bias.shape[0]
    parts,_,Ct=W.shape; Cg=Ct-3*(D//parts)
    sd=jax.ShapeDtypeStruct
    outs=[sd((nW,WIN,D),BF),sd((nW,WIN,D),F32),sd((nW,3,WIN,D),BF),sd((nW,WIN,D),BF),sd((nW,D,WIN),BF),sd((nW,NH,WIN),F32),
          sd((nW,NH,WIN,WIN),BF),sd((parts,D,Cg),BF),sd((8,D),F32)]
    return pl.pallas_call(functools.partial(kernel_a,NH),grid=(nW,),
      in_specs=[per((WIN,D)),per((WIN,D)),per((WIN,1)),per((1,WIN)),full((NH,WIN,WIN),pipeline_mode=ONE),
        full((parts,D,Ct),pipeline_mode=ONE),full(gains.shape),full(shifts.shape)],
      out_specs=[per((WIN,D)),per((WIN,D)),per((3,WIN,D)),per((WIN,D)),per((D,WIN)),per((NH,WIN)),ANY,full((parts,D,Cg)),full((8,D))],
      out_shape=outs,
      scratch_shapes=[pltpu.VMEM((D,WIN),BF),pltpu.VMEM((D,WIN),BF),pltpu.VMEM((D,WIN),F32),pltpu.VMEM((2,PER,WIN,WIN),BF),
        pltpu.VMEM((parts,D,Cg),F32),pltpu.SemaphoreType.DMA((2,)),
        pltpu.VMEM((WIN,D),BF),pltpu.VMEM((D,WIN),BF),pltpu.VMEM((WIN,D),BF),pltpu.VMEM((D,WIN),BF),pltpu.VMEM((WIN,D),F32),pltpu.VMEM((WIN,D),F32)],
      compiler_params=pltpu.CompilerParams(vmem_limit_bytes=62*1024*1024,dimension_semantics=("arbitrary",)),
      name="kernel_a")(x,og,labc,labr,bias,W,gains,shifts)

def kernel_b(nheads,x_ref,gln2_ref,qkv_ref,g_ref,gT_ref,D_ref,P_ref,W_ref,gains_ref,shifts_ref,
             dd_ref,dqkv_ref,G_hbm,small_ref,G_s,aq,kT_s,gq_s,gqT_s,sem):
    w=pl.program_id(0); nw=pl.num_programs(0)
    D=x_ref.shape[-1]; WIN=x_ref.shape[-2]
    parts=W_ref.shape[0]; cq=D//parts
    groups=nheads//PER
    @pl.when(w==0)
    def _():
        aq[...]=jnp.zeros_like(aq); G_s[...]=jnp.zeros_like(G_s); small_ref[...]=jnp.zeros_like(small_ref)
    kT_s[...]=qkv_ref[0,1].T
    lane=lax.broadcasted_iota(jnp.int32,(WIN,GROUP),1)
    hl=lane//HD
    def group(gi,_):
        o=pl.multiple_of(gi*GROUP,GROUP)
        gTg=gT_ref[0,pl.ds(o,GROUP),:]
        vg=qkv_ref[0,2,:,pl.ds(o,GROUP)]
        qg=qkv_ref[0,0,:,pl.ds(o,GROUP)]
        gg=g_ref[0,:,pl.ds(o,GROUP)]
        dv=jnp.zeros((WIN,GROUP),F32); dk=jnp.zeros((WIN,GROUP),F32)
        zero=jnp.zeros_like(vg)
        for hh in range(PER):
            h=gi*PER+hh
            p=P_ref[0,h]
            dp=mm(jnp.where(hl==hh,vg,zero),gTg)
            ds_=p.astype(F32)*(dp-D_ref[0,pl.ds(h,1),:])
            for c in range(G_s.shape[0]):
                wd=min(128,WIN-c*128)
                G_s[c,pl.ds(pl.multiple_of(h*WIN,8),WIN),:wd]+=ds_[:,c*128:c*128+wd]
            dsl=ds_.astype(BF)
            dv+=mm(p,jnp.where(hl==hh,gg,zero))
            dk+=mm(dsl,jnp.where(hl==hh,qg,zero))
            gqT_s[pl.ds(o+hh*HD,HD),:]=mm(kT_s[pl.ds(o+hh*HD,HD),:],dsl)
        gq_s[1,:,pl.ds(o,GROUP)]=(dk*(1.0/SQ)).astype(BF)
        gq_s[2,:,pl.ds(o,GROUP)]=dv.astype(BF)
        return 0
    lax.fori_loop(0,groups,group,0)
    gq_s[0]=(gqT_s[...]*(1.0/SQ)).astype(BF).T
    x=x_ref[0]
    xhat,rstd=norm_stats(x)
    xn=(xhat*gains_ref[0:1,:]+shifts_ref[0:1,:]).astype(BF)
    xnT=xn.T
    gr=jnp.zeros((WIN,D),F32)
    for m in range(parts):
        for c in range(3):
            gc=gq_s[c,:,m*cq:(m+1)*cq]
            gr=gr+mm_nt(gc,W_ref[m,:,c*cq:(c+1)*cq])
            aq[m,:,c*cq:(c+1)*cq]+=mm(xnT,gc)
    dd_ref[0]=(gln2_ref[0]+norm_back(gr,xhat,rstd,gains_ref[0:1,:])).astype(BF)
    small_ref[0:1,:]+=jnp.sum(gr*xhat,axis=0,keepdims=True)
    small_ref[2:3,:]+=jnp.sum(gr,axis=0,keepdims=True)
    @pl.when(w==nw-1)
    def _():
        dqkv_ref[...]=aq[...].astype(BF)
        cp=pltpu.make_async_copy(G_s,G_hbm,sem); cp.start(); cp.wait()

def call_b(x,gln2,qkv,g,gT,Dd,Pp,W,gains,shifts):
    nW,WIN,D=x.shape; NH=Dd.shape[1]
    parts=W.shape[0]; cq=D//parts; tiles=-(-WIN//128)
    sd=jax.ShapeDtypeStruct
    return pl.pallas_call(functools.partial(kernel_b,NH),grid=(nW,),
      in_specs=[per((WIN,D)),per((WIN,D)),per((3,WIN,D)),per((WIN,D)),per((D,WIN)),per((NH,WIN)),per((NH,WIN,WIN)),
        full((parts,D,3*cq),pipeline_mode=ONE),full(gains.shape),full(shifts.shape)],
      out_specs=[per((WIN,D)),full((parts,D,3*cq)),ANY,full((8,D))],
      out_shape=[sd((nW,WIN,D),BF),sd((parts,D,3*cq),BF),sd((tiles,NH*WIN,128),F32),sd((8,D),F32)],
      scratch_shapes=[pltpu.VMEM((tiles,NH*WIN,128),F32),pltpu.VMEM((parts,D,3*cq),F32),pltpu.VMEM((D,WIN),BF),pltpu.VMEM((3,WIN,D),BF),pltpu.VMEM((D,WIN),F32),
        pltpu.SemaphoreType.DMA],
      compiler_params=pltpu.CompilerParams(vmem_limit_bytes=62*1024*1024,dimension_semantics=("arbitrary",)),
      name="kernel_b")(x,gln2,qkv,g,gT,Dd,Pp,W,gains,shifts)

FIX=8191.0

def pack_table(table):
    NH,T=table.shape
    n=-(-T//128)
    q=jnp.round(jnp.clip(table,-4.0,4.0)*FIX).astype(jnp.int32)
    q=jnp.pad(q,((0,0),(0,n*128-T)))
    q=q.reshape(NH//2,2,n,128)
    return (q[:,0]*65536)|(q[:,1]&65535)

def kernel_p(pos_ref,tab_ref,bias_ref):
    npair,n,_=tab_ref.shape
    WIN=bias_ref.shape[-1]
    tiles=-(-WIN//128)
    def row(r,_):
        r8=pl.multiple_of(r*8,8)
        for c in range(tiles):
            width=min(128,WIN-c*128)
            idx=pos_ref[pl.ds(r8,8),c*128:(c+1)*128]
            lo=idx&127; hi=idx>>7
            masks=[hi==k for k in range(n)]
            for p in range(npair):
                acc=jnp.zeros((8,128),jnp.int32)
                for k in range(n):
                    src=jnp.broadcast_to(tab_ref[p,k:k+1,:],(8,128))
                    acc=jnp.where(masks[k],jnp.take_along_axis(src,lo,axis=1),acc)
                a=(acc>>16).astype(F32)*(SQ/FIX)
                b=((acc<<16)>>16).astype(F32)*(SQ/FIX)
                bias_ref[2*p,pl.ds(r8,8),c*128:c*128+width]=a[:,:width]
                bias_ref[2*p+1,pl.ds(r8,8),c*128:c*128+width]=b[:,:width]
        return 0
    lax.fori_loop(0,bias_ref.shape[1]//8,row,0)

def call_p(posT_pad,tab,WIN):
    NH=tab.shape[0]*2
    return pl.pallas_call(kernel_p,out_shape=jax.ShapeDtypeStruct((NH,WIN,WIN),F32),
      compiler_params=pltpu.CompilerParams(vmem_limit_bytes=40*1024*1024),name="kernel_p")(posT_pad,tab)

def kernel_t(NH,G_ref,hi_ref,lo_ref,out_ref):
    WIN=hi_ref.shape[0]; LW=G_ref.shape[0]*128
    nh=out_ref.shape[0]//NH
    out_ref[...]=jnp.zeros_like(out_ref)
    def rows(r,_):
        r8=pl.multiple_of(r*8,8)
        hi8=hi_ref[pl.ds(r8,8),:]; lo8=lo_ref[pl.ds(r8,8),:]
        tot=jnp.zeros(out_ref.shape,F32)
        iota=lax.broadcasted_iota(jnp.int32,(256,LW),0).astype(F32).astype(BF)
        for k in range(8):
            g=jnp.concatenate([G_ref[c,pl.ds(r8+k,NH,stride=WIN),:] for c in range(LW//128)],axis=1)
            hr=hi8[k:k+1,:]; lr=lo8[k:k+1,:].astype(F32).astype(BF)
            A=jnp.concatenate([jnp.where(hr==m,g,0.0) for m in range(nh)],axis=0).astype(BF)
            oh=jnp.where(iota==lr,jnp.ones((),BF),jnp.zeros((),BF))
            tot=tot+lax.dot_general(A,oh,(((1,),(1,)),((),())),preferred_element_type=F32)
        out_ref[...]+=tot
        return 0
    lax.fori_loop(0,WIN//8,rows,0)

def call_t(G,posT,T,NH):
    WIN=posT.shape[0]; nt=G.shape[0]
    nh=-(-T//256)
    pp=jnp.pad(posT,((0,0),(0,nt*128-WIN)),constant_values=nh*256)
    hi=pp>>8; lo=pp&255
    o=pl.pallas_call(functools.partial(kernel_t,NH),out_shape=jax.ShapeDtypeStruct((nh*NH,256),F32),
      compiler_params=pltpu.CompilerParams(vmem_limit_bytes=40*1024*1024),name="kernel_t")(G,hi,lo)
    return o.reshape(nh,NH,256).transpose(1,0,2).reshape(NH,nh*256)[:,:T]


MESHID=pl.DeviceIdType.MESH

def place_of():
    s=lax.axis_index("seq"); y=lax.axis_index("heads")
    return s//4,(s//2)%2,s%2,y

def dev(z,x,c,y):
    return ((z*2+x)*2+c,y)

def peers_of(z,x,c,y):
    return [dev(z,x,1-c,y),dev(z,1-x,c,y),dev(z,x,c,1-y)]+[dev((z+i)%4,x,c,y) for i in (1,2,3)]

def hail(devices):
    bar=pltpu.get_barrier_semaphore()
    for d in devices:
        pl.semaphore_signal(bar,inc=1,device_id=d,device_id_type=MESHID)

def heard(devices):
    pl.semaphore_wait(pltpu.get_barrier_semaphore(),len(devices))

def greet(devices):
    hail(devices)
    heard(devices)

def send(src,dst,ss,rs,to):
    return pltpu.make_async_remote_copy(src_ref=src,dst_ref=dst,send_sem=ss,recv_sem=rs,device_id=to,device_id_type=MESHID)


class Gather:
    def __init__(self,src,dst,ss,rs,own):
        self.src,self.dst,self.ss,self.rs,self.own=src,dst,ss,rs,own
        z,x,c,y=self.at=place_of()
        self.xa=x+(1-2*x)*(1-c); self.ya=y+(1-2*y)*c
        self.xb=x+(1-2*x)*c; self.yb=y+(1-2*y)*(1-c)
        self.sib=dev(z,x,1-c,y); self.pa=dev(z,self.xa,c,self.ya); self.pb=dev(z,self.xb,c,self.yb)
    def slot(self,zz,xx,cc,yy):
        n=self.src.shape[0]
        return self.dst.at[yy,pl.ds(pl.multiple_of(((zz*2+xx)*2+cc)*n,n),n)]
    def copy(self,src,where,k,to):
        return send(src,self.slot(*where),self.ss.at[k],self.rs.at[k],to)
    def go(self,where,k,to,src=None):
        self.copy(self.slot(*where) if src is None else src,where,k,to).start()
    def came(self,where,k):
        self.copy(self.src,where,k,self.sib).wait_recv()
    def keep(self):
        z,x,c,y=self.at
        return pltpu.make_async_copy(self.src,self.slot(z,x,c,y),self.own)
    def start(self):
        z,x,c,y=self.at
        me=(z,x,c,y)
        self.keep().start()
        for i in (1,2,3):
            self.go(me,i-1,dev((z+i)%4,x,c,y),self.src)
        self.go(me,3,self.pa,self.src); self.go(me,7,self.pb,self.src); self.go(me,15,self.sib,self.src)
    def z(self,i):
        return (self.at[0]+4-i)%4
    def turn_z(self,i):
        z,x,c,y=self.at
        at=(self.z(i),x,c,y); self.came(at,i-1)
        self.go(at,3+i,self.pa); self.go(at,7+i,self.pb); self.go(at,15+i,self.sib)
    def turn_a(self,i):
        at=(self.z(i),self.xa,self.at[2],self.ya); self.came(at,3+i)
        self.go(at,11+i,self.pb); self.go(at,19+i,self.sib)
    def turn_b(self,i):
        at=(self.z(i),self.xb,self.at[2],self.yb); self.came(at,7+i)
        self.go(at,23+i,self.sib)
    def turn_ab(self,i):
        z,x,c,y=self.at
        at=(self.z(i),1-x,c,1-y); self.came(at,11+i)
        self.go(at,27+i,self.sib)
    def last(self):
        z,x,c,y=self.at
        for i in range(4):
            zz=self.z(i)
            self.came((zz,x,1-c,y),15+i); self.came((zz,self.xb,1-c,self.yb),19+i)
            self.came((zz,self.xa,1-c,self.ya),23+i); self.came((zz,1-x,1-c,1-y),27+i)
    def drain(self):
        z,x,c,y=self.at
        for k in range(31):
            self.copy(self.src,(z,x,c,y),k,self.sib).wait_send()
        self.keep().wait()

def gather_sems():
    return [pltpu.SemaphoreType.DMA((31,)),pltpu.SemaphoreType.DMA((31,)),pltpu.SemaphoreType.DMA]

STEPS=7
def kernel_w(qkv_ref,proj_ref,fc1_ref,fc2_ref,pos_ref,tab_ref,W_hbm,bias_hbm,wf_ref,posT_ref,
             bias_s,wq_s,tb,tq,ss,rs,own,bs,br,bl,tsem):
    z,x,c,y=place_of()
    cq=qkv_ref.shape[2]; cf=fc1_ref.shape[1]
    for k in range(3): wq_s[:,k*cq:(k+1)*cq]=qkv_ref[k].astype(BF)
    wq_s[:,3*cq:4*cq]=proj_ref[...].astype(BF)
    half,T=tab_ref.shape
    tb[2]=jnp.zeros(tb.shape[1:],F32)
    tb[2,:,0:T]=tab_ref[...]
    greet(peers_of(z,x,c,y))
    gather=Gather(wq_s,W_hbm,ss,rs,own)
    swap=send(tb.at[2],tb.at[y],tsem.at[0],tsem.at[1],dev(z,x,c,1-y))
    swap.start()
    gather.start()
    tb[y]=tb[2]
    wf_ref[:,0:cf]=fc1_ref[...].astype(BF)
    wf_ref[:,cf:2*cf]=fc2_ref[...].astype(BF)
    WIN=bias_s.shape[-1]; tiles=-(-WIN//128); n=tb.shape[2]//128
    posT_ref[...]=jnp.full(posT_ref.shape,1<<15,jnp.int32)
    posT_ref[:,0:WIN]=pos_ref[...].astype(F32).T.astype(jnp.int32)
    swap.wait()
    npair=half//2
    for p in range(npair):
        a,b=[jnp.floor(jnp.clip(tb[c,2*p+k:2*p+k+1,:],-4.0,4.0)*FIX+0.5).astype(jnp.int32) for k in range(2)]
        tq[p:p+1,:]=(a*65536)|(b&65535)
    nrow=WIN//8
    cuts=[nrow*k//STEPS for k in range(STEPS+1)]
    sib=dev(z,x,1-c,y)
    def rows_of(k): return pl.ds(cuts[k]*8,(cuts[k+1]-cuts[k])*8)
    def kept(k): return pltpu.make_async_copy(bias_s.at[:,rows_of(k)],bias_hbm.at[pl.ds(c*half,half),rows_of(k)],bl.at[k])
    def sent(k,cc): return send(bias_s.at[:,rows_of(k)],bias_hbm.at[pl.ds(cc*half,half),rows_of(k)],bs.at[k],br.at[k],sib)
    def rows(k):
        def row(r,_):
            r8=pl.multiple_of(r*8,8)
            for t in range(tiles):
                width=min(128,WIN-t*128)
                idx=posT_ref[pl.ds(r8,8),t*128:(t+1)*128]
                lo=idx&127; hi=idx>>7
                masks=[hi==q for q in range(n)]
                for p in range(npair):
                    acc=jnp.zeros((8,128),jnp.int32)
                    for q in range(n):
                        src=jnp.broadcast_to(tq[p:p+1,q*128:(q+1)*128],(8,128))
                        acc=jnp.where(masks[q],jnp.take_along_axis(src,lo,axis=1),acc)
                    a=(acc>>16).astype(F32)*(SQ/FIX)
                    b=((acc<<16)>>16).astype(F32)*(SQ/FIX)
                    bias_s[2*p,pl.ds(r8,8),t*128:t*128+width]=a[:,:width]
                    bias_s[2*p+1,pl.ds(r8,8),t*128:t*128+width]=b[:,:width]
            return 0
        lax.fori_loop(cuts[k],cuts[k+1],row,0)
        kept(k).start(); sent(k,c).start()
    rows(0)
    for i in (1,3,2): gather.turn_z(i)
    rows(1)
    for i in (0,): gather.turn_a(i); gather.turn_b(i)
    rows(2)
    for i in (1,3): gather.turn_a(i); gather.turn_b(i)
    rows(3)
    for i in (2,): gather.turn_a(i); gather.turn_b(i)
    gather.turn_ab(0)
    rows(4)
    for i in (1,3): gather.turn_ab(i)
    rows(5)
    gather.turn_ab(2)
    rows(6)
    gather.last()
    for k in range(STEPS):
        kept(k).wait(); sent(k,c).wait_send(); sent(k,1-c).wait_recv()
    gather.drain()

def call_w(w_qkv,w_proj,w_fc1,w_fc2,pos_index,rel_table):
    rows,cq=w_qkv.shape[1:]; cf=w_fc1.shape[1]; WIN=pos_index.shape[0]; half,T=rel_table.shape; dma=pltpu.SemaphoreType.DMA
    wide=-(-WIN//128)*128; n=-(-T//128); mem=pltpu.VMEM
    sd=jax.ShapeDtypeStruct
    return pl.pallas_call(kernel_w,grid=(1,),
      out_shape=[sd((2,16*rows,4*cq),BF),sd((2*half,WIN,WIN),F32),sd((rows,2*cf),BF),sd((WIN,wide),jnp.int32)],
      in_specs=[full(v.shape) for v in (w_qkv,w_proj,w_fc1,w_fc2,pos_index,rel_table)],out_specs=[ANY,ANY,full((rows,2*cf)),full((WIN,wide))],
      scratch_shapes=[mem((half,WIN,WIN),F32),mem((rows,4*cq),BF),mem((3,half,n*128),F32),mem((half//2,n*128),jnp.int32)]
        +gather_sems()+[dma((STEPS,)),dma((STEPS,)),dma((STEPS,)),dma((2,))],
      compiler_params=pltpu.CompilerParams(vmem_limit_bytes=63*1024*1024,collective_id=1,has_side_effects=True),name="kernel_w")(w_qkv,w_proj,w_fc1,w_fc2,pos_index,rel_table)

def neighbours(z,x,c,y):
    s=(z*2+x)*2+c
    return [((s+k)%16,yy) for k in (1,15) for yy in (y,1-y)]

def kernel_a2(nheads,in_hbm,og_hbm,wf_hbm,lab_ref,bias_ref,W1,gains_ref,shifts_ref,
              qkv_ref,x_ref,P_hbm,gln2_ref,g_ref,gT_ref,D_ref,ev_hbm,dlast_hbm,dcat_hbm,small_ref,
              x_s,og_s,W2,OT_s,qT_s,vT_s,P_s,acc,pst,xn2_s,xn2T_s,tg_s,tgT_s,up_s,gn2_s,dl_s,
              lab_s,psem,xsem,hsem,ss,rs,own,dl,ds,dr,fin):
    i=pl.program_id(0); nw=x_s.shape[0]
    w=i%nw
    z,xc,c,y=place_of()
    s=(z*2+xc)*2+c
    D=x_s.shape[-1]; WIN=qkv_ref.shape[-2]; SLAB=x_s.shape[1]; HALF=SLAB//2
    OFF=(SLAB-WIN)//2
    cq=D//2; cf=W2.shape[2]//2
    groups=nheads//PER
    gather=Gather(wf_hbm,W2,ss,rs,own)
    mate=dev(z,xc,c,1-y)
    def local(k,half,t):
        hbm,buf=((in_hbm,x_s),(og_hbm,og_s))[t]
        r=pl.multiple_of(y*(nw*WIN)+k*WIN+(WIN//2-OFF)+half*HALF,8)
        return pltpu.make_async_copy(hbm.at[pl.ds(r,HALF)],buf.at[k,pl.ds(half*HALF,HALF)],xsem.at[t,2*k+half])
    def edge(t):
        hbm,buf=((in_hbm,x_s),(og_hbm,og_s))[t]
        return send(hbm.at[pl.ds(0,HALF)],buf.at[nw-1,pl.ds(HALF,HALF)],hsem.at[t,0],hsem.at[t,1],((s+15)%16,1))
    def ready(t):
        local(w,0,t).wait()
        far=jnp.logical_and(w==nw-1,y==1)
        @pl.when(far)
        def _(): edge(t).wait_recv()
        @pl.when(jnp.logical_not(far))
        def _(): local(w,1,t).wait()
    def slab(k,to=None):
        if k is None: return pltpu.make_async_copy(dl_s.at[nw-1],dlast_hbm,dl.at[nw-1])
        at=ev_hbm.at[y*nw+k]
        if to is None: return pltpu.make_async_copy(dl_s.at[k],at,dl.at[k])
        return send(dl_s.at[k],at,ds.at[k],dr.at[k],to)
    @pl.when(i==0)
    def _():
        greet(peers_of(z,xc,c,y)+neighbours(z,xc,c,y))
        for k in range(nw):
            for t in range(2):
                local(k,0,t).start()
                if k<nw-1: local(k,1,t).start()
        for t in range(2):
            @pl.when(y==1)
            def _(): edge(t).start()
            @pl.when(y==0)
            def _(): local(nw-1,1,t).start()
        gather.start()
        lab_s[...]=lab_ref[...].astype(F32).T
        acc[...]=jnp.zeros_like(acc)
        small_ref[...]=jnp.zeros_like(small_ref)
        dl_s[:,SLAB-16:,:]=jnp.zeros((nw,16,D),BF)

    @pl.when(i<nw)
    def _():
        ready(0)
        x=x_s[w,OFF:OFF+WIN,:]
        x_ref[0]=x
        xhat,_=norm_stats(x)
        xn=(xhat*gains_ref[0:1,:]+shifts_ref[0:1,:]).astype(BF)
        for k in range(3):
            for m in range(2):
                at=slice(m*cq,(m+1)*cq)
                v=mm(xn,W1[m,:,k*cq:(k+1)*cq]).astype(BF)
                qkv_ref[0,k,:,at]=v
                if k==0: qT_s[at,:]=v.T
                if k==2: vT_s[at,:]=v.T
        mine=y*nw+w
        labr=lab_ref[pl.ds(mine,1),:]
        labc=jnp.sum(jnp.where(lax.broadcasted_iota(jnp.int32,lab_s.shape,1)==mine,lab_s[...],0.0),axis=1,keepdims=True).astype(jnp.int32)
        lane=lax.broadcasted_iota(jnp.int32,(WIN,GROUP),1)
        oh=jnp.where((labc==lane)|((labc+3)==lane),1.0,0.0).astype(BF)
        hi=564.0
        lo=MASK-hi
        sub=lax.broadcasted_iota(jnp.int32,(GROUP,WIN),0)
        nm=jnp.where(sub<3,jnp.where(sub!=labr,-hi,0.0),jnp.where(sub<6,jnp.where(sub-3!=labr,-lo,0.0),0.0)).astype(BF)
        hl=lane//HD
        def group(gi,_):
            slot=gi%2
            @pl.when(w*groups+gi>=2)
            def _():
                pltpu.make_async_copy(P_s.at[slot],P_hbm.at[0,pl.ds(0,PER)],psem.at[slot]).wait()
            o=pl.multiple_of(gi*GROUP,GROUP)
            qTg=jnp.concatenate([qT_s[pl.ds(o,GROUP),:],nm],axis=0)
            kg=qkv_ref[0,1,:,pl.ds(o,GROUP)]
            for hh in range(PER):
                kh=jnp.concatenate([jnp.where(hl==hh,kg,jnp.zeros_like(kg)),oh],axis=1)
                t=mm(kh,qTg)+bias_ref[gi*PER+hh]
                m=jnp.max(t,axis=0,keepdims=True)
                e=jnp.exp2((t-m)*CEXP)
                l=jnp.sum(e,axis=0,keepdims=True)
                p=(e*(1.0/l)).astype(BF)
                P_s[slot,hh]=p
                OT_s[w,pl.ds(o+hh*HD,HD),:]=mm(vT_s[pl.ds(o+hh*HD,HD),:],p)
            pltpu.make_async_copy(P_s.at[slot],P_hbm.at[w,pl.ds(gi*PER,PER)],psem.at[slot]).start()
            return 0
        lax.fori_loop(0,groups,group,0)

    @pl.when(i==0)
    def _():
        for k in (1,3,2): gather.turn_z(k)
    @pl.when(i==1)
    def _():
        for k in (0,1,3,2): gather.turn_a(k); gather.turn_b(k)
    @pl.when(i==2)
    def _():
        for k in (0,1,3,2): gather.turn_ab(k)
    @pl.when(i==nw-1)
    def _():
        gather.last(); gather.drain()

    @pl.when(i>=nw)
    def _():
        ready(1)
        x=x_s[w,OFF:OFF+WIN,:]
        og=og_s[w,OFF:OFF+WIN,:]
        attn=OT_s[w].astype(BF).T
        branch=shifts_ref[2:3,:]
        for m in range(2):
            branch=branch+mm_nt(attn[:,m*cq:(m+1)*cq],W1[m,:,3*cq:4*cq])
        branch=branch.astype(BF).astype(F32)
        middle=x+branch
        xhat2,rstd2=norm_stats(middle)
        xn2=(xhat2*gains_ref[1:2,:]+shifts_ref[1:2,:]).astype(BF)
        tg=og.astype(BF)
        xn2_s[...]=xn2; xn2T_s[...]=xn2.T; tg_s[...]=tg; tgT_s[...]=tg.T
        up_s[...]=jnp.zeros_like(up_s); gn2_s[...]=jnp.zeros_like(gn2_s)
        CH=512; each=cf//CH
        def chunk(k,_):
            m=k//each
            o=pl.multiple_of((k%each)*CH,CH)
            f1=W2[m,:,pl.ds(o,CH)]; f2=W2[m,:,pl.ds(cf+o,CH)]
            hid=mm(xn2_s[...],f1)
            act,dact=gelu_both(hid)
            a=act.astype(BF)
            up_s[...]+=mm_nt(a,f2)
            gh=(mm(tg_s[...],f2)*dact).astype(BF)
            gn2_s[...]+=mm_nt(gh,f1)
            acc[m,:,pl.ds(cq+o,CH)]+=mm(xn2T_s[...],gh)
            acc[m,:,pl.ds(cq+cf+o,CH)]+=mm(tgT_s[...],a)
            return 0
        lax.fori_loop(0,2*each,chunk,0)
        dl_s[w,0:WIN,:]=(branch+up_s[...]+shifts_ref[3:4,:]).astype(BF)
        @pl.when(w<nw-1)
        def _():
            slab(w).start(); slab(w,mate).start()
        @pl.when(w==nw-1)
        def _(): slab(None).start()
        gn2=gn2_s[...]
        gln2=norm_back(gn2,xhat2,rstd2,gains_ref[1:2,:])
        gln2_ref[0]=gln2
        gb=(og+gln2).astype(BF)
        gbT=gb.T
        for m in range(2):
            at=slice(m*cq,(m+1)*cq)
            acc[m,:,0:cq]+=mm(gbT,attn[:,at])
            g=mm(gb,W1[m,:,3*cq:4*cq]).astype(BF)
            g_ref[0,:,at]=g
            gT=g.T
            gT_ref[0,at,:]=gT
            prod=gT.astype(F32)*OT_s[w,at,:]
            nh=nheads//2
            D_ref[0,m*nh:(m+1)*nh,:]=jnp.sum(prod.reshape(nh,HD,WIN),axis=1)
        small_ref[1:2,:]+=jnp.sum(gn2*xhat2,axis=0,keepdims=True)
        small_ref[3:4,:]+=jnp.sum(gn2,axis=0,keepdims=True)
        small_ref[4:5,:]+=jnp.sum(gb.astype(F32),axis=0,keepdims=True)
        small_ref[5:6,:]+=jnp.sum(tg.astype(F32),axis=0,keepdims=True)

    @pl.when(i==2*nw-1)
    def _():
        W2[...]=acc[:,:,cq:].astype(BF)
        pst[...]=acc[:,:,:cq].astype(BF)
        a=pltpu.make_async_copy(W2,dcat_hbm.at[:,:,pl.ds(cq,2*cf)],fin.at[0])
        b=pltpu.make_async_copy(pst,dcat_hbm.at[:,:,pl.ds(0,cq)],fin.at[1])
        a.start(); b.start()
        for k in range(2):
            pltpu.make_async_copy(P_s.at[k],P_hbm.at[0,pl.ds(0,PER)],psem.at[k]).wait()
        for k in range(nw-1):
            slab(k).wait(); slab(k,mate).wait()
        slab(None).wait()
        @pl.when(y==1)
        def _():
            for t in range(2): edge(t).wait_send()
        a.wait(); b.wait()

def call_a2(inputs,og,wf,lab,bias,W1,gains,shifts):
    nW=lab.shape[0]//2; WIN=lab.shape[1]; D=inputs.shape[1]; NH=bias.shape[0]
    cf=wf.shape[1]//2; cq=D//2; SLAB=-(-WIN//16)*16
    sd=jax.ShapeDtypeStruct; dma=pltpu.SemaphoreType.DMA; v=pltpu.VMEM
    early=lambda shape: pl.BlockSpec((1,)+shape,lambda i:(jnp.minimum(i,nW-1),)+(0,)*len(shape))
    late=lambda shape: pl.BlockSpec((1,)+shape,lambda i:(jnp.maximum(i-nW,0),)+(0,)*len(shape))
    outs=[sd((nW,3,WIN,D),BF),sd((nW,WIN,D),F32),sd((nW,NH,WIN,WIN),BF),sd((nW,WIN,D),F32),sd((nW,WIN,D),BF),sd((nW,D,WIN),BF),sd((nW,NH,WIN),F32),
          sd((2*nW,SLAB,D),BF),sd((SLAB,D),BF),sd((2,D,cq+2*cf),BF),sd((8,D),F32)]
    return pl.pallas_call(functools.partial(kernel_a2,NH),grid=(2*nW,),
      in_specs=[ANY,ANY,ANY,full(lab.shape),full((NH,WIN,WIN),pipeline_mode=ONE),full(W1.shape,pipeline_mode=ONE),full(gains.shape),full(shifts.shape)],
      out_specs=[early((3,WIN,D)),early((WIN,D)),ANY,late((WIN,D)),late((WIN,D)),late((D,WIN)),late((NH,WIN)),ANY,ANY,ANY,full((8,D))],
      out_shape=outs,
      scratch_shapes=[v((nW,SLAB,D),F32),v((nW,SLAB,D),F32),v((2,D,2*cf),BF),v((nW,D,WIN),F32),v((D,WIN),BF),v((D,WIN),BF),v((2,PER,WIN,WIN),BF),
        v((2,D,cq+2*cf),F32),v((2,D,cq),BF),v((WIN,D),BF),v((D,WIN),BF),v((WIN,D),BF),v((D,WIN),BF),v((WIN,D),F32),v((WIN,D),F32),v((nW,SLAB,D),BF),
        v((WIN,2*nW),F32),dma((2,)),dma((2,2*nW)),dma((2,2))]+gather_sems()+[dma((nW,)),dma((nW,)),dma((nW,)),dma((2,))],
      compiler_params=pltpu.CompilerParams(vmem_limit_bytes=63*1024*1024,dimension_semantics=("arbitrary",),collective_id=2,has_side_effects=True),
      name="kernel_a2")(inputs,og,wf,lab,bias,W1,gains,shifts)

class Reduce:
    def __init__(self,src,out,own,r1,bufs,ss,rs,ls):
        self.src,self.out,self.own,self.r1,self.bufs=src,out,own,r1,bufs
        self.ss,self.rs,self.ls=ss,rs,ls
        z,x,c,y=place_of()
        self.x,self.c,self.y,self.h,self.l=x,c,y,z//2,z%2
    def to(self,x=None,h=None,l=None,c=None,y=None):
        pick=lambda new,old: old if new is None else new
        return dev(pick(h,self.h)*2+pick(l,self.l),pick(x,self.x),pick(c,self.c),pick(y,self.y))
    def mine(self,k):
        return pltpu.make_async_copy(self.src.at[k%2,:,:,k//2,self.c],self.own.at[k//2,:,:,k%2],self.ls.at[k])
    def theirs(self,k):
        return send(self.src.at[k%2,:,:,k//2,1-self.c],self.r1.at[k//2,:,:,k%2],self.ss.at[k],self.rs.at[k],self.to(c=1-self.c))
    def turns(self,core):
        x,h,l,y=self.x,self.h,self.l,self.y
        s=slice(None)
        if core==0:
            return [((1-x,),dict(x=1-x),lambda a,b,d:(x,a,b,d)),((x,s,1-l),dict(l=1-l),lambda a,d:(x,a,l,d)),
                    ((x,1-h,l),dict(h=1-h),lambda d:(x,h,l,d)),((x,h,l,1-y),dict(y=1-y),None)]
        return [((s,s,1-l),dict(l=1-l),lambda a,b,d:(a,b,l,d)),((s,1-h,l),dict(h=1-h),lambda a,d:(a,h,l,d)),
                ((1-x,h,l),dict(x=1-x),lambda d:(x,h,l,d)),((x,h,l,1-y),dict(y=1-y),None)]
    def give(self,k,core):
        at,where,_=self.turns(core)[k]
        return send(self.own.at[at],self.bufs[k],self.ss.at[4+k],self.rs.at[4+k],self.to(**where))
    def start(self):
        for k in range(4):
            self.theirs(k).start(); self.mine(k).start()
    def add(self,dst,*srcs):
        total=srcs[0][...].astype(F32)
        for s in srcs[1:]: total=total+s[...].astype(F32)
        dst[...]=total.astype(dst.dtype)
    def by_core(self,f):
        for core in range(2):
            @pl.when(self.c==core)
            def _(): f(core)
    def one(self):
        for k in range(4):
            self.mine(k).wait(); self.theirs(k).wait_recv()
        def step(k,_):
            at=(k//8,(k//4)%2,(k//2)%2,k%2)
            self.add(self.own.at[at],self.own.at[at],self.r1.at[at])
            return 0
        lax.fori_loop(0,16,step,0)
        self.by_core(lambda core: self.give(0,core).start())
    def turn(self,k):
        def f(core):
            stay=self.turns(core)[k][2]
            self.give(k,core).wait_recv()
            def step(i,_):
                at=[(i//4,(i//2)%2,i%2),(i//2,i%2),(i,)][k]
                self.add(self.own.at[stay(*at)],self.own.at[stay(*at)],self.bufs[k].at[at])
                return 0
            lax.fori_loop(0,8>>k,step,0)
            self.give(k+1,core).start()
        self.by_core(f)
    def four(self):
        def f(core):
            self.give(3,core).wait_recv()
            self.add(self.out,self.own.at[self.x,self.h,self.l,self.y],self.bufs[3])
            for k in range(4): self.give(k,core).wait_send()
        self.by_core(f)
        for k in range(4): self.theirs(k).wait_send()

def reduce_scratch(rows,cols):
    v=lambda *d: pltpu.VMEM(d+(rows,cols),BF); dma=pltpu.SemaphoreType.DMA
    return [v(2,2,2,2),v(2,2,2,2),v(2,2,2),v(2,2),v(2),v(),dma((8,)),dma((8,)),dma((4,))]

class Sums:
    def __init__(self,slabs,got,res,ss,rs,ts,us):
        self.slabs,self.got,self.res,self.ss,self.rs,self.ts,self.us=slabs,got,res,ss,rs,ts,us
        z,x,c,y=place_of()
        self.s=(z*2+x)*2+c; self.y=y; self.n=slabs.shape[1]
    def part(self,k,yy):
        me=self.y*16+self.s
        return send(self.slabs.at[yy,k],self.got.at[me],self.ss.at[yy*self.n+k],self.rs.at[me],(k,yy))
    def other(self,k,yy):
        return jnp.logical_or(self.s!=k,self.y!=yy)
    def scatter(self):
        for k in range(self.n):
            for yy in range(2):
                @pl.when(self.other(k,yy))
                def _(): self.part(k,yy).start()
    def back(self,to,k):
        return send(self.res.at[k],self.res.at[k],self.ts.at[to],self.us.at[k],(to,self.y))
    def collect(self):
        me=self.y*16+self.s
        @pl.when(self.s<self.n)
        def _():
            self.got[me]=self.slabs[self.y,self.s]
            def wait(i,_):
                @pl.when(i!=me)
                def _():
                    send(self.slabs.at[0,0],self.got.at[i],self.ss.at[0],self.rs.at[i],(self.s,1-self.y)).wait_recv()
                return 0
            lax.fori_loop(0,32,wait,0)
            total=self.got[0]
            for i in range(1,32): total=total+self.got[i]
            self.res[self.s]=total
            for to in range(16):
                @pl.when(self.s!=to)
                def _(): self.back(to,self.s).start()
    def finish(self):
        for k in range(self.n):
            @pl.when(self.s!=k)
            def _(): self.back(k,k).wait_recv()
        @pl.when(self.s<self.n)
        def _():
            for to in range(16):
                @pl.when(self.s!=to)
                def _(): self.back(to,self.s).wait_send()
        for k in range(self.n):
            for yy in range(2):
                @pl.when(self.other(k,yy))
                def _(): self.part(k,yy).wait_send()

def kernel_bc(nheads,x_ref,gln2_ref,qkv_ref,g_ref,gT_ref,D_ref,P_ref,W1,gains_ref,shifts_ref,sm_ref,pos_ref,dcat_hbm,dlast_hbm,
              ev_hbm,hd_hbm,evl_hbm,hdl_hbm,redq_ref,redm_ref,tab_ref,sum_ref,
              G_s,Gx,aq,dq_s,kT_s,gq_s,gqT_s,dd_s,small_ref,acc,slabs,got,res,
              gs,gr_,dl,ds,dr,es,er,us,ss0,rs0,ts0,us0,
              *more):
    w=pl.program_id(0); nw=dd_s.shape[0]
    z,xc,c,y=place_of()
    s=(z*2+xc)*2+c
    mate=dev(z,xc,c,1-y); sib=dev(z,xc,1-c,y)
    D=x_ref.shape[-1]; WIN=x_ref.shape[-2]; SLAB=dd_s.shape[1]
    cq=D//2
    groups=nheads//PER
    tiles=G_s.shape[0]; part=Gx.shape[1]//nheads
    big=Reduce(dcat_hbm,redm_ref,more[9],more[10],more[11:15],*more[15:18])
    red=Reduce(dq_s,redq_ref,more[0],more[1],more[2:6],*more[6:9])
    def slab(k,to=None):
        at=ev_hbm.at[y*nw+k]
        if to is None: return pltpu.make_async_copy(dd_s.at[k],at,dl.at[k])
        return send(dd_s.at[k],at,ds.at[k],dr.at[k],to)
    def tail(k):
        lead=SLAB-hd_hbm.shape[0]
        return send(dd_s.at[nw-1,pl.ds(lead,hd_hbm.shape[0])],hd_hbm,es.at[k],er,((s+1)%16,k))
    def early(k):
        lead=SLAB-hdl_hbm.shape[0]
        if k==0: return pltpu.make_async_copy(dlast_hbm,evl_hbm.at[y],us.at[0])
        if k==1: return send(dlast_hbm,evl_hbm.at[y],us.at[1],us.at[2],mate)
        return send(dlast_hbm.at[pl.ds(lead,hdl_hbm.shape[0])],hdl_hbm,us.at[k+1],us.at[5],((s+1)%16,k-2))
    def trade(h):
        r=pl.multiple_of(h*WIN+(1-c)*(WIN-part),8)
        return send(G_s.at[:,pl.ds(r,part)],Gx.at[:,pl.ds(pl.multiple_of(h*part,8),part)],gs.at[h],gr_.at[h],sib)
    everyone=[((s+t)%16,yy) for t in range(1,16) for yy in (y,1-y)]+[mate]
    @pl.when(w==0)
    def _():
        hail(everyone)
        aq[...]=jnp.zeros_like(aq); G_s[...]=jnp.zeros_like(G_s); small_ref[...]=sm_ref[...]
        dd_s[:,SLAB-16:,:]=jnp.zeros((nw,16,D),BF)
    def met():
        heard(everyone)
        big.start()
        early(0).start(); early(1).start()
        @pl.when(y==1)
        def _():
            early(2).start(); early(3).start()
    plan=((0,met),(2,big.one),(6,lambda: big.turn(0)),(10,lambda: big.turn(1)),(13,lambda: big.turn(2)))
    kT_s[...]=qkv_ref[0,1].T
    lane=lax.broadcasted_iota(jnp.int32,(WIN,GROUP),1)
    hl=lane//HD
    def group(gi,_):
        o=pl.multiple_of(gi*GROUP,GROUP)
        gTg=gT_ref[0,pl.ds(o,GROUP),:]
        vg=qkv_ref[0,2,:,pl.ds(o,GROUP)]
        qg=qkv_ref[0,0,:,pl.ds(o,GROUP)]
        gg=g_ref[0,:,pl.ds(o,GROUP)]
        dv=jnp.zeros((WIN,GROUP),F32); dk=jnp.zeros((WIN,GROUP),F32)
        zero=jnp.zeros_like(vg)
        for hh in range(PER):
            h=gi*PER+hh
            p=P_ref[0,h]
            dp=mm(jnp.where(hl==hh,vg,zero),gTg)
            dsc=p.astype(F32)*(dp-D_ref[0,pl.ds(h,1),:])
            for k in range(tiles):
                wd=min(128,WIN-k*128)
                G_s[k,pl.ds(pl.multiple_of(h*WIN,8),WIN),:wd]+=dsc[:,k*128:k*128+wd]
            dsl=dsc.astype(BF)
            dv+=mm(p,jnp.where(hl==hh,gg,zero))
            dk+=mm(dsl,jnp.where(hl==hh,qg,zero))
            gqT_s[pl.ds(o+hh*HD,HD),:]=mm(kT_s[pl.ds(o+hh*HD,HD),:],dsl)
        gq_s[1,:,pl.ds(o,GROUP)]=(dk*(1.0/SQ)).astype(BF)
        gq_s[2,:,pl.ds(o,GROUP)]=dv.astype(BF)
        for when,what in plan:
            pl.when(w*groups+gi==min(when,nw*groups-1))(what)
        @pl.when(w==nw-1)
        def _():
            for hh in range(PER): trade(gi*PER+hh).start()
        return 0
    lax.fori_loop(0,groups,group,0)
    gq_s[0]=(gqT_s[...]*(1.0/SQ)).astype(BF).T
    x=x_ref[0]
    xhat,rstd=norm_stats(x)
    xn=(xhat*gains_ref[0:1,:]+shifts_ref[0:1,:]).astype(BF)
    xnT=xn.T
    gr=jnp.zeros((WIN,D),F32)
    for m in range(2):
        for k in range(3):
            gc=gq_s[k,:,m*cq:(m+1)*cq]
            gr=gr+mm_nt(gc,W1[m,:,k*cq:(k+1)*cq])
            aq[m,:,k*cq:(k+1)*cq]+=mm(xnT,gc)
    @pl.when(w==nw-1)
    def _():
        dq_s[...]=aq[...].astype(BF).reshape(dq_s.shape)
        red.start()
    dd_s[w,0:WIN,:]=(gln2_ref[0]+norm_back(gr,xhat,rstd,gains_ref[0:1,:])).astype(BF)
    slab(w).start(); slab(w,mate).start()
    @pl.when(jnp.logical_and(w==nw-1,y==1))
    def _():
        tail(0).start(); tail(1).start()
    small_ref[0:1,:]+=jnp.sum(gr*xhat,axis=0,keepdims=True)
    small_ref[2:3,:]+=jnp.sum(gr,axis=0,keepdims=True)
    @pl.when(w==nw-1)
    def _():
        for h in range(nheads): trade(h).wait()
        acc[...]=jnp.zeros_like(acc)
        nh=acc.shape[0]; LW=tiles*128
        base=c*(WIN-part)
        def rows(r,_):
            r8=pl.multiple_of(r*8,8)
            f8=pl.multiple_of(base+r*8,8)
            pos=pos_ref[pl.ds(f8,8),:]
            hi8=pos>>8; lo8=pos&255
            tot=jnp.zeros((nh*nheads,256),F32)
            iota=lax.broadcasted_iota(jnp.int32,(256,LW),0).astype(F32).astype(BF)
            for k in range(8):
                g=jnp.concatenate([G_s[q,pl.ds(f8+k,nheads,stride=WIN),:]+Gx[q,pl.ds(r8+k,nheads,stride=part),:] for q in range(tiles)],axis=1)
                hr=hi8[k:k+1,:]; lr=lo8[k:k+1,:].astype(F32).astype(BF)
                A=jnp.concatenate([jnp.where(hr==m,g,0.0) for m in range(nh)],axis=0).astype(BF)
                oh=jnp.where(iota==lr,jnp.ones((),BF),jnp.zeros((),BF))
                tot=tot+mm_nt(A,oh)
            acc[...]+=tot.reshape(acc.shape)
            return 0
        n=part//8
        cuts=[c]+[n*f//25 for f in (4,9,14,19)]+[n]
        after=(red.one,lambda: red.turn(0),lambda: red.turn(1),lambda: red.turn(2),None)
        for f in range(5):
            lax.fori_loop(cuts[f],cuts[f+1],rows,0)
            if after[f]: after[f]()
        half=nheads//2
        for yy in range(2):
            for k in range(nh): slabs[yy,k]=acc[k,yy*half:(yy+1)*half]
            for k in range(2): slabs[yy,nh+k]=small_ref[:,k*256:(k+1)*256]
        sums=Sums(slabs,got,res,ss0,rs0,ts0,us0)
        sums.scatter()
        red.four()
        sums.collect()
        big.four()
        sums.finish()
        for m in range(nh):
            tab_ref[:,m*256:(m+1)*256]=res[m]
        for k in range(2): sum_ref[:,k*256:(k+1)*256]=res[nh+k]
        for k in range(nw):
            slab(k).wait(); slab(k,mate).wait()
        @pl.when(y==1)
        def _():
            tail(0).wait_send(); tail(1).wait_send(); early(2).wait_send(); early(3).wait_send()
        tail(0).wait_recv(); early(2).wait_recv()
        early(0).wait(); early(1).wait()

def call_bc(x,gln2,qkv,g,gT,Dd,Pp,W1,gains,shifts,sm,pp,dcat,dlast,T):
    nW,WIN,D=x.shape; NH=Dd.shape[1]
    cq=D//2; tiles=-(-WIN//128); SLAB=-(-WIN//16)*16; EDGE=-(-(SLAB-WIN//2)//16)*16
    part=-(-WIN//16)*8
    nh=-(-T//256)
    rows,more=dcat.shape[-2:]; cols=3*cq
    sd=jax.ShapeDtypeStruct; dma=pltpu.SemaphoreType.DMA; v=pltpu.VMEM
    return pl.pallas_call(functools.partial(kernel_bc,NH),grid=(nW,),
      in_specs=[per((WIN,D)),per((WIN,D),pipeline_mode=ONE),per((3,WIN,D)),per((WIN,D)),per((D,WIN)),per((NH,WIN)),per((NH,WIN,WIN)),
        full((2,D,cols),pipeline_mode=ONE),full(gains.shape),full(shifts.shape),full(sm.shape),full(pp.shape,pipeline_mode=ONE),ANY,ANY],
      out_specs=[ANY,ANY,ANY,ANY,full((rows,cols),pipeline_mode=ONE),full((rows,more),pipeline_mode=ONE),full((NH//2,nh*256),pipeline_mode=ONE),full(sm.shape)],
      out_shape=[sd((2*nW,SLAB,D),BF),sd((EDGE,D),BF),sd((2,SLAB,D),BF),sd((EDGE,D),BF),sd((rows,cols),F32),sd((rows,more),F32),sd((NH//2,nh*256),F32),sd(sm.shape,F32)],
      scratch_shapes=[v((tiles,NH*WIN,128),F32),v((tiles,NH*part,128),F32),v((2,D,cols),F32),v((2,2,2,2,2,rows,cols),BF),v((D,WIN),BF),v((3,WIN,D),BF),v((D,WIN),F32),
        v((nW,SLAB,D),BF),v(sm.shape,F32),v((nh,NH,256),F32),v((2,nh+2,8,256),F32),v((32,8,256),F32),v((nh+2,8,256),F32),
        dma((NH,)),dma((NH,)),dma((nW,)),dma((nW,)),dma((nW,)),dma((2,)),dma,dma((6,)),dma((2*nh+4,)),dma((32,)),dma((16,)),dma((nh+2,))]+reduce_scratch(rows,cols)+reduce_scratch(rows,more),
      compiler_params=pltpu.CompilerParams(vmem_limit_bytes=63*1024*1024,dimension_semantics=("arbitrary",),collective_id=3,has_side_effects=True),
      name="kernel_bc")(x,gln2,qkv,g,gT,Dd,Pp,W1,gains,shifts,sm,pp,dcat,dlast)


def kernel_f(in_ref,og_ref,ev_ref,evl_ref,ev2_ref,hd_ref,hd2_ref,redq_ref,redm_ref,tab_ref,sum_ref,
             out_ref,din_ref,dqkv_ref,dproj_ref,dfc1_ref,dfc2_ref,dgain_ref,dshift_ref,dtab_ref,end_s):
    j=pl.program_id(0); nw=pl.num_programs(0)//2
    shift=in_ref.shape[0]//2; WIN=2*shift
    edge,SLAB=hd_ref.shape[0],ev_ref.shape[1]
    off=edge-(SLAB-shift)
    @pl.when(j==0)
    def _():
        end_s[0]=hd_ref[...].astype(F32); end_s[1]=hd2_ref[...].astype(F32)
        cq=dqkv_ref.shape[2]; cf=dfc1_ref.shape[1]
        for k in range(3): dqkv_ref[k]=redq_ref[:,k*cq:(k+1)*cq]
        dproj_ref[...]=redm_ref[:,0:cq]
        dfc1_ref[...]=redm_ref[:,cq:cq+cf]
        dfc2_ref[...]=redm_ref[:,cq+cf:]
        dgain_ref[...]=sum_ref[0:2,:]; dshift_ref[...]=sum_ref[2:6,:]
        dtab_ref[...]=tab_ref[:,0:dtab_ref.shape[1]]
    e=jnp.where(j%nw==nw-1,evl_ref[0],ev_ref[0]).astype(F32)
    for k,(base,res,v) in enumerate(((in_ref,out_ref,e),(og_ref,din_ref,ev2_ref[0].astype(F32)))):
        res[0:shift,:]=base[0:shift,:]+end_s[k,off:off+shift,:]
        res[shift:WIN,:]=base[shift:WIN,:]+v[0:shift,:]
        end_s[k]=v[SLAB-edge:,:]

def call_f(inputs,og,ev,evl,ev2,hd,hd2,redq,redm,tab,small,cq,cf,T):
    tok,D=inputs.shape; n,SLAB,_=ev.shape; WIN=tok//n; rows=redq.shape[0]
    sd=jax.ShapeDtypeStruct
    blk=pl.BlockSpec((WIN,D),lambda j:(j,0)); slab=pl.BlockSpec((1,SLAB,D),lambda j:(j,0,0))
    shapes=[(3,rows,cq),(rows,cq),(rows,cf),(rows,cf),(2,D),(4,D),(tab.shape[0],T)]
    return pl.pallas_call(kernel_f,grid=(n,),
      in_specs=[blk,blk,slab,pl.BlockSpec((1,SLAB,D),lambda j:(j//(n//2),0,0)),slab]+[full(v.shape) for v in (hd,hd2,redq,redm,tab,small)],
      out_specs=[blk,blk]+[full(v) for v in shapes],
      out_shape=[sd((tok,D),F32),sd((tok,D),F32)]+[sd(v,F32) for v in shapes],
      scratch_shapes=[pltpu.VMEM((2,)+hd.shape,F32)],
      compiler_params=pltpu.CompilerParams(vmem_limit_bytes=63*1024*1024,dimension_semantics=("arbitrary",)),
      name="kernel_f")(inputs,og,ev,evl,ev2,hd,hd2,redq,redm,tab,small)

def gathered(piece,names,nseq,nheads):
    full=lax.all_gather(piece,names,axis=0,tiled=False)
    return full.reshape((nseq,nheads)+piece.shape)

def natural(block):
    s,h,r,c=block.shape
    return block.transpose(0,2,1,3).reshape(s*r,h*c)

def owners(grad,nseq,nheads):
    r,c=grad.shape
    return grad.reshape(nseq,r//nseq,nheads,c//nheads).transpose(0,2,1,3).reshape(nseq*nheads,r//nseq,c//nheads)

def from_next(rows):
    n=lax.axis_size("seq")
    return lax.ppermute(rows,"seq",[(i,(i-1)%n) for i in range(n)])

def to_next(rows):
    n=lax.axis_size("seq")
    return lax.ppermute(rows,"seq",[(i,(i+1)%n) for i in range(n)])

def spread(rows):
    n=lax.axis_size("heads")
    flat=rows.reshape(-1,rows.shape[-1])
    if n==2:
        other=lax.ppermute(flat,"heads",[(0,1),(1,0)])
        me=lax.axis_index("heads")
        return jnp.where(me==0,jnp.concatenate([flat,other]),jnp.concatenate([other,flat]))
    return lax.all_gather(flat,"heads",axis=0,tiled=True)

def place(rows,base,shift):
    every=spread(rows)
    keep=every.shape[0]-shift
    return base+jnp.concatenate([to_next(every[keep:]),every[:keep]]).astype(F32)

def body(inputs,w_qkv,w_proj,w_fc1,w_fc2,gains,shifts,rel_table,region,pos_index,out_grad):
    nseq=lax.axis_size("seq"); nheads=lax.axis_size("heads"); me=lax.axis_index("heads")
    linked=nseq==16 and nheads==2
    names=("seq","heads")
    tok,D=inputs.shape; WIN=pos_index.shape[0]; shift=WIN//2; T=rel_table.shape[1]
    nW=tok//WIN//nheads
    rows=w_qkv.shape[1]; cq=w_qkv.shape[2]; cf=w_fc1.shape[1]
    lab=region.reshape(-1,WIN)
    if linked:
        W1,bias,wf,posT=call_w(w_qkv,w_proj.T,w_fc1,w_fc2.T,pos_index,rel_table)
        qkv,x,Pp,gln2,g,gT,Dd,ev,dlast,dcat,sm=call_a2(inputs,out_grad,wf,lab,bias,W1,gains,shifts)
        ev2,hd2,evl,hd,redq,redm,d_table,small=call_bc(x,gln2,qkv,g,gT,Dd,Pp,W1,gains,shifts,sm,posT,dcat.reshape(2,2,2,2,2,rows,-1),dlast,T)
        out,din,dq,dp,d1,d2,dg,dsh,dt=call_f(inputs,out_grad,ev,evl,ev2,hd,hd2,redq,redm,d_table,small,cq,cf,T)
        return (out,din,dq,dp.T,d1,d2.T,dg,dsh,dt)
    posT=pos_index.T
    wide=-(-WIN//128)*128
    posP=jnp.pad(posT,((0,0),(0,wide-WIN)))
    start=me*nW*WIN
    lab=lax.dynamic_slice_in_dim(lab,me*nW,nW,0)
    labc=lab[:,:,None]; labr=lab[:,None,:]
    wq=jnp.concatenate([w_qkv[0],w_qkv[1],w_qkv[2],w_proj.T],axis=1).astype(BF)
    wf=jnp.concatenate([w_fc1,w_fc2.T],axis=1).astype(BF)
    table=lax.all_gather(rel_table,"heads",axis=0,tiled=True)
    NH=table.shape[0]
    every=gathered(jnp.concatenate([wq,wf],axis=1),names,nseq,nheads)
    ends=[i*cq for i in range(5)]+[4*cq+cf,4*cq+2*cf]
    W=jnp.concatenate([natural(every[...,a:b]) for a,b in zip(ends[:-1],ends[1:])],axis=1)[None]
    bias=call_p(posP,pack_table(table),WIN)
    def mine(v):
        ext=jnp.concatenate([v,from_next(v[:shift])])
        return lax.dynamic_slice_in_dim(ext,start+shift,nW*WIN,0).reshape(nW,WIN,-1)
    x=mine(inputs); og=mine(out_grad)
    delta,gln2,qkv,g,gT,Dd,Pp,dcat,sm_a=call_a(x,og,labc,labr,bias,W,gains,shifts)
    dd,dqkv,G,sm_b=call_b(x,gln2,qkv,g,gT,Dd,Pp,W,gains,shifts)
    grads=[dqkv[0,:,c*D:(c+1)*D] for c in range(3)]+[dcat[0,:,:D],dcat[0,:,D:D+cf*nheads],dcat[0,:,D+cf*nheads:]]
    red=lax.psum_scatter(jnp.concatenate([owners(v,nseq,nheads) for v in grads],axis=2),names,scatter_dimension=0,tiled=False).astype(F32)
    redq,redm=red[:,:3*cq],red[:,3*cq:]
    d_table,small=lax.psum((call_t(G,posT,T,NH),sm_a+sm_b),names)
    nl=rel_table.shape[0]
    d_table=lax.dynamic_slice_in_dim(d_table,me*nl,nl,0)
    output=place(delta,inputs,shift)
    d_inputs=place(dd,out_grad,shift)
    d_qkv=redq.reshape(rows,3,cq).transpose(1,0,2)
    d_proj=redm[:,:cq].T; d_fc1=redm[:,cq:cq+cf]; d_fc2=redm[:,cq+cf:].T
    return (output,d_inputs,d_qkv,d_proj,d_fc1,d_fc2,small[0:2],small[2:6],d_table)

def solution(mesh):
    placed=(P("seq",None),P(None,"seq","heads"),P("heads","seq"),P("seq","heads"),P("heads","seq"),P(),P(),P("heads",None),P("seq"),P(),P("seq",None))
    return jax.shard_map(body,mesh=mesh,in_specs=placed,
    out_specs=(P("seq",None),P("seq",None),P(None,"seq","heads"),P("heads","seq"),P("seq","heads"),P("heads","seq"),P(),P(),P("heads",None)),
    check_vma=False)
```

```python
import functools
import math

import jax, jax.numpy as jnp
from jax import lax
from jax.experimental import pallas as pl
from jax.experimental.pallas import tpu as pltpu
from jax.sharding import PartitionSpec as P

BF=jnp.bfloat16; F32=jnp.float32
HD=32; GROUP=128; PER=4
EPS=1e-5
SQ=math.sqrt(32.0)
CEXP=math.log2(math.e)/SQ
MASK=100.0*SQ

def mm(a,b):
    return lax.dot_general(a,b,(((1,),(0,)),((),())),preferred_element_type=F32)
def mm_nt(a,b):
    return lax.dot_general(a,b,(((1,),(1,)),((),())),preferred_element_type=F32)

def norm_stats(v):
    mean=jnp.mean(v,axis=-1,keepdims=True)
    c=v-mean
    var=jnp.mean(c*c,axis=-1,keepdims=True)
    rstd=lax.rsqrt(var+EPS)
    return c*rstd, rstd

def norm_back(gy,xhat,rstd,gain):
    gx=gy*gain
    m1=jnp.mean(gx,axis=-1,keepdims=True)
    m2=jnp.mean(gx*xhat,axis=-1,keepdims=True)
    return rstd*(gx-m1-xhat*m2)

P0=0.3275911
A1,A2,A3,A4,A5=0.254829592,-0.284496736,1.421413741,-1.453152027,1.061405429
def gelu_both(x):
    e=jnp.exp2(x*x*(-0.5*math.log2(math.e)))
    t=1.0/(1.0+(P0/math.sqrt(2.0))*jnp.abs(x))
    poly=t*(0.5*A1+t*(0.5*A2+t*(0.5*A3+t*(0.5*A4+t*(0.5*A5)))))
    half=poly*e
    phi=jnp.where(x>=0,1.0-half,half)
    return x*phi, phi+x*e*(1.0/math.sqrt(2.0*math.pi))

def kernel_a(nheads,x_ref,og_ref,labc_ref,labr_ref,bias_ref,W_ref,gains_ref,shifts_ref,
             delta_ref,gln2_ref,qkv_ref,g_ref,gT_ref,D_ref,P_hbm,dcat_ref,small_ref,
             qT_s,vT_s,OT_s,P_s,acc,sem,xn2_s,xn2T_s,tg_s,tgT_s,up_s,gn2_s):
    w=pl.program_id(0); nw=pl.num_programs(0)
    D=x_ref.shape[-1]; WIN=x_ref.shape[-2]
    parts=W_ref.shape[0]; cq=D//parts; cf=(W_ref.shape[2]-4*cq)//2
    groups=nheads//PER
    x=x_ref[0]
    xhat,_=norm_stats(x)
    xn=(xhat*gains_ref[0:1,:]+shifts_ref[0:1,:]).astype(BF)
    for c in range(3):
        for m in range(parts):
            at=slice(m*cq,(m+1)*cq)
            y=mm(xn,W_ref[m,:,c*cq:(c+1)*cq]).astype(BF)
            qkv_ref[0,c,:,at]=y
            if c==0: qT_s[at,:]=y.T
            if c==2: vT_s[at,:]=y.T
    labc=labc_ref[0]; labr=labr_ref[0]
    lane=lax.broadcasted_iota(jnp.int32,(WIN,GROUP),1)
    oh=jnp.where((labc==lane)|((labc+3)==lane),1.0,0.0).astype(BF)
    hi=564.0
    lo=MASK-hi
    sub=lax.broadcasted_iota(jnp.int32,(GROUP,WIN),0)
    nm=jnp.where(sub<3,jnp.where(sub!=labr,-hi,0.0),jnp.where(sub<6,jnp.where(sub-3!=labr,-lo,0.0),0.0)).astype(BF)
    hl=lane//HD

    def group(gi,_):
        slot=gi%2
        step=w*groups+gi
        @pl.when(step>=2)
        def _():
            pltpu.make_async_copy(P_s.at[slot],P_hbm.at[0,pl.ds(0,PER)],sem.at[slot]).wait()
        o=pl.multiple_of(gi*GROUP,GROUP)
        qTg=jnp.concatenate([qT_s[pl.ds(o,GROUP),:],nm],axis=0)
        kg=qkv_ref[0,1,:,pl.ds(o,GROUP)]
        for hh in range(PER):
            kh=jnp.concatenate([jnp.where(hl==hh,kg,jnp.zeros_like(kg)),oh],axis=1)
            t=mm(kh,qTg)+bias_ref[gi*PER+hh]
            m=jnp.max(t,axis=0,keepdims=True)
            e=jnp.exp2((t-m)*CEXP)
            l=jnp.sum(e,axis=0,keepdims=True)
            p=(e*(1.0/l)).astype(BF)
            P_s[slot,hh]=p
            OT_s[pl.ds(o+hh*HD,HD),:]=mm(vT_s[pl.ds(o+hh*HD,HD),:],p)
        pltpu.make_async_copy(P_s.at[slot],P_hbm.at[w,pl.ds(gi*PER,PER)],sem.at[slot]).start()
        return 0
    lax.fori_loop(0,groups,group,0)

    attn=OT_s[...].astype(BF).T
    branch=shifts_ref[2:3,:]
    for m in range(parts):
        branch=branch+mm_nt(attn[:,m*cq:(m+1)*cq],W_ref[m,:,3*cq:4*cq])
    branch=branch.astype(BF).astype(F32)
    middle=x+branch
    xhat2,rstd2=norm_stats(middle)
    xn2=(xhat2*gains_ref[1:2,:]+shifts_ref[1:2,:]).astype(BF)
    og=og_ref[0]
    tg=og.astype(BF)
    xn2_s[...]=xn2; xn2T_s[...]=xn2.T; tg_s[...]=tg; tgT_s[...]=tg.T
    up_s[...]=jnp.zeros_like(up_s); gn2_s[...]=jnp.zeros_like(gn2_s)
    CH=min(512,cf); each=cf//CH
    @pl.when(w==0)
    def _():
        acc[...]=jnp.zeros_like(acc)
        small_ref[...]=jnp.zeros_like(small_ref)
    def chunk(c,_):
        m=c//each
        o=pl.multiple_of((c%each)*CH,CH)
        f1=W_ref[m,:,pl.ds(4*cq+o,CH)]; f2=W_ref[m,:,pl.ds(4*cq+cf+o,CH)]
        hid=mm(xn2_s[...],f1)
        act,dact=gelu_both(hid)
        a=act.astype(BF)
        up_s[...]+=mm_nt(a,f2)
        gh=(mm(tg_s[...],f2)*dact).astype(BF)
        gn2_s[...]+=mm_nt(gh,f1)
        acc[m,:,pl.ds(cq+o,CH)]+=mm(xn2T_s[...],gh)
        acc[m,:,pl.ds(cq+cf+o,CH)]+=mm(tgT_s[...],a)
        return 0
    lax.fori_loop(0,parts*each,chunk,0)
    delta_ref[0]=(branch+up_s[...]+shifts_ref[3:4,:]).astype(BF)
    gn2=gn2_s[...]
    gln2=norm_back(gn2,xhat2,rstd2,gains_ref[1:2,:])
    gln2_ref[0]=gln2
    gb=(og+gln2).astype(BF)
    gbT=gb.T
    for m in range(parts):
        at=slice(m*cq,(m+1)*cq)
        acc[m,:,0:cq]+=mm(gbT,attn[:,at])
        g=mm(gb,W_ref[m,:,3*cq:4*cq]).astype(BF)
        g_ref[0,:,at]=g
        gT=g.T
        gT_ref[0,at,:]=gT
        prod=gT.astype(F32)*OT_s[at,:]
        nh=nheads//parts
        D_ref[0,m*nh:(m+1)*nh,:]=jnp.sum(prod.reshape(nh,HD,WIN),axis=1)
    small_ref[1:2,:]+=jnp.sum(gn2*xhat2,axis=0,keepdims=True)
    small_ref[3:4,:]+=jnp.sum(gn2,axis=0,keepdims=True)
    small_ref[4:5,:]+=jnp.sum(gb.astype(F32),axis=0,keepdims=True)
    small_ref[5:6,:]+=jnp.sum(tg.astype(F32),axis=0,keepdims=True)
    @pl.when(w==nw-1)
    def _():
        dcat_ref[...]=acc[...].astype(BF)
        for s in range(2):
            pltpu.make_async_copy(P_s.at[s],P_hbm.at[0,pl.ds(0,PER)],sem.at[s]).wait()

def full(shape,**kw):
    return pl.BlockSpec(shape,lambda w:(0,)*len(shape),**kw)
def per(shape,**kw):
    return pl.BlockSpec((1,)+shape,lambda w:(w,)+(0,)*len(shape),**kw)
ONE=pl.Buffered(1)
ANY=pl.BlockSpec(memory_space=pl.ANY)

def call_a(x,og,labc,labr,bias,W,gains,shifts):
    nW,WIN,D=x.shape; NH=bias.shape[0]
    parts,_,Ct=W.shape; Cg=Ct-3*(D//parts)
    sd=jax.ShapeDtypeStruct
    outs=[sd((nW,WIN,D),BF),sd((nW,WIN,D),F32),sd((nW,3,WIN,D),BF),sd((nW,WIN,D),BF),sd((nW,D,WIN),BF),sd((nW,NH,WIN),F32),
          sd((nW,NH,WIN,WIN),BF),sd((parts,D,Cg),BF),sd((8,D),F32)]
    return pl.pallas_call(functools.partial(kernel_a,NH),grid=(nW,),
      in_specs=[per((WIN,D)),per((WIN,D)),per((WIN,1)),per((1,WIN)),full((NH,WIN,WIN),pipeline_mode=ONE),
        full((parts,D,Ct),pipeline_mode=ONE),full(gains.shape),full(shifts.shape)],
      out_specs=[per((WIN,D)),per((WIN,D)),per((3,WIN,D)),per((WIN,D)),per((D,WIN)),per((NH,WIN)),ANY,full((parts,D,Cg)),full((8,D))],
      out_shape=outs,
      scratch_shapes=[pltpu.VMEM((D,WIN),BF),pltpu.VMEM((D,WIN),BF),pltpu.VMEM((D,WIN),F32),pltpu.VMEM((2,PER,WIN,WIN),BF),
        pltpu.VMEM((parts,D,Cg),F32),pltpu.SemaphoreType.DMA((2,)),
        pltpu.VMEM((WIN,D),BF),pltpu.VMEM((D,WIN),BF),pltpu.VMEM((WIN,D),BF),pltpu.VMEM((D,WIN),BF),pltpu.VMEM((WIN,D),F32),pltpu.VMEM((WIN,D),F32)],
      compiler_params=pltpu.CompilerParams(vmem_limit_bytes=62*1024*1024,dimension_semantics=("arbitrary",)),
      name="kernel_a")(x,og,labc,labr,bias,W,gains,shifts)

def kernel_b(nheads,x_ref,gln2_ref,qkv_ref,g_ref,gT_ref,D_ref,P_ref,W_ref,gains_ref,shifts_ref,
             dd_ref,dqkv_ref,G_hbm,small_ref,G_s,aq,kT_s,gq_s,gqT_s,sem):
    w=pl.program_id(0); nw=pl.num_programs(0)
    D=x_ref.shape[-1]; WIN=x_ref.shape[-2]
    parts=W_ref.shape[0]; cq=D//parts
    groups=nheads//PER
    @pl.when(w==0)
    def _():
        aq[...]=jnp.zeros_like(aq); G_s[...]=jnp.zeros_like(G_s); small_ref[...]=jnp.zeros_like(small_ref)
    kT_s[...]=qkv_ref[0,1].T
    lane=lax.broadcasted_iota(jnp.int32,(WIN,GROUP),1)
    hl=lane//HD
    def group(gi,_):
        o=pl.multiple_of(gi*GROUP,GROUP)
        gTg=gT_ref[0,pl.ds(o,GROUP),:]
        vg=qkv_ref[0,2,:,pl.ds(o,GROUP)]
        qg=qkv_ref[0,0,:,pl.ds(o,GROUP)]
        gg=g_ref[0,:,pl.ds(o,GROUP)]
        dv=jnp.zeros((WIN,GROUP),F32); dk=jnp.zeros((WIN,GROUP),F32)
        zero=jnp.zeros_like(vg)
        for hh in range(PER):
            h=gi*PER+hh
            p=P_ref[0,h]
            dp=mm(jnp.where(hl==hh,vg,zero),gTg)
            ds_=p.astype(F32)*(dp-D_ref[0,pl.ds(h,1),:])
            for c in range(G_s.shape[0]):
                wd=min(128,WIN-c*128)
                G_s[c,pl.ds(pl.multiple_of(h*WIN,8),WIN),:wd]+=ds_[:,c*128:c*128+wd]
            dsl=ds_.astype(BF)
            dv+=mm(p,jnp.where(hl==hh,gg,zero))
            dk+=mm(dsl,jnp.where(hl==hh,qg,zero))
            gqT_s[pl.ds(o+hh*HD,HD),:]=mm(kT_s[pl.ds(o+hh*HD,HD),:],dsl)
        gq_s[1,:,pl.ds(o,GROUP)]=(dk*(1.0/SQ)).astype(BF)
        gq_s[2,:,pl.ds(o,GROUP)]=dv.astype(BF)
        return 0
    lax.fori_loop(0,groups,group,0)
    gq_s[0]=(gqT_s[...]*(1.0/SQ)).astype(BF).T
    x=x_ref[0]
    xhat,rstd=norm_stats(x)
    xn=(xhat*gains_ref[0:1,:]+shifts_ref[0:1,:]).astype(BF)
    xnT=xn.T
    gr=jnp.zeros((WIN,D),F32)
    for m in range(parts):
        for c in range(3):
            gc=gq_s[c,:,m*cq:(m+1)*cq]
            gr=gr+mm_nt(gc,W_ref[m,:,c*cq:(c+1)*cq])
            aq[m,:,c*cq:(c+1)*cq]+=mm(xnT,gc)
    dd_ref[0]=(gln2_ref[0]+norm_back(gr,xhat,rstd,gains_ref[0:1,:])).astype(BF)
    small_ref[0:1,:]+=jnp.sum(gr*xhat,axis=0,keepdims=True)
    small_ref[2:3,:]+=jnp.sum(gr,axis=0,keepdims=True)
    @pl.when(w==nw-1)
    def _():
        dqkv_ref[...]=aq[...].astype(BF)
        cp=pltpu.make_async_copy(G_s,G_hbm,sem); cp.start(); cp.wait()

def call_b(x,gln2,qkv,g,gT,Dd,Pp,W,gains,shifts):
    nW,WIN,D=x.shape; NH=Dd.shape[1]
    parts=W.shape[0]; cq=D//parts; tiles=-(-WIN//128)
    sd=jax.ShapeDtypeStruct
    return pl.pallas_call(functools.partial(kernel_b,NH),grid=(nW,),
      in_specs=[per((WIN,D)),per((WIN,D)),per((3,WIN,D)),per((WIN,D)),per((D,WIN)),per((NH,WIN)),per((NH,WIN,WIN)),
        full((parts,D,3*cq),pipeline_mode=ONE),full(gains.shape),full(shifts.shape)],
      out_specs=[per((WIN,D)),full((parts,D,3*cq)),ANY,full((8,D))],
      out_shape=[sd((nW,WIN,D),BF),sd((parts,D,3*cq),BF),sd((tiles,NH*WIN,128),F32),sd((8,D),F32)],
      scratch_shapes=[pltpu.VMEM((tiles,NH*WIN,128),F32),pltpu.VMEM((parts,D,3*cq),F32),pltpu.VMEM((D,WIN),BF),pltpu.VMEM((3,WIN,D),BF),pltpu.VMEM((D,WIN),F32),
        pltpu.SemaphoreType.DMA],
      compiler_params=pltpu.CompilerParams(vmem_limit_bytes=62*1024*1024,dimension_semantics=("arbitrary",)),
      name="kernel_b")(x,gln2,qkv,g,gT,Dd,Pp,W,gains,shifts)

FIX=8191.0

def pack_table(table):
    NH,T=table.shape
    n=-(-T//128)
    q=jnp.round(jnp.clip(table,-4.0,4.0)*FIX).astype(jnp.int32)
    q=jnp.pad(q,((0,0),(0,n*128-T)))
    q=q.reshape(NH//2,2,n,128)
    return (q[:,0]*65536)|(q[:,1]&65535)

def kernel_p(pos_ref,tab_ref,bias_ref):
    npair,n,_=tab_ref.shape
    WIN=bias_ref.shape[-1]
    tiles=-(-WIN//128)
    def row(r,_):
        r8=pl.multiple_of(r*8,8)
        for c in range(tiles):
            width=min(128,WIN-c*128)
            idx=pos_ref[pl.ds(r8,8),c*128:(c+1)*128]
            lo=idx&127; hi=idx>>7
            masks=[hi==k for k in range(n)]
            for p in range(npair):
                acc=jnp.zeros((8,128),jnp.int32)
                for k in range(n):
                    src=jnp.broadcast_to(tab_ref[p,k:k+1,:],(8,128))
                    acc=jnp.where(masks[k],jnp.take_along_axis(src,lo,axis=1),acc)
                a=(acc>>16).astype(F32)*(SQ/FIX)
                b=((acc<<16)>>16).astype(F32)*(SQ/FIX)
                bias_ref[2*p,pl.ds(r8,8),c*128:c*128+width]=a[:,:width]
                bias_ref[2*p+1,pl.ds(r8,8),c*128:c*128+width]=b[:,:width]
        return 0
    lax.fori_loop(0,bias_ref.shape[1]//8,row,0)

def call_p(posT_pad,tab,WIN):
    NH=tab.shape[0]*2
    return pl.pallas_call(kernel_p,out_shape=jax.ShapeDtypeStruct((NH,WIN,WIN),F32),
      compiler_params=pltpu.CompilerParams(vmem_limit_bytes=40*1024*1024),name="kernel_p")(posT_pad,tab)

def kernel_t(NH,G_ref,hi_ref,lo_ref,out_ref):
    WIN=hi_ref.shape[0]; LW=G_ref.shape[0]*128
    nh=out_ref.shape[0]//NH
    out_ref[...]=jnp.zeros_like(out_ref)
    def rows(r,_):
        r8=pl.multiple_of(r*8,8)
        hi8=hi_ref[pl.ds(r8,8),:]; lo8=lo_ref[pl.ds(r8,8),:]
        tot=jnp.zeros(out_ref.shape,F32)
        iota=lax.broadcasted_iota(jnp.int32,(256,LW),0).astype(F32).astype(BF)
        for k in range(8):
            g=jnp.concatenate([G_ref[c,pl.ds(r8+k,NH,stride=WIN),:] for c in range(LW//128)],axis=1)
            hr=hi8[k:k+1,:]; lr=lo8[k:k+1,:].astype(F32).astype(BF)
            A=jnp.concatenate([jnp.where(hr==m,g,0.0) for m in range(nh)],axis=0).astype(BF)
            oh=jnp.where(iota==lr,jnp.ones((),BF),jnp.zeros((),BF))
            tot=tot+lax.dot_general(A,oh,(((1,),(1,)),((),())),preferred_element_type=F32)
        out_ref[...]+=tot
        return 0
    lax.fori_loop(0,WIN//8,rows,0)

def call_t(G,posT,T,NH):
    WIN=posT.shape[0]; nt=G.shape[0]
    nh=-(-T//256)
    pp=jnp.pad(posT,((0,0),(0,nt*128-WIN)),constant_values=nh*256)
    hi=pp>>8; lo=pp&255
    o=pl.pallas_call(functools.partial(kernel_t,NH),out_shape=jax.ShapeDtypeStruct((nh*NH,256),F32),
      compiler_params=pltpu.CompilerParams(vmem_limit_bytes=40*1024*1024),name="kernel_t")(G,hi,lo)
    return o.reshape(nh,NH,256).transpose(1,0,2).reshape(NH,nh*256)[:,:T]


MESHID=pl.DeviceIdType.MESH

def place_of():
    s=lax.axis_index("seq"); y=lax.axis_index("heads")
    return s//4,(s//2)%2,s%2,y

def dev(z,x,c,y):
    return ((z*2+x)*2+c,y)

def peers_of(z,x,c,y):
    return [dev(z,x,1-c,y),dev(z,1-x,c,y),dev(z,x,c,1-y)]+[dev((z+i)%4,x,c,y) for i in (1,2,3)]

def hail(devices):
    bar=pltpu.get_barrier_semaphore()
    for d in devices:
        pl.semaphore_signal(bar,inc=1,device_id=d,device_id_type=MESHID)

def heard(devices):
    pl.semaphore_wait(pltpu.get_barrier_semaphore(),len(devices))

def greet(devices):
    hail(devices)
    heard(devices)

def send(src,dst,ss,rs,to):
    return pltpu.make_async_remote_copy(src_ref=src,dst_ref=dst,send_sem=ss,recv_sem=rs,device_id=to,device_id_type=MESHID)


class Gather:
    def __init__(self,src,dst,ss,rs,own):
        self.src,self.dst,self.ss,self.rs,self.own=src,dst,ss,rs,own
        z,x,c,y=self.at=place_of()
        self.xa=x+(1-2*x)*(1-c); self.ya=y+(1-2*y)*c
        self.xb=x+(1-2*x)*c; self.yb=y+(1-2*y)*(1-c)
        self.sib=dev(z,x,1-c,y); self.pa=dev(z,self.xa,c,self.ya); self.pb=dev(z,self.xb,c,self.yb)
    def slot(self,zz,xx,cc,yy):
        n=self.src.shape[0]
        return self.dst.at[yy,pl.ds(pl.multiple_of(((zz*2+xx)*2+cc)*n,n),n)]
    def copy(self,src,where,k,to):
        return send(src,self.slot(*where),self.ss.at[k],self.rs.at[k],to)
    def go(self,where,k,to,src=None):
        self.copy(self.slot(*where) if src is None else src,where,k,to).start()
    def came(self,where,k):
        self.copy(self.src,where,k,self.sib).wait_recv()
    def keep(self):
        z,x,c,y=self.at
        return pltpu.make_async_copy(self.src,self.slot(z,x,c,y),self.own)
    def start(self):
        z,x,c,y=self.at
        me=(z,x,c,y)
        self.keep().start()
        for i in (1,2,3):
            self.go(me,i-1,dev((z+i)%4,x,c,y),self.src)
        self.go(me,3,self.pa,self.src); self.go(me,7,self.pb,self.src); self.go(me,15,self.sib,self.src)
    def z(self,i):
        return (self.at[0]+4-i)%4
    def turn_z(self,i):
        z,x,c,y=self.at
        at=(self.z(i),x,c,y); self.came(at,i-1)
        self.go(at,3+i,self.pa); self.go(at,7+i,self.pb); self.go(at,15+i,self.sib)
    def turn_a(self,i):
        at=(self.z(i),self.xa,self.at[2],self.ya); self.came(at,3+i)
        self.go(at,11+i,self.pb); self.go(at,19+i,self.sib)
    def turn_b(self,i):
        at=(self.z(i),self.xb,self.at[2],self.yb); self.came(at,7+i)
        self.go(at,23+i,self.sib)
    def turn_ab(self,i):
        z,x,c,y=self.at
        at=(self.z(i),1-x,c,1-y); self.came(at,11+i)
        self.go(at,27+i,self.sib)
    def last(self):
        z,x,c,y=self.at
        for i in range(4):
            zz=self.z(i)
            self.came((zz,x,1-c,y),15+i); self.came((zz,self.xb,1-c,self.yb),19+i)
            self.came((zz,self.xa,1-c,self.ya),23+i); self.came((zz,1-x,1-c,1-y),27+i)
    def drain(self):
        z,x,c,y=self.at
        for k in range(31):
            self.copy(self.src,(z,x,c,y),k,self.sib).wait_send()
        self.keep().wait()

def gather_sems():
    return [pltpu.SemaphoreType.DMA((31,)),pltpu.SemaphoreType.DMA((31,)),pltpu.SemaphoreType.DMA]

STEPS=7
def kernel_w(qkv_ref,proj_ref,fc1_ref,fc2_ref,pos_ref,tab_ref,W_hbm,bias_hbm,brem_hbm,wf_ref,posT_ref,
             bias_s,brem_s,wq_s,tb,tq,ss,rs,own,bs,br,bl,tsem,ed):
    z,x,c,y=place_of()
    cq=qkv_ref.shape[2]; cf=fc1_ref.shape[1]
    for k in range(3): wq_s[:,k*cq:(k+1)*cq]=qkv_ref[k].astype(BF)
    wq_s[:,3*cq:4*cq]=proj_ref[...].astype(BF)
    half,T=tab_ref.shape
    tb[2]=jnp.zeros(tb.shape[1:],F32)
    tb[2,:,0:T]=tab_ref[...]
    greet(peers_of(z,x,c,y))
    gather=Gather(wq_s,W_hbm,ss,rs,own)
    swap=send(tb.at[2],tb.at[y],tsem.at[0],tsem.at[1],dev(z,x,c,1-y))
    swap.start()
    gather.start()
    tb[y]=tb[2]
    wf_ref[:,0:cf]=fc1_ref[...].astype(BF)
    wf_ref[:,cf:2*cf]=fc2_ref[...].astype(BF)
    WIN,Q=bias_s.shape[-2:]; tiles=-(-WIN//128); n=tb.shape[2]//128
    posT_ref[...]=jnp.full(posT_ref.shape,1<<15,jnp.int32)
    posT_ref[:,0:WIN]=pos_ref[...].astype(F32).T.astype(jnp.int32)
    swap.wait()
    npair=half//2
    for p in range(npair):
        a,b=[jnp.floor(jnp.clip(tb[c,2*p+k:2*p+k+1,:],-4.0,4.0)*FIX+0.5).astype(jnp.int32) for k in range(2)]
        tq[p:p+1,:]=(a*65536)|(b&65535)
    nrow=WIN//8
    cuts=[nrow*k//STEPS for k in range(STEPS+1)]
    sib=dev(z,x,1-c,y)
    def rows_of(k): return pl.ds(cuts[k]*8,(cuts[k+1]-cuts[k])*8)
    def kept(k): return pltpu.make_async_copy(bias_s.at[:,rows_of(k)],bias_hbm.at[pl.ds(c*half,half),rows_of(k)],bl.at[k])
    def sent(k,cc): return send(bias_s.at[:,rows_of(k)],bias_hbm.at[pl.ds(cc*half,half),rows_of(k)],bs.at[k],br.at[k],sib)
    def rows(k):
        def row(r,_):
            r8=pl.multiple_of(r*8,8)
            for t in range(tiles):
                width=min(128,WIN-t*128)
                idx=posT_ref[pl.ds(r8,8),t*128:(t+1)*128]
                lo=idx&127; hi=idx>>7
                masks=[hi==q for q in range(n)]
                for p in range(npair):
                    acc=jnp.zeros((8,128),jnp.int32)
                    for q in range(n):
                        src=jnp.broadcast_to(tq[p:p+1,q*128:(q+1)*128],(8,128))
                        acc=jnp.where(masks[q],jnp.take_along_axis(src,lo,axis=1),acc)
                    a=(acc>>16).astype(F32)*(SQ/FIX)
                    b=((acc<<16)>>16).astype(F32)*(SQ/FIX)
                    for h,v in ((2*p,a),(2*p+1,b)):
                        if width==128: bias_s[h,pl.ds(r8,8),t*128:(t+1)*128]=v
                        else: brem_s[pl.ds(r8,8),h*width:(h+1)*width]=v[:,:width]
            return 0
        lax.fori_loop(cuts[k],cuts[k+1],row,0)
        kept(k).start(); sent(k,c).start()
    rows(0)
    for i in (1,3,2): gather.turn_z(i)
    rows(1)
    for i in (0,): gather.turn_a(i); gather.turn_b(i)
    rows(2)
    for i in (1,3): gather.turn_a(i); gather.turn_b(i)
    rows(3)
    for i in (2,): gather.turn_a(i); gather.turn_b(i)
    gather.turn_ab(0)
    rows(4)
    for i in (1,3): gather.turn_ab(i)
    rows(5)
    gather.turn_ab(2)
    rows(6)
    edges=[pltpu.make_async_copy(brem_s,brem_hbm.at[c],ed.at[0]),send(brem_s,brem_hbm.at[c],ed.at[1],ed.at[2],sib)]
    for e in edges: e.start()
    gather.last()
    for e in edges: e.wait()
    for k in range(STEPS):
        kept(k).wait(); sent(k,c).wait_send(); sent(k,1-c).wait_recv()
    gather.drain()

def call_w(w_qkv,w_proj,w_fc1,w_fc2,pos_index,rel_table):
    rows,cq=w_qkv.shape[1:]; cf=w_fc1.shape[1]; WIN=pos_index.shape[0]; half,T=rel_table.shape; dma=pltpu.SemaphoreType.DMA
    wide=-(-WIN//128)*128; Q=WIN//128*128; n=-(-T//128); mem=pltpu.VMEM
    sd=jax.ShapeDtypeStruct
    return pl.pallas_call(kernel_w,grid=(1,),
      out_shape=[sd((2,16*rows,4*cq),BF),sd((2*half,WIN,Q),F32),sd((2,WIN,half*(WIN-Q)),F32),sd((rows,2*cf),BF),sd((WIN,wide),jnp.int32)],
      in_specs=[full(v.shape) for v in (w_qkv,w_proj,w_fc1,w_fc2,pos_index,rel_table)],out_specs=[ANY,ANY,ANY,full((rows,2*cf)),full((WIN,wide))],
      scratch_shapes=[mem((half,WIN,Q),F32),mem((WIN,half*(WIN-Q)),F32),mem((rows,4*cq),BF),mem((3,half,n*128),F32),mem((half//2,n*128),jnp.int32)]
        +gather_sems()+[dma((STEPS,)),dma((STEPS,)),dma((STEPS,)),dma((2,)),dma((3,))],
      compiler_params=pltpu.CompilerParams(vmem_limit_bytes=63*1024*1024,collective_id=1,has_side_effects=True),name="kernel_w")(w_qkv,w_proj,w_fc1,w_fc2,pos_index,rel_table)

def neighbours(z,x,c,y):
    s=(z*2+x)*2+c
    return [((s+k)%16,yy) for k in (1,15) for yy in (y,1-y)]

def pick(shape,test):
    r=lax.broadcasted_iota(jnp.int32,shape,0); c=lax.broadcasted_iota(jnp.int32,shape,1)
    return jnp.where(test(r,c),1.0,0.0)

def exact(a,b):
    return lax.dot_general(a,b,(((1,),(0,)),((),())),precision=lax.Precision.HIGHEST,preferred_element_type=F32)

def kernel_a2(nheads,in_hbm,og_hbm,wf_hbm,lab_ref,bias_ref,brem_ref,W1,gains_ref,shifts_ref,
              qkv_ref,x_ref,P_hbm,pr_ref,gln2_ref,g_ref,gT_ref,D_ref,ev_hbm,dlast_hbm,dcat_hbm,small_ref,
              x_s,og_s,W2,OT_s,qT_s,vT_s,P_s,kst_s,acc,pst,xn2_s,xn2T_s,tg_s,tgT_s,up_s,gn2_s,dl_s,
              lab_s,psem,xsem,hsem,ss,rs,own,dl,ds,dr,fin):
    i=pl.program_id(0); nw=x_s.shape[0]
    w=i%nw
    z,xc,c,y=place_of()
    s=(z*2+xc)*2+c
    D=x_s.shape[-1]; WIN=qkv_ref.shape[-2]; SLAB=x_s.shape[1]; HALF=SLAB//2
    OFF=(SLAB-WIN)//2
    cq=D//2; cf=W2.shape[2]//2
    groups=nheads//PER; Q=bias_ref.shape[2]; R=WIN-Q
    gather=Gather(wf_hbm,W2,ss,rs,own)
    mate=dev(z,xc,c,1-y)
    def local(k,half,t):
        hbm,buf=((in_hbm,x_s),(og_hbm,og_s))[t]
        r=pl.multiple_of(y*(nw*WIN)+k*WIN+(WIN//2-OFF)+half*HALF,8)
        return pltpu.make_async_copy(hbm.at[pl.ds(r,HALF)],buf.at[k,pl.ds(half*HALF,HALF)],xsem.at[t,2*k+half])
    def edge(t):
        hbm,buf=((in_hbm,x_s),(og_hbm,og_s))[t]
        return send(hbm.at[pl.ds(0,HALF)],buf.at[nw-1,pl.ds(HALF,HALF)],hsem.at[t,0],hsem.at[t,1],((s+15)%16,1))
    def ready(t):
        local(w,0,t).wait()
        far=jnp.logical_and(w==nw-1,y==1)
        @pl.when(far)
        def _(): edge(t).wait_recv()
        @pl.when(jnp.logical_not(far))
        def _(): local(w,1,t).wait()
    def slab(k,to=None):
        if k is None: return pltpu.make_async_copy(dl_s.at[nw-1],dlast_hbm,dl.at[nw-1])
        at=ev_hbm.at[y*nw+k]
        if to is None: return pltpu.make_async_copy(dl_s.at[k],at,dl.at[k])
        return send(dl_s.at[k],at,ds.at[k],dr.at[k],to)
    @pl.when(i==0)
    def _():
        greet(peers_of(z,xc,c,y)+neighbours(z,xc,c,y))
        for k in range(nw):
            for t in range(2):
                local(k,0,t).start()
                if k<nw-1: local(k,1,t).start()
        for t in range(2):
            @pl.when(y==1)
            def _(): edge(t).start()
            @pl.when(y==0)
            def _(): local(nw-1,1,t).start()
        gather.start()
        lab_s[...]=lab_ref[...].astype(F32).T
        acc[...]=jnp.zeros_like(acc)
        for hh in range(PER): kst_s[(hh+1)*SLAB-16:(hh+1)*SLAB,:]=jnp.zeros((16,2*GROUP),BF)
        small_ref[...]=jnp.zeros_like(small_ref)
        dl_s[:,SLAB-16:,:]=jnp.zeros((nw,16,D),BF)

    @pl.when(i<nw)
    def _():
        ready(0)
        x=x_s[w,OFF:OFF+WIN,:]
        x_ref[0]=x
        xhat,_=norm_stats(x)
        xn=(xhat*gains_ref[0:1,:]+shifts_ref[0:1,:]).astype(BF)
        for k in range(3):
            for m in range(2):
                at=slice(m*cq,(m+1)*cq)
                v=mm(xn,W1[m,:,k*cq:(k+1)*cq]).astype(BF)
                qkv_ref[0,k,:,at]=v
                if k==0: qT_s[at,:]=v.T
                if k==2: vT_s[at,:]=v.T
        mine=y*nw+w
        labr=lab_ref[pl.ds(mine,1),:]
        labc=jnp.sum(jnp.where(lax.broadcasted_iota(jnp.int32,lab_s.shape,1)==mine,lab_s[...],0.0),axis=1,keepdims=True).astype(jnp.int32)
        lane=lax.broadcasted_iota(jnp.int32,(WIN,GROUP),1)
        oh=jnp.where((labc==lane)|((labc+3)==lane),1.0,0.0).astype(BF)
        hi=564.0
        lo=MASK-hi
        sub=lax.broadcasted_iota(jnp.int32,(GROUP,WIN),0)
        nm=jnp.where(sub<3,jnp.where(sub!=labr,-hi,0.0),jnp.where(sub<6,jnp.where(sub-3!=labr,-lo,0.0),0.0)).astype(BF)
        hl=lane//HD
        for hh in range(PER): kst_s[hh*SLAB:hh*SLAB+WIN,GROUP:]=oh
        nmq=nm[:,0:Q]
        def soften(t):
            m=jnp.max(t,axis=0,keepdims=True)
            e=jnp.exp2((t-m)*CEXP)
            l=jnp.sum(e,axis=0,keepdims=True)
            return (e*(1.0/l)).astype(BF)
        def group(gi,_):
            slot=gi%2
            @pl.when(w*groups+gi>=2)
            def _():
                pltpu.make_async_copy(P_s.at[slot],P_hbm.at[0,0],psem.at[slot]).wait()
            o=pl.multiple_of(gi*GROUP,GROUP)
            qTg=jnp.concatenate([qT_s[pl.ds(o,GROUP),0:Q],nmq],axis=0)
            kg=qkv_ref[0,1,:,pl.ds(o,GROUP)]
            for hh in range(PER): kst_s[hh*SLAB:hh*SLAB+WIN,0:GROUP]=jnp.where(hl==hh,kg,jnp.zeros_like(kg))
            t4=mm(kst_s[...],qTg)
            for hh in range(PER):
                p=soften(t4[hh*SLAB:hh*SLAB+WIN]+bias_ref[gi*PER+hh])
                P_s[slot,:,hh*Q:(hh+1)*Q]=p
                OT_s[w,pl.ds(o+hh*HD,HD),0:Q]=mm(vT_s[pl.ds(o+hh*HD,HD),:],p)
            pltpu.make_async_copy(P_s.at[slot],P_hbm.at[w,gi],psem.at[slot]).start()
            return 0
        lax.fori_loop(0,groups,group,0)
        spread=pick((R,GROUP),lambda r,c: c%R==r).astype(BF)
        own_rows=pick((D,GROUP),lambda r,c: r//HD==c//R)
        qbd=(mm(qT_s[:,Q:WIN],spread)*own_rows).astype(BF)
        nmr=mm(nm[:,Q:WIN],spread).astype(BF)
        brem=jnp.concatenate([brem_ref[0],brem_ref[1]],axis=1)
        pr=soften(mm(qkv_ref[0,1],qbd)+mm(oh,nmr)+brem)
        pr_ref[0]=pr
        OT_s[w,:,Q:WIN]=exact(mm(vT_s[...],pr)*own_rows,pick((GROUP,R),lambda r,c: r%R==c))

    @pl.when(i==0)
    def _():
        for k in (1,3,2): gather.turn_z(k)
    @pl.when(i==1)
    def _():
        for k in (0,1,3,2): gather.turn_a(k); gather.turn_b(k)
    @pl.when(i==2)
    def _():
        for k in (0,1,3,2): gather.turn_ab(k)
    @pl.when(i==nw-1)
    def _():
        gather.last(); gather.drain()

    @pl.when(i>=nw)
    def _():
        ready(1)
        x=x_s[w,OFF:OFF+WIN,:]
        og=og_s[w,OFF:OFF+WIN,:]
        attn=OT_s[w].astype(BF).T
        branch=shifts_ref[2:3,:]
        for m in range(2):
            branch=branch+mm_nt(attn[:,m*cq:(m+1)*cq],W1[m,:,3*cq:4*cq])
        branch=branch.astype(BF).astype(F32)
        middle=x+branch
        xhat2,rstd2=norm_stats(middle)
        xn2=(xhat2*gains_ref[1:2,:]+shifts_ref[1:2,:]).astype(BF)
        tg=og.astype(BF)
        xn2_s[...]=xn2; xn2T_s[...]=xn2.T; tg_s[...]=tg; tgT_s[...]=tg.T
        up_s[...]=jnp.zeros_like(up_s); gn2_s[...]=jnp.zeros_like(gn2_s)
        CH=512; each=cf//CH
        def chunk(k,_):
            m=k//each
            o=pl.multiple_of((k%each)*CH,CH)
            f1=W2[m,:,pl.ds(o,CH)]; f2=W2[m,:,pl.ds(cf+o,CH)]
            hid=mm(xn2_s[...],f1)
            act,dact=gelu_both(hid)
            a=act.astype(BF)
            up_s[...]+=mm_nt(a,f2)
            gh=(mm(tg_s[...],f2)*dact).astype(BF)
            gn2_s[...]+=mm_nt(gh,f1)
            acc[m,:,pl.ds(cq+o,CH)]+=mm(xn2T_s[...],gh)
            acc[m,:,pl.ds(cq+cf+o,CH)]+=mm(tgT_s[...],a)
            return 0
        lax.fori_loop(0,2*each,chunk,0)
        dl_s[w,0:WIN,:]=(branch+up_s[...]+shifts_ref[3:4,:]).astype(BF)
        @pl.when(w<nw-1)
        def _():
            slab(w).start(); slab(w,mate).start()
        @pl.when(w==nw-1)
        def _(): slab(None).start()
        gn2=gn2_s[...]
        gln2=norm_back(gn2,xhat2,rstd2,gains_ref[1:2,:])
        gln2_ref[0]=gln2
        gb=(og+gln2).astype(BF)
        gbT=gb.T
        for m in range(2):
            at=slice(m*cq,(m+1)*cq)
            acc[m,:,0:cq]+=mm(gbT,attn[:,at])
            g=mm(gb,W1[m,:,3*cq:4*cq]).astype(BF)
            g_ref[0,:,at]=g
            gT=g.T
            gT_ref[0,at,:]=gT
            prod=gT.astype(F32)*OT_s[w,at,:]
            nh=nheads//2
            D_ref[0,m*nh:(m+1)*nh,:]=jnp.sum(prod.reshape(nh,HD,WIN),axis=1)
        small_ref[1:2,:]+=jnp.sum(gn2*xhat2,axis=0,keepdims=True)
        small_ref[3:4,:]+=jnp.sum(gn2,axis=0,keepdims=True)
        small_ref[4:5,:]+=jnp.sum(gb.astype(F32),axis=0,keepdims=True)
        small_ref[5:6,:]+=jnp.sum(tg.astype(F32),axis=0,keepdims=True)

    @pl.when(i==2*nw-1)
    def _():
        W2[...]=acc[:,:,cq:].astype(BF)
        pst[...]=acc[:,:,:cq].astype(BF)
        a=pltpu.make_async_copy(W2,dcat_hbm.at[:,:,pl.ds(cq,2*cf)],fin.at[0])
        b=pltpu.make_async_copy(pst,dcat_hbm.at[:,:,pl.ds(0,cq)],fin.at[1])
        a.start(); b.start()
        for k in range(2):
            pltpu.make_async_copy(P_s.at[k],P_hbm.at[0,0],psem.at[k]).wait()
        for k in range(nw-1):
            slab(k).wait(); slab(k,mate).wait()
        slab(None).wait()
        @pl.when(y==1)
        def _():
            for t in range(2): edge(t).wait_send()
        a.wait(); b.wait()

def call_a2(inputs,og,wf,lab,bias,brem,W1,gains,shifts):
    nW=lab.shape[0]//2; WIN=lab.shape[1]; D=inputs.shape[1]; NH=bias.shape[0]
    cf=wf.shape[1]//2; cq=D//2; SLAB=-(-WIN//16)*16
    Q=bias.shape[2]
    sd=jax.ShapeDtypeStruct; dma=pltpu.SemaphoreType.DMA; v=pltpu.VMEM
    early=lambda shape: pl.BlockSpec((1,)+shape,lambda i:(jnp.minimum(i,nW-1),)+(0,)*len(shape))
    late=lambda shape: pl.BlockSpec((1,)+shape,lambda i:(jnp.maximum(i-nW,0),)+(0,)*len(shape))
    outs=[sd((nW,3,WIN,D),BF),sd((nW,WIN,D),F32),sd((nW,NH//PER,WIN,PER*Q),BF),sd((nW,WIN,GROUP),BF),sd((nW,WIN,D),F32),sd((nW,WIN,D),BF),sd((nW,D,WIN),BF),sd((nW,NH,WIN),F32),
          sd((2*nW,SLAB,D),BF),sd((SLAB,D),BF),sd((2,D,cq+2*cf),BF),sd((8,D),F32)]
    return pl.pallas_call(functools.partial(kernel_a2,NH),grid=(2*nW,),
      in_specs=[ANY,ANY,ANY,full(lab.shape),full(bias.shape,pipeline_mode=ONE),full(brem.shape),full(W1.shape,pipeline_mode=ONE),full(gains.shape),full(shifts.shape)],
      out_specs=[early((3,WIN,D)),early((WIN,D)),ANY,early((WIN,GROUP)),late((WIN,D)),late((WIN,D)),late((D,WIN)),late((NH,WIN)),ANY,ANY,ANY,full((8,D))],
      out_shape=outs,
      scratch_shapes=[v((nW,SLAB,D),F32),v((nW,SLAB,D),F32),v((2,D,2*cf),BF),v((nW,D,WIN),F32),v((D,WIN),BF),v((D,WIN),BF),v((2,WIN,PER*Q),BF),v((PER*SLAB,2*GROUP),BF),
        v((2,D,cq+2*cf),F32),v((2,D,cq),BF),v((WIN,D),BF),v((D,WIN),BF),v((WIN,D),BF),v((D,WIN),BF),v((WIN,D),F32),v((WIN,D),F32),v((nW,SLAB,D),BF),
        v((WIN,2*nW),F32),dma((2,)),dma((2,2*nW)),dma((2,2))]+gather_sems()+[dma((nW,)),dma((nW,)),dma((nW,)),dma((2,))],
      compiler_params=pltpu.CompilerParams(vmem_limit_bytes=63*1024*1024,dimension_semantics=("arbitrary",),collective_id=2,has_side_effects=True),
      name="kernel_a2")(inputs,og,wf,lab,bias,brem,W1,gains,shifts)

class Reduce:
    def __init__(self,src,out,own,r1,bufs,ss,rs,ls):
        self.src,self.out,self.own,self.r1,self.bufs=src,out,own,r1,bufs
        self.ss,self.rs,self.ls=ss,rs,ls
        z,x,c,y=place_of()
        self.x,self.c,self.y,self.h,self.l=x,c,y,z//2,z%2
    def to(self,x=None,h=None,l=None,c=None,y=None):
        pick=lambda new,old: old if new is None else new
        return dev(pick(h,self.h)*2+pick(l,self.l),pick(x,self.x),pick(c,self.c),pick(y,self.y))
    def mine(self,k):
        return pltpu.make_async_copy(self.src.at[k%2,:,:,k//2,self.c],self.own.at[k//2,:,:,k%2],self.ls.at[k])
    def theirs(self,k):
        return send(self.src.at[k%2,:,:,k//2,1-self.c],self.r1.at[k//2,:,:,k%2],self.ss.at[k],self.rs.at[k],self.to(c=1-self.c))
    def turns(self,core):
        x,h,l,y=self.x,self.h,self.l,self.y
        s=slice(None)
        if core==0:
            return [((1-x,),dict(x=1-x),lambda a,b,d:(x,a,b,d)),((x,s,1-l),dict(l=1-l),lambda a,d:(x,a,l,d)),
                    ((x,1-h,l),dict(h=1-h),lambda d:(x,h,l,d)),((x,h,l,1-y),dict(y=1-y),None)]
        return [((s,s,1-l),dict(l=1-l),lambda a,b,d:(a,b,l,d)),((s,1-h,l),dict(h=1-h),lambda a,d:(a,h,l,d)),
                ((1-x,h,l),dict(x=1-x),lambda d:(x,h,l,d)),((x,h,l,1-y),dict(y=1-y),None)]
    def give(self,k,core):
        at,where,_=self.turns(core)[k]
        return send(self.own.at[at],self.bufs[k],self.ss.at[4+k],self.rs.at[4+k],self.to(**where))
    def start(self):
        for k in range(4):
            self.theirs(k).start(); self.mine(k).start()
    def add(self,dst,*srcs):
        total=srcs[0][...].astype(F32)
        for s in srcs[1:]: total=total+s[...].astype(F32)
        dst[...]=total.astype(dst.dtype)
    def by_core(self,f):
        for core in range(2):
            @pl.when(self.c==core)
            def _(): f(core)
    def one(self):
        for k in range(4):
            self.mine(k).wait(); self.theirs(k).wait_recv()
        def step(k,_):
            at=(k//8,(k//4)%2,(k//2)%2,k%2)
            self.add(self.own.at[at],self.own.at[at],self.r1.at[at])
            return 0
        lax.fori_loop(0,16,step,0)
        self.by_core(lambda core: self.give(0,core).start())
    def turn(self,k):
        def f(core):
            stay=self.turns(core)[k][2]
            self.give(k,core).wait_recv()
            def step(i,_):
                at=[(i//4,(i//2)%2,i%2),(i//2,i%2),(i,)][k]
                self.add(self.own.at[stay(*at)],self.own.at[stay(*at)],self.bufs[k].at[at])
                return 0
            lax.fori_loop(0,8>>k,step,0)
            self.give(k+1,core).start()
        self.by_core(f)
    def four(self):
        def f(core):
            self.give(3,core).wait_recv()
            self.add(self.out,self.own.at[self.x,self.h,self.l,self.y],self.bufs[3])
            for k in range(4): self.give(k,core).wait_send()
        self.by_core(f)
        for k in range(4): self.theirs(k).wait_send()

def reduce_scratch(rows,cols):
    v=lambda *d: pltpu.VMEM(d+(rows,cols),BF); dma=pltpu.SemaphoreType.DMA
    return [v(2,2,2,2),v(2,2,2,2),v(2,2,2),v(2,2),v(2),v(),dma((8,)),dma((8,)),dma((4,))]

class Sums:
    def __init__(self,slabs,got,res,ss,rs,ts,us):
        self.slabs,self.got,self.res,self.ss,self.rs,self.ts,self.us=slabs,got,res,ss,rs,ts,us
        z,x,c,y=place_of()
        self.s=(z*2+x)*2+c; self.y=y; self.n=slabs.shape[1]
    def part(self,k,yy):
        me=self.y*16+self.s
        return send(self.slabs.at[yy,k],self.got.at[me],self.ss.at[yy*self.n+k],self.rs.at[me],(k,yy))
    def other(self,k,yy):
        return jnp.logical_or(self.s!=k,self.y!=yy)
    def scatter(self):
        for k in range(self.n):
            for yy in range(2):
                @pl.when(self.other(k,yy))
                def _(): self.part(k,yy).start()
    def back(self,to,k):
        return send(self.res.at[k],self.res.at[k],self.ts.at[to],self.us.at[k],(to,self.y))
    def collect(self):
        me=self.y*16+self.s
        @pl.when(self.s<self.n)
        def _():
            self.got[me]=self.slabs[self.y,self.s]
            def wait(i,_):
                @pl.when(i!=me)
                def _():
                    send(self.slabs.at[0,0],self.got.at[i],self.ss.at[0],self.rs.at[i],(self.s,1-self.y)).wait_recv()
                return 0
            lax.fori_loop(0,32,wait,0)
            total=self.got[0]
            for i in range(1,32): total=total+self.got[i]
            self.res[self.s]=total
            for to in range(16):
                @pl.when(self.s!=to)
                def _(): self.back(to,self.s).start()
    def finish(self):
        for k in range(self.n):
            @pl.when(self.s!=k)
            def _(): self.back(k,k).wait_recv()
        @pl.when(self.s<self.n)
        def _():
            for to in range(16):
                @pl.when(self.s!=to)
                def _(): self.back(to,self.s).wait_send()
        for k in range(self.n):
            for yy in range(2):
                @pl.when(self.other(k,yy))
                def _(): self.part(k,yy).wait_send()

def kernel_bc(nheads,x_ref,gln2_ref,qkv_ref,g_ref,gT_ref,D_ref,P_ref,pr_ref,W1,gains_ref,shifts_ref,sm_ref,pos_ref,pose_ref,dcat_hbm,dlast_hbm,
              ev_hbm,hd_hbm,evl_hbm,hdl_hbm,redq_ref,redm_ref,tab_ref,sum_ref,
              G_s,Gx,Gr_s,Gxr,vst_s,dS_s,dsr_s,gbd_s,qbd_s,aq,dq_s,kT_s,gq_s,gqT_s,dd_s,small_ref,acc,slabs,got,res,
              gs,gr_,ge,dl,ds,dr,es,er,us,ss0,rs0,ts0,us0,
              *more):
    w=pl.program_id(0); nw=dd_s.shape[0]
    z,xc,c,y=place_of()
    s=(z*2+xc)*2+c
    mate=dev(z,xc,c,1-y); sib=dev(z,xc,1-c,y)
    D=x_ref.shape[-1]; WIN=x_ref.shape[-2]; SLAB=dd_s.shape[1]
    cq=D//2
    groups=nheads//PER
    tiles=G_s.shape[0]; Q=tiles*128; R=WIN-Q; part=Gx.shape[1]//nheads
    big=Reduce(dcat_hbm,redm_ref,more[9],more[10],more[11:15],*more[15:18])
    red=Reduce(dq_s,redq_ref,more[0],more[1],more[2:6],*more[6:9])
    def slab(k,to=None):
        at=ev_hbm.at[y*nw+k]
        if to is None: return pltpu.make_async_copy(dd_s.at[k],at,dl.at[k])
        return send(dd_s.at[k],at,ds.at[k],dr.at[k],to)
    def tail(k):
        lead=SLAB-hd_hbm.shape[0]
        return send(dd_s.at[nw-1,pl.ds(lead,hd_hbm.shape[0])],hd_hbm,es.at[k],er,((s+1)%16,k))
    def early(k):
        lead=SLAB-hdl_hbm.shape[0]
        if k==0: return pltpu.make_async_copy(dlast_hbm,evl_hbm.at[y],us.at[0])
        if k==1: return send(dlast_hbm,evl_hbm.at[y],us.at[1],us.at[2],mate)
        return send(dlast_hbm.at[pl.ds(lead,hdl_hbm.shape[0])],hdl_hbm,us.at[k+1],us.at[5],((s+1)%16,k-2))
    def edge_trade():
        return send(Gr_s,Gxr,ge.at[0],ge.at[1],sib)
    def trade(h):
        r=pl.multiple_of(h*WIN+(1-c)*(WIN-part),8)
        return send(G_s.at[:,pl.ds(r,part)],Gx.at[:,pl.ds(pl.multiple_of(h*part,8),part)],gs.at[h],gr_.at[h],sib)
    everyone=[((s+t)%16,yy) for t in range(1,16) for yy in (y,1-y)]+[mate]
    @pl.when(w==0)
    def _():
        hail(everyone)
        aq[...]=jnp.zeros_like(aq); G_s[...]=jnp.zeros_like(G_s); Gr_s[...]=jnp.zeros_like(Gr_s); small_ref[...]=sm_ref[...]
        dd_s[:,SLAB-16:,:]=jnp.zeros((nw,16,D),BF)
        for hh in range(PER): vst_s[(hh+1)*SLAB-16:(hh+1)*SLAB,:]=jnp.zeros((16,GROUP),BF)
    def met():
        heard(everyone)
        big.start()
        early(0).start(); early(1).start()
        @pl.when(y==1)
        def _():
            early(2).start(); early(3).start()
    plan=((0,met),(2,big.one),(6,lambda: big.turn(0)),(10,lambda: big.turn(1)),(13,lambda: big.turn(2)))
    kT_s[...]=qkv_ref[0,1].T
    lane=lax.broadcasted_iota(jnp.int32,(WIN,GROUP),1)
    hl=lane//HD
    lift=pick((GROUP,R),lambda r,c: r%R==c).astype(BF)
    own_cols=pick((GROUP,D),lambda r,c: r//R==c//HD)
    gbd_s[...]=(mm(lift,g_ref[0,Q:WIN,:])*own_cols).astype(BF)
    qbd_s[...]=(mm(lift,qkv_ref[0,0,Q:WIN,:])*own_cols).astype(BF)
    Dr=exact(D_ref[0,:,Q:WIN],pick((R,GROUP),lambda r,c: c%R==r))
    Dr=jnp.sum(Dr*pick((nheads,GROUP),lambda r,c: c//R==r),axis=0,keepdims=True)
    dsr=pr_ref[0].astype(F32)*(mm_nt(qkv_ref[0,2],gbd_s[...])-Dr)
    Gr_s[...]+=dsr
    dsr_s[...]=dsr.astype(BF)
    gqT_s[:,Q:WIN]=exact(mm(kT_s[...],dsr_s[...])*pick((D,GROUP),lambda r,c: r//HD==c//R),pick((GROUP,R),lambda r,c: r%R==c))
    def group(gi,_):
        o=pl.multiple_of(gi*GROUP,GROUP)
        gTg=gT_ref[0,pl.ds(o,GROUP),0:Q]
        vg=qkv_ref[0,2,:,pl.ds(o,GROUP)]
        qg=qkv_ref[0,0,0:Q,pl.ds(o,GROUP)]
        gg=g_ref[0,0:Q,pl.ds(o,GROUP)]
        for hh in range(PER): vst_s[hh*SLAB:hh*SLAB+WIN,:]=jnp.where(hl==hh,vg,jnp.zeros_like(vg))
        dp4=mm(vst_s[...],gTg)
        for hh in range(PER):
            h=gi*PER+hh
            dsc=P_ref[0,gi,:,hh*Q:(hh+1)*Q].astype(F32)*(dp4[hh*SLAB:hh*SLAB+WIN]-D_ref[0,pl.ds(h,1),0:Q])
            for k in range(tiles):
                G_s[k,pl.ds(pl.multiple_of(h*WIN,8),WIN),:]+=dsc[:,k*128:(k+1)*128]
            dsl=dsc.astype(BF)
            dS_s[:,hh*Q:(hh+1)*Q]=dsl
            gqT_s[pl.ds(o+hh*HD,HD),0:Q]=mm(kT_s[pl.ds(o+hh*HD,HD),:],dsl)
        zero=jnp.zeros_like(gg); hq=hl[0:Q]
        gst=jnp.concatenate([jnp.where(hq==hh,gg,zero) for hh in range(PER)],axis=0)
        qst=jnp.concatenate([jnp.where(hq==hh,qg,zero) for hh in range(PER)],axis=0)
        dv=mm(P_ref[0,gi],gst)+mm(pr_ref[0],gbd_s[:,pl.ds(o,GROUP)])
        dk=mm(dS_s[...],qst)+mm(dsr_s[...],qbd_s[:,pl.ds(o,GROUP)])
        gq_s[1,:,pl.ds(o,GROUP)]=(dk*(1.0/SQ)).astype(BF)
        gq_s[2,:,pl.ds(o,GROUP)]=dv.astype(BF)
        for when,what in plan:
            pl.when(w*groups+gi==min(when,nw*groups-1))(what)
        @pl.when(w==nw-1)
        def _():
            for hh in range(PER): trade(gi*PER+hh).start()
            @pl.when(gi==0)
            def _(): edge_trade().start()
        return 0
    lax.fori_loop(0,groups,group,0)
    gq_s[0]=(gqT_s[...]*(1.0/SQ)).astype(BF).T
    x=x_ref[0]
    xhat,rstd=norm_stats(x)
    xn=(xhat*gains_ref[0:1,:]+shifts_ref[0:1,:]).astype(BF)
    xnT=xn.T
    gr=jnp.zeros((WIN,D),F32)
    for m in range(2):
        for k in range(3):
            gc=gq_s[k,:,m*cq:(m+1)*cq]
            gr=gr+mm_nt(gc,W1[m,:,k*cq:(k+1)*cq])
            aq[m,:,k*cq:(k+1)*cq]+=mm(xnT,gc)
    @pl.when(w==nw-1)
    def _():
        dq_s[...]=aq[...].astype(BF).reshape(dq_s.shape)
        red.start()
    dd_s[w,0:WIN,:]=(gln2_ref[0]+norm_back(gr,xhat,rstd,gains_ref[0:1,:])).astype(BF)
    slab(w).start(); slab(w,mate).start()
    @pl.when(jnp.logical_and(w==nw-1,y==1))
    def _():
        tail(0).start(); tail(1).start()
    small_ref[0:1,:]+=jnp.sum(gr*xhat,axis=0,keepdims=True)
    small_ref[2:3,:]+=jnp.sum(gr,axis=0,keepdims=True)
    @pl.when(w==nw-1)
    def _():
        for h in range(nheads): trade(h).wait()
        edge_trade().wait()
        acc[...]=jnp.zeros_like(acc)
        nh=acc.shape[0]; LW=tiles*128
        base=c*(WIN-part)
        def one_hots(g,hr,lr,width):
            iota=lax.broadcasted_iota(jnp.int32,(256,width),0).astype(F32).astype(BF)
            A=jnp.concatenate([jnp.where(hr==m,g,0.0) for m in range(nh)],axis=0).astype(BF)
            oh=jnp.where(iota==lr.astype(F32).astype(BF),jnp.ones((),BF),jnp.zeros((),BF))
            return mm_nt(A,oh)
        def rows(r,_):
            r8=pl.multiple_of(r*8,8)
            f8=pl.multiple_of(base+r*8,8)
            pos=pos_ref[pl.ds(f8,8),0:LW]
            hi8=pos>>8; lo8=pos&255
            tot=jnp.zeros((nh*nheads,256),F32)
            for k in range(8):
                g=jnp.concatenate([G_s[q,pl.ds(f8+k,nheads,stride=WIN),:]+Gx[q,pl.ds(r8+k,nheads,stride=part),:] for q in range(tiles)],axis=1)
                tot=tot+one_hots(g,hi8[k:k+1,:],lo8[k:k+1,:],LW)
            acc[...]+=tot.reshape(acc.shape)
            return 0
        turned=mm_nt(pick((GROUP,GROUP),lambda r,c: c==(r%nheads)*R+r//nheads).astype(BF),(Gr_s[...]+Gxr[...]).astype(BF))
        tot=jnp.zeros((nh*nheads,256),F32)
        for k in range(R):
            pos=pose_ref[k:k+1,:]
            hi=jnp.where(c==k//(R//2),pos>>8,-1)
            tot=tot+one_hots(turned[k*nheads:(k+1)*nheads],hi,pos&255,WIN)
        acc[...]+=tot.reshape(acc.shape)
        n=part//8
        cuts=[c]+[n*f//25 for f in (4,9,14,19)]+[n]
        after=(red.one,lambda: red.turn(0),lambda: red.turn(1),lambda: red.turn(2),None)
        for f in range(5):
            lax.fori_loop(cuts[f],cuts[f+1],rows,0)
            if after[f]: after[f]()
        half=nheads//2
        for yy in range(2):
            for k in range(nh): slabs[yy,k]=acc[k,yy*half:(yy+1)*half]
            for k in range(2): slabs[yy,nh+k]=small_ref[:,k*256:(k+1)*256]
        sums=Sums(slabs,got,res,ss0,rs0,ts0,us0)
        sums.scatter()
        red.four()
        sums.collect()
        big.four()
        sums.finish()
        for m in range(nh):
            tab_ref[:,m*256:(m+1)*256]=res[m]
        for k in range(2): sum_ref[:,k*256:(k+1)*256]=res[nh+k]
        for k in range(nw):
            slab(k).wait(); slab(k,mate).wait()
        @pl.when(y==1)
        def _():
            tail(0).wait_send(); tail(1).wait_send(); early(2).wait_send(); early(3).wait_send()
        tail(0).wait_recv(); early(2).wait_recv()
        early(0).wait(); early(1).wait()

def call_bc(x,gln2,qkv,g,gT,Dd,Pp,Pr,W1,gains,shifts,sm,pp,pos_index,dcat,dlast,T):
    nW,WIN,D=x.shape; NH=Dd.shape[1]
    cq=D//2; tiles=WIN//128; Q=tiles*128; SLAB=-(-WIN//16)*16; EDGE=-(-(SLAB-WIN//2)//16)*16
    part=-(-WIN//16)*8
    nh=-(-T//256)
    rows,more=dcat.shape[-2:]; cols=3*cq
    sd=jax.ShapeDtypeStruct; dma=pltpu.SemaphoreType.DMA; v=pltpu.VMEM
    return pl.pallas_call(functools.partial(kernel_bc,NH),grid=(nW,),
      in_specs=[per((WIN,D)),per((WIN,D),pipeline_mode=ONE),per((3,WIN,D)),per((WIN,D)),per((D,WIN)),per((NH,WIN)),per(Pp.shape[1:]),per((WIN,GROUP)),
        full((2,D,cols),pipeline_mode=ONE),full(gains.shape),full(shifts.shape),full(sm.shape),full(pp.shape,pipeline_mode=ONE),pl.BlockSpec((WIN-Q,WIN),lambda w:(Q//(WIN-Q),0)),ANY,ANY],
      out_specs=[ANY,ANY,ANY,ANY,full((rows,cols),pipeline_mode=ONE),full((rows,more),pipeline_mode=ONE),full((NH//2,nh*256),pipeline_mode=ONE),full(sm.shape)],
      out_shape=[sd((2*nW,SLAB,D),BF),sd((EDGE,D),BF),sd((2,SLAB,D),BF),sd((EDGE,D),BF),sd((rows,cols),F32),sd((rows,more),F32),sd((NH//2,nh*256),F32),sd(sm.shape,F32)],
      scratch_shapes=[v((tiles,NH*WIN,128),F32),v((tiles,NH*part,128),F32),v((WIN,GROUP),F32),v((WIN,GROUP),F32),v((PER*SLAB,GROUP),BF),v((WIN,PER*Q),BF),v((WIN,GROUP),BF),v((GROUP,D),BF),v((GROUP,D),BF),v((2,D,cols),F32),v((2,2,2,2,2,rows,cols),BF),v((D,WIN),BF),v((3,WIN,D),BF),v((D,WIN),F32),
        v((nW,SLAB,D),BF),v(sm.shape,F32),v((nh,NH,256),F32),v((2,nh+2,8,256),F32),v((32,8,256),F32),v((nh+2,8,256),F32),
        dma((NH,)),dma((NH,)),dma((2,)),dma((nW,)),dma((nW,)),dma((nW,)),dma((2,)),dma,dma((6,)),dma((2*nh+4,)),dma((32,)),dma((16,)),dma((nh+2,))]+reduce_scratch(rows,cols)+reduce_scratch(rows,more),
      compiler_params=pltpu.CompilerParams(vmem_limit_bytes=63*1024*1024,dimension_semantics=("arbitrary",),collective_id=3,has_side_effects=True),
      name="kernel_bc")(x,gln2,qkv,g,gT,Dd,Pp,Pr,W1,gains,shifts,sm,pp,pos_index,dcat,dlast)


def kernel_f(in_ref,og_ref,ev_ref,evl_ref,ev2_ref,hd_ref,hd2_ref,redq_ref,redm_ref,tab_ref,sum_ref,
             out_ref,din_ref,dqkv_ref,dproj_ref,dfc1_ref,dfc2_ref,dgain_ref,dshift_ref,dtab_ref,end_s):
    j=pl.program_id(0); nw=pl.num_programs(0)//2
    shift=in_ref.shape[0]//2; WIN=2*shift
    edge,SLAB=hd_ref.shape[0],ev_ref.shape[1]
    off=edge-(SLAB-shift)
    @pl.when(j==0)
    def _():
        end_s[0]=hd_ref[...].astype(F32); end_s[1]=hd2_ref[...].astype(F32)
        cq=dqkv_ref.shape[2]; cf=dfc1_ref.shape[1]
        for k in range(3): dqkv_ref[k]=redq_ref[:,k*cq:(k+1)*cq]
        dproj_ref[...]=redm_ref[:,0:cq]
        dfc1_ref[...]=redm_ref[:,cq:cq+cf]
        dfc2_ref[...]=redm_ref[:,cq+cf:]
        dgain_ref[...]=sum_ref[0:2,:]; dshift_ref[...]=sum_ref[2:6,:]
        dtab_ref[...]=tab_ref[:,0:dtab_ref.shape[1]]
    e=jnp.where(j%nw==nw-1,evl_ref[0],ev_ref[0]).astype(F32)
    for k,(base,res,v) in enumerate(((in_ref,out_ref,e),(og_ref,din_ref,ev2_ref[0].astype(F32)))):
        res[0:shift,:]=base[0:shift,:]+end_s[k,off:off+shift,:]
        res[shift:WIN,:]=base[shift:WIN,:]+v[0:shift,:]
        end_s[k]=v[SLAB-edge:,:]

def call_f(inputs,og,ev,evl,ev2,hd,hd2,redq,redm,tab,small,cq,cf,T):
    tok,D=inputs.shape; n,SLAB,_=ev.shape; WIN=tok//n; rows=redq.shape[0]
    sd=jax.ShapeDtypeStruct
    blk=pl.BlockSpec((WIN,D),lambda j:(j,0)); slab=pl.BlockSpec((1,SLAB,D),lambda j:(j,0,0))
    shapes=[(3,rows,cq),(rows,cq),(rows,cf),(rows,cf),(2,D),(4,D),(tab.shape[0],T)]
    return pl.pallas_call(kernel_f,grid=(n,),
      in_specs=[blk,blk,slab,pl.BlockSpec((1,SLAB,D),lambda j:(j//(n//2),0,0)),slab]+[full(v.shape) for v in (hd,hd2,redq,redm,tab,small)],
      out_specs=[blk,blk]+[full(v) for v in shapes],
      out_shape=[sd((tok,D),F32),sd((tok,D),F32)]+[sd(v,F32) for v in shapes],
      scratch_shapes=[pltpu.VMEM((2,)+hd.shape,F32)],
      compiler_params=pltpu.CompilerParams(vmem_limit_bytes=63*1024*1024,dimension_semantics=("arbitrary",)),
      name="kernel_f")(inputs,og,ev,evl,ev2,hd,hd2,redq,redm,tab,small)

def gathered(piece,names,nseq,nheads):
    full=lax.all_gather(piece,names,axis=0,tiled=False)
    return full.reshape((nseq,nheads)+piece.shape)

def natural(block):
    s,h,r,c=block.shape
    return block.transpose(0,2,1,3).reshape(s*r,h*c)

def owners(grad,nseq,nheads):
    r,c=grad.shape
    return grad.reshape(nseq,r//nseq,nheads,c//nheads).transpose(0,2,1,3).reshape(nseq*nheads,r//nseq,c//nheads)

def from_next(rows):
    n=lax.axis_size("seq")
    return lax.ppermute(rows,"seq",[(i,(i-1)%n) for i in range(n)])

def to_next(rows):
    n=lax.axis_size("seq")
    return lax.ppermute(rows,"seq",[(i,(i+1)%n) for i in range(n)])

def spread(rows):
    n=lax.axis_size("heads")
    flat=rows.reshape(-1,rows.shape[-1])
    if n==2:
        other=lax.ppermute(flat,"heads",[(0,1),(1,0)])
        me=lax.axis_index("heads")
        return jnp.where(me==0,jnp.concatenate([flat,other]),jnp.concatenate([other,flat]))
    return lax.all_gather(flat,"heads",axis=0,tiled=True)

def place(rows,base,shift):
    every=spread(rows)
    keep=every.shape[0]-shift
    return base+jnp.concatenate([to_next(every[keep:]),every[:keep]]).astype(F32)

def body(inputs,w_qkv,w_proj,w_fc1,w_fc2,gains,shifts,rel_table,region,pos_index,out_grad):
    nseq=lax.axis_size("seq"); nheads=lax.axis_size("heads"); me=lax.axis_index("heads")
    linked=nseq==16 and nheads==2
    names=("seq","heads")
    tok,D=inputs.shape; WIN=pos_index.shape[0]; shift=WIN//2; T=rel_table.shape[1]
    nW=tok//WIN//nheads
    rows=w_qkv.shape[1]; cq=w_qkv.shape[2]; cf=w_fc1.shape[1]
    lab=region.reshape(-1,WIN)
    if linked:
        W1,bias,brem,wf,posT=call_w(w_qkv,w_proj.T,w_fc1,w_fc2.T,pos_index,rel_table)
        qkv,x,Pp,Pr,gln2,g,gT,Dd,ev,dlast,dcat,sm=call_a2(inputs,out_grad,wf,lab,bias,brem,W1,gains,shifts)
        ev2,hd2,evl,hd,redq,redm,d_table,small=call_bc(x,gln2,qkv,g,gT,Dd,Pp,Pr,W1,gains,shifts,sm,posT,pos_index,dcat.reshape(2,2,2,2,2,rows,-1),dlast,T)
        out,din,dq,dp,d1,d2,dg,dsh,dt=call_f(inputs,out_grad,ev,evl,ev2,hd,hd2,redq,redm,d_table,small,cq,cf,T)
        return (out,din,dq,dp.T,d1,d2.T,dg,dsh,dt)
    posT=pos_index.T
    wide=-(-WIN//128)*128
    posP=jnp.pad(posT,((0,0),(0,wide-WIN)))
    start=me*nW*WIN
    lab=lax.dynamic_slice_in_dim(lab,me*nW,nW,0)
    labc=lab[:,:,None]; labr=lab[:,None,:]
    wq=jnp.concatenate([w_qkv[0],w_qkv[1],w_qkv[2],w_proj.T],axis=1).astype(BF)
    wf=jnp.concatenate([w_fc1,w_fc2.T],axis=1).astype(BF)
    table=lax.all_gather(rel_table,"heads",axis=0,tiled=True)
    NH=table.shape[0]
    every=gathered(jnp.concatenate([wq,wf],axis=1),names,nseq,nheads)
    ends=[i*cq for i in range(5)]+[4*cq+cf,4*cq+2*cf]
    W=jnp.concatenate([natural(every[...,a:b]) for a,b in zip(ends[:-1],ends[1:])],axis=1)[None]
    bias=call_p(posP,pack_table(table),WIN)
    def mine(v):
        ext=jnp.concatenate([v,from_next(v[:shift])])
        return lax.dynamic_slice_in_dim(ext,start+shift,nW*WIN,0).reshape(nW,WIN,-1)
    x=mine(inputs); og=mine(out_grad)
    delta,gln2,qkv,g,gT,Dd,Pp,dcat,sm_a=call_a(x,og,labc,labr,bias,W,gains,shifts)
    dd,dqkv,G,sm_b=call_b(x,gln2,qkv,g,gT,Dd,Pp,W,gains,shifts)
    grads=[dqkv[0,:,c*D:(c+1)*D] for c in range(3)]+[dcat[0,:,:D],dcat[0,:,D:D+cf*nheads],dcat[0,:,D+cf*nheads:]]
    red=lax.psum_scatter(jnp.concatenate([owners(v,nseq,nheads) for v in grads],axis=2),names,scatter_dimension=0,tiled=False).astype(F32)
    redq,redm=red[:,:3*cq],red[:,3*cq:]
    d_table,small=lax.psum((call_t(G,posT,T,NH),sm_a+sm_b),names)
    nl=rel_table.shape[0]
    d_table=lax.dynamic_slice_in_dim(d_table,me*nl,nl,0)
    output=place(delta,inputs,shift)
    d_inputs=place(dd,out_grad,shift)
    d_qkv=redq.reshape(rows,3,cq).transpose(1,0,2)
    d_proj=redm[:,:cq].T; d_fc1=redm[:,cq:cq+cf]; d_fc2=redm[:,cq+cf:].T
    return (output,d_inputs,d_qkv,d_proj,d_fc1,d_fc2,small[0:2],small[2:6],d_table)

def solution(mesh):
    placed=(P("seq",None),P(None,"seq","heads"),P("heads","seq"),P("seq","heads"),P("heads","seq"),P(),P(),P("heads",None),P("seq"),P(),P("seq",None))
    return jax.shard_map(body,mesh=mesh,in_specs=placed,
    out_specs=(P("seq",None),P("seq",None),P(None,"seq","heads"),P("heads","seq"),P("seq","heads"),P("heads","seq"),P(),P(),P("heads",None)),
    check_vma=False)
```

```python
import functools
import math

import jax, jax.numpy as jnp
from jax import lax
from jax.experimental import pallas as pl
from jax.experimental.pallas import tpu as pltpu
from jax.sharding import PartitionSpec as P

BF=jnp.bfloat16; F32=jnp.float32
HD=32; GROUP=128; PER=4
EPS=1e-5
SQ=math.sqrt(32.0)
CEXP=math.log2(math.e)/SQ
MASK=100.0*SQ

def mm(a,b):
    return lax.dot_general(a,b,(((1,),(0,)),((),())),preferred_element_type=F32)
def mm_nt(a,b):
    return lax.dot_general(a,b,(((1,),(1,)),((),())),preferred_element_type=F32)

def norm_stats(v):
    mean=jnp.mean(v,axis=-1,keepdims=True)
    c=v-mean
    var=jnp.mean(c*c,axis=-1,keepdims=True)
    rstd=lax.rsqrt(var+EPS)
    return c*rstd, rstd

def norm_back(gy,xhat,rstd,gain):
    gx=gy*gain
    m1=jnp.mean(gx,axis=-1,keepdims=True)
    m2=jnp.mean(gx*xhat,axis=-1,keepdims=True)
    return rstd*(gx-m1-xhat*m2)

P0=0.3275911
A1,A2,A3,A4,A5=0.254829592,-0.284496736,1.421413741,-1.453152027,1.061405429
def gelu_both(x):
    e=jnp.exp2(x*x*(-0.5*math.log2(math.e)))
    t=1.0/(1.0+(P0/math.sqrt(2.0))*jnp.abs(x))
    poly=t*(0.5*A1+t*(0.5*A2+t*(0.5*A3+t*(0.5*A4+t*(0.5*A5)))))
    half=poly*e
    phi=jnp.where(x>=0,1.0-half,half)
    return x*phi, phi+x*e*(1.0/math.sqrt(2.0*math.pi))

def kernel_a(nheads,x_ref,og_ref,labc_ref,labr_ref,bias_ref,W_ref,gains_ref,shifts_ref,
             delta_ref,gln2_ref,qkv_ref,g_ref,gT_ref,D_ref,P_hbm,dcat_ref,small_ref,
             qT_s,vT_s,OT_s,P_s,acc,sem,xn2_s,xn2T_s,tg_s,tgT_s,up_s,gn2_s):
    w=pl.program_id(0); nw=pl.num_programs(0)
    D=x_ref.shape[-1]; WIN=x_ref.shape[-2]
    parts=W_ref.shape[0]; cq=D//parts; cf=(W_ref.shape[2]-4*cq)//2
    groups=nheads//PER
    x=x_ref[0]
    xhat,_=norm_stats(x)
    xn=(xhat*gains_ref[0:1,:]+shifts_ref[0:1,:]).astype(BF)
    for c in range(3):
        for m in range(parts):
            at=slice(m*cq,(m+1)*cq)
            y=mm(xn,W_ref[m,:,c*cq:(c+1)*cq]).astype(BF)
            qkv_ref[0,c,:,at]=y
            if c==0: qT_s[at,:]=y.T
            if c==2: vT_s[at,:]=y.T
    labc=labc_ref[0]; labr=labr_ref[0]
    lane=lax.broadcasted_iota(jnp.int32,(WIN,GROUP),1)
    oh=jnp.where((labc==lane)|((labc+3)==lane),1.0,0.0).astype(BF)
    hi=564.0
    lo=MASK-hi
    sub=lax.broadcasted_iota(jnp.int32,(GROUP,WIN),0)
    nm=jnp.where(sub<3,jnp.where(sub!=labr,-hi,0.0),jnp.where(sub<6,jnp.where(sub-3!=labr,-lo,0.0),0.0)).astype(BF)
    hl=lane//HD

    def group(gi,_):
        slot=gi%2
        step=w*groups+gi
        @pl.when(step>=2)
        def _():
            pltpu.make_async_copy(P_s.at[slot],P_hbm.at[0,pl.ds(0,PER)],sem.at[slot]).wait()
        o=pl.multiple_of(gi*GROUP,GROUP)
        qTg=jnp.concatenate([qT_s[pl.ds(o,GROUP),:],nm],axis=0)
        kg=qkv_ref[0,1,:,pl.ds(o,GROUP)]
        for hh in range(PER):
            kh=jnp.concatenate([jnp.where(hl==hh,kg,jnp.zeros_like(kg)),oh],axis=1)
            t=mm(kh,qTg)+bias_ref[gi*PER+hh]
            m=jnp.max(t,axis=0,keepdims=True)
            e=jnp.exp2((t-m)*CEXP)
            l=jnp.sum(e,axis=0,keepdims=True)
            p=(e*(1.0/l)).astype(BF)
            P_s[slot,hh]=p
            OT_s[pl.ds(o+hh*HD,HD),:]=mm(vT_s[pl.ds(o+hh*HD,HD),:],p)
        pltpu.make_async_copy(P_s.at[slot],P_hbm.at[w,pl.ds(gi*PER,PER)],sem.at[slot]).start()
        return 0
    lax.fori_loop(0,groups,group,0)

    attn=OT_s[...].astype(BF).T
    branch=shifts_ref[2:3,:]
    for m in range(parts):
        branch=branch+mm_nt(attn[:,m*cq:(m+1)*cq],W_ref[m,:,3*cq:4*cq])
    branch=branch.astype(BF).astype(F32)
    middle=x+branch
    xhat2,rstd2=norm_stats(middle)
    xn2=(xhat2*gains_ref[1:2,:]+shifts_ref[1:2,:]).astype(BF)
    og=og_ref[0]
    tg=og.astype(BF)
    xn2_s[...]=xn2; xn2T_s[...]=xn2.T; tg_s[...]=tg; tgT_s[...]=tg.T
    up_s[...]=jnp.zeros_like(up_s); gn2_s[...]=jnp.zeros_like(gn2_s)
    CH=min(512,cf); each=cf//CH
    @pl.when(w==0)
    def _():
        acc[...]=jnp.zeros_like(acc)
        small_ref[...]=jnp.zeros_like(small_ref)
    def chunk(c,_):
        m=c//each
        o=pl.multiple_of((c%each)*CH,CH)
        f1=W_ref[m,:,pl.ds(4*cq+o,CH)]; f2=W_ref[m,:,pl.ds(4*cq+cf+o,CH)]
        hid=mm(xn2_s[...],f1)
        act,dact=gelu_both(hid)
        a=act.astype(BF)
        up_s[...]+=mm_nt(a,f2)
        gh=(mm(tg_s[...],f2)*dact).astype(BF)
        gn2_s[...]+=mm_nt(gh,f1)
        acc[m,:,pl.ds(cq+o,CH)]+=mm(xn2T_s[...],gh)
        acc[m,:,pl.ds(cq+cf+o,CH)]+=mm(tgT_s[...],a)
        return 0
    lax.fori_loop(0,parts*each,chunk,0)
    delta_ref[0]=(branch+up_s[...]+shifts_ref[3:4,:]).astype(BF)
    gn2=gn2_s[...]
    gln2=norm_back(gn2,xhat2,rstd2,gains_ref[1:2,:])
    gln2_ref[0]=gln2
    gb=(og+gln2).astype(BF)
    gbT=gb.T
    for m in range(parts):
        at=slice(m*cq,(m+1)*cq)
        acc[m,:,0:cq]+=mm(gbT,attn[:,at])
        g=mm(gb,W_ref[m,:,3*cq:4*cq]).astype(BF)
        g_ref[0,:,at]=g
        gT=g.T
        gT_ref[0,at,:]=gT
        prod=gT.astype(F32)*OT_s[at,:]
        nh=nheads//parts
        D_ref[0,m*nh:(m+1)*nh,:]=jnp.sum(prod.reshape(nh,HD,WIN),axis=1)
    small_ref[1:2,:]+=jnp.sum(gn2*xhat2,axis=0,keepdims=True)
    small_ref[3:4,:]+=jnp.sum(gn2,axis=0,keepdims=True)
    small_ref[4:5,:]+=jnp.sum(gb.astype(F32),axis=0,keepdims=True)
    small_ref[5:6,:]+=jnp.sum(tg.astype(F32),axis=0,keepdims=True)
    @pl.when(w==nw-1)
    def _():
        dcat_ref[...]=acc[...].astype(BF)
        for s in range(2):
            pltpu.make_async_copy(P_s.at[s],P_hbm.at[0,pl.ds(0,PER)],sem.at[s]).wait()

def full(shape,**kw):
    return pl.BlockSpec(shape,lambda w:(0,)*len(shape),**kw)
def per(shape,**kw):
    return pl.BlockSpec((1,)+shape,lambda w:(w,)+(0,)*len(shape),**kw)
ONE=pl.Buffered(1)
ANY=pl.BlockSpec(memory_space=pl.ANY)

def call_a(x,og,labc,labr,bias,W,gains,shifts):
    nW,WIN,D=x.shape; NH=bias.shape[0]
    parts,_,Ct=W.shape; Cg=Ct-3*(D//parts)
    sd=jax.ShapeDtypeStruct
    outs=[sd((nW,WIN,D),BF),sd((nW,WIN,D),F32),sd((nW,3,WIN,D),BF),sd((nW,WIN,D),BF),sd((nW,D,WIN),BF),sd((nW,NH,WIN),F32),
          sd((nW,NH,WIN,WIN),BF),sd((parts,D,Cg),BF),sd((8,D),F32)]
    return pl.pallas_call(functools.partial(kernel_a,NH),grid=(nW,),
      in_specs=[per((WIN,D)),per((WIN,D)),per((WIN,1)),per((1,WIN)),full((NH,WIN,WIN),pipeline_mode=ONE),
        full((parts,D,Ct),pipeline_mode=ONE),full(gains.shape),full(shifts.shape)],
      out_specs=[per((WIN,D)),per((WIN,D)),per((3,WIN,D)),per((WIN,D)),per((D,WIN)),per((NH,WIN)),ANY,full((parts,D,Cg)),full((8,D))],
      out_shape=outs,
      scratch_shapes=[pltpu.VMEM((D,WIN),BF),pltpu.VMEM((D,WIN),BF),pltpu.VMEM((D,WIN),F32),pltpu.VMEM((2,PER,WIN,WIN),BF),
        pltpu.VMEM((parts,D,Cg),F32),pltpu.SemaphoreType.DMA((2,)),
        pltpu.VMEM((WIN,D),BF),pltpu.VMEM((D,WIN),BF),pltpu.VMEM((WIN,D),BF),pltpu.VMEM((D,WIN),BF),pltpu.VMEM((WIN,D),F32),pltpu.VMEM((WIN,D),F32)],
      compiler_params=pltpu.CompilerParams(vmem_limit_bytes=62*1024*1024,dimension_semantics=("arbitrary",)),
      name="kernel_a")(x,og,labc,labr,bias,W,gains,shifts)

def kernel_b(nheads,x_ref,gln2_ref,qkv_ref,g_ref,gT_ref,D_ref,P_ref,W_ref,gains_ref,shifts_ref,
             dd_ref,dqkv_ref,G_hbm,small_ref,G_s,aq,kT_s,gq_s,gqT_s,sem):
    w=pl.program_id(0); nw=pl.num_programs(0)
    D=x_ref.shape[-1]; WIN=x_ref.shape[-2]
    parts=W_ref.shape[0]; cq=D//parts
    groups=nheads//PER
    @pl.when(w==0)
    def _():
        aq[...]=jnp.zeros_like(aq); G_s[...]=jnp.zeros_like(G_s); small_ref[...]=jnp.zeros_like(small_ref)
    kT_s[...]=qkv_ref[0,1].T
    lane=lax.broadcasted_iota(jnp.int32,(WIN,GROUP),1)
    hl=lane//HD
    def group(gi,_):
        o=pl.multiple_of(gi*GROUP,GROUP)
        gTg=gT_ref[0,pl.ds(o,GROUP),:]
        vg=qkv_ref[0,2,:,pl.ds(o,GROUP)]
        qg=qkv_ref[0,0,:,pl.ds(o,GROUP)]
        gg=g_ref[0,:,pl.ds(o,GROUP)]
        dv=jnp.zeros((WIN,GROUP),F32); dk=jnp.zeros((WIN,GROUP),F32)
        zero=jnp.zeros_like(vg)
        for hh in range(PER):
            h=gi*PER+hh
            p=P_ref[0,h]
            dp=mm(jnp.where(hl==hh,vg,zero),gTg)
            ds_=p.astype(F32)*(dp-D_ref[0,pl.ds(h,1),:])
            for c in range(G_s.shape[0]):
                wd=min(128,WIN-c*128)
                G_s[c,pl.ds(pl.multiple_of(h*WIN,8),WIN),:wd]+=ds_[:,c*128:c*128+wd]
            dsl=ds_.astype(BF)
            dv+=mm(p,jnp.where(hl==hh,gg,zero))
            dk+=mm(dsl,jnp.where(hl==hh,qg,zero))
            gqT_s[pl.ds(o+hh*HD,HD),:]=mm(kT_s[pl.ds(o+hh*HD,HD),:],dsl)
        gq_s[1,:,pl.ds(o,GROUP)]=(dk*(1.0/SQ)).astype(BF)
        gq_s[2,:,pl.ds(o,GROUP)]=dv.astype(BF)
        return 0
    lax.fori_loop(0,groups,group,0)
    gq_s[0]=(gqT_s[...]*(1.0/SQ)).astype(BF).T
    x=x_ref[0]
    xhat,rstd=norm_stats(x)
    xn=(xhat*gains_ref[0:1,:]+shifts_ref[0:1,:]).astype(BF)
    xnT=xn.T
    gr=jnp.zeros((WIN,D),F32)
    for m in range(parts):
        for c in range(3):
            gc=gq_s[c,:,m*cq:(m+1)*cq]
            gr=gr+mm_nt(gc,W_ref[m,:,c*cq:(c+1)*cq])
            aq[m,:,c*cq:(c+1)*cq]+=mm(xnT,gc)
    dd_ref[0]=(gln2_ref[0]+norm_back(gr,xhat,rstd,gains_ref[0:1,:])).astype(BF)
    small_ref[0:1,:]+=jnp.sum(gr*xhat,axis=0,keepdims=True)
    small_ref[2:3,:]+=jnp.sum(gr,axis=0,keepdims=True)
    @pl.when(w==nw-1)
    def _():
        dqkv_ref[...]=aq[...].astype(BF)
        cp=pltpu.make_async_copy(G_s,G_hbm,sem); cp.start(); cp.wait()

def call_b(x,gln2,qkv,g,gT,Dd,Pp,W,gains,shifts):
    nW,WIN,D=x.shape; NH=Dd.shape[1]
    parts=W.shape[0]; cq=D//parts; tiles=-(-WIN//128)
    sd=jax.ShapeDtypeStruct
    return pl.pallas_call(functools.partial(kernel_b,NH),grid=(nW,),
      in_specs=[per((WIN,D)),per((WIN,D)),per((3,WIN,D)),per((WIN,D)),per((D,WIN)),per((NH,WIN)),per((NH,WIN,WIN)),
        full((parts,D,3*cq),pipeline_mode=ONE),full(gains.shape),full(shifts.shape)],
      out_specs=[per((WIN,D)),full((parts,D,3*cq)),ANY,full((8,D))],
      out_shape=[sd((nW,WIN,D),BF),sd((parts,D,3*cq),BF),sd((tiles,NH*WIN,128),F32),sd((8,D),F32)],
      scratch_shapes=[pltpu.VMEM((tiles,NH*WIN,128),F32),pltpu.VMEM((parts,D,3*cq),F32),pltpu.VMEM((D,WIN),BF),pltpu.VMEM((3,WIN,D),BF),pltpu.VMEM((D,WIN),F32),
        pltpu.SemaphoreType.DMA],
      compiler_params=pltpu.CompilerParams(vmem_limit_bytes=62*1024*1024,dimension_semantics=("arbitrary",)),
      name="kernel_b")(x,gln2,qkv,g,gT,Dd,Pp,W,gains,shifts)

FIX=8191.0

def pack_table(table):
    NH,T=table.shape
    n=-(-T//128)
    q=jnp.round(jnp.clip(table,-4.0,4.0)*FIX).astype(jnp.int32)
    q=jnp.pad(q,((0,0),(0,n*128-T)))
    q=q.reshape(NH//2,2,n,128)
    return (q[:,0]*65536)|(q[:,1]&65535)

def kernel_p(pos_ref,tab_ref,bias_ref):
    npair,n,_=tab_ref.shape
    WIN=bias_ref.shape[-1]
    tiles=-(-WIN//128)
    def row(r,_):
        r8=pl.multiple_of(r*8,8)
        for c in range(tiles):
            width=min(128,WIN-c*128)
            idx=pos_ref[pl.ds(r8,8),c*128:(c+1)*128]
            lo=idx&127; hi=idx>>7
            masks=[hi==k for k in range(n)]
            for p in range(npair):
                acc=jnp.zeros((8,128),jnp.int32)
                for k in range(n):
                    src=jnp.broadcast_to(tab_ref[p,k:k+1,:],(8,128))
                    acc=jnp.where(masks[k],jnp.take_along_axis(src,lo,axis=1),acc)
                a=(acc>>16).astype(F32)*(SQ/FIX)
                b=((acc<<16)>>16).astype(F32)*(SQ/FIX)
                bias_ref[2*p,pl.ds(r8,8),c*128:c*128+width]=a[:,:width]
                bias_ref[2*p+1,pl.ds(r8,8),c*128:c*128+width]=b[:,:width]
        return 0
    lax.fori_loop(0,bias_ref.shape[1]//8,row,0)

def call_p(posT_pad,tab,WIN):
    NH=tab.shape[0]*2
    return pl.pallas_call(kernel_p,out_shape=jax.ShapeDtypeStruct((NH,WIN,WIN),F32),
      compiler_params=pltpu.CompilerParams(vmem_limit_bytes=40*1024*1024),name="kernel_p")(posT_pad,tab)

def kernel_t(NH,G_ref,hi_ref,lo_ref,out_ref):
    WIN=hi_ref.shape[0]; LW=G_ref.shape[0]*128
    nh=out_ref.shape[0]//NH
    out_ref[...]=jnp.zeros_like(out_ref)
    def rows(r,_):
        r8=pl.multiple_of(r*8,8)
        hi8=hi_ref[pl.ds(r8,8),:]; lo8=lo_ref[pl.ds(r8,8),:]
        tot=jnp.zeros(out_ref.shape,F32)
        iota=lax.broadcasted_iota(jnp.int32,(256,LW),0).astype(F32).astype(BF)
        for k in range(8):
            g=jnp.concatenate([G_ref[c,pl.ds(r8+k,NH,stride=WIN),:] for c in range(LW//128)],axis=1)
            hr=hi8[k:k+1,:]; lr=lo8[k:k+1,:].astype(F32).astype(BF)
            A=jnp.concatenate([jnp.where(hr==m,g,0.0) for m in range(nh)],axis=0).astype(BF)
            oh=jnp.where(iota==lr,jnp.ones((),BF),jnp.zeros((),BF))
            tot=tot+lax.dot_general(A,oh,(((1,),(1,)),((),())),preferred_element_type=F32)
        out_ref[...]+=tot
        return 0
    lax.fori_loop(0,WIN//8,rows,0)

def call_t(G,posT,T,NH):
    WIN=posT.shape[0]; nt=G.shape[0]
    nh=-(-T//256)
    pp=jnp.pad(posT,((0,0),(0,nt*128-WIN)),constant_values=nh*256)
    hi=pp>>8; lo=pp&255
    o=pl.pallas_call(functools.partial(kernel_t,NH),out_shape=jax.ShapeDtypeStruct((nh*NH,256),F32),
      compiler_params=pltpu.CompilerParams(vmem_limit_bytes=40*1024*1024),name="kernel_t")(G,hi,lo)
    return o.reshape(nh,NH,256).transpose(1,0,2).reshape(NH,nh*256)[:,:T]


MESHID=pl.DeviceIdType.MESH

def place_of():
    s=lax.axis_index("seq"); y=lax.axis_index("heads")
    return s//4,(s//2)%2,s%2,y

def dev(z,x,c,y):
    return ((z*2+x)*2+c,y)

def peers_of(z,x,c,y):
    return [dev(z,x,1-c,y),dev(z,1-x,c,y),dev(z,x,c,1-y)]+[dev((z+i)%4,x,c,y) for i in (1,2,3)]

def hail(devices):
    bar=pltpu.get_barrier_semaphore()
    for d in devices:
        pl.semaphore_signal(bar,inc=1,device_id=d,device_id_type=MESHID)

def heard(devices):
    pl.semaphore_wait(pltpu.get_barrier_semaphore(),len(devices))

def greet(devices):
    hail(devices)
    heard(devices)

def send(src,dst,ss,rs,to):
    return pltpu.make_async_remote_copy(src_ref=src,dst_ref=dst,send_sem=ss,recv_sem=rs,device_id=to,device_id_type=MESHID)


class Gather:
    def __init__(self,src,dst,ss,rs,own):
        self.src,self.dst,self.ss,self.rs,self.own=src,dst,ss,rs,own
        z,x,c,y=self.at=place_of()
        self.xa=x+(1-2*x)*(1-c); self.ya=y+(1-2*y)*c
        self.xb=x+(1-2*x)*c; self.yb=y+(1-2*y)*(1-c)
        self.sib=dev(z,x,1-c,y); self.pa=dev(z,self.xa,c,self.ya); self.pb=dev(z,self.xb,c,self.yb)
    def slot(self,zz,xx,cc,yy):
        n=self.src.shape[0]
        return self.dst.at[yy,pl.ds(pl.multiple_of(((zz*2+xx)*2+cc)*n,n),n)]
    def copy(self,src,where,k,to):
        return send(src,self.slot(*where),self.ss.at[k],self.rs.at[k],to)
    def go(self,where,k,to,src=None):
        self.copy(self.slot(*where) if src is None else src,where,k,to).start()
    def came(self,where,k):
        self.copy(self.src,where,k,self.sib).wait_recv()
    def keep(self):
        z,x,c,y=self.at
        return pltpu.make_async_copy(self.src,self.slot(z,x,c,y),self.own)
    def start(self):
        z,x,c,y=self.at
        me=(z,x,c,y)
        self.keep().start()
        for i in (1,2,3):
            self.go(me,i-1,dev((z+i)%4,x,c,y),self.src)
        self.go(me,3,self.pa,self.src); self.go(me,7,self.pb,self.src); self.go(me,15,self.sib,self.src)
    def z(self,i):
        return (self.at[0]+4-i)%4
    def turn_z(self,i):
        z,x,c,y=self.at
        at=(self.z(i),x,c,y); self.came(at,i-1)
        self.go(at,3+i,self.pa); self.go(at,7+i,self.pb); self.go(at,15+i,self.sib)
    def turn_a(self,i):
        at=(self.z(i),self.xa,self.at[2],self.ya); self.came(at,3+i)
        self.go(at,11+i,self.pb); self.go(at,19+i,self.sib)
    def turn_b(self,i):
        at=(self.z(i),self.xb,self.at[2],self.yb); self.came(at,7+i)
        self.go(at,23+i,self.sib)
    def turn_ab(self,i):
        z,x,c,y=self.at
        at=(self.z(i),1-x,c,1-y); self.came(at,11+i)
        self.go(at,27+i,self.sib)
    def last(self):
        z,x,c,y=self.at
        for i in range(4):
            zz=self.z(i)
            self.came((zz,x,1-c,y),15+i); self.came((zz,self.xb,1-c,self.yb),19+i)
            self.came((zz,self.xa,1-c,self.ya),23+i); self.came((zz,1-x,1-c,1-y),27+i)
    def drain(self):
        z,x,c,y=self.at
        for k in range(31):
            self.copy(self.src,(z,x,c,y),k,self.sib).wait_send()
        self.keep().wait()

def gather_sems():
    return [pltpu.SemaphoreType.DMA((31,)),pltpu.SemaphoreType.DMA((31,)),pltpu.SemaphoreType.DMA]

STEPS=7
def kernel_w(qkv_ref,proj_ref,fc1_ref,fc2_ref,pos_ref,tab_ref,W_hbm,bias_hbm,brem_hbm,wf_ref,posT_ref,
             bias_s,brem_s,tail_s,wq_s,tb,tq,ss,rs,own,bs,br,bl,tsem,ed):
    z,x,c,y=place_of()
    cq=qkv_ref.shape[2]; cf=fc1_ref.shape[1]
    for k in range(3): wq_s[:,k*cq:(k+1)*cq]=qkv_ref[k].astype(BF)
    wq_s[:,3*cq:4*cq]=proj_ref[...].astype(BF)
    lead=wq_s.shape[1]-4*cq
    wq_s[:,4*cq:]=fc1_ref[:,0:lead].astype(BF)
    half,T=tab_ref.shape
    tb[2]=jnp.zeros(tb.shape[1:],F32)
    tb[2,:,0:T]=tab_ref[...]
    greet(peers_of(z,x,c,y))
    gather=Gather(wq_s,W_hbm,ss,rs,own)
    swap=send(tb.at[2],tb.at[y],tsem.at[0],tsem.at[1],dev(z,x,c,1-y))
    swap.start()
    gather.start()
    tb[y]=tb[2]
    wf_ref[:,0:cf-lead]=fc1_ref[:,lead:].astype(BF)
    wf_ref[:,cf-lead:]=fc2_ref[...].astype(BF)
    WIN,Q=bias_s.shape[-2:]; tiles=-(-WIN//128); n=tb.shape[2]//128
    posT_ref[...]=jnp.full(posT_ref.shape,1<<15,jnp.int32)
    posT_ref[:,0:WIN]=pos_ref[...].astype(F32).T.astype(jnp.int32)
    swap.wait()
    npair=half//2
    for p in range(npair):
        a,b=[jnp.floor(jnp.clip(tb[c,2*p+k:2*p+k+1,:],-4.0,4.0)*FIX+0.5).astype(jnp.int32) for k in range(2)]
        tq[p:p+1,:]=(a*65536)|(b&65535)
    nrow=WIN//8
    cuts=[nrow*k//STEPS for k in range(STEPS+1)]
    sib=dev(z,x,1-c,y)
    def rows_of(k): return pl.ds(cuts[k]*8,(cuts[k+1]-cuts[k])*8)
    def kept(k): return pltpu.make_async_copy(bias_s.at[:,rows_of(k)],bias_hbm.at[pl.ds(c*half,half),rows_of(k)],bl.at[k])
    def sent(k,cc): return send(bias_s.at[:,rows_of(k)],bias_hbm.at[pl.ds(cc*half,half),rows_of(k)],bs.at[k],br.at[k],sib)
    def rows(k):
        def row(r,_):
            r8=pl.multiple_of(r*8,8)
            for t in range(tiles):
                width=min(128,WIN-t*128)
                idx=posT_ref[pl.ds(r8,8),t*128:(t+1)*128]
                lo=idx&127; hi=idx>>7
                masks=[hi==q for q in range(n)]
                for p in range(npair):
                    acc=jnp.zeros((8,128),jnp.int32)
                    for q in range(n):
                        src=jnp.broadcast_to(tq[p:p+1,q*128:(q+1)*128],(8,128))
                        acc=jnp.where(masks[q],jnp.take_along_axis(src,lo,axis=1),acc)
                    a=(acc>>16).astype(F32)*(SQ/FIX)
                    b=((acc<<16)>>16).astype(F32)*(SQ/FIX)
                    for h,v in ((2*p,a),(2*p+1,b)):
                        if width==128: bias_s[h,pl.ds(r8,8),t*128:(t+1)*128]=v
                        else: tail_s[h,pl.ds(r8,8),:]=v
            return 0
        lax.fori_loop(cuts[k],cuts[k+1],row,0)
        kept(k).start(); sent(k,c).start()
    rows(0)
    rows(1)
    for i in (1,3,2): gather.turn_z(i)
    for i in (0,): gather.turn_a(i); gather.turn_b(i)
    rows(2)
    rows(3)
    for i in (1,3,2): gather.turn_a(i); gather.turn_b(i)
    gather.turn_ab(0)
    rows(4)
    rows(5)
    for i in (1,3,2): gather.turn_ab(i)
    rows(6)
    R=WIN-Q
    owner=lax.broadcasted_iota(jnp.int32,brem_s.shape,1)//R
    joined=tail_s[0]
    for h in range(1,half): joined=jnp.where(owner==h,pltpu.roll(tail_s[h],h*R,1),joined)
    brem_s[...]=joined
    edges=[pltpu.make_async_copy(brem_s,brem_hbm.at[c],ed.at[0]),send(brem_s,brem_hbm.at[c],ed.at[1],ed.at[2],sib)]
    for e in edges: e.start()
    gather.last()
    for e in edges: e.wait()
    for k in range(STEPS):
        kept(k).wait(); sent(k,c).wait_send(); sent(k,1-c).wait_recv()
    gather.drain()

def call_w(w_qkv,w_proj,w_fc1,w_fc2,pos_index,rel_table):
    rows,cq=w_qkv.shape[1:]; cf=w_fc1.shape[1]; WIN=pos_index.shape[0]; half,T=rel_table.shape; dma=pltpu.SemaphoreType.DMA
    wide=-(-WIN//128)*128; Q=WIN//128*128; n=-(-T//128); mem=pltpu.VMEM
    early=4*cq+min(512,cf); late=4*cq+2*cf-early
    sd=jax.ShapeDtypeStruct
    return pl.pallas_call(kernel_w,grid=(1,),
      out_shape=[sd((2,16*rows,early),BF),sd((2*half,WIN,Q),F32),sd((2,WIN,128),F32),sd((rows,late),BF),sd((WIN,wide),jnp.int32)],
      in_specs=[full(v.shape) for v in (w_qkv,w_proj,w_fc1,w_fc2,pos_index,rel_table)],out_specs=[ANY,ANY,ANY,full((rows,late)),full((WIN,wide))],
      scratch_shapes=[mem((half,WIN,Q),F32),mem((WIN,128),F32),mem((half,WIN,128),F32),mem((rows,early),BF),mem((3,half,n*128),F32),mem((half//2,n*128),jnp.int32)]
        +gather_sems()+[dma((STEPS,)),dma((STEPS,)),dma((STEPS,)),dma((2,)),dma((3,))],
      compiler_params=pltpu.CompilerParams(vmem_limit_bytes=63*1024*1024,collective_id=1,has_side_effects=True),name="kernel_w")(w_qkv,w_proj,w_fc1,w_fc2,pos_index,rel_table)

def neighbours(z,x,c,y):
    s=(z*2+x)*2+c
    return [((s+k)%16,yy) for k in (1,15) for yy in (y,1-y)]

def pick(shape,test):
    r=lax.broadcasted_iota(jnp.int32,shape,0); c=lax.broadcasted_iota(jnp.int32,shape,1)
    return jnp.where(test(r,c),1.0,0.0)

def exact(a,b):
    return lax.dot_general(a,b,(((1,),(0,)),((),())),precision=lax.Precision.HIGHEST,preferred_element_type=F32)

def kernel_a2(nheads,in_hbm,og_hbm,wf_hbm,lab_ref,bias_ref,brem_ref,W1,gains_ref,shifts_ref,
              qkv_ref,x_ref,P_hbm,pr_ref,gln2_ref,g_ref,gT_ref,D_ref,ev_hbm,dlast_hbm,dcat_hbm,small_ref,
              x_s,og_s,W2,OT_s,qT_s,vT_s,P_s,kst_s,acc,pst,xn2_s,xn2T_s,tg_s,tgT_s,up_s,gn2_s,dl_s,
              lab_s,psem,xsem,hsem,ss,rs,own,dl,ds,dr,fin):
    i=pl.program_id(0); nw=x_s.shape[0]
    w=i%nw
    z,xc,c,y=place_of()
    s=(z*2+xc)*2+c
    D=x_s.shape[-1]; WIN=qkv_ref.shape[-2]; SLAB=x_s.shape[1]; HALF=SLAB//2
    OFF=(SLAB-WIN)//2
    cq=D//2; lead=W1.shape[2]-4*cq; cf=(W2.shape[2]+lead)//2
    groups=nheads//PER; Q=bias_ref.shape[2]; R=WIN-Q
    gather=Gather(wf_hbm,W2,ss,rs,own)
    mate=dev(z,xc,c,1-y)
    def local(k,half,t):
        hbm,buf=((in_hbm,x_s),(og_hbm,og_s))[t]
        r=pl.multiple_of(y*(nw*WIN)+k*WIN+(WIN//2-OFF)+half*HALF,8)
        return pltpu.make_async_copy(hbm.at[pl.ds(r,HALF)],buf.at[k,pl.ds(half*HALF,HALF)],xsem.at[t,2*k+half])
    def edge(t):
        hbm,buf=((in_hbm,x_s),(og_hbm,og_s))[t]
        return send(hbm.at[pl.ds(0,HALF)],buf.at[nw-1,pl.ds(HALF,HALF)],hsem.at[t,0],hsem.at[t,1],((s+15)%16,1))
    def ready(t):
        local(w,0,t).wait()
        far=jnp.logical_and(w==nw-1,y==1)
        @pl.when(far)
        def _(): edge(t).wait_recv()
        @pl.when(jnp.logical_not(far))
        def _(): local(w,1,t).wait()
    def slab(k,to=None):
        if k is None: return pltpu.make_async_copy(dl_s.at[nw-1],dlast_hbm,dl.at[nw-1])
        at=ev_hbm.at[y*nw+k]
        if to is None: return pltpu.make_async_copy(dl_s.at[k],at,dl.at[k])
        return send(dl_s.at[k],at,ds.at[k],dr.at[k],to)
    everyone=peers_of(z,xc,c,y)+neighbours(z,xc,c,y)
    def met():
        heard(everyone)
        gather.start()
        @pl.when(y==1)
        def _():
            for t in range(2): edge(t).start()
    def first():
        for k in (1,3,2): gather.turn_z(k)
    def second():
        for k in (0,1,3,2): gather.turn_a(k); gather.turn_b(k)
    def third():
        for k in (0,1,3,2): gather.turn_ab(k)
    plan=((0,met),(6,first),(10,second),(14,third))
    @pl.when(i==0)
    def _():
        hail(everyone)
        for k in range(nw):
            for t in range(2):
                local(k,0,t).start()
                if k<nw-1: local(k,1,t).start()
        for t in range(2):
            @pl.when(y==0)
            def _(): local(nw-1,1,t).start()
        lab_s[...]=lab_ref[...].astype(F32).T
        acc[...]=jnp.zeros_like(acc)
        for hh in range(PER): kst_s[(hh+1)*SLAB-16:(hh+1)*SLAB,:]=jnp.zeros((16,2*GROUP),BF)
        small_ref[...]=jnp.zeros_like(small_ref)
        dl_s[:,SLAB-16:,:]=jnp.zeros((nw,16,D),BF)

    @pl.when(i<nw)
    def _():
        ready(0)
        x=x_s[w,OFF:OFF+WIN,:]
        x_ref[0]=x
        xhat,_=norm_stats(x)
        xn=(xhat*gains_ref[0:1,:]+shifts_ref[0:1,:]).astype(BF)
        for k in range(3):
            for m in range(2):
                at=slice(m*cq,(m+1)*cq)
                v=mm(xn,W1[m,:,k*cq:(k+1)*cq]).astype(BF)
                qkv_ref[0,k,:,at]=v
                if k==0: qT_s[at,:]=v.T
                if k==2: vT_s[at,:]=v.T
        mine=y*nw+w
        labr=lab_ref[pl.ds(mine,1),:]
        labc=jnp.sum(jnp.where(lax.broadcasted_iota(jnp.int32,lab_s.shape,1)==mine,lab_s[...],0.0),axis=1,keepdims=True).astype(jnp.int32)
        lane=lax.broadcasted_iota(jnp.int32,(WIN,GROUP),1)
        oh=jnp.where((labc==lane)|((labc+3)==lane),1.0,0.0).astype(BF)
        hi=564.0
        lo=MASK-hi
        sub=lax.broadcasted_iota(jnp.int32,(GROUP,WIN),0)
        nm=jnp.where(sub<3,jnp.where(sub!=labr,-hi,0.0),jnp.where(sub<6,jnp.where(sub-3!=labr,-lo,0.0),0.0)).astype(BF)
        hl=lane//HD
        for hh in range(PER): kst_s[hh*SLAB:hh*SLAB+WIN,GROUP:]=oh
        nmq=nm[:,0:Q]
        def soften(t):
            m=jnp.max(t,axis=0,keepdims=True)
            e=jnp.exp2((t-m)*CEXP)
            l=jnp.sum(e,axis=0,keepdims=True)
            return (e*(1.0/l)).astype(BF)
        def group(gi,_):
            slot=gi%2
            @pl.when(w*groups+gi>=2)
            def _():
                pltpu.make_async_copy(P_s.at[slot],P_hbm.at[0,0],psem.at[slot]).wait()
            o=pl.multiple_of(gi*GROUP,GROUP)
            qTg=jnp.concatenate([qT_s[pl.ds(o,GROUP),0:Q],nmq],axis=0)
            kg=qkv_ref[0,1,:,pl.ds(o,GROUP)]
            for hh in range(PER): kst_s[hh*SLAB:hh*SLAB+WIN,0:GROUP]=jnp.where(hl==hh,kg,jnp.zeros_like(kg))
            t4=mm(kst_s[...],qTg)
            for hh in range(PER):
                p=soften(t4[hh*SLAB:hh*SLAB+WIN]+bias_ref[gi*PER+hh])
                P_s[slot,:,hh*Q:(hh+1)*Q]=p
                OT_s[w,pl.ds(o+hh*HD,HD),0:Q]=mm(vT_s[pl.ds(o+hh*HD,HD),:],p)
            pltpu.make_async_copy(P_s.at[slot],P_hbm.at[w,gi],psem.at[slot]).start()
            for when,what in plan:
                pl.when(w*groups+gi==min(when,nw*groups-1))(what)
            return 0
        lax.fori_loop(0,groups,group,0)
        spread=pick((R,GROUP),lambda r,c: c%R==r).astype(BF)
        own_rows=pick((D,GROUP),lambda r,c: r//HD==c//R)
        qbd=(mm(qT_s[:,Q:WIN],spread)*own_rows).astype(BF)
        nmr=mm(nm[:,Q:WIN],spread).astype(BF)
        brem=jnp.concatenate([brem_ref[0,:,0:GROUP//2],brem_ref[1,:,0:GROUP//2]],axis=1)
        pr=soften(mm(qkv_ref[0,1],qbd)+mm(oh,nmr)+brem)
        pr_ref[0]=pr
        OT_s[w,:,Q:WIN]=exact(mm(vT_s[...],pr)*own_rows,pick((GROUP,R),lambda r,c: r%R==c))

    @pl.when(i==nw-1)
    def _():
        gather.last(); gather.drain()

    @pl.when(i>=nw)
    def _():
        ready(1)
        x=x_s[w,OFF:OFF+WIN,:]
        og=og_s[w,OFF:OFF+WIN,:]
        attn=OT_s[w].astype(BF).T
        branch=shifts_ref[2:3,:]
        for m in range(2):
            branch=branch+mm_nt(attn[:,m*cq:(m+1)*cq],W1[m,:,3*cq:4*cq])
        branch=branch.astype(BF).astype(F32)
        middle=x+branch
        xhat2,rstd2=norm_stats(middle)
        xn2=(xhat2*gains_ref[1:2,:]+shifts_ref[1:2,:]).astype(BF)
        tg=og.astype(BF)
        xn2_s[...]=xn2; xn2T_s[...]=xn2.T; tg_s[...]=tg; tgT_s[...]=tg.T
        up_s[...]=jnp.zeros_like(up_s); gn2_s[...]=jnp.zeros_like(gn2_s)
        CH=lead
        def side(m,_):
            for o in range(0,cf,CH):
                f1=W1[m,:,4*cq:] if o==0 else W2[m,:,o-lead:o-lead+CH]
                f2=W2[m,:,cf-lead+o:cf-lead+o+CH]
                hid=mm(xn2_s[...],f1)
                act,dact=gelu_both(hid)
                a=act.astype(BF)
                up_s[...]+=mm_nt(a,f2)
                gh=(mm(tg_s[...],f2)*dact).astype(BF)
                gn2_s[...]+=mm_nt(gh,f1)
                acc[m,:,cq+o:cq+o+CH]+=mm(xn2T_s[...],gh)
                acc[m,:,cq+cf+o:cq+cf+o+CH]+=mm(tgT_s[...],a)
            return 0
        lax.fori_loop(0,2,side,0)
        dl_s[w,0:WIN,:]=(branch+up_s[...]+shifts_ref[3:4,:]).astype(BF)
        @pl.when(w<nw-1)
        def _():
            slab(w).start(); slab(w,mate).start()
        @pl.when(w==nw-1)
        def _(): slab(None).start()
        gn2=gn2_s[...]
        gln2=norm_back(gn2,xhat2,rstd2,gains_ref[1:2,:])
        gln2_ref[0]=gln2
        gb=(og+gln2).astype(BF)
        gbT=gb.T
        for m in range(2):
            at=slice(m*cq,(m+1)*cq)
            acc[m,:,0:cq]+=mm(gbT,attn[:,at])
            g=mm(gb,W1[m,:,3*cq:4*cq]).astype(BF)
            g_ref[0,:,at]=g
            gT=g.T
            gT_ref[0,at,:]=gT
            prod=gT.astype(F32)*OT_s[w,at,:]
            nh=nheads//2
            D_ref[0,m*nh:(m+1)*nh,:]=jnp.sum(prod.reshape(nh,HD,WIN),axis=1)
        small_ref[1:2,:]+=jnp.sum(gn2*xhat2,axis=0,keepdims=True)
        small_ref[3:4,:]+=jnp.sum(gn2,axis=0,keepdims=True)
        small_ref[4:5,:]+=jnp.sum(gb.astype(F32),axis=0,keepdims=True)
        small_ref[5:6,:]+=jnp.sum(tg.astype(F32),axis=0,keepdims=True)

    @pl.when(i==2*nw-1)
    def _():
        W2[...]=acc[:,:,cq+lead:].astype(BF)
        pst[...]=acc[:,:,:cq+lead].astype(BF)
        a=pltpu.make_async_copy(W2,dcat_hbm.at[:,:,pl.ds(cq+lead,W2.shape[2])],fin.at[0])
        b=pltpu.make_async_copy(pst,dcat_hbm.at[:,:,pl.ds(0,cq+lead)],fin.at[1])
        a.start(); b.start()
        for k in range(2):
            pltpu.make_async_copy(P_s.at[k],P_hbm.at[0,0],psem.at[k]).wait()
        for k in range(nw-1):
            slab(k).wait(); slab(k,mate).wait()
        slab(None).wait()
        @pl.when(y==1)
        def _():
            for t in range(2): edge(t).wait_send()
        a.wait(); b.wait()

def call_a2(inputs,og,wf,lab,bias,brem,W1,gains,shifts):
    nW=lab.shape[0]//2; WIN=lab.shape[1]; D=inputs.shape[1]; NH=bias.shape[0]
    cq=D//2; lead=W1.shape[2]-4*cq; cf=(wf.shape[1]+lead)//2; SLAB=-(-WIN//16)*16
    Q=bias.shape[2]
    sd=jax.ShapeDtypeStruct; dma=pltpu.SemaphoreType.DMA; v=pltpu.VMEM
    early=lambda shape: pl.BlockSpec((1,)+shape,lambda i:(jnp.minimum(i,nW-1),)+(0,)*len(shape))
    late=lambda shape: pl.BlockSpec((1,)+shape,lambda i:(jnp.maximum(i-nW,0),)+(0,)*len(shape))
    outs=[sd((nW,3,WIN,D),BF),sd((nW,WIN,D),F32),sd((nW,NH//PER,WIN,PER*Q),BF),sd((nW,WIN,GROUP),BF),sd((nW,WIN,D),F32),sd((nW,WIN,D),BF),sd((nW,D,WIN),BF),sd((nW,NH,WIN),F32),
          sd((2*nW,SLAB,D),BF),sd((SLAB,D),BF),sd((2,D,cq+2*cf),BF),sd((8,D),F32)]
    return pl.pallas_call(functools.partial(kernel_a2,NH),grid=(2*nW,),
      in_specs=[ANY,ANY,ANY,full(lab.shape),full(bias.shape,pipeline_mode=ONE),full(brem.shape),full(W1.shape,pipeline_mode=ONE),full(gains.shape),full(shifts.shape)],
      out_specs=[early((3,WIN,D)),early((WIN,D)),ANY,early((WIN,GROUP)),late((WIN,D)),late((WIN,D)),late((D,WIN)),late((NH,WIN)),ANY,ANY,ANY,full((8,D))],
      out_shape=outs,
      scratch_shapes=[v((nW,SLAB,D),F32),v((nW,SLAB,D),F32),v((2,D,2*cf-lead),BF),v((nW,D,WIN),F32),v((D,WIN),BF),v((D,WIN),BF),v((2,WIN,PER*Q),BF),v((PER*SLAB,2*GROUP),BF),
        v((2,D,cq+2*cf),F32),v((2,D,cq+lead),BF),v((WIN,D),BF),v((D,WIN),BF),v((WIN,D),BF),v((D,WIN),BF),v((WIN,D),F32),v((WIN,D),F32),v((nW,SLAB,D),BF),
        v((WIN,2*nW),F32),dma((2,)),dma((2,2*nW)),dma((2,2))]+gather_sems()+[dma((nW,)),dma((nW,)),dma((nW,)),dma((2,))],
      compiler_params=pltpu.CompilerParams(vmem_limit_bytes=63*1024*1024,dimension_semantics=("arbitrary",),collective_id=2,has_side_effects=True),
      name="kernel_a2")(inputs,og,wf,lab,bias,brem,W1,gains,shifts)

class Reduce:
    def __init__(self,src,out,own,r1,bufs,ss,rs,ls):
        self.src,self.out,self.own,self.r1,self.bufs=src,out,own,r1,bufs
        self.ss,self.rs,self.ls=ss,rs,ls
        z,x,c,y=place_of()
        self.x,self.c,self.y,self.h,self.l=x,c,y,z//2,z%2
    def to(self,x=None,h=None,l=None,c=None,y=None):
        pick=lambda new,old: old if new is None else new
        return dev(pick(h,self.h)*2+pick(l,self.l),pick(x,self.x),pick(c,self.c),pick(y,self.y))
    def mine(self,k):
        return pltpu.make_async_copy(self.src.at[k%2,:,:,k//2,self.c],self.own.at[k//2,:,:,k%2],self.ls.at[k])
    def theirs(self,k):
        return send(self.src.at[k%2,:,:,k//2,1-self.c],self.r1.at[k//2,:,:,k%2],self.ss.at[k],self.rs.at[k],self.to(c=1-self.c))
    def turns(self,core):
        x,h,l,y=self.x,self.h,self.l,self.y
        s=slice(None)
        if core==0:
            return [((1-x,),dict(x=1-x),lambda a,b,d:(x,a,b,d)),((x,s,1-l),dict(l=1-l),lambda a,d:(x,a,l,d)),
                    ((x,1-h,l),dict(h=1-h),lambda d:(x,h,l,d)),((x,h,l,1-y),dict(y=1-y),None)]
        return [((s,s,1-l),dict(l=1-l),lambda a,b,d:(a,b,l,d)),((s,1-h,l),dict(h=1-h),lambda a,d:(a,h,l,d)),
                ((1-x,h,l),dict(x=1-x),lambda d:(x,h,l,d)),((x,h,l,1-y),dict(y=1-y),None)]
    def give(self,k,core):
        at,where,_=self.turns(core)[k]
        return send(self.own.at[at],self.bufs[k],self.ss.at[4+k],self.rs.at[4+k],self.to(**where))
    def start(self):
        for k in range(4):
            self.theirs(k).start(); self.mine(k).start()
    def add(self,dst,*srcs):
        total=srcs[0][...].astype(F32)
        for s in srcs[1:]: total=total+s[...].astype(F32)
        dst[...]=total.astype(dst.dtype)
    def by_core(self,f):
        for core in range(2):
            @pl.when(self.c==core)
            def _(): f(core)
    def one(self):
        for k in range(4):
            self.mine(k).wait(); self.theirs(k).wait_recv()
        def step(k,_):
            at=(k//8,(k//4)%2,(k//2)%2,k%2)
            self.add(self.own.at[at],self.own.at[at],self.r1.at[at])
            return 0
        lax.fori_loop(0,16,step,0)
        self.by_core(lambda core: self.give(0,core).start())
    def turn(self,k):
        def f(core):
            stay=self.turns(core)[k][2]
            self.give(k,core).wait_recv()
            def step(i,_):
                at=[(i//4,(i//2)%2,i%2),(i//2,i%2),(i,)][k]
                self.add(self.own.at[stay(*at)],self.own.at[stay(*at)],self.bufs[k].at[at])
                return 0
            lax.fori_loop(0,8>>k,step,0)
            self.give(k+1,core).start()
        self.by_core(f)
    def four(self):
        def f(core):
            self.give(3,core).wait_recv()
            self.add(self.out,self.own.at[self.x,self.h,self.l,self.y],self.bufs[3])
            for k in range(4): self.give(k,core).wait_send()
        self.by_core(f)
        for k in range(4): self.theirs(k).wait_send()

def reduce_scratch(rows,cols):
    v=lambda *d: pltpu.VMEM(d+(rows,cols),BF); dma=pltpu.SemaphoreType.DMA
    return [v(2,2,2,2),v(2,2,2,2),v(2,2,2),v(2,2),v(2),v(),dma((8,)),dma((8,)),dma((4,))]

class Sums:
    def __init__(self,slabs,got,res,ss,rs,ts,us):
        self.slabs,self.got,self.res,self.ss,self.rs,self.ts,self.us=slabs,got,res,ss,rs,ts,us
        z,x,c,y=place_of()
        self.s=(z*2+x)*2+c; self.y=y; self.n=slabs.shape[1]
    def part(self,k,yy):
        me=self.y*16+self.s
        return send(self.slabs.at[yy,k],self.got.at[me],self.ss.at[yy*self.n+k],self.rs.at[me],(k,yy))
    def other(self,k,yy):
        return jnp.logical_or(self.s!=k,self.y!=yy)
    def scatter(self):
        for k in range(self.n):
            for yy in range(2):
                @pl.when(self.other(k,yy))
                def _(): self.part(k,yy).start()
    def back(self,to,k):
        return send(self.res.at[k],self.res.at[k],self.ts.at[to],self.us.at[k],(to,self.y))
    def collect(self):
        me=self.y*16+self.s
        @pl.when(self.s<self.n)
        def _():
            self.got[me]=self.slabs[self.y,self.s]
            def wait(i,_):
                @pl.when(i!=me)
                def _():
                    send(self.slabs.at[0,0],self.got.at[i],self.ss.at[0],self.rs.at[i],(self.s,1-self.y)).wait_recv()
                return 0
            lax.fori_loop(0,32,wait,0)
            total=self.got[0]
            for i in range(1,32): total=total+self.got[i]
            self.res[self.s]=total
            for to in range(16):
                @pl.when(self.s!=to)
                def _(): self.back(to,self.s).start()
    def finish(self):
        for k in range(self.n):
            @pl.when(self.s!=k)
            def _(): self.back(k,k).wait_recv()
        @pl.when(self.s<self.n)
        def _():
            for to in range(16):
                @pl.when(self.s!=to)
                def _(): self.back(to,self.s).wait_send()
        for k in range(self.n):
            for yy in range(2):
                @pl.when(self.other(k,yy))
                def _(): self.part(k,yy).wait_send()

def kernel_bc(nheads,x_ref,gln2_ref,qkv_ref,g_ref,gT_ref,D_ref,P_ref,pr_ref,W1,gains_ref,shifts_ref,sm_ref,pos_ref,pose_ref,dcat_hbm,dlast_hbm,
              ev_hbm,hd_hbm,evl_hbm,hdl_hbm,redq_ref,redm_ref,tab_ref,sum_ref,
              G_s,Gx,Gr_s,Gxr,vst_s,dS_s,dsr_s,gbd_s,qbd_s,aq,dq_s,kT_s,gq_s,gqT_s,dd_s,small_ref,acc,slabs,got,res,
              gs,gr_,ge,dl,ds,dr,es,er,us,ss0,rs0,ts0,us0,
              *more):
    w=pl.program_id(0); nw=dd_s.shape[0]
    z,xc,c,y=place_of()
    s=(z*2+xc)*2+c
    mate=dev(z,xc,c,1-y); sib=dev(z,xc,1-c,y)
    D=x_ref.shape[-1]; WIN=x_ref.shape[-2]; SLAB=dd_s.shape[1]
    cq=D//2
    groups=nheads//PER
    tiles=G_s.shape[0]; Q=tiles*128; R=WIN-Q; part=Gx.shape[1]//nheads
    big=Reduce(dcat_hbm,redm_ref,more[9],more[10],more[11:15],*more[15:18])
    red=Reduce(dq_s,redq_ref,more[0],more[1],more[2:6],*more[6:9])
    def slab(k,to=None):
        at=ev_hbm.at[y*nw+k]
        if to is None: return pltpu.make_async_copy(dd_s.at[k],at,dl.at[k])
        return send(dd_s.at[k],at,ds.at[k],dr.at[k],to)
    def tail(k):
        lead=SLAB-hd_hbm.shape[0]
        return send(dd_s.at[nw-1,pl.ds(lead,hd_hbm.shape[0])],hd_hbm,es.at[k],er,((s+1)%16,k))
    def early(k):
        lead=SLAB-hdl_hbm.shape[0]
        if k==0: return pltpu.make_async_copy(dlast_hbm,evl_hbm.at[y],us.at[0])
        if k==1: return send(dlast_hbm,evl_hbm.at[y],us.at[1],us.at[2],mate)
        return send(dlast_hbm.at[pl.ds(lead,hdl_hbm.shape[0])],hdl_hbm,us.at[k+1],us.at[5],((s+1)%16,k-2))
    def edge_trade():
        return send(Gr_s,Gxr,ge.at[0],ge.at[1],sib)
    def trade(h):
        r=pl.multiple_of(h*WIN+(1-c)*(WIN-part),8)
        return send(G_s.at[:,pl.ds(r,part)],Gx.at[:,pl.ds(pl.multiple_of(h*part,8),part)],gs.at[h],gr_.at[h],sib)
    everyone=[((s+t)%16,yy) for t in range(1,16) for yy in (y,1-y)]+[mate]
    @pl.when(w==0)
    def _():
        hail(everyone)
        aq[...]=jnp.zeros_like(aq); G_s[...]=jnp.zeros_like(G_s); Gr_s[...]=jnp.zeros_like(Gr_s); small_ref[...]=sm_ref[...]
        dd_s[:,SLAB-16:,:]=jnp.zeros((nw,16,D),BF)
        for hh in range(PER): vst_s[(hh+1)*SLAB-16:(hh+1)*SLAB,:]=jnp.zeros((16,GROUP),BF)
    def met():
        heard(everyone)
        big.start()
        early(0).start(); early(1).start()
        @pl.when(y==1)
        def _():
            early(2).start(); early(3).start()
    plan=((0,met),(2,big.one),(6,lambda: big.turn(0)),(10,lambda: big.turn(1)),(13,lambda: big.turn(2)))
    kT_s[...]=qkv_ref[0,1].T
    lane=lax.broadcasted_iota(jnp.int32,(WIN,GROUP),1)
    hl=lane//HD
    lift=pick((GROUP,R),lambda r,c: r%R==c).astype(BF)
    own_cols=pick((GROUP,D),lambda r,c: r//R==c//HD)
    gbd_s[...]=(mm(lift,g_ref[0,Q:WIN,:])*own_cols).astype(BF)
    qbd_s[...]=(mm(lift,qkv_ref[0,0,Q:WIN,:])*own_cols).astype(BF)
    Dr=exact(D_ref[0,:,Q:WIN],pick((R,GROUP),lambda r,c: c%R==r))
    Dr=jnp.sum(Dr*pick((nheads,GROUP),lambda r,c: c//R==r),axis=0,keepdims=True)
    dsr=pr_ref[0].astype(F32)*(mm_nt(qkv_ref[0,2],gbd_s[...])-Dr)
    Gr_s[...]+=dsr
    dsr_s[...]=dsr.astype(BF)
    gqT_s[:,Q:WIN]=exact(mm(kT_s[...],dsr_s[...])*pick((D,GROUP),lambda r,c: r//HD==c//R),pick((GROUP,R),lambda r,c: r%R==c))
    def group(gi,_):
        o=pl.multiple_of(gi*GROUP,GROUP)
        gTg=gT_ref[0,pl.ds(o,GROUP),0:Q]
        vg=qkv_ref[0,2,:,pl.ds(o,GROUP)]
        qg=qkv_ref[0,0,0:Q,pl.ds(o,GROUP)]
        gg=g_ref[0,0:Q,pl.ds(o,GROUP)]
        for hh in range(PER): vst_s[hh*SLAB:hh*SLAB+WIN,:]=jnp.where(hl==hh,vg,jnp.zeros_like(vg))
        dp4=mm(vst_s[...],gTg)
        for hh in range(PER):
            h=gi*PER+hh
            dsc=P_ref[0,gi,:,hh*Q:(hh+1)*Q].astype(F32)*(dp4[hh*SLAB:hh*SLAB+WIN]-D_ref[0,pl.ds(h,1),0:Q])
            for k in range(tiles):
                G_s[k,pl.ds(pl.multiple_of(h*WIN,8),WIN),:]+=dsc[:,k*128:(k+1)*128]
            dsl=dsc.astype(BF)
            dS_s[:,hh*Q:(hh+1)*Q]=dsl
            gqT_s[pl.ds(o+hh*HD,HD),0:Q]=mm(kT_s[pl.ds(o+hh*HD,HD),:],dsl)
        zero=jnp.zeros_like(gg); hq=hl[0:Q]
        gst=jnp.concatenate([jnp.where(hq==hh,gg,zero) for hh in range(PER)],axis=0)
        qst=jnp.concatenate([jnp.where(hq==hh,qg,zero) for hh in range(PER)],axis=0)
        dv=mm(P_ref[0,gi],gst)+mm(pr_ref[0],gbd_s[:,pl.ds(o,GROUP)])
        dk=mm(dS_s[...],qst)+mm(dsr_s[...],qbd_s[:,pl.ds(o,GROUP)])
        gq_s[1,:,pl.ds(o,GROUP)]=(dk*(1.0/SQ)).astype(BF)
        gq_s[2,:,pl.ds(o,GROUP)]=dv.astype(BF)
        for when,what in plan:
            pl.when(w*groups+gi==min(when,nw*groups-1))(what)
        @pl.when(w==nw-1)
        def _():
            for hh in range(PER): trade(gi*PER+hh).start()
            @pl.when(gi==0)
            def _(): edge_trade().start()
        return 0
    lax.fori_loop(0,groups,group,0)
    gq_s[0]=(gqT_s[...]*(1.0/SQ)).astype(BF).T
    x=x_ref[0]
    xhat,rstd=norm_stats(x)
    xn=(xhat*gains_ref[0:1,:]+shifts_ref[0:1,:]).astype(BF)
    xnT=xn.T
    gr=jnp.zeros((WIN,D),F32)
    for m in range(2):
        for k in range(3):
            gc=gq_s[k,:,m*cq:(m+1)*cq]
            gr=gr+mm_nt(gc,W1[m,:,k*cq:(k+1)*cq])
            aq[m,:,k*cq:(k+1)*cq]+=mm(xnT,gc)
    @pl.when(w==nw-1)
    def _():
        dq_s[...]=aq[...].astype(BF).reshape(dq_s.shape)
        red.start()
    dd_s[w,0:WIN,:]=(gln2_ref[0]+norm_back(gr,xhat,rstd,gains_ref[0:1,:])).astype(BF)
    slab(w).start(); slab(w,mate).start()
    @pl.when(jnp.logical_and(w==nw-1,y==1))
    def _():
        tail(0).start(); tail(1).start()
    small_ref[0:1,:]+=jnp.sum(gr*xhat,axis=0,keepdims=True)
    small_ref[2:3,:]+=jnp.sum(gr,axis=0,keepdims=True)
    @pl.when(w==nw-1)
    def _():
        for h in range(nheads): trade(h).wait()
        edge_trade().wait()
        acc[...]=jnp.zeros_like(acc)
        nh=acc.shape[0]; LW=tiles*128
        base=c*(WIN-part)
        def one_hots(g,hr,lr,width):
            iota=lax.broadcasted_iota(jnp.int32,(256,width),0).astype(F32).astype(BF)
            A=jnp.concatenate([jnp.where(hr==m,g,0.0) for m in range(nh)],axis=0).astype(BF)
            oh=jnp.where(iota==lr.astype(F32).astype(BF),jnp.ones((),BF),jnp.zeros((),BF))
            return mm_nt(A,oh)
        def rows(r,_):
            r8=pl.multiple_of(r*8,8)
            f8=pl.multiple_of(base+r*8,8)
            pos=pos_ref[pl.ds(f8,8),0:LW]
            hi8=pos>>8; lo8=pos&255
            tot=jnp.zeros((nh*nheads,256),F32)
            for k in range(8):
                g=jnp.concatenate([G_s[q,pl.ds(f8+k,nheads,stride=WIN),:]+Gx[q,pl.ds(r8+k,nheads,stride=part),:] for q in range(tiles)],axis=1)
                tot=tot+one_hots(g,hi8[k:k+1,:],lo8[k:k+1,:],LW)
            acc[...]+=tot.reshape(acc.shape)
            return 0
        turned=mm_nt(pick((GROUP,GROUP),lambda r,c: c==(r%nheads)*R+r//nheads).astype(BF),(Gr_s[...]+Gxr[...]).astype(BF))
        tot=jnp.zeros((nh*nheads,256),F32)
        for k in range(R):
            pos=pose_ref[k:k+1,:]
            hi=jnp.where(c==k//(R//2),pos>>8,-1)
            tot=tot+one_hots(turned[k*nheads:(k+1)*nheads],hi,pos&255,WIN)
        acc[...]+=tot.reshape(acc.shape)
        n=part//8
        cuts=[c,n*5//25,n*15//25,n]
        for f,after in enumerate((red.one,lambda: red.turn(0),None)):
            lax.fori_loop(cuts[f],cuts[f+1],rows,0)
            if after: after()
        half=nheads//2
        for yy in range(2):
            for k in range(nh): slabs[yy,k]=acc[k,yy*half:(yy+1)*half]
            for k in range(2): slabs[yy,nh+k]=small_ref[:,k*256:(k+1)*256]
        sums=Sums(slabs,got,res,ss0,rs0,ts0,us0)
        sums.scatter()
        red.turn(1)
        sums.collect()
        red.turn(2)
        big.four()
        sums.finish()
        red.four()
        for m in range(nh):
            tab_ref[:,m*256:(m+1)*256]=res[m]
        for k in range(2): sum_ref[:,k*256:(k+1)*256]=res[nh+k]
        for k in range(nw):
            slab(k).wait(); slab(k,mate).wait()
        @pl.when(y==1)
        def _():
            tail(0).wait_send(); tail(1).wait_send(); early(2).wait_send(); early(3).wait_send()
        tail(0).wait_recv(); early(2).wait_recv()
        early(0).wait(); early(1).wait()

def call_bc(x,gln2,qkv,g,gT,Dd,Pp,Pr,W1,gains,shifts,sm,pp,pos_index,dcat,dlast,T):
    nW,WIN,D=x.shape; NH=Dd.shape[1]
    cq=D//2; tiles=WIN//128; Q=tiles*128; SLAB=-(-WIN//16)*16; EDGE=-(-(SLAB-WIN//2)//16)*16
    part=-(-WIN//16)*8
    nh=-(-T//256)
    rows,more=dcat.shape[-2:]; cols=3*cq
    sd=jax.ShapeDtypeStruct; dma=pltpu.SemaphoreType.DMA; v=pltpu.VMEM
    return pl.pallas_call(functools.partial(kernel_bc,NH),grid=(nW,),
      in_specs=[per((WIN,D)),per((WIN,D),pipeline_mode=ONE),per((3,WIN,D)),per((WIN,D)),per((D,WIN)),per((NH,WIN)),per(Pp.shape[1:]),per((WIN,GROUP)),
        full((2,D,cols),pipeline_mode=ONE),full(gains.shape),full(shifts.shape),full(sm.shape),full(pp.shape,pipeline_mode=ONE),pl.BlockSpec((WIN-Q,WIN),lambda w:(Q//(WIN-Q),0)),ANY,ANY],
      out_specs=[ANY,ANY,ANY,ANY,full((rows,cols),pipeline_mode=ONE),full((rows,more),pipeline_mode=ONE),full((NH//2,nh*256),pipeline_mode=ONE),full(sm.shape)],
      out_shape=[sd((2*nW,SLAB,D),BF),sd((EDGE,D),BF),sd((2,SLAB,D),BF),sd((EDGE,D),BF),sd((rows,cols),F32),sd((rows,more),F32),sd((NH//2,nh*256),F32),sd(sm.shape,F32)],
      scratch_shapes=[v((tiles,NH*WIN,128),F32),v((tiles,NH*part,128),F32),v((WIN,GROUP),F32),v((WIN,GROUP),F32),v((PER*SLAB,GROUP),BF),v((WIN,PER*Q),BF),v((WIN,GROUP),BF),v((GROUP,D),BF),v((GROUP,D),BF),v((2,D,cols),F32),v((2,2,2,2,2,rows,cols),BF),v((D,WIN),BF),v((3,WIN,D),BF),v((D,WIN),F32),
        v((nW,SLAB,D),BF),v(sm.shape,F32),v((nh,NH,256),F32),v((2,nh+2,8,256),F32),v((32,8,256),F32),v((nh+2,8,256),F32),
        dma((NH,)),dma((NH,)),dma((2,)),dma((nW,)),dma((nW,)),dma((nW,)),dma((2,)),dma,dma((6,)),dma((2*nh+4,)),dma((32,)),dma((16,)),dma((nh+2,))]+reduce_scratch(rows,cols)+reduce_scratch(rows,more),
      compiler_params=pltpu.CompilerParams(vmem_limit_bytes=63*1024*1024,dimension_semantics=("arbitrary",),collective_id=3,has_side_effects=True),
      name="kernel_bc")(x,gln2,qkv,g,gT,Dd,Pp,Pr,W1,gains,shifts,sm,pp,pos_index,dcat,dlast)


def kernel_f(in_ref,og_ref,ev_ref,evl_ref,ev2_ref,hd_ref,hd2_ref,redq_ref,redm_ref,tab_ref,sum_ref,
             out_ref,din_ref,dqkv_ref,dproj_ref,dfc1_ref,dfc2_ref,dgain_ref,dshift_ref,dtab_ref,end_s):
    j=pl.program_id(0); nw=pl.num_programs(0)//2
    shift=in_ref.shape[0]//2; WIN=2*shift
    edge,SLAB=hd_ref.shape[0],ev_ref.shape[1]
    off=edge-(SLAB-shift)
    @pl.when(j==0)
    def _():
        end_s[0]=hd_ref[...].astype(F32); end_s[1]=hd2_ref[...].astype(F32)
        cq=dqkv_ref.shape[2]; cf=dfc1_ref.shape[1]
        for k in range(3): dqkv_ref[k]=redq_ref[:,k*cq:(k+1)*cq]
        dproj_ref[...]=redm_ref[:,0:cq]
        dfc1_ref[...]=redm_ref[:,cq:cq+cf]
        dfc2_ref[...]=redm_ref[:,cq+cf:]
        dgain_ref[...]=sum_ref[0:2,:]; dshift_ref[...]=sum_ref[2:6,:]
        dtab_ref[...]=tab_ref[:,0:dtab_ref.shape[1]]
    e=jnp.where(j%nw==nw-1,evl_ref[0],ev_ref[0]).astype(F32)
    for k,(base,res,v) in enumerate(((in_ref,out_ref,e),(og_ref,din_ref,ev2_ref[0].astype(F32)))):
        res[0:shift,:]=base[0:shift,:]+end_s[k,off:off+shift,:]
        res[shift:WIN,:]=base[shift:WIN,:]+v[0:shift,:]
        end_s[k]=v[SLAB-edge:,:]

def call_f(inputs,og,ev,evl,ev2,hd,hd2,redq,redm,tab,small,cq,cf,T):
    tok,D=inputs.shape; n,SLAB,_=ev.shape; WIN=tok//n; rows=redq.shape[0]
    sd=jax.ShapeDtypeStruct
    blk=pl.BlockSpec((WIN,D),lambda j:(j,0)); slab=pl.BlockSpec((1,SLAB,D),lambda j:(j,0,0))
    shapes=[(3,rows,cq),(rows,cq),(rows,cf),(rows,cf),(2,D),(4,D),(tab.shape[0],T)]
    return pl.pallas_call(kernel_f,grid=(n,),
      in_specs=[blk,blk,slab,pl.BlockSpec((1,SLAB,D),lambda j:(j//(n//2),0,0)),slab]+[full(v.shape) for v in (hd,hd2,redq,redm,tab,small)],
      out_specs=[blk,blk]+[full(v) for v in shapes],
      out_shape=[sd((tok,D),F32),sd((tok,D),F32)]+[sd(v,F32) for v in shapes],
      scratch_shapes=[pltpu.VMEM((2,)+hd.shape,F32)],
      compiler_params=pltpu.CompilerParams(vmem_limit_bytes=63*1024*1024,dimension_semantics=("arbitrary",)),
      name="kernel_f")(inputs,og,ev,evl,ev2,hd,hd2,redq,redm,tab,small)

def gathered(piece,names,nseq,nheads):
    full=lax.all_gather(piece,names,axis=0,tiled=False)
    return full.reshape((nseq,nheads)+piece.shape)

def natural(block):
    s,h,r,c=block.shape
    return block.transpose(0,2,1,3).reshape(s*r,h*c)

def owners(grad,nseq,nheads):
    r,c=grad.shape
    return grad.reshape(nseq,r//nseq,nheads,c//nheads).transpose(0,2,1,3).reshape(nseq*nheads,r//nseq,c//nheads)

def from_next(rows):
    n=lax.axis_size("seq")
    return lax.ppermute(rows,"seq",[(i,(i-1)%n) for i in range(n)])

def to_next(rows):
    n=lax.axis_size("seq")
    return lax.ppermute(rows,"seq",[(i,(i+1)%n) for i in range(n)])

def spread(rows):
    n=lax.axis_size("heads")
    flat=rows.reshape(-1,rows.shape[-1])
    if n==2:
        other=lax.ppermute(flat,"heads",[(0,1),(1,0)])
        me=lax.axis_index("heads")
        return jnp.where(me==0,jnp.concatenate([flat,other]),jnp.concatenate([other,flat]))
    return lax.all_gather(flat,"heads",axis=0,tiled=True)

def place(rows,base,shift):
    every=spread(rows)
    keep=every.shape[0]-shift
    return base+jnp.concatenate([to_next(every[keep:]),every[:keep]]).astype(F32)

def body(inputs,w_qkv,w_proj,w_fc1,w_fc2,gains,shifts,rel_table,region,pos_index,out_grad):
    nseq=lax.axis_size("seq"); nheads=lax.axis_size("heads"); me=lax.axis_index("heads")
    linked=nseq==16 and nheads==2
    names=("seq","heads")
    tok,D=inputs.shape; WIN=pos_index.shape[0]; shift=WIN//2; T=rel_table.shape[1]
    nW=tok//WIN//nheads
    rows=w_qkv.shape[1]; cq=w_qkv.shape[2]; cf=w_fc1.shape[1]
    lab=region.reshape(-1,WIN)
    if linked:
        W1,bias,brem,wf,posT=call_w(w_qkv,w_proj.T,w_fc1,w_fc2.T,pos_index,rel_table)
        qkv,x,Pp,Pr,gln2,g,gT,Dd,ev,dlast,dcat,sm=call_a2(inputs,out_grad,wf,lab,bias,brem,W1,gains,shifts)
        ev2,hd2,evl,hd,redq,redm,d_table,small=call_bc(x,gln2,qkv,g,gT,Dd,Pp,Pr,W1,gains,shifts,sm,posT,pos_index,dcat.reshape(2,2,2,2,2,rows,-1),dlast,T)
        out,din,dq,dp,d1,d2,dg,dsh,dt=call_f(inputs,out_grad,ev,evl,ev2,hd,hd2,redq,redm,d_table,small,cq,cf,T)
        return (out,din,dq,dp.T,d1,d2.T,dg,dsh,dt)
    posT=pos_index.T
    wide=-(-WIN//128)*128
    posP=jnp.pad(posT,((0,0),(0,wide-WIN)))
    start=me*nW*WIN
    lab=lax.dynamic_slice_in_dim(lab,me*nW,nW,0)
    labc=lab[:,:,None]; labr=lab[:,None,:]
    wq=jnp.concatenate([w_qkv[0],w_qkv[1],w_qkv[2],w_proj.T],axis=1).astype(BF)
    wf=jnp.concatenate([w_fc1,w_fc2.T],axis=1).astype(BF)
    table=lax.all_gather(rel_table,"heads",axis=0,tiled=True)
    NH=table.shape[0]
    every=gathered(jnp.concatenate([wq,wf],axis=1),names,nseq,nheads)
    ends=[i*cq for i in range(5)]+[4*cq+cf,4*cq+2*cf]
    W=jnp.concatenate([natural(every[...,a:b]) for a,b in zip(ends[:-1],ends[1:])],axis=1)[None]
    bias=call_p(posP,pack_table(table),WIN)
    def mine(v):
        ext=jnp.concatenate([v,from_next(v[:shift])])
        return lax.dynamic_slice_in_dim(ext,start+shift,nW*WIN,0).reshape(nW,WIN,-1)
    x=mine(inputs); og=mine(out_grad)
    delta,gln2,qkv,g,gT,Dd,Pp,dcat,sm_a=call_a(x,og,labc,labr,bias,W,gains,shifts)
    dd,dqkv,G,sm_b=call_b(x,gln2,qkv,g,gT,Dd,Pp,W,gains,shifts)
    grads=[dqkv[0,:,c*D:(c+1)*D] for c in range(3)]+[dcat[0,:,:D],dcat[0,:,D:D+cf*nheads],dcat[0,:,D+cf*nheads:]]
    red=lax.psum_scatter(jnp.concatenate([owners(v,nseq,nheads) for v in grads],axis=2),names,scatter_dimension=0,tiled=False).astype(F32)
    redq,redm=red[:,:3*cq],red[:,3*cq:]
    d_table,small=lax.psum((call_t(G,posT,T,NH),sm_a+sm_b),names)
    nl=rel_table.shape[0]
    d_table=lax.dynamic_slice_in_dim(d_table,me*nl,nl,0)
    output=place(delta,inputs,shift)
    d_inputs=place(dd,out_grad,shift)
    d_qkv=redq.reshape(rows,3,cq).transpose(1,0,2)
    d_proj=redm[:,:cq].T; d_fc1=redm[:,cq:cq+cf]; d_fc2=redm[:,cq+cf:].T
    return (output,d_inputs,d_qkv,d_proj,d_fc1,d_fc2,small[0:2],small[2:6],d_table)

def solution(mesh):
    placed=(P("seq",None),P(None,"seq","heads"),P("heads","seq"),P("seq","heads"),P("heads","seq"),P(),P(),P("heads",None),P("seq"),P(),P("seq",None))
    return jax.shard_map(body,mesh=mesh,in_specs=placed,
    out_specs=(P("seq",None),P("seq",None),P(None,"seq","heads"),P("heads","seq"),P("seq","heads"),P("heads","seq"),P(),P(),P("heads",None)),
    check_vma=False)
```

```python
import functools
import math

import jax, jax.numpy as jnp
from jax import lax
from jax.experimental import pallas as pl
from jax.experimental.pallas import tpu as pltpu
from jax.sharding import PartitionSpec as P

BF=jnp.bfloat16; F32=jnp.float32
HD=32; GROUP=128; PER=4
EPS=1e-5
SQ=math.sqrt(32.0)
CEXP=math.log2(math.e)/SQ
MASK=100.0*SQ

def mm(a,b):
    return lax.dot_general(a,b,(((1,),(0,)),((),())),preferred_element_type=F32)
def mm_nt(a,b):
    return lax.dot_general(a,b,(((1,),(1,)),((),())),preferred_element_type=F32)

def norm_stats(v):
    mean=jnp.mean(v,axis=-1,keepdims=True)
    c=v-mean
    var=jnp.mean(c*c,axis=-1,keepdims=True)
    rstd=lax.rsqrt(var+EPS)
    return c*rstd, rstd

def norm_back(gy,xhat,rstd,gain):
    gx=gy*gain
    m1=jnp.mean(gx,axis=-1,keepdims=True)
    m2=jnp.mean(gx*xhat,axis=-1,keepdims=True)
    return rstd*(gx-m1-xhat*m2)

P0=0.3275911
A1,A2,A3,A4,A5=0.254829592,-0.284496736,1.421413741,-1.453152027,1.061405429
def gelu_both(x):
    e=jnp.exp2(x*x*(-0.5*math.log2(math.e)))
    t=1.0/(1.0+(P0/math.sqrt(2.0))*jnp.abs(x))
    poly=t*(0.5*A1+t*(0.5*A2+t*(0.5*A3+t*(0.5*A4+t*(0.5*A5)))))
    half=poly*e
    phi=jnp.where(x>=0,1.0-half,half)
    return x*phi, phi+x*e*(1.0/math.sqrt(2.0*math.pi))

def kernel_a(nheads,x_ref,og_ref,labc_ref,labr_ref,bias_ref,W_ref,gains_ref,shifts_ref,
             delta_ref,gln2_ref,qkv_ref,g_ref,gT_ref,D_ref,P_hbm,dcat_ref,small_ref,
             qT_s,vT_s,OT_s,P_s,acc,sem,xn2_s,xn2T_s,tg_s,tgT_s,up_s,gn2_s):
    w=pl.program_id(0); nw=pl.num_programs(0)
    D=x_ref.shape[-1]; WIN=x_ref.shape[-2]
    parts=W_ref.shape[0]; cq=D//parts; cf=(W_ref.shape[2]-4*cq)//2
    groups=nheads//PER
    x=x_ref[0]
    xhat,_=norm_stats(x)
    xn=(xhat*gains_ref[0:1,:]+shifts_ref[0:1,:]).astype(BF)
    for c in range(3):
        for m in range(parts):
            at=slice(m*cq,(m+1)*cq)
            y=mm(xn,W_ref[m,:,c*cq:(c+1)*cq]).astype(BF)
            qkv_ref[0,c,:,at]=y
            if c==0: qT_s[at,:]=y.T
            if c==2: vT_s[at,:]=y.T
    labc=labc_ref[0]; labr=labr_ref[0]
    lane=lax.broadcasted_iota(jnp.int32,(WIN,GROUP),1)
    oh=jnp.where((labc==lane)|((labc+3)==lane),1.0,0.0).astype(BF)
    hi=564.0
    lo=MASK-hi
    sub=lax.broadcasted_iota(jnp.int32,(GROUP,WIN),0)
    nm=jnp.where(sub<3,jnp.where(sub!=labr,-hi,0.0),jnp.where(sub<6,jnp.where(sub-3!=labr,-lo,0.0),0.0)).astype(BF)
    hl=lane//HD

    def group(gi,_):
        slot=gi%2
        step=w*groups+gi
        @pl.when(step>=2)
        def _():
            pltpu.make_async_copy(P_s.at[slot],P_hbm.at[0,pl.ds(0,PER)],sem.at[slot]).wait()
        o=pl.multiple_of(gi*GROUP,GROUP)
        qTg=jnp.concatenate([qT_s[pl.ds(o,GROUP),:],nm],axis=0)
        kg=qkv_ref[0,1,:,pl.ds(o,GROUP)]
        for hh in range(PER):
            kh=jnp.concatenate([jnp.where(hl==hh,kg,jnp.zeros_like(kg)),oh],axis=1)
            t=mm(kh,qTg)+bias_ref[gi*PER+hh]
            m=jnp.max(t,axis=0,keepdims=True)
            e=jnp.exp2((t-m)*CEXP)
            l=jnp.sum(e,axis=0,keepdims=True)
            p=(e*(1.0/l)).astype(BF)
            P_s[slot,hh]=p
            OT_s[pl.ds(o+hh*HD,HD),:]=mm(vT_s[pl.ds(o+hh*HD,HD),:],p)
        pltpu.make_async_copy(P_s.at[slot],P_hbm.at[w,pl.ds(gi*PER,PER)],sem.at[slot]).start()
        return 0
    lax.fori_loop(0,groups,group,0)

    attn=OT_s[...].astype(BF).T
    branch=shifts_ref[2:3,:]
    for m in range(parts):
        branch=branch+mm_nt(attn[:,m*cq:(m+1)*cq],W_ref[m,:,3*cq:4*cq])
    branch=branch.astype(BF).astype(F32)
    middle=x+branch
    xhat2,rstd2=norm_stats(middle)
    xn2=(xhat2*gains_ref[1:2,:]+shifts_ref[1:2,:]).astype(BF)
    og=og_ref[0]
    tg=og.astype(BF)
    xn2_s[...]=xn2; xn2T_s[...]=xn2.T; tg_s[...]=tg; tgT_s[...]=tg.T
    up_s[...]=jnp.zeros_like(up_s); gn2_s[...]=jnp.zeros_like(gn2_s)
    CH=min(512,cf); each=cf//CH
    @pl.when(w==0)
    def _():
        acc[...]=jnp.zeros_like(acc)
        small_ref[...]=jnp.zeros_like(small_ref)
    def chunk(c,_):
        m=c//each
        o=pl.multiple_of((c%each)*CH,CH)
        f1=W_ref[m,:,pl.ds(4*cq+o,CH)]; f2=W_ref[m,:,pl.ds(4*cq+cf+o,CH)]
        hid=mm(xn2_s[...],f1)
        act,dact=gelu_both(hid)
        a=act.astype(BF)
        up_s[...]+=mm_nt(a,f2)
        gh=(mm(tg_s[...],f2)*dact).astype(BF)
        gn2_s[...]+=mm_nt(gh,f1)
        acc[m,:,pl.ds(cq+o,CH)]+=mm(xn2T_s[...],gh)
        acc[m,:,pl.ds(cq+cf+o,CH)]+=mm(tgT_s[...],a)
        return 0
    lax.fori_loop(0,parts*each,chunk,0)
    delta_ref[0]=(branch+up_s[...]+shifts_ref[3:4,:]).astype(BF)
    gn2=gn2_s[...]
    gln2=norm_back(gn2,xhat2,rstd2,gains_ref[1:2,:])
    gln2_ref[0]=gln2
    gb=(og+gln2).astype(BF)
    gbT=gb.T
    for m in range(parts):
        at=slice(m*cq,(m+1)*cq)
        acc[m,:,0:cq]+=mm(gbT,attn[:,at])
        g=mm(gb,W_ref[m,:,3*cq:4*cq]).astype(BF)
        g_ref[0,:,at]=g
        gT=g.T
        gT_ref[0,at,:]=gT
        prod=gT.astype(F32)*OT_s[at,:]
        nh=nheads//parts
        D_ref[0,m*nh:(m+1)*nh,:]=jnp.sum(prod.reshape(nh,HD,WIN),axis=1)
    small_ref[1:2,:]+=jnp.sum(gn2*xhat2,axis=0,keepdims=True)
    small_ref[3:4,:]+=jnp.sum(gn2,axis=0,keepdims=True)
    small_ref[4:5,:]+=jnp.sum(gb.astype(F32),axis=0,keepdims=True)
    small_ref[5:6,:]+=jnp.sum(tg.astype(F32),axis=0,keepdims=True)
    @pl.when(w==nw-1)
    def _():
        dcat_ref[...]=acc[...].astype(BF)
        for s in range(2):
            pltpu.make_async_copy(P_s.at[s],P_hbm.at[0,pl.ds(0,PER)],sem.at[s]).wait()

def full(shape,**kw):
    return pl.BlockSpec(shape,lambda w:(0,)*len(shape),**kw)
def per(shape,**kw):
    return pl.BlockSpec((1,)+shape,lambda w:(w,)+(0,)*len(shape),**kw)
ONE=pl.Buffered(1)
ANY=pl.BlockSpec(memory_space=pl.ANY)

def call_a(x,og,labc,labr,bias,W,gains,shifts):
    nW,WIN,D=x.shape; NH=bias.shape[0]
    parts,_,Ct=W.shape; Cg=Ct-3*(D//parts)
    sd=jax.ShapeDtypeStruct
    outs=[sd((nW,WIN,D),BF),sd((nW,WIN,D),F32),sd((nW,3,WIN,D),BF),sd((nW,WIN,D),BF),sd((nW,D,WIN),BF),sd((nW,NH,WIN),F32),
          sd((nW,NH,WIN,WIN),BF),sd((parts,D,Cg),BF),sd((8,D),F32)]
    return pl.pallas_call(functools.partial(kernel_a,NH),grid=(nW,),
      in_specs=[per((WIN,D)),per((WIN,D)),per((WIN,1)),per((1,WIN)),full((NH,WIN,WIN),pipeline_mode=ONE),
        full((parts,D,Ct),pipeline_mode=ONE),full(gains.shape),full(shifts.shape)],
      out_specs=[per((WIN,D)),per((WIN,D)),per((3,WIN,D)),per((WIN,D)),per((D,WIN)),per((NH,WIN)),ANY,full((parts,D,Cg)),full((8,D))],
      out_shape=outs,
      scratch_shapes=[pltpu.VMEM((D,WIN),BF),pltpu.VMEM((D,WIN),BF),pltpu.VMEM((D,WIN),F32),pltpu.VMEM((2,PER,WIN,WIN),BF),
        pltpu.VMEM((parts,D,Cg),F32),pltpu.SemaphoreType.DMA((2,)),
        pltpu.VMEM((WIN,D),BF),pltpu.VMEM((D,WIN),BF),pltpu.VMEM((WIN,D),BF),pltpu.VMEM((D,WIN),BF),pltpu.VMEM((WIN,D),F32),pltpu.VMEM((WIN,D),F32)],
      compiler_params=pltpu.CompilerParams(vmem_limit_bytes=62*1024*1024,dimension_semantics=("arbitrary",)),
      name="kernel_a")(x,og,labc,labr,bias,W,gains,shifts)

def kernel_b(nheads,x_ref,gln2_ref,qkv_ref,g_ref,gT_ref,D_ref,P_ref,W_ref,gains_ref,shifts_ref,
             dd_ref,dqkv_ref,G_hbm,small_ref,G_s,aq,kT_s,gq_s,gqT_s,sem):
    w=pl.program_id(0); nw=pl.num_programs(0)
    D=x_ref.shape[-1]; WIN=x_ref.shape[-2]
    parts=W_ref.shape[0]; cq=D//parts
    groups=nheads//PER
    @pl.when(w==0)
    def _():
        aq[...]=jnp.zeros_like(aq); G_s[...]=jnp.zeros_like(G_s); small_ref[...]=jnp.zeros_like(small_ref)
    kT_s[...]=qkv_ref[0,1].T
    lane=lax.broadcasted_iota(jnp.int32,(WIN,GROUP),1)
    hl=lane//HD
    def group(gi,_):
        o=pl.multiple_of(gi*GROUP,GROUP)
        gTg=gT_ref[0,pl.ds(o,GROUP),:]
        vg=qkv_ref[0,2,:,pl.ds(o,GROUP)]
        qg=qkv_ref[0,0,:,pl.ds(o,GROUP)]
        gg=g_ref[0,:,pl.ds(o,GROUP)]
        dv=jnp.zeros((WIN,GROUP),F32); dk=jnp.zeros((WIN,GROUP),F32)
        zero=jnp.zeros_like(vg)
        for hh in range(PER):
            h=gi*PER+hh
            p=P_ref[0,h]
            dp=mm(jnp.where(hl==hh,vg,zero),gTg)
            ds_=p.astype(F32)*(dp-D_ref[0,pl.ds(h,1),:])
            for c in range(G_s.shape[0]):
                wd=min(128,WIN-c*128)
                G_s[c,pl.ds(pl.multiple_of(h*WIN,8),WIN),:wd]+=ds_[:,c*128:c*128+wd]
            dsl=ds_.astype(BF)
            dv+=mm(p,jnp.where(hl==hh,gg,zero))
            dk+=mm(dsl,jnp.where(hl==hh,qg,zero))
            gqT_s[pl.ds(o+hh*HD,HD),:]=mm(kT_s[pl.ds(o+hh*HD,HD),:],dsl)
        gq_s[1,:,pl.ds(o,GROUP)]=(dk*(1.0/SQ)).astype(BF)
        gq_s[2,:,pl.ds(o,GROUP)]=dv.astype(BF)
        return 0
    lax.fori_loop(0,groups,group,0)
    gq_s[0]=(gqT_s[...]*(1.0/SQ)).astype(BF).T
    x=x_ref[0]
    xhat,rstd=norm_stats(x)
    xn=(xhat*gains_ref[0:1,:]+shifts_ref[0:1,:]).astype(BF)
    xnT=xn.T
    gr=jnp.zeros((WIN,D),F32)
    for m in range(parts):
        for c in range(3):
            gc=gq_s[c,:,m*cq:(m+1)*cq]
            gr=gr+mm_nt(gc,W_ref[m,:,c*cq:(c+1)*cq])
            aq[m,:,c*cq:(c+1)*cq]+=mm(xnT,gc)
    dd_ref[0]=(gln2_ref[0]+norm_back(gr,xhat,rstd,gains_ref[0:1,:])).astype(BF)
    small_ref[0:1,:]+=jnp.sum(gr*xhat,axis=0,keepdims=True)
    small_ref[2:3,:]+=jnp.sum(gr,axis=0,keepdims=True)
    @pl.when(w==nw-1)
    def _():
        dqkv_ref[...]=aq[...].astype(BF)
        cp=pltpu.make_async_copy(G_s,G_hbm,sem); cp.start(); cp.wait()

def call_b(x,gln2,qkv,g,gT,Dd,Pp,W,gains,shifts):
    nW,WIN,D=x.shape; NH=Dd.shape[1]
    parts=W.shape[0]; cq=D//parts; tiles=-(-WIN//128)
    sd=jax.ShapeDtypeStruct
    return pl.pallas_call(functools.partial(kernel_b,NH),grid=(nW,),
      in_specs=[per((WIN,D)),per((WIN,D)),per((3,WIN,D)),per((WIN,D)),per((D,WIN)),per((NH,WIN)),per((NH,WIN,WIN)),
        full((parts,D,3*cq),pipeline_mode=ONE),full(gains.shape),full(shifts.shape)],
      out_specs=[per((WIN,D)),full((parts,D,3*cq)),ANY,full((8,D))],
      out_shape=[sd((nW,WIN,D),BF),sd((parts,D,3*cq),BF),sd((tiles,NH*WIN,128),F32),sd((8,D),F32)],
      scratch_shapes=[pltpu.VMEM((tiles,NH*WIN,128),F32),pltpu.VMEM((parts,D,3*cq),F32),pltpu.VMEM((D,WIN),BF),pltpu.VMEM((3,WIN,D),BF),pltpu.VMEM((D,WIN),F32),
        pltpu.SemaphoreType.DMA],
      compiler_params=pltpu.CompilerParams(vmem_limit_bytes=62*1024*1024,dimension_semantics=("arbitrary",)),
      name="kernel_b")(x,gln2,qkv,g,gT,Dd,Pp,W,gains,shifts)

FIX=8191.0

def pack_table(table):
    NH,T=table.shape
    n=-(-T//128)
    q=jnp.round(jnp.clip(table,-4.0,4.0)*FIX).astype(jnp.int32)
    q=jnp.pad(q,((0,0),(0,n*128-T)))
    q=q.reshape(NH//2,2,n,128)
    return (q[:,0]*65536)|(q[:,1]&65535)

def kernel_p(pos_ref,tab_ref,bias_ref):
    npair,n,_=tab_ref.shape
    WIN=bias_ref.shape[-1]
    tiles=-(-WIN//128)
    def row(r,_):
        r8=pl.multiple_of(r*8,8)
        for c in range(tiles):
            width=min(128,WIN-c*128)
            idx=pos_ref[pl.ds(r8,8),c*128:(c+1)*128]
            lo=idx&127; hi=idx>>7
            masks=[hi==k for k in range(n)]
            for p in range(npair):
                acc=jnp.zeros((8,128),jnp.int32)
                for k in range(n):
                    src=jnp.broadcast_to(tab_ref[p,k:k+1,:],(8,128))
                    acc=jnp.where(masks[k],jnp.take_along_axis(src,lo,axis=1),acc)
                a=(acc>>16).astype(F32)*(SQ/FIX)
                b=((acc<<16)>>16).astype(F32)*(SQ/FIX)
                bias_ref[2*p,pl.ds(r8,8),c*128:c*128+width]=a[:,:width]
                bias_ref[2*p+1,pl.ds(r8,8),c*128:c*128+width]=b[:,:width]
        return 0
    lax.fori_loop(0,bias_ref.shape[1]//8,row,0)

def call_p(posT_pad,tab,WIN):
    NH=tab.shape[0]*2
    return pl.pallas_call(kernel_p,out_shape=jax.ShapeDtypeStruct((NH,WIN,WIN),F32),
      compiler_params=pltpu.CompilerParams(vmem_limit_bytes=40*1024*1024),name="kernel_p")(posT_pad,tab)

def kernel_t(NH,G_ref,hi_ref,lo_ref,out_ref):
    WIN=hi_ref.shape[0]; LW=G_ref.shape[0]*128
    nh=out_ref.shape[0]//NH
    out_ref[...]=jnp.zeros_like(out_ref)
    def rows(r,_):
        r8=pl.multiple_of(r*8,8)
        hi8=hi_ref[pl.ds(r8,8),:]; lo8=lo_ref[pl.ds(r8,8),:]
        tot=jnp.zeros(out_ref.shape,F32)
        iota=lax.broadcasted_iota(jnp.int32,(256,LW),0).astype(F32).astype(BF)
        for k in range(8):
            g=jnp.concatenate([G_ref[c,pl.ds(r8+k,NH,stride=WIN),:] for c in range(LW//128)],axis=1)
            hr=hi8[k:k+1,:]; lr=lo8[k:k+1,:].astype(F32).astype(BF)
            A=jnp.concatenate([jnp.where(hr==m,g,0.0) for m in range(nh)],axis=0).astype(BF)
            oh=jnp.where(iota==lr,jnp.ones((),BF),jnp.zeros((),BF))
            tot=tot+lax.dot_general(A,oh,(((1,),(1,)),((),())),preferred_element_type=F32)
        out_ref[...]+=tot
        return 0
    lax.fori_loop(0,WIN//8,rows,0)

def call_t(G,posT,T,NH):
    WIN=posT.shape[0]; nt=G.shape[0]
    nh=-(-T//256)
    pp=jnp.pad(posT,((0,0),(0,nt*128-WIN)),constant_values=nh*256)
    hi=pp>>8; lo=pp&255
    o=pl.pallas_call(functools.partial(kernel_t,NH),out_shape=jax.ShapeDtypeStruct((nh*NH,256),F32),
      compiler_params=pltpu.CompilerParams(vmem_limit_bytes=40*1024*1024),name="kernel_t")(G,hi,lo)
    return o.reshape(nh,NH,256).transpose(1,0,2).reshape(NH,nh*256)[:,:T]


MESHID=pl.DeviceIdType.MESH

def place_of():
    s=lax.axis_index("seq"); y=lax.axis_index("heads")
    return s//4,(s//2)%2,s%2,y

def dev(z,x,c,y):
    return ((z*2+x)*2+c,y)

def peers_of(z,x,c,y):
    return [dev(z,x,1-c,y),dev(z,1-x,c,y),dev(z,x,c,1-y)]+[dev((z+i)%4,x,c,y) for i in (1,2,3)]

def hail(devices):
    bar=pltpu.get_barrier_semaphore()
    for d in devices:
        pl.semaphore_signal(bar,inc=1,device_id=d,device_id_type=MESHID)

def heard(devices):
    pl.semaphore_wait(pltpu.get_barrier_semaphore(),len(devices))

def greet(devices):
    hail(devices)
    heard(devices)

def send(src,dst,ss,rs,to):
    return pltpu.make_async_remote_copy(src_ref=src,dst_ref=dst,send_sem=ss,recv_sem=rs,device_id=to,device_id_type=MESHID)


class Gather:
    def __init__(self,src,dst,ss,rs,own,cols=None):
        self.src,self.dst,self.ss,self.rs,self.own=src,dst,ss,rs,own
        self.cols=pl.ds(0,dst.shape[2]) if cols is None else cols
        z,x,c,y=self.at=place_of()
        self.xa=x+(1-2*x)*(1-c); self.ya=y+(1-2*y)*c
        self.xb=x+(1-2*x)*c; self.yb=y+(1-2*y)*(1-c)
        self.sib=dev(z,x,1-c,y); self.pa=dev(z,self.xa,c,self.ya); self.pb=dev(z,self.xb,c,self.yb)
    def slot(self,zz,xx,cc,yy):
        n=self.src.shape[0]
        return self.dst.at[yy,pl.ds(pl.multiple_of(((zz*2+xx)*2+cc)*n,n),n),self.cols]
    def copy(self,src,where,k,to):
        return send(src,self.slot(*where),self.ss.at[k],self.rs.at[k],to)
    def go(self,where,k,to,src=None):
        self.copy(self.slot(*where) if src is None else src,where,k,to).start()
    def came(self,where,k):
        self.copy(self.src,where,k,self.sib).wait_recv()
    def keep(self):
        z,x,c,y=self.at
        return pltpu.make_async_copy(self.src,self.slot(z,x,c,y),self.own)
    def start(self):
        z,x,c,y=self.at
        me=(z,x,c,y)
        self.keep().start()
        for i in (1,2,3):
            self.go(me,i-1,dev((z+i)%4,x,c,y),self.src)
        self.go(me,3,self.pa,self.src); self.go(me,7,self.pb,self.src); self.go(me,15,self.sib,self.src)
    def z(self,i):
        return (self.at[0]+4-i)%4
    def turn_z(self,i):
        z,x,c,y=self.at
        at=(self.z(i),x,c,y); self.came(at,i-1)
        self.go(at,3+i,self.pa); self.go(at,7+i,self.pb); self.go(at,15+i,self.sib)
    def turn_a(self,i):
        at=(self.z(i),self.xa,self.at[2],self.ya); self.came(at,3+i)
        self.go(at,11+i,self.pb); self.go(at,19+i,self.sib)
    def turn_b(self,i):
        at=(self.z(i),self.xb,self.at[2],self.yb); self.came(at,7+i)
        self.go(at,23+i,self.sib)
    def turn_ab(self,i):
        z,x,c,y=self.at
        at=(self.z(i),1-x,c,1-y); self.came(at,11+i)
        self.go(at,27+i,self.sib)
    def last(self):
        z,x,c,y=self.at
        for i in range(4):
            zz=self.z(i)
            self.came((zz,x,1-c,y),15+i); self.came((zz,self.xb,1-c,self.yb),19+i)
            self.came((zz,self.xa,1-c,self.ya),23+i); self.came((zz,1-x,1-c,1-y),27+i)
    def drain(self):
        z,x,c,y=self.at
        for k in range(31):
            self.copy(self.src,(z,x,c,y),k,self.sib).wait_send()
        self.keep().wait()

class GatherLate(Gather):
    def start(self):
        z,x,c,y=self.at
        me=(z,x,c,y)
        self.keep().start()
        self.go(me,0,self.pa,self.src)
        for i in (1,2,3):
            self.go(me,i,dev((z+i)%4,x,c,y),self.src)
        self.go(me,7,self.pb,self.src); self.go(me,15,self.sib,self.src)
    def pair(self):
        z,x,c,y=self.at
        at=(z,self.xa,c,self.ya); self.came(at,0)
        for i in (1,2,3):
            self.go(at,3+i,dev((z+i)%4,x,c,y))
        self.go(at,11,self.pb); self.go(at,19,self.sib)
    def along(self,i):
        z,x,c,y=self.at
        at=(self.z(i),x,c,y); self.came(at,i)
        self.go(at,7+i,self.pb); self.go(at,15+i,self.sib)
        at=(self.z(i),self.xa,c,self.ya); self.came(at,3+i)
        self.go(at,11+i,self.pb); self.go(at,19+i,self.sib)
    def over(self,i):
        z,x,c,y=self.at
        at=(self.z(i),self.xb,c,self.yb); self.came(at,7+i)
        self.go(at,23+i,self.sib)
        at=(self.z(i),1-x,c,1-y); self.came(at,11+i)
        self.go(at,27+i,self.sib)

def gather_sems():
    return [pltpu.SemaphoreType.DMA((31,)),pltpu.SemaphoreType.DMA((31,)),pltpu.SemaphoreType.DMA]

STEPS=7
def kernel_w(qkv_ref,proj_ref,fc1_ref,fc2_ref,pos_ref,tab_ref,W_hbm,bias_hbm,brem_hbm,wf_ref,posT_ref,
             bias_s,brem_s,short_s,found_s,wq_s,tb,tq,ss,rs,own,bs,br,bl,tsem,ed):
    z,x,c,y=place_of()
    cq=qkv_ref.shape[2]; cf=fc1_ref.shape[1]
    for k in range(3): wq_s[:,k*cq:(k+1)*cq]=qkv_ref[k].astype(BF)
    wq_s[:,3*cq:4*cq]=proj_ref[...].astype(BF)
    lead=wq_s.shape[1]-4*cq
    wq_s[:,4*cq:]=fc1_ref[:,0:lead].astype(BF)
    half,T=tab_ref.shape
    tb[2]=jnp.zeros(tb.shape[1:],F32)
    tb[2,:,0:T]=tab_ref[...]
    greet(peers_of(z,x,c,y))
    mid=wq_s.shape[1]//2
    gather=Gather(wq_s.at[:,pl.ds(0,mid)],W_hbm,ss.at[0],rs.at[0],own.at[0],pl.ds(0,mid))
    other=GatherLate(wq_s.at[:,pl.ds(mid,mid)],W_hbm,ss.at[1],rs.at[1],own.at[1],pl.ds(mid,mid))
    swap=send(tb.at[2],tb.at[y],tsem.at[0],tsem.at[1],dev(z,x,c,1-y))
    swap.start()
    gather.start(); other.start()
    tb[y]=tb[2]
    wf_ref[:,0:cf-lead]=fc1_ref[:,lead:].astype(BF)
    wf_ref[:,cf-lead:]=fc2_ref[...].astype(BF)
    WIN,Q=bias_s.shape[-2:]; tiles=Q//128; n=tb.shape[2]//128; R=WIN-Q; per_row=128//R; nr=found_s.shape[1]
    posT_ref[...]=jnp.full(posT_ref.shape,1<<15,jnp.int32)
    posT_ref[:,0:WIN]=pos_ref[...].astype(F32).T.astype(jnp.int32)
    swap.wait()
    npair=half//2
    for p in range(npair):
        a,b=[jnp.floor(jnp.clip(tb[c,2*p+k:2*p+k+1,:],-4.0,4.0)*FIX+0.5).astype(jnp.int32) for k in range(2)]
        tq[p:p+1,:]=(a*65536)|(b&65535)
    nrow=WIN//8
    cuts=[nrow*k//STEPS for k in range(STEPS+1)]
    sib=dev(z,x,1-c,y)
    def rows_of(k): return pl.ds(cuts[k]*8,(cuts[k+1]-cuts[k])*8)
    def kept(k): return pltpu.make_async_copy(bias_s.at[:,rows_of(k)],bias_hbm.at[pl.ds(c*half,half),rows_of(k)],bl.at[k])
    def sent(k,cc): return send(bias_s.at[:,rows_of(k)],bias_hbm.at[pl.ds(cc*half,half),rows_of(k)],bs.at[k],br.at[k],sib)
    def look(idx):
        lo=idx&127; hi=idx>>7
        masks=[hi==q for q in range(n)]
        for p in range(npair):
            acc=jnp.zeros((8,128),jnp.int32)
            for q in range(n):
                src=jnp.broadcast_to(tq[p:p+1,q*128:(q+1)*128],(8,128))
                acc=jnp.where(masks[q],jnp.take_along_axis(src,lo,axis=1),acc)
            yield 2*p,(acc>>16).astype(F32)*(SQ/FIX)
            yield 2*p+1,((acc<<16)>>16).astype(F32)*(SQ/FIX)
    slots=lax.broadcasted_iota(jnp.int32,(nr,128),1)//R
    def short_in():
        short_s[...]=jnp.full(short_s.shape,1<<15,jnp.int32)
        short_s[0:WIN,:]=posT_ref[:,Q:Q+128]
        packed=jnp.zeros((nr,128),jnp.int32)
        for u in range(per_row):
            v=short_s[pl.ds(u,nr,stride=per_row),:]
            packed=jnp.where(slots==u,pltpu.roll(v,u*R,1) if u else v,packed)
        for t in range(nr//8):
            for h,v in look(packed[t*8:(t+1)*8]): found_s[h,t*8:(t+1)*8,:]=v
    def short_out():
        for u in range(per_row):
            row=jnp.zeros((nr,128),F32)
            for h in range(half):
                by=((h-u)*R)%128
                v=found_s[h]
                row=jnp.where(slots==h,pltpu.roll(v,by,1) if by else v,row)
            brem_s[pl.ds(u,nr,stride=per_row),:]=row
    def rows(k):
        def row(r,_):
            r8=pl.multiple_of(r*8,8)
            for t in range(tiles):
                for h,v in look(posT_ref[pl.ds(r8,8),t*128:(t+1)*128]):
                    bias_s[h,pl.ds(r8,8),t*128:(t+1)*128]=v
            return 0
        lax.fori_loop(cuts[k],cuts[k+1],row,0)
        kept(k).start(); sent(k,c).start()
    rows(0)
    short_in()
    short_out()
    other.pair()
    rows(1)
    for i in (1,3,2): gather.turn_z(i)
    for i in (0,): gather.turn_a(i); gather.turn_b(i)
    rows(2)
    for i in (1,3,2): other.along(i)
    rows(3)
    for i in (1,3,2): gather.turn_a(i); gather.turn_b(i)
    rows(4)
    for i in (0,1,3,2): gather.turn_ab(i); other.over(i)
    rows(5)
    rows(6)
    edges=[pltpu.make_async_copy(brem_s.at[pl.ds(0,WIN)],brem_hbm.at[c],ed.at[0]),send(brem_s.at[pl.ds(0,WIN)],brem_hbm.at[c],ed.at[1],ed.at[2],sib)]
    for e in edges: e.start()
    gather.last(); other.last()
    for e in edges: e.wait()
    for k in range(STEPS):
        kept(k).wait(); sent(k,c).wait_send(); sent(k,1-c).wait_recv()
    gather.drain(); other.drain()

def call_w(w_qkv,w_proj,w_fc1,w_fc2,pos_index,rel_table):
    rows,cq=w_qkv.shape[1:]; cf=w_fc1.shape[1]; WIN=pos_index.shape[0]; half,T=rel_table.shape; dma=pltpu.SemaphoreType.DMA
    wide=-(-WIN//128)*128; Q=WIN//128*128; n=-(-T//128); mem=pltpu.VMEM
    keys=-(-WIN//(1024//(WIN-Q)))*(1024//(WIN-Q))
    early=4*cq+min(512,cf); late=4*cq+2*cf-early
    sd=jax.ShapeDtypeStruct
    return pl.pallas_call(kernel_w,grid=(1,),
      out_shape=[sd((2,16*rows,early),BF),sd((2*half,WIN,Q),F32),sd((2,WIN,128),F32),sd((rows,late),BF),sd((WIN,wide),jnp.int32)],
      in_specs=[full(v.shape) for v in (w_qkv,w_proj,w_fc1,w_fc2,pos_index,rel_table)],out_specs=[ANY,ANY,ANY,full((rows,late)),full((WIN,wide))],
      scratch_shapes=[mem((half,WIN,Q),F32),mem((keys,128),F32),mem((keys,128),jnp.int32),mem((half,keys*(WIN-Q)//128,128),F32),mem((rows,early),BF),mem((3,half,n*128),F32),mem((half//2,n*128),jnp.int32)]
        +[dma((2,31)),dma((2,31)),dma((2,))]+[dma((STEPS,)),dma((STEPS,)),dma((STEPS,)),dma((2,)),dma((3,))],
      compiler_params=pltpu.CompilerParams(vmem_limit_bytes=63*1024*1024,collective_id=1,has_side_effects=True),name="kernel_w")(w_qkv,w_proj,w_fc1,w_fc2,pos_index,rel_table)

def neighbours(z,x,c,y):
    s=(z*2+x)*2+c
    return [((s+k)%16,yy) for k in (1,15) for yy in (y,1-y)]

def pick(shape,test):
    r=lax.broadcasted_iota(jnp.int32,shape,0); c=lax.broadcasted_iota(jnp.int32,shape,1)
    return jnp.where(test(r,c),1.0,0.0)

def exact(a,b):
    return lax.dot_general(a,b,(((1,),(0,)),((),())),precision=lax.Precision.HIGHEST,preferred_element_type=F32)

def kernel_a2(nheads,in_hbm,og_hbm,wf_hbm,lab_ref,bias_ref,brem_ref,W1,gains_ref,shifts_ref,
              qkv_ref,x_ref,P_hbm,pr_ref,gln2_ref,g_ref,gT_ref,D_ref,ev_hbm,dlast_hbm,dcat_hbm,small_ref,
              x_s,og_s,W2,OT_s,qT_s,vT_s,P_s,kst_s,acc,pst,xn2_s,xn2T_s,tg_s,tgT_s,up_s,gn2_s,dl_s,
              lab_s,psem,xsem,hsem,ss,rs,own,dl,ds,dr,fin):
    i=pl.program_id(0); nw=x_s.shape[0]
    w=i%nw
    z,xc,c,y=place_of()
    s=(z*2+xc)*2+c
    D=x_s.shape[-1]; WIN=qkv_ref.shape[-2]; SLAB=x_s.shape[1]; HALF=SLAB//2
    OFF=(SLAB-WIN)//2
    cq=D//2; lead=W1.shape[2]-4*cq; cf=(W2.shape[2]+lead)//2
    groups=nheads//PER; Q=bias_ref.shape[2]; R=WIN-Q
    gather=Gather(wf_hbm,W2,ss,rs,own)
    mate=dev(z,xc,c,1-y)
    def local(k,half,t):
        hbm,buf=((in_hbm,x_s),(og_hbm,og_s))[t]
        r=pl.multiple_of(y*(nw*WIN)+k*WIN+(WIN//2-OFF)+half*HALF,8)
        return pltpu.make_async_copy(hbm.at[pl.ds(r,HALF)],buf.at[k,pl.ds(half*HALF,HALF)],xsem.at[t,2*k+half])
    def edge(t):
        hbm,buf=((in_hbm,x_s),(og_hbm,og_s))[t]
        return send(hbm.at[pl.ds(0,HALF)],buf.at[nw-1,pl.ds(HALF,HALF)],hsem.at[t,0],hsem.at[t,1],((s+15)%16,1))
    def ready(t):
        local(w,0,t).wait()
        far=jnp.logical_and(w==nw-1,y==1)
        @pl.when(far)
        def _(): edge(t).wait_recv()
        @pl.when(jnp.logical_not(far))
        def _(): local(w,1,t).wait()
    def slab(k,to=None):
        if k is None: return pltpu.make_async_copy(dl_s.at[nw-1],dlast_hbm,dl.at[nw-1])
        at=ev_hbm.at[y*nw+k]
        if to is None: return pltpu.make_async_copy(dl_s.at[k],at,dl.at[k])
        return send(dl_s.at[k],at,ds.at[k],dr.at[k],to)
    everyone=peers_of(z,xc,c,y)+neighbours(z,xc,c,y)
    def met():
        heard(everyone)
        gather.start()
        @pl.when(y==1)
        def _():
            for t in range(2): edge(t).start()
    def first():
        for k in (1,3,2): gather.turn_z(k)
    def second():
        for k in (0,1,3,2): gather.turn_a(k); gather.turn_b(k)
    def third():
        for k in (0,1,3,2): gather.turn_ab(k)
    plan=((0,met),(6,first),(10,second),(14,third))
    @pl.when(i==0)
    def _():
        hail(everyone)
        for k in range(nw):
            for t in range(2):
                local(k,0,t).start()
                if k<nw-1: local(k,1,t).start()
        for t in range(2):
            @pl.when(y==0)
            def _(): local(nw-1,1,t).start()
        lab_s[...]=lab_ref[...].astype(F32).T
        acc[...]=jnp.zeros_like(acc)
        for hh in range(PER): kst_s[(hh+1)*SLAB-16:(hh+1)*SLAB,:]=jnp.zeros((16,2*GROUP),BF)
        small_ref[...]=jnp.zeros_like(small_ref)
        dl_s[:,SLAB-16:,:]=jnp.zeros((nw,16,D),BF)

    @pl.when(i<nw)
    def _():
        ready(0)
        x=x_s[w,OFF:OFF+WIN,:]
        x_ref[0]=x
        xhat,_=norm_stats(x)
        xn=(xhat*gains_ref[0:1,:]+shifts_ref[0:1,:]).astype(BF)
        for k in range(3):
            for m in range(2):
                at=slice(m*cq,(m+1)*cq)
                v=mm(xn,W1[m,:,k*cq:(k+1)*cq]).astype(BF)
                qkv_ref[0,k,:,at]=v
                if k==0: qT_s[at,:]=v.T
                if k==2: vT_s[at,:]=v.T
        mine=y*nw+w
        labr=lab_ref[pl.ds(mine,1),:]
        labc=jnp.sum(jnp.where(lax.broadcasted_iota(jnp.int32,lab_s.shape,1)==mine,lab_s[...],0.0),axis=1,keepdims=True).astype(jnp.int32)
        lane=lax.broadcasted_iota(jnp.int32,(WIN,GROUP),1)
        oh=jnp.where((labc==lane)|((labc+3)==lane),1.0,0.0).astype(BF)
        hi=564.0
        lo=MASK-hi
        sub=lax.broadcasted_iota(jnp.int32,(GROUP,WIN),0)
        nm=jnp.where(sub<3,jnp.where(sub!=labr,-hi,0.0),jnp.where(sub<6,jnp.where(sub-3!=labr,-lo,0.0),0.0)).astype(BF)
        hl=lane//HD
        for hh in range(PER): kst_s[hh*SLAB:hh*SLAB+WIN,GROUP:]=oh
        nmq=nm[:,0:Q]
        def soften(t):
            m=jnp.max(t,axis=0,keepdims=True)
            e=jnp.exp2((t-m)*CEXP)
            l=jnp.sum(e,axis=0,keepdims=True)
            return (e*(1.0/l)).astype(BF)
        def group(gi,_):
            slot=gi%2
            @pl.when(w*groups+gi>=2)
            def _():
                pltpu.make_async_copy(P_s.at[slot],P_hbm.at[0,0],psem.at[slot]).wait()
            o=pl.multiple_of(gi*GROUP,GROUP)
            qTg=jnp.concatenate([qT_s[pl.ds(o,GROUP),0:Q],nmq],axis=0)
            kg=qkv_ref[0,1,:,pl.ds(o,GROUP)]
            for hh in range(PER): kst_s[hh*SLAB:hh*SLAB+WIN,0:GROUP]=jnp.where(hl==hh,kg,jnp.zeros_like(kg))
            t4=mm(kst_s[...],qTg)
            for hh in range(PER):
                p=soften(t4[hh*SLAB:hh*SLAB+WIN]+bias_ref[gi*PER+hh])
                P_s[slot,:,hh*Q:(hh+1)*Q]=p
                OT_s[w,pl.ds(o+hh*HD,HD),0:Q]=mm(vT_s[pl.ds(o+hh*HD,HD),:],p)
            pltpu.make_async_copy(P_s.at[slot],P_hbm.at[w,gi],psem.at[slot]).start()
            for when,what in plan:
                pl.when(w*groups+gi==min(when,nw*groups-1))(what)
            return 0
        lax.fori_loop(0,groups,group,0)
        spread=pick((R,GROUP),lambda r,c: c%R==r).astype(BF)
        own_rows=pick((D,GROUP),lambda r,c: r//HD==c//R)
        qbd=(mm(qT_s[:,Q:WIN],spread)*own_rows).astype(BF)
        nmr=mm(nm[:,Q:WIN],spread).astype(BF)
        brem=jnp.concatenate([brem_ref[0,:,0:GROUP//2],brem_ref[1,:,0:GROUP//2]],axis=1)
        pr=soften(mm(qkv_ref[0,1],qbd)+mm(oh,nmr)+brem)
        pr_ref[0]=pr
        OT_s[w,:,Q:WIN]=exact(mm(vT_s[...],pr)*own_rows,pick((GROUP,R),lambda r,c: r%R==c))

    @pl.when(i==nw-1)
    def _():
        gather.last(); gather.drain()

    @pl.when(i>=nw)
    def _():
        ready(1)
        x=x_s[w,OFF:OFF+WIN,:]
        og=og_s[w,OFF:OFF+WIN,:]
        attn=OT_s[w].astype(BF).T
        branch=shifts_ref[2:3,:]
        for m in range(2):
            branch=branch+mm_nt(attn[:,m*cq:(m+1)*cq],W1[m,:,3*cq:4*cq])
        branch=branch.astype(BF).astype(F32)
        middle=x+branch
        xhat2,rstd2=norm_stats(middle)
        xn2=(xhat2*gains_ref[1:2,:]+shifts_ref[1:2,:]).astype(BF)
        tg=og.astype(BF)
        xn2_s[...]=xn2; xn2T_s[...]=xn2.T; tg_s[...]=tg; tgT_s[...]=tg.T
        up_s[...]=jnp.zeros_like(up_s); gn2_s[...]=jnp.zeros_like(gn2_s)
        CH=lead
        def side(m,_):
            for o in range(0,cf,CH):
                f1=W1[m,:,4*cq:] if o==0 else W2[m,:,o-lead:o-lead+CH]
                f2=W2[m,:,cf-lead+o:cf-lead+o+CH]
                hid=mm(xn2_s[...],f1)
                act,dact=gelu_both(hid)
                a=act.astype(BF)
                up_s[...]+=mm_nt(a,f2)
                gh=(mm(tg_s[...],f2)*dact).astype(BF)
                gn2_s[...]+=mm_nt(gh,f1)
                acc[m,:,cq+o:cq+o+CH]+=mm(xn2T_s[...],gh)
                acc[m,:,cq+cf+o:cq+cf+o+CH]+=mm(tgT_s[...],a)
            return 0
        lax.fori_loop(0,2,side,0)
        dl_s[w,0:WIN,:]=(branch+up_s[...]+shifts_ref[3:4,:]).astype(BF)
        @pl.when(w<nw-1)
        def _():
            slab(w).start(); slab(w,mate).start()
        @pl.when(w==nw-1)
        def _(): slab(None).start()
        gn2=gn2_s[...]
        gln2=norm_back(gn2,xhat2,rstd2,gains_ref[1:2,:])
        gln2_ref[0]=gln2
        gb=(og+gln2).astype(BF)
        gbT=gb.T
        for m in range(2):
            at=slice(m*cq,(m+1)*cq)
            acc[m,:,0:cq]+=mm(gbT,attn[:,at])
            g=mm(gb,W1[m,:,3*cq:4*cq]).astype(BF)
            g_ref[0,:,at]=g
            gT=g.T
            gT_ref[0,at,:]=gT
            prod=gT.astype(F32)*OT_s[w,at,:]
            nh=nheads//2
            D_ref[0,m*nh:(m+1)*nh,:]=jnp.sum(prod.reshape(nh,HD,WIN),axis=1)
        small_ref[1:2,:]+=jnp.sum(gn2*xhat2,axis=0,keepdims=True)
        small_ref[3:4,:]+=jnp.sum(gn2,axis=0,keepdims=True)
        small_ref[4:5,:]+=jnp.sum(gb.astype(F32),axis=0,keepdims=True)
        small_ref[5:6,:]+=jnp.sum(tg.astype(F32),axis=0,keepdims=True)

    @pl.when(i==2*nw-1)
    def _():
        W2[...]=acc[:,:,cq+lead:].astype(BF)
        pst[...]=acc[:,:,:cq+lead].astype(BF)
        a=pltpu.make_async_copy(W2,dcat_hbm.at[:,:,pl.ds(cq+lead,W2.shape[2])],fin.at[0])
        b=pltpu.make_async_copy(pst,dcat_hbm.at[:,:,pl.ds(0,cq+lead)],fin.at[1])
        a.start(); b.start()
        for k in range(2):
            pltpu.make_async_copy(P_s.at[k],P_hbm.at[0,0],psem.at[k]).wait()
        for k in range(nw-1):
            slab(k).wait(); slab(k,mate).wait()
        slab(None).wait()
        @pl.when(y==1)
        def _():
            for t in range(2): edge(t).wait_send()
        a.wait(); b.wait()

def call_a2(inputs,og,wf,lab,bias,brem,W1,gains,shifts):
    nW=lab.shape[0]//2; WIN=lab.shape[1]; D=inputs.shape[1]; NH=bias.shape[0]
    cq=D//2; lead=W1.shape[2]-4*cq; cf=(wf.shape[1]+lead)//2; SLAB=-(-WIN//16)*16
    Q=bias.shape[2]
    sd=jax.ShapeDtypeStruct; dma=pltpu.SemaphoreType.DMA; v=pltpu.VMEM
    early=lambda shape: pl.BlockSpec((1,)+shape,lambda i:(jnp.minimum(i,nW-1),)+(0,)*len(shape))
    late=lambda shape: pl.BlockSpec((1,)+shape,lambda i:(jnp.maximum(i-nW,0),)+(0,)*len(shape))
    outs=[sd((nW,3,WIN,D),BF),sd((nW,WIN,D),F32),sd((nW,NH//PER,WIN,PER*Q),BF),sd((nW,WIN,GROUP),BF),sd((nW,WIN,D),F32),sd((nW,WIN,D),BF),sd((nW,D,WIN),BF),sd((nW,NH,WIN),F32),
          sd((2*nW,SLAB,D),BF),sd((SLAB,D),BF),sd((2,D,cq+2*cf),BF),sd((8,D),F32)]
    return pl.pallas_call(functools.partial(kernel_a2,NH),grid=(2*nW,),
      in_specs=[ANY,ANY,ANY,full(lab.shape),full(bias.shape,pipeline_mode=ONE),full(brem.shape),full(W1.shape,pipeline_mode=ONE),full(gains.shape),full(shifts.shape)],
      out_specs=[early((3,WIN,D)),early((WIN,D)),ANY,early((WIN,GROUP)),late((WIN,D)),late((WIN,D)),late((D,WIN)),late((NH,WIN)),ANY,ANY,ANY,full((8,D))],
      out_shape=outs,
      scratch_shapes=[v((nW,SLAB,D),F32),v((nW,SLAB,D),F32),v((2,D,2*cf-lead),BF),v((nW,D,WIN),F32),v((D,WIN),BF),v((D,WIN),BF),v((2,WIN,PER*Q),BF),v((PER*SLAB,2*GROUP),BF),
        v((2,D,cq+2*cf),F32),v((2,D,cq+lead),BF),v((WIN,D),BF),v((D,WIN),BF),v((WIN,D),BF),v((D,WIN),BF),v((WIN,D),F32),v((WIN,D),F32),v((nW,SLAB,D),BF),
        v((WIN,2*nW),F32),dma((2,)),dma((2,2*nW)),dma((2,2))]+gather_sems()+[dma((nW,)),dma((nW,)),dma((nW,)),dma((2,))],
      compiler_params=pltpu.CompilerParams(vmem_limit_bytes=63*1024*1024,dimension_semantics=("arbitrary",),collective_id=2,has_side_effects=True),
      name="kernel_a2")(inputs,og,wf,lab,bias,brem,W1,gains,shifts)

class Reduce:
    def __init__(self,src,out,own,r1,bufs,ss,rs,ls):
        self.src,self.out,self.own,self.r1,self.bufs=src,out,own,r1,bufs
        self.ss,self.rs,self.ls=ss,rs,ls
        z,x,c,y=place_of()
        self.x,self.c,self.y,self.h,self.l=x,c,y,z//2,z%2
    def to(self,x=None,h=None,l=None,c=None,y=None):
        pick=lambda new,old: old if new is None else new
        return dev(pick(h,self.h)*2+pick(l,self.l),pick(x,self.x),pick(c,self.c),pick(y,self.y))
    def mine(self,k):
        return pltpu.make_async_copy(self.src.at[k%2,:,:,k//2,self.c],self.own.at[k//2,:,:,k%2],self.ls.at[k])
    def theirs(self,k):
        return send(self.src.at[k%2,:,:,k//2,1-self.c],self.r1.at[k//2,:,:,k%2],self.ss.at[k],self.rs.at[k],self.to(c=1-self.c))
    def turns(self,core):
        x,h,l,y=self.x,self.h,self.l,self.y
        s=slice(None)
        if core==0:
            return [((1-x,),dict(x=1-x),lambda a,b,d:(x,a,b,d)),((x,s,1-l),dict(l=1-l),lambda a,d:(x,a,l,d)),
                    ((x,1-h,l),dict(h=1-h),lambda d:(x,h,l,d)),((x,h,l,1-y),dict(y=1-y),None)]
        return [((s,s,1-l),dict(l=1-l),lambda a,b,d:(a,b,l,d)),((s,1-h,l),dict(h=1-h),lambda a,d:(a,h,l,d)),
                ((1-x,h,l),dict(x=1-x),lambda d:(x,h,l,d)),((x,h,l,1-y),dict(y=1-y),None)]
    def give(self,k,core):
        at,where,_=self.turns(core)[k]
        return send(self.own.at[at],self.bufs[k],self.ss.at[4+k],self.rs.at[4+k],self.to(**where))
    def start(self):
        for k in range(4):
            self.theirs(k).start(); self.mine(k).start()
    def add(self,dst,*srcs):
        total=srcs[0][...].astype(F32)
        for s in srcs[1:]: total=total+s[...].astype(F32)
        dst[...]=total.astype(dst.dtype)
    def by_core(self,f):
        for core in range(2):
            @pl.when(self.c==core)
            def _(): f(core)
    def one(self):
        for k in range(4):
            self.mine(k).wait(); self.theirs(k).wait_recv()
        def step(k,_):
            at=(k//8,(k//4)%2,(k//2)%2,k%2)
            self.add(self.own.at[at],self.own.at[at],self.r1.at[at])
            return 0
        lax.fori_loop(0,16,step,0)
        self.by_core(lambda core: self.give(0,core).start())
    def turn(self,k):
        def f(core):
            stay=self.turns(core)[k][2]
            self.give(k,core).wait_recv()
            def step(i,_):
                at=[(i//4,(i//2)%2,i%2),(i//2,i%2),(i,)][k]
                self.add(self.own.at[stay(*at)],self.own.at[stay(*at)],self.bufs[k].at[at])
                return 0
            lax.fori_loop(0,8>>k,step,0)
            self.give(k+1,core).start()
        self.by_core(f)
    def four(self):
        def f(core):
            self.give(3,core).wait_recv()
            self.add(self.out,self.own.at[self.x,self.h,self.l,self.y],self.bufs[3])
            for k in range(4): self.give(k,core).wait_send()
        self.by_core(f)
        for k in range(4): self.theirs(k).wait_send()

def reduce_scratch(rows,cols):
    v=lambda *d: pltpu.VMEM(d+(rows,cols),BF); dma=pltpu.SemaphoreType.DMA
    return [v(2,2,2,2),v(2,2,2,2),v(2,2,2),v(2,2),v(2),v(),dma((8,)),dma((8,)),dma((4,))]

class Sums:
    def __init__(self,slabs,got,res,ss,rs,ts,us):
        self.slabs,self.got,self.res,self.ss,self.rs,self.ts,self.us=slabs,got,res,ss,rs,ts,us
        z,x,c,y=place_of()
        self.s=(z*2+x)*2+c; self.y=y; self.n=slabs.shape[1]
    def part(self,k,yy):
        me=self.y*16+self.s
        return send(self.slabs.at[yy,k],self.got.at[me],self.ss.at[yy*self.n+k],self.rs.at[me],(k,yy))
    def other(self,k,yy):
        return jnp.logical_or(self.s!=k,self.y!=yy)
    def scatter(self):
        for k in range(self.n):
            for yy in range(2):
                @pl.when(self.other(k,yy))
                def _(): self.part(k,yy).start()
    def back(self,to,k):
        return send(self.res.at[k],self.res.at[k],self.ts.at[to],self.us.at[k],(to,self.y))
    def collect(self):
        me=self.y*16+self.s
        @pl.when(self.s<self.n)
        def _():
            self.got[me]=self.slabs[self.y,self.s]
            def wait(i,_):
                @pl.when(i!=me)
                def _():
                    send(self.slabs.at[0,0],self.got.at[i],self.ss.at[0],self.rs.at[i],(self.s,1-self.y)).wait_recv()
                return 0
            lax.fori_loop(0,32,wait,0)
            total=self.got[0]
            for i in range(1,32): total=total+self.got[i]
            self.res[self.s]=total
            for to in range(16):
                @pl.when(self.s!=to)
                def _(): self.back(to,self.s).start()
    def finish(self):
        for k in range(self.n):
            @pl.when(self.s!=k)
            def _(): self.back(k,k).wait_recv()
        @pl.when(self.s<self.n)
        def _():
            for to in range(16):
                @pl.when(self.s!=to)
                def _(): self.back(to,self.s).wait_send()
        for k in range(self.n):
            for yy in range(2):
                @pl.when(self.other(k,yy))
                def _(): self.part(k,yy).wait_send()

def kernel_bc(nheads,x_ref,gln2_ref,qkv_ref,g_ref,gT_ref,D_ref,P_ref,pr_ref,W1,gains_ref,shifts_ref,sm_ref,pos_ref,pose_ref,dcat_hbm,dlast_hbm,
              ev_hbm,hd_hbm,evl_hbm,hdl_hbm,redq_ref,redm_ref,tab_ref,sum_ref,
              G_s,Gx,Gr_s,Gxr,vst_s,dS_s,dsr_s,gbd_s,qbd_s,aq,dq_s,kT_s,gq_s,gqT_s,dd_s,small_ref,acc,slabs,got,res,
              gs,gr_,ge,dl,ds,dr,es,er,us,ss0,rs0,ts0,us0,
              *more):
    w=pl.program_id(0); nw=dd_s.shape[0]
    z,xc,c,y=place_of()
    s=(z*2+xc)*2+c
    mate=dev(z,xc,c,1-y); sib=dev(z,xc,1-c,y)
    D=x_ref.shape[-1]; WIN=x_ref.shape[-2]; SLAB=dd_s.shape[1]
    cq=D//2
    groups=nheads//PER
    tiles=G_s.shape[0]; Q=tiles*128; R=WIN-Q; part=Gx.shape[1]//nheads
    big=Reduce(dcat_hbm,redm_ref,more[9],more[10],more[11:15],*more[15:18])
    red=Reduce(dq_s,redq_ref,more[0],more[1],more[2:6],*more[6:9])
    def slab(k,to=None):
        at=ev_hbm.at[y*nw+k]
        if to is None: return pltpu.make_async_copy(dd_s.at[k],at,dl.at[k])
        return send(dd_s.at[k],at,ds.at[k],dr.at[k],to)
    def tail(k):
        lead=SLAB-hd_hbm.shape[0]
        return send(dd_s.at[nw-1,pl.ds(lead,hd_hbm.shape[0])],hd_hbm,es.at[k],er,((s+1)%16,k))
    def early(k):
        lead=SLAB-hdl_hbm.shape[0]
        if k==0: return pltpu.make_async_copy(dlast_hbm,evl_hbm.at[y],us.at[0])
        if k==1: return send(dlast_hbm,evl_hbm.at[y],us.at[1],us.at[2],mate)
        return send(dlast_hbm.at[pl.ds(lead,hdl_hbm.shape[0])],hdl_hbm,us.at[k+1],us.at[5],((s+1)%16,k-2))
    def edge_trade():
        return send(Gr_s,Gxr,ge.at[0],ge.at[1],sib)
    def trade(h):
        r=pl.multiple_of(h*WIN+(1-c)*(WIN-part),8)
        return send(G_s.at[:,pl.ds(r,part)],Gx.at[:,pl.ds(pl.multiple_of(h*part,8),part)],gs.at[h],gr_.at[h],sib)
    everyone=[((s+t)%16,yy) for t in range(1,16) for yy in (y,1-y)]+[mate]
    @pl.when(w==0)
    def _():
        hail(everyone)
        aq[...]=jnp.zeros_like(aq); G_s[...]=jnp.zeros_like(G_s); Gr_s[...]=jnp.zeros_like(Gr_s); small_ref[...]=sm_ref[...]
        dd_s[:,SLAB-16:,:]=jnp.zeros((nw,16,D),BF)
        for hh in range(PER): vst_s[(hh+1)*SLAB-16:(hh+1)*SLAB,:]=jnp.zeros((16,GROUP),BF)
    def met():
        heard(everyone)
        big.start()
        early(0).start(); early(1).start()
        @pl.when(y==1)
        def _():
            early(2).start(); early(3).start()
    plan=((0,met),(2,big.one),(6,lambda: big.turn(0)),(10,lambda: big.turn(1)),(13,lambda: big.turn(2)))
    kT_s[...]=qkv_ref[0,1].T
    lane=lax.broadcasted_iota(jnp.int32,(WIN,GROUP),1)
    hl=lane//HD
    lift=pick((GROUP,R),lambda r,c: r%R==c).astype(BF)
    own_cols=pick((GROUP,D),lambda r,c: r//R==c//HD)
    gbd_s[...]=(mm(lift,g_ref[0,Q:WIN,:])*own_cols).astype(BF)
    qbd_s[...]=(mm(lift,qkv_ref[0,0,Q:WIN,:])*own_cols).astype(BF)
    Dr=exact(D_ref[0,:,Q:WIN],pick((R,GROUP),lambda r,c: c%R==r))
    Dr=jnp.sum(Dr*pick((nheads,GROUP),lambda r,c: c//R==r),axis=0,keepdims=True)
    dsr=pr_ref[0].astype(F32)*(mm_nt(qkv_ref[0,2],gbd_s[...])-Dr)
    Gr_s[...]+=dsr
    dsr_s[...]=dsr.astype(BF)
    gqT_s[:,Q:WIN]=exact(mm(kT_s[...],dsr_s[...])*pick((D,GROUP),lambda r,c: r//HD==c//R),pick((GROUP,R),lambda r,c: r%R==c))
    def group(gi,_):
        o=pl.multiple_of(gi*GROUP,GROUP)
        gTg=gT_ref[0,pl.ds(o,GROUP),0:Q]
        vg=qkv_ref[0,2,:,pl.ds(o,GROUP)]
        qg=qkv_ref[0,0,0:Q,pl.ds(o,GROUP)]
        gg=g_ref[0,0:Q,pl.ds(o,GROUP)]
        for hh in range(PER): vst_s[hh*SLAB:hh*SLAB+WIN,:]=jnp.where(hl==hh,vg,jnp.zeros_like(vg))
        dp4=mm(vst_s[...],gTg)
        for hh in range(PER):
            h=gi*PER+hh
            dsc=P_ref[0,gi,:,hh*Q:(hh+1)*Q].astype(F32)*(dp4[hh*SLAB:hh*SLAB+WIN]-D_ref[0,pl.ds(h,1),0:Q])
            for k in range(tiles):
                G_s[k,pl.ds(pl.multiple_of(h*WIN,8),WIN),:]+=dsc[:,k*128:(k+1)*128]
            dsl=dsc.astype(BF)
            dS_s[:,hh*Q:(hh+1)*Q]=dsl
            gqT_s[pl.ds(o+hh*HD,HD),0:Q]=mm(kT_s[pl.ds(o+hh*HD,HD),:],dsl)
        zero=jnp.zeros_like(gg); hq=hl[0:Q]
        gst=jnp.concatenate([jnp.where(hq==hh,gg,zero) for hh in range(PER)],axis=0)
        qst=jnp.concatenate([jnp.where(hq==hh,qg,zero) for hh in range(PER)],axis=0)
        dv=mm(P_ref[0,gi],gst)+mm(pr_ref[0],gbd_s[:,pl.ds(o,GROUP)])
        dk=mm(dS_s[...],qst)+mm(dsr_s[...],qbd_s[:,pl.ds(o,GROUP)])
        gq_s[1,:,pl.ds(o,GROUP)]=(dk*(1.0/SQ)).astype(BF)
        gq_s[2,:,pl.ds(o,GROUP)]=dv.astype(BF)
        for when,what in plan:
            pl.when(w*groups+gi==min(when,nw*groups-1))(what)
        @pl.when(w==nw-1)
        def _():
            for hh in range(PER): trade(gi*PER+hh).start()
            @pl.when(gi==0)
            def _(): edge_trade().start()
        return 0
    lax.fori_loop(0,groups,group,0)
    gq_s[0]=(gqT_s[...]*(1.0/SQ)).astype(BF).T
    x=x_ref[0]
    xhat,rstd=norm_stats(x)
    xn=(xhat*gains_ref[0:1,:]+shifts_ref[0:1,:]).astype(BF)
    xnT=xn.T
    gr=jnp.zeros((WIN,D),F32)
    for m in range(2):
        for k in range(3):
            gc=gq_s[k,:,m*cq:(m+1)*cq]
            gr=gr+mm_nt(gc,W1[m,:,k*cq:(k+1)*cq])
            aq[m,:,k*cq:(k+1)*cq]+=mm(xnT,gc)
    @pl.when(w==nw-1)
    def _():
        dq_s[...]=aq[...].astype(BF).reshape(dq_s.shape)
        red.start()
    dd_s[w,0:WIN,:]=(gln2_ref[0]+norm_back(gr,xhat,rstd,gains_ref[0:1,:])).astype(BF)
    slab(w).start(); slab(w,mate).start()
    @pl.when(jnp.logical_and(w==nw-1,y==1))
    def _():
        tail(0).start(); tail(1).start()
    small_ref[0:1,:]+=jnp.sum(gr*xhat,axis=0,keepdims=True)
    small_ref[2:3,:]+=jnp.sum(gr,axis=0,keepdims=True)
    @pl.when(w==nw-1)
    def _():
        for h in range(nheads): trade(h).wait()
        edge_trade().wait()
        acc[...]=jnp.zeros_like(acc)
        nh=acc.shape[0]; LW=tiles*128
        base=c*(WIN-part)
        def one_hots(g,hr,lr,width):
            iota=lax.broadcasted_iota(jnp.int32,(256,width),0).astype(F32).astype(BF)
            A=jnp.concatenate([jnp.where(hr==m,g,0.0) for m in range(nh)],axis=0).astype(BF)
            oh=jnp.where(iota==lr.astype(F32).astype(BF),jnp.ones((),BF),jnp.zeros((),BF))
            return mm_nt(A,oh)
        def rows(r,_):
            r8=pl.multiple_of(r*8,8)
            f8=pl.multiple_of(base+r*8,8)
            pos=pos_ref[pl.ds(f8,8),0:LW]
            hi8=pos>>8; lo8=pos&255
            tot=jnp.zeros((nh*nheads,256),F32)
            for k in range(8):
                g=jnp.concatenate([G_s[q,pl.ds(f8+k,nheads,stride=WIN),:]+Gx[q,pl.ds(r8+k,nheads,stride=part),:] for q in range(tiles)],axis=1)
                tot=tot+one_hots(g,hi8[k:k+1,:],lo8[k:k+1,:],LW)
            acc[...]+=tot.reshape(acc.shape)
            return 0
        turned=mm_nt(pick((GROUP,GROUP),lambda r,c: c==(r%nheads)*R+r//nheads).astype(BF),(Gr_s[...]+Gxr[...]).astype(BF))
        tot=jnp.zeros((nh*nheads,256),F32)
        for k in range(R):
            pos=pose_ref[k:k+1,:]
            hi=jnp.where(c==k//(R//2),pos>>8,-1)
            tot=tot+one_hots(turned[k*nheads:(k+1)*nheads],hi,pos&255,WIN)
        acc[...]+=tot.reshape(acc.shape)
        n=part//8
        cuts=[c,n*5//25,n*15//25,n]
        for f,after in enumerate((red.one,lambda: red.turn(0),None)):
            lax.fori_loop(cuts[f],cuts[f+1],rows,0)
            if after: after()
        half=nheads//2
        for yy in range(2):
            for k in range(nh): slabs[yy,k]=acc[k,yy*half:(yy+1)*half]
            for k in range(2): slabs[yy,nh+k]=small_ref[:,k*256:(k+1)*256]
        sums=Sums(slabs,got,res,ss0,rs0,ts0,us0)
        sums.scatter()
        red.turn(1)
        sums.collect()
        red.turn(2)
        big.four()
        sums.finish()
        red.four()
        for m in range(nh):
            tab_ref[:,m*256:(m+1)*256]=res[m]
        for k in range(2): sum_ref[:,k*256:(k+1)*256]=res[nh+k]
        for k in range(nw):
            slab(k).wait(); slab(k,mate).wait()
        @pl.when(y==1)
        def _():
            tail(0).wait_send(); tail(1).wait_send(); early(2).wait_send(); early(3).wait_send()
        tail(0).wait_recv(); early(2).wait_recv()
        early(0).wait(); early(1).wait()

def call_bc(x,gln2,qkv,g,gT,Dd,Pp,Pr,W1,gains,shifts,sm,pp,pos_index,dcat,dlast,T):
    nW,WIN,D=x.shape; NH=Dd.shape[1]
    cq=D//2; tiles=WIN//128; Q=tiles*128; SLAB=-(-WIN//16)*16; EDGE=-(-(SLAB-WIN//2)//16)*16
    part=-(-WIN//16)*8
    nh=-(-T//256)
    rows,more=dcat.shape[-2:]; cols=3*cq
    sd=jax.ShapeDtypeStruct; dma=pltpu.SemaphoreType.DMA; v=pltpu.VMEM
    return pl.pallas_call(functools.partial(kernel_bc,NH),grid=(nW,),
      in_specs=[per((WIN,D)),per((WIN,D),pipeline_mode=ONE),per((3,WIN,D)),per((WIN,D)),per((D,WIN)),per((NH,WIN)),per(Pp.shape[1:]),per((WIN,GROUP)),
        full((2,D,cols),pipeline_mode=ONE),full(gains.shape),full(shifts.shape),full(sm.shape),full(pp.shape,pipeline_mode=ONE),pl.BlockSpec((WIN-Q,WIN),lambda w:(Q//(WIN-Q),0)),ANY,ANY],
      out_specs=[ANY,ANY,ANY,ANY,full((rows,cols),pipeline_mode=ONE),full((rows,more),pipeline_mode=ONE),full((NH//2,nh*256),pipeline_mode=ONE),full(sm.shape)],
      out_shape=[sd((2*nW,SLAB,D),BF),sd((EDGE,D),BF),sd((2,SLAB,D),BF),sd((EDGE,D),BF),sd((rows,cols),F32),sd((rows,more),F32),sd((NH//2,nh*256),F32),sd(sm.shape,F32)],
      scratch_shapes=[v((tiles,NH*WIN,128),F32),v((tiles,NH*part,128),F32),v((WIN,GROUP),F32),v((WIN,GROUP),F32),v((PER*SLAB,GROUP),BF),v((WIN,PER*Q),BF),v((WIN,GROUP),BF),v((GROUP,D),BF),v((GROUP,D),BF),v((2,D,cols),F32),v((2,2,2,2,2,rows,cols),BF),v((D,WIN),BF),v((3,WIN,D),BF),v((D,WIN),F32),
        v((nW,SLAB,D),BF),v(sm.shape,F32),v((nh,NH,256),F32),v((2,nh+2,8,256),F32),v((32,8,256),F32),v((nh+2,8,256),F32),
        dma((NH,)),dma((NH,)),dma((2,)),dma((nW,)),dma((nW,)),dma((nW,)),dma((2,)),dma,dma((6,)),dma((2*nh+4,)),dma((32,)),dma((16,)),dma((nh+2,))]+reduce_scratch(rows,cols)+reduce_scratch(rows,more),
      compiler_params=pltpu.CompilerParams(vmem_limit_bytes=63*1024*1024,dimension_semantics=("arbitrary",),collective_id=3,has_side_effects=True),
      name="kernel_bc")(x,gln2,qkv,g,gT,Dd,Pp,Pr,W1,gains,shifts,sm,pp,pos_index,dcat,dlast)


def kernel_f(in_ref,og_ref,ev_ref,evl_ref,ev2_ref,hd_ref,hd2_ref,redq_ref,redm_ref,tab_ref,sum_ref,
             out_ref,din_ref,dqkv_ref,dproj_ref,dfc1_ref,dfc2_ref,dgain_ref,dshift_ref,dtab_ref,end_s):
    j=pl.program_id(0); nw=pl.num_programs(0)//2
    shift=in_ref.shape[0]//2; WIN=2*shift
    edge,SLAB=hd_ref.shape[0],ev_ref.shape[1]
    off=edge-(SLAB-shift)
    @pl.when(j==0)
    def _():
        end_s[0]=hd_ref[...].astype(F32); end_s[1]=hd2_ref[...].astype(F32)
        cq=dqkv_ref.shape[2]; cf=dfc1_ref.shape[1]
        for k in range(3): dqkv_ref[k]=redq_ref[:,k*cq:(k+1)*cq]
        dproj_ref[...]=redm_ref[:,0:cq]
        dfc1_ref[...]=redm_ref[:,cq:cq+cf]
        dfc2_ref[...]=redm_ref[:,cq+cf:]
        dgain_ref[...]=sum_ref[0:2,:]; dshift_ref[...]=sum_ref[2:6,:]
        dtab_ref[...]=tab_ref[:,0:dtab_ref.shape[1]]
    e=jnp.where(j%nw==nw-1,evl_ref[0],ev_ref[0]).astype(F32)
    for k,(base,res,v) in enumerate(((in_ref,out_ref,e),(og_ref,din_ref,ev2_ref[0].astype(F32)))):
        res[0:shift,:]=base[0:shift,:]+end_s[k,off:off+shift,:]
        res[shift:WIN,:]=base[shift:WIN,:]+v[0:shift,:]
        end_s[k]=v[SLAB-edge:,:]

def call_f(inputs,og,ev,evl,ev2,hd,hd2,redq,redm,tab,small,cq,cf,T):
    tok,D=inputs.shape; n,SLAB,_=ev.shape; WIN=tok//n; rows=redq.shape[0]
    sd=jax.ShapeDtypeStruct
    blk=pl.BlockSpec((WIN,D),lambda j:(j,0)); slab=pl.BlockSpec((1,SLAB,D),lambda j:(j,0,0))
    shapes=[(3,rows,cq),(rows,cq),(rows,cf),(rows,cf),(2,D),(4,D),(tab.shape[0],T)]
    return pl.pallas_call(kernel_f,grid=(n,),
      in_specs=[blk,blk,slab,pl.BlockSpec((1,SLAB,D),lambda j:(j//(n//2),0,0)),slab]+[full(v.shape) for v in (hd,hd2,redq,redm,tab,small)],
      out_specs=[blk,blk]+[full(v) for v in shapes],
      out_shape=[sd((tok,D),F32),sd((tok,D),F32)]+[sd(v,F32) for v in shapes],
      scratch_shapes=[pltpu.VMEM((2,)+hd.shape,F32)],
      compiler_params=pltpu.CompilerParams(vmem_limit_bytes=63*1024*1024,dimension_semantics=("arbitrary",)),
      name="kernel_f")(inputs,og,ev,evl,ev2,hd,hd2,redq,redm,tab,small)

def gathered(piece,names,nseq,nheads):
    full=lax.all_gather(piece,names,axis=0,tiled=False)
    return full.reshape((nseq,nheads)+piece.shape)

def natural(block):
    s,h,r,c=block.shape
    return block.transpose(0,2,1,3).reshape(s*r,h*c)

def owners(grad,nseq,nheads):
    r,c=grad.shape
    return grad.reshape(nseq,r//nseq,nheads,c//nheads).transpose(0,2,1,3).reshape(nseq*nheads,r//nseq,c//nheads)

def from_next(rows):
    n=lax.axis_size("seq")
    return lax.ppermute(rows,"seq",[(i,(i-1)%n) for i in range(n)])

def to_next(rows):
    n=lax.axis_size("seq")
    return lax.ppermute(rows,"seq",[(i,(i+1)%n) for i in range(n)])

def spread(rows):
    n=lax.axis_size("heads")
    flat=rows.reshape(-1,rows.shape[-1])
    if n==2:
        other=lax.ppermute(flat,"heads",[(0,1),(1,0)])
        me=lax.axis_index("heads")
        return jnp.where(me==0,jnp.concatenate([flat,other]),jnp.concatenate([other,flat]))
    return lax.all_gather(flat,"heads",axis=0,tiled=True)

def place(rows,base,shift):
    every=spread(rows)
    keep=every.shape[0]-shift
    return base+jnp.concatenate([to_next(every[keep:]),every[:keep]]).astype(F32)

def body(inputs,w_qkv,w_proj,w_fc1,w_fc2,gains,shifts,rel_table,region,pos_index,out_grad):
    nseq=lax.axis_size("seq"); nheads=lax.axis_size("heads"); me=lax.axis_index("heads")
    linked=nseq==16 and nheads==2
    names=("seq","heads")
    tok,D=inputs.shape; WIN=pos_index.shape[0]; shift=WIN//2; T=rel_table.shape[1]
    nW=tok//WIN//nheads
    rows=w_qkv.shape[1]; cq=w_qkv.shape[2]; cf=w_fc1.shape[1]
    lab=region.reshape(-1,WIN)
    if linked:
        W1,bias,brem,wf,posT=call_w(w_qkv,w_proj.T,w_fc1,w_fc2.T,pos_index,rel_table)
        qkv,x,Pp,Pr,gln2,g,gT,Dd,ev,dlast,dcat,sm=call_a2(inputs,out_grad,wf,lab,bias,brem,W1,gains,shifts)
        ev2,hd2,evl,hd,redq,redm,d_table,small=call_bc(x,gln2,qkv,g,gT,Dd,Pp,Pr,W1,gains,shifts,sm,posT,pos_index,dcat.reshape(2,2,2,2,2,rows,-1),dlast,T)
        out,din,dq,dp,d1,d2,dg,dsh,dt=call_f(inputs,out_grad,ev,evl,ev2,hd,hd2,redq,redm,d_table,small,cq,cf,T)
        return (out,din,dq,dp.T,d1,d2.T,dg,dsh,dt)
    posT=pos_index.T
    wide=-(-WIN//128)*128
    posP=jnp.pad(posT,((0,0),(0,wide-WIN)))
    start=me*nW*WIN
    lab=lax.dynamic_slice_in_dim(lab,me*nW,nW,0)
    labc=lab[:,:,None]; labr=lab[:,None,:]
    wq=jnp.concatenate([w_qkv[0],w_qkv[1],w_qkv[2],w_proj.T],axis=1).astype(BF)
    wf=jnp.concatenate([w_fc1,w_fc2.T],axis=1).astype(BF)
    table=lax.all_gather(rel_table,"heads",axis=0,tiled=True)
    NH=table.shape[0]
    every=gathered(jnp.concatenate([wq,wf],axis=1),names,nseq,nheads)
    ends=[i*cq for i in range(5)]+[4*cq+cf,4*cq+2*cf]
    W=jnp.concatenate([natural(every[...,a:b]) for a,b in zip(ends[:-1],ends[1:])],axis=1)[None]
    bias=call_p(posP,pack_table(table),WIN)
    def mine(v):
        ext=jnp.concatenate([v,from_next(v[:shift])])
        return lax.dynamic_slice_in_dim(ext,start+shift,nW*WIN,0).reshape(nW,WIN,-1)
    x=mine(inputs); og=mine(out_grad)
    delta,gln2,qkv,g,gT,Dd,Pp,dcat,sm_a=call_a(x,og,labc,labr,bias,W,gains,shifts)
    dd,dqkv,G,sm_b=call_b(x,gln2,qkv,g,gT,Dd,Pp,W,gains,shifts)
    grads=[dqkv[0,:,c*D:(c+1)*D] for c in range(3)]+[dcat[0,:,:D],dcat[0,:,D:D+cf*nheads],dcat[0,:,D+cf*nheads:]]
    red=lax.psum_scatter(jnp.concatenate([owners(v,nseq,nheads) for v in grads],axis=2),names,scatter_dimension=0,tiled=False).astype(F32)
    redq,redm=red[:,:3*cq],red[:,3*cq:]
    d_table,small=lax.psum((call_t(G,posT,T,NH),sm_a+sm_b),names)
    nl=rel_table.shape[0]
    d_table=lax.dynamic_slice_in_dim(d_table,me*nl,nl,0)
    output=place(delta,inputs,shift)
    d_inputs=place(dd,out_grad,shift)
    d_qkv=redq.reshape(rows,3,cq).transpose(1,0,2)
    d_proj=redm[:,:cq].T; d_fc1=redm[:,cq:cq+cf]; d_fc2=redm[:,cq+cf:].T
    return (output,d_inputs,d_qkv,d_proj,d_fc1,d_fc2,small[0:2],small[2:6],d_table)

def solution(mesh):
    placed=(P("seq",None),P(None,"seq","heads"),P("heads","seq"),P("seq","heads"),P("heads","seq"),P(),P(),P("heads",None),P("seq"),P(),P("seq",None))
    return jax.shard_map(body,mesh=mesh,in_specs=placed,
    out_specs=(P("seq",None),P("seq",None),P(None,"seq","heads"),P("heads","seq"),P("seq","heads"),P("heads","seq"),P(),P(),P("heads",None)),
    check_vma=False)
```

```python
import functools
import math

import jax, jax.numpy as jnp
from jax import lax
from jax.experimental import pallas as pl
from jax.experimental.pallas import tpu as pltpu
from jax.sharding import PartitionSpec as P

BF=jnp.bfloat16; F32=jnp.float32
HD=32; GROUP=128; PER=4
EPS=1e-5
SQ=math.sqrt(32.0)
CEXP=math.log2(math.e)/SQ
MASK=100.0*SQ

def mm(a,b):
    return lax.dot_general(a,b,(((1,),(0,)),((),())),preferred_element_type=F32)
def mm_nt(a,b):
    return lax.dot_general(a,b,(((1,),(1,)),((),())),preferred_element_type=F32)

def norm_stats(v):
    mean=jnp.mean(v,axis=-1,keepdims=True)
    c=v-mean
    var=jnp.mean(c*c,axis=-1,keepdims=True)
    rstd=lax.rsqrt(var+EPS)
    return c*rstd, rstd

def norm_back(gy,xhat,rstd,gain):
    gx=gy*gain
    m1=jnp.mean(gx,axis=-1,keepdims=True)
    m2=jnp.mean(gx*xhat,axis=-1,keepdims=True)
    return rstd*(gx-m1-xhat*m2)

P0=0.3275911
A1,A2,A3,A4,A5=0.254829592,-0.284496736,1.421413741,-1.453152027,1.061405429
def gelu_both(x):
    e=jnp.exp2(x*x*(-0.5*math.log2(math.e)))
    t=1.0/(1.0+(P0/math.sqrt(2.0))*jnp.abs(x))
    poly=t*(0.5*A1+t*(0.5*A2+t*(0.5*A3+t*(0.5*A4+t*(0.5*A5)))))
    half=poly*e
    phi=jnp.where(x>=0,1.0-half,half)
    return x*phi, phi+x*e*(1.0/math.sqrt(2.0*math.pi))

def kernel_a(nheads,x_ref,og_ref,labc_ref,labr_ref,bias_ref,W_ref,gains_ref,shifts_ref,
             delta_ref,gln2_ref,qkv_ref,g_ref,gT_ref,D_ref,P_hbm,dcat_ref,small_ref,
             qT_s,vT_s,OT_s,P_s,acc,sem,xn2_s,xn2T_s,tg_s,tgT_s,up_s,gn2_s):
    w=pl.program_id(0); nw=pl.num_programs(0)
    D=x_ref.shape[-1]; WIN=x_ref.shape[-2]
    parts=W_ref.shape[0]; cq=D//parts; cf=(W_ref.shape[2]-4*cq)//2
    groups=nheads//PER
    x=x_ref[0]
    xhat,_=norm_stats(x)
    xn=(xhat*gains_ref[0:1,:]+shifts_ref[0:1,:]).astype(BF)
    for c in range(3):
        for m in range(parts):
            at=slice(m*cq,(m+1)*cq)
            y=mm(xn,W_ref[m,:,c*cq:(c+1)*cq]).astype(BF)
            qkv_ref[0,c,:,at]=y
            if c==0: qT_s[at,:]=y.T
            if c==2: vT_s[at,:]=y.T
    labc=labc_ref[0]; labr=labr_ref[0]
    lane=lax.broadcasted_iota(jnp.int32,(WIN,GROUP),1)
    oh=jnp.where((labc==lane)|((labc+3)==lane),1.0,0.0).astype(BF)
    hi=564.0
    lo=MASK-hi
    sub=lax.broadcasted_iota(jnp.int32,(GROUP,WIN),0)
    nm=jnp.where(sub<3,jnp.where(sub!=labr,-hi,0.0),jnp.where(sub<6,jnp.where(sub-3!=labr,-lo,0.0),0.0)).astype(BF)
    hl=lane//HD

    def group(gi,_):
        slot=gi%2
        step=w*groups+gi
        @pl.when(step>=2)
        def _():
            pltpu.make_async_copy(P_s.at[slot],P_hbm.at[0,pl.ds(0,PER)],sem.at[slot]).wait()
        o=pl.multiple_of(gi*GROUP,GROUP)
        qTg=jnp.concatenate([qT_s[pl.ds(o,GROUP),:],nm],axis=0)
        kg=qkv_ref[0,1,:,pl.ds(o,GROUP)]
        for hh in range(PER):
            kh=jnp.concatenate([jnp.where(hl==hh,kg,jnp.zeros_like(kg)),oh],axis=1)
            t=mm(kh,qTg)+bias_ref[gi*PER+hh]
            m=jnp.max(t,axis=0,keepdims=True)
            e=jnp.exp2((t-m)*CEXP)
            l=jnp.sum(e,axis=0,keepdims=True)
            p=(e*(1.0/l)).astype(BF)
            P_s[slot,hh]=p
            OT_s[pl.ds(o+hh*HD,HD),:]=mm(vT_s[pl.ds(o+hh*HD,HD),:],p)
        pltpu.make_async_copy(P_s.at[slot],P_hbm.at[w,pl.ds(gi*PER,PER)],sem.at[slot]).start()
        return 0
    lax.fori_loop(0,groups,group,0)

    attn=OT_s[...].astype(BF).T
    branch=shifts_ref[2:3,:]
    for m in range(parts):
        branch=branch+mm_nt(attn[:,m*cq:(m+1)*cq],W_ref[m,:,3*cq:4*cq])
    branch=branch.astype(BF).astype(F32)
    middle=x+branch
    xhat2,rstd2=norm_stats(middle)
    xn2=(xhat2*gains_ref[1:2,:]+shifts_ref[1:2,:]).astype(BF)
    og=og_ref[0]
    tg=og.astype(BF)
    xn2_s[...]=xn2; xn2T_s[...]=xn2.T; tg_s[...]=tg; tgT_s[...]=tg.T
    up_s[...]=jnp.zeros_like(up_s); gn2_s[...]=jnp.zeros_like(gn2_s)
    CH=min(512,cf); each=cf//CH
    @pl.when(w==0)
    def _():
        acc[...]=jnp.zeros_like(acc)
        small_ref[...]=jnp.zeros_like(small_ref)
    def chunk(c,_):
        m=c//each
        o=pl.multiple_of((c%each)*CH,CH)
        f1=W_ref[m,:,pl.ds(4*cq+o,CH)]; f2=W_ref[m,:,pl.ds(4*cq+cf+o,CH)]
        hid=mm(xn2_s[...],f1)
        act,dact=gelu_both(hid)
        a=act.astype(BF)
        up_s[...]+=mm_nt(a,f2)
        gh=(mm(tg_s[...],f2)*dact).astype(BF)
        gn2_s[...]+=mm_nt(gh,f1)
        acc[m,:,pl.ds(cq+o,CH)]+=mm(xn2T_s[...],gh)
        acc[m,:,pl.ds(cq+cf+o,CH)]+=mm(tgT_s[...],a)
        return 0
    lax.fori_loop(0,parts*each,chunk,0)
    delta_ref[0]=(branch+up_s[...]+shifts_ref[3:4,:]).astype(BF)
    gn2=gn2_s[...]
    gln2=norm_back(gn2,xhat2,rstd2,gains_ref[1:2,:])
    gln2_ref[0]=gln2
    gb=(og+gln2).astype(BF)
    gbT=gb.T
    for m in range(parts):
        at=slice(m*cq,(m+1)*cq)
        acc[m,:,0:cq]+=mm(gbT,attn[:,at])
        g=mm(gb,W_ref[m,:,3*cq:4*cq]).astype(BF)
        g_ref[0,:,at]=g
        gT=g.T
        gT_ref[0,at,:]=gT
        prod=gT.astype(F32)*OT_s[at,:]
        nh=nheads//parts
        D_ref[0,m*nh:(m+1)*nh,:]=jnp.sum(prod.reshape(nh,HD,WIN),axis=1)
    small_ref[1:2,:]+=jnp.sum(gn2*xhat2,axis=0,keepdims=True)
    small_ref[3:4,:]+=jnp.sum(gn2,axis=0,keepdims=True)
    small_ref[4:5,:]+=jnp.sum(gb.astype(F32),axis=0,keepdims=True)
    small_ref[5:6,:]+=jnp.sum(tg.astype(F32),axis=0,keepdims=True)
    @pl.when(w==nw-1)
    def _():
        dcat_ref[...]=acc[...].astype(BF)
        for s in range(2):
            pltpu.make_async_copy(P_s.at[s],P_hbm.at[0,pl.ds(0,PER)],sem.at[s]).wait()

def full(shape,**kw):
    return pl.BlockSpec(shape,lambda w:(0,)*len(shape),**kw)
def per(shape,**kw):
    return pl.BlockSpec((1,)+shape,lambda w:(w,)+(0,)*len(shape),**kw)
ONE=pl.Buffered(1)
ANY=pl.BlockSpec(memory_space=pl.ANY)

def call_a(x,og,labc,labr,bias,W,gains,shifts):
    nW,WIN,D=x.shape; NH=bias.shape[0]
    parts,_,Ct=W.shape; Cg=Ct-3*(D//parts)
    sd=jax.ShapeDtypeStruct
    outs=[sd((nW,WIN,D),BF),sd((nW,WIN,D),F32),sd((nW,3,WIN,D),BF),sd((nW,WIN,D),BF),sd((nW,D,WIN),BF),sd((nW,NH,WIN),F32),
          sd((nW,NH,WIN,WIN),BF),sd((parts,D,Cg),BF),sd((8,D),F32)]
    return pl.pallas_call(functools.partial(kernel_a,NH),grid=(nW,),
      in_specs=[per((WIN,D)),per((WIN,D)),per((WIN,1)),per((1,WIN)),full((NH,WIN,WIN),pipeline_mode=ONE),
        full((parts,D,Ct),pipeline_mode=ONE),full(gains.shape),full(shifts.shape)],
      out_specs=[per((WIN,D)),per((WIN,D)),per((3,WIN,D)),per((WIN,D)),per((D,WIN)),per((NH,WIN)),ANY,full((parts,D,Cg)),full((8,D))],
      out_shape=outs,
      scratch_shapes=[pltpu.VMEM((D,WIN),BF),pltpu.VMEM((D,WIN),BF),pltpu.VMEM((D,WIN),F32),pltpu.VMEM((2,PER,WIN,WIN),BF),
        pltpu.VMEM((parts,D,Cg),F32),pltpu.SemaphoreType.DMA((2,)),
        pltpu.VMEM((WIN,D),BF),pltpu.VMEM((D,WIN),BF),pltpu.VMEM((WIN,D),BF),pltpu.VMEM((D,WIN),BF),pltpu.VMEM((WIN,D),F32),pltpu.VMEM((WIN,D),F32)],
      compiler_params=pltpu.CompilerParams(vmem_limit_bytes=62*1024*1024,dimension_semantics=("arbitrary",)),
      name="kernel_a")(x,og,labc,labr,bias,W,gains,shifts)

def kernel_b(nheads,x_ref,gln2_ref,qkv_ref,g_ref,gT_ref,D_ref,P_ref,W_ref,gains_ref,shifts_ref,
             dd_ref,dqkv_ref,G_hbm,small_ref,G_s,aq,kT_s,gq_s,gqT_s,sem):
    w=pl.program_id(0); nw=pl.num_programs(0)
    D=x_ref.shape[-1]; WIN=x_ref.shape[-2]
    parts=W_ref.shape[0]; cq=D//parts
    groups=nheads//PER
    @pl.when(w==0)
    def _():
        aq[...]=jnp.zeros_like(aq); G_s[...]=jnp.zeros_like(G_s); small_ref[...]=jnp.zeros_like(small_ref)
    kT_s[...]=qkv_ref[0,1].T
    lane=lax.broadcasted_iota(jnp.int32,(WIN,GROUP),1)
    hl=lane//HD
    def group(gi,_):
        o=pl.multiple_of(gi*GROUP,GROUP)
        gTg=gT_ref[0,pl.ds(o,GROUP),:]
        vg=qkv_ref[0,2,:,pl.ds(o,GROUP)]
        qg=qkv_ref[0,0,:,pl.ds(o,GROUP)]
        gg=g_ref[0,:,pl.ds(o,GROUP)]
        dv=jnp.zeros((WIN,GROUP),F32); dk=jnp.zeros((WIN,GROUP),F32)
        zero=jnp.zeros_like(vg)
        for hh in range(PER):
            h=gi*PER+hh
            p=P_ref[0,h]
            dp=mm(jnp.where(hl==hh,vg,zero),gTg)
            ds_=p.astype(F32)*(dp-D_ref[0,pl.ds(h,1),:])
            for c in range(G_s.shape[0]):
                wd=min(128,WIN-c*128)
                G_s[c,pl.ds(pl.multiple_of(h*WIN,8),WIN),:wd]+=ds_[:,c*128:c*128+wd]
            dsl=ds_.astype(BF)
            dv+=mm(p,jnp.where(hl==hh,gg,zero))
            dk+=mm(dsl,jnp.where(hl==hh,qg,zero))
            gqT_s[pl.ds(o+hh*HD,HD),:]=mm(kT_s[pl.ds(o+hh*HD,HD),:],dsl)
        gq_s[1,:,pl.ds(o,GROUP)]=(dk*(1.0/SQ)).astype(BF)
        gq_s[2,:,pl.ds(o,GROUP)]=dv.astype(BF)
        return 0
    lax.fori_loop(0,groups,group,0)
    gq_s[0]=(gqT_s[...]*(1.0/SQ)).astype(BF).T
    x=x_ref[0]
    xhat,rstd=norm_stats(x)
    xn=(xhat*gains_ref[0:1,:]+shifts_ref[0:1,:]).astype(BF)
    xnT=xn.T
    gr=jnp.zeros((WIN,D),F32)
    for m in range(parts):
        for c in range(3):
            gc=gq_s[c,:,m*cq:(m+1)*cq]
            gr=gr+mm_nt(gc,W_ref[m,:,c*cq:(c+1)*cq])
            aq[m,:,c*cq:(c+1)*cq]+=mm(xnT,gc)
    dd_ref[0]=(gln2_ref[0]+norm_back(gr,xhat,rstd,gains_ref[0:1,:])).astype(BF)
    small_ref[0:1,:]+=jnp.sum(gr*xhat,axis=0,keepdims=True)
    small_ref[2:3,:]+=jnp.sum(gr,axis=0,keepdims=True)
    @pl.when(w==nw-1)
    def _():
        dqkv_ref[...]=aq[...].astype(BF)
        cp=pltpu.make_async_copy(G_s,G_hbm,sem); cp.start(); cp.wait()

def call_b(x,gln2,qkv,g,gT,Dd,Pp,W,gains,shifts):
    nW,WIN,D=x.shape; NH=Dd.shape[1]
    parts=W.shape[0]; cq=D//parts; tiles=-(-WIN//128)
    sd=jax.ShapeDtypeStruct
    return pl.pallas_call(functools.partial(kernel_b,NH),grid=(nW,),
      in_specs=[per((WIN,D)),per((WIN,D)),per((3,WIN,D)),per((WIN,D)),per((D,WIN)),per((NH,WIN)),per((NH,WIN,WIN)),
        full((parts,D,3*cq),pipeline_mode=ONE),full(gains.shape),full(shifts.shape)],
      out_specs=[per((WIN,D)),full((parts,D,3*cq)),ANY,full((8,D))],
      out_shape=[sd((nW,WIN,D),BF),sd((parts,D,3*cq),BF),sd((tiles,NH*WIN,128),F32),sd((8,D),F32)],
      scratch_shapes=[pltpu.VMEM((tiles,NH*WIN,128),F32),pltpu.VMEM((parts,D,3*cq),F32),pltpu.VMEM((D,WIN),BF),pltpu.VMEM((3,WIN,D),BF),pltpu.VMEM((D,WIN),F32),
        pltpu.SemaphoreType.DMA],
      compiler_params=pltpu.CompilerParams(vmem_limit_bytes=62*1024*1024,dimension_semantics=("arbitrary",)),
      name="kernel_b")(x,gln2,qkv,g,gT,Dd,Pp,W,gains,shifts)

FIX=8191.0

def pack_table(table):
    NH,T=table.shape
    n=-(-T//128)
    q=jnp.round(jnp.clip(table,-4.0,4.0)*FIX).astype(jnp.int32)
    q=jnp.pad(q,((0,0),(0,n*128-T)))
    q=q.reshape(NH//2,2,n,128)
    return (q[:,0]*65536)|(q[:,1]&65535)

def kernel_p(pos_ref,tab_ref,bias_ref):
    npair,n,_=tab_ref.shape
    WIN=bias_ref.shape[-1]
    tiles=-(-WIN//128)
    def row(r,_):
        r8=pl.multiple_of(r*8,8)
        for c in range(tiles):
            width=min(128,WIN-c*128)
            idx=pos_ref[pl.ds(r8,8),c*128:(c+1)*128]
            lo=idx&127; hi=idx>>7
            masks=[hi==k for k in range(n)]
            for p in range(npair):
                acc=jnp.zeros((8,128),jnp.int32)
                for k in range(n):
                    src=jnp.broadcast_to(tab_ref[p,k:k+1,:],(8,128))
                    acc=jnp.where(masks[k],jnp.take_along_axis(src,lo,axis=1),acc)
                a=(acc>>16).astype(F32)*(SQ/FIX)
                b=((acc<<16)>>16).astype(F32)*(SQ/FIX)
                bias_ref[2*p,pl.ds(r8,8),c*128:c*128+width]=a[:,:width]
                bias_ref[2*p+1,pl.ds(r8,8),c*128:c*128+width]=b[:,:width]
        return 0
    lax.fori_loop(0,bias_ref.shape[1]//8,row,0)

def call_p(posT_pad,tab,WIN):
    NH=tab.shape[0]*2
    return pl.pallas_call(kernel_p,out_shape=jax.ShapeDtypeStruct((NH,WIN,WIN),F32),
      compiler_params=pltpu.CompilerParams(vmem_limit_bytes=40*1024*1024),name="kernel_p")(posT_pad,tab)

def kernel_t(NH,G_ref,hi_ref,lo_ref,out_ref):
    WIN=hi_ref.shape[0]; LW=G_ref.shape[0]*128
    nh=out_ref.shape[0]//NH
    out_ref[...]=jnp.zeros_like(out_ref)
    def rows(r,_):
        r8=pl.multiple_of(r*8,8)
        hi8=hi_ref[pl.ds(r8,8),:]; lo8=lo_ref[pl.ds(r8,8),:]
        tot=jnp.zeros(out_ref.shape,F32)
        iota=lax.broadcasted_iota(jnp.int32,(256,LW),0).astype(F32).astype(BF)
        for k in range(8):
            g=jnp.concatenate([G_ref[c,pl.ds(r8+k,NH,stride=WIN),:] for c in range(LW//128)],axis=1)
            hr=hi8[k:k+1,:]; lr=lo8[k:k+1,:].astype(F32).astype(BF)
            A=jnp.concatenate([jnp.where(hr==m,g,0.0) for m in range(nh)],axis=0).astype(BF)
            oh=jnp.where(iota==lr,jnp.ones((),BF),jnp.zeros((),BF))
            tot=tot+lax.dot_general(A,oh,(((1,),(1,)),((),())),preferred_element_type=F32)
        out_ref[...]+=tot
        return 0
    lax.fori_loop(0,WIN//8,rows,0)

def call_t(G,posT,T,NH):
    WIN=posT.shape[0]; nt=G.shape[0]
    nh=-(-T//256)
    pp=jnp.pad(posT,((0,0),(0,nt*128-WIN)),constant_values=nh*256)
    hi=pp>>8; lo=pp&255
    o=pl.pallas_call(functools.partial(kernel_t,NH),out_shape=jax.ShapeDtypeStruct((nh*NH,256),F32),
      compiler_params=pltpu.CompilerParams(vmem_limit_bytes=40*1024*1024),name="kernel_t")(G,hi,lo)
    return o.reshape(nh,NH,256).transpose(1,0,2).reshape(NH,nh*256)[:,:T]


MESHID=pl.DeviceIdType.MESH

def place_of():
    s=lax.axis_index("seq"); y=lax.axis_index("heads")
    return s//4,(s//2)%2,s%2,y

def dev(z,x,c,y):
    return ((z*2+x)*2+c,y)

def peers_of(z,x,c,y):
    return [dev(z,x,1-c,y),dev(z,1-x,c,y),dev(z,x,c,1-y)]+[dev((z+i)%4,x,c,y) for i in (1,2,3)]

def hail(devices):
    bar=pltpu.get_barrier_semaphore()
    for d in devices:
        pl.semaphore_signal(bar,inc=1,device_id=d,device_id_type=MESHID)

def heard(devices):
    pl.semaphore_wait(pltpu.get_barrier_semaphore(),len(devices))

def greet(devices):
    hail(devices)
    heard(devices)

def send(src,dst,ss,rs,to):
    return pltpu.make_async_remote_copy(src_ref=src,dst_ref=dst,send_sem=ss,recv_sem=rs,device_id=to,device_id_type=MESHID)


class Gather:
    def __init__(self,src,dst,ss,rs,own,cols=None):
        self.src,self.dst,self.ss,self.rs,self.own=src,dst,ss,rs,own
        self.cols=pl.ds(0,dst.shape[2]) if cols is None else cols
        z,x,c,y=self.at=place_of()
        self.xa=x+(1-2*x)*(1-c); self.ya=y+(1-2*y)*c
        self.xb=x+(1-2*x)*c; self.yb=y+(1-2*y)*(1-c)
        self.sib=dev(z,x,1-c,y); self.pa=dev(z,self.xa,c,self.ya); self.pb=dev(z,self.xb,c,self.yb)
    def slot(self,zz,xx,cc,yy):
        n=self.src.shape[0]
        return self.dst.at[yy,pl.ds(pl.multiple_of(((zz*2+xx)*2+cc)*n,n),n),self.cols]
    def copy(self,src,where,k,to):
        return send(src,self.slot(*where),self.ss.at[k],self.rs.at[k],to)
    def go(self,where,k,to,src=None):
        self.copy(self.slot(*where) if src is None else src,where,k,to).start()
    def came(self,where,k):
        self.copy(self.src,where,k,self.sib).wait_recv()
    def keep(self):
        z,x,c,y=self.at
        return pltpu.make_async_copy(self.src,self.slot(z,x,c,y),self.own)
    def start(self):
        z,x,c,y=self.at
        me=(z,x,c,y)
        self.keep().start()
        for i in (1,2,3):
            self.go(me,i-1,dev((z+i)%4,x,c,y),self.src)
        self.go(me,3,self.pa,self.src); self.go(me,7,self.pb,self.src); self.go(me,15,self.sib,self.src)
    def z(self,i):
        return (self.at[0]+4-i)%4
    def turn_z(self,i):
        z,x,c,y=self.at
        at=(self.z(i),x,c,y); self.came(at,i-1)
        self.go(at,3+i,self.pa); self.go(at,7+i,self.pb); self.go(at,15+i,self.sib)
    def turn_a(self,i):
        at=(self.z(i),self.xa,self.at[2],self.ya); self.came(at,3+i)
        self.go(at,11+i,self.pb); self.go(at,19+i,self.sib)
    def turn_b(self,i):
        at=(self.z(i),self.xb,self.at[2],self.yb); self.came(at,7+i)
        self.go(at,23+i,self.sib)
    def turn_ab(self,i):
        z,x,c,y=self.at
        at=(self.z(i),1-x,c,1-y); self.came(at,11+i)
        self.go(at,27+i,self.sib)
    def last(self):
        z,x,c,y=self.at
        for i in range(4):
            zz=self.z(i)
            self.came((zz,x,1-c,y),15+i); self.came((zz,self.xb,1-c,self.yb),19+i)
            self.came((zz,self.xa,1-c,self.ya),23+i); self.came((zz,1-x,1-c,1-y),27+i)
    def drain(self):
        z,x,c,y=self.at
        for k in range(31):
            self.copy(self.src,(z,x,c,y),k,self.sib).wait_send()
        self.keep().wait()

class GatherLate(Gather):
    def start(self):
        z,x,c,y=self.at
        me=(z,x,c,y)
        self.keep().start()
        self.go(me,0,self.pa,self.src)
        for i in (1,2,3):
            self.go(me,i,dev((z+i)%4,x,c,y),self.src)
        self.go(me,7,self.pb,self.src); self.go(me,15,self.sib,self.src)
    def pair(self):
        z,x,c,y=self.at
        at=(z,self.xa,c,self.ya); self.came(at,0)
        for i in (1,2,3):
            self.go(at,3+i,dev((z+i)%4,x,c,y))
        self.go(at,11,self.pb); self.go(at,19,self.sib)
    def along(self,i):
        z,x,c,y=self.at
        at=(self.z(i),x,c,y); self.came(at,i)
        self.go(at,7+i,self.pb); self.go(at,15+i,self.sib)
        at=(self.z(i),self.xa,c,self.ya); self.came(at,3+i)
        self.go(at,11+i,self.pb); self.go(at,19+i,self.sib)
    def over(self,i):
        z,x,c,y=self.at
        at=(self.z(i),self.xb,c,self.yb); self.came(at,7+i)
        self.go(at,23+i,self.sib)
        at=(self.z(i),1-x,c,1-y); self.came(at,11+i)
        self.go(at,27+i,self.sib)

def gather_sems():
    return [pltpu.SemaphoreType.DMA((31,)),pltpu.SemaphoreType.DMA((31,)),pltpu.SemaphoreType.DMA]

STEPS=7
def kernel_w(qkv_ref,proj_ref,fc1_ref,fc2_ref,pos_ref,tab_ref,W_hbm,bias_hbm,brem_hbm,wf_ref,posT_ref,
             bias_s,brem_s,short_s,found_s,wq_s,tb,tq,ss,rs,own,bs,br,bl,tsem,ed):
    z,x,c,y=place_of()
    cq=qkv_ref.shape[2]; cf=fc1_ref.shape[1]
    for k in range(3): wq_s[:,k*cq:(k+1)*cq]=qkv_ref[k].astype(BF)
    wq_s[:,3*cq:4*cq]=proj_ref[...].astype(BF)
    lead=wq_s.shape[1]-4*cq
    wq_s[:,4*cq:]=fc1_ref[:,0:lead].astype(BF)
    half,T=tab_ref.shape
    tb[2]=jnp.zeros(tb.shape[1:],F32)
    tb[2,:,0:T]=tab_ref[...]
    greet(peers_of(z,x,c,y))
    mid=wq_s.shape[1]//2
    gather=Gather(wq_s.at[:,pl.ds(0,mid)],W_hbm,ss.at[0],rs.at[0],own.at[0],pl.ds(0,mid))
    other=GatherLate(wq_s.at[:,pl.ds(mid,mid)],W_hbm,ss.at[1],rs.at[1],own.at[1],pl.ds(mid,mid))
    swap=send(tb.at[2],tb.at[y],tsem.at[0],tsem.at[1],dev(z,x,c,1-y))
    swap.start()
    gather.start(); other.start()
    tb[y]=tb[2]
    wf_ref[:,0:cf-lead]=fc1_ref[:,lead:].astype(BF)
    wf_ref[:,cf-lead:]=fc2_ref[...].astype(BF)
    WIN,Q=bias_s.shape[-2:]; tiles=Q//128; n=tb.shape[2]//128; R=WIN-Q; per_row=128//R; nr=found_s.shape[1]
    posT_ref[...]=jnp.full(posT_ref.shape,1<<15,jnp.int32)
    posT_ref[:,0:WIN]=pos_ref[...].astype(F32).T.astype(jnp.int32)
    swap.wait()
    npair=half//2
    for p in range(npair):
        a,b=[jnp.floor(jnp.clip(tb[c,2*p+k:2*p+k+1,:],-4.0,4.0)*FIX+0.5).astype(jnp.int32) for k in range(2)]
        tq[p:p+1,:]=(a*65536)|(b&65535)
    nrow=WIN//8
    cuts=[nrow*k//STEPS for k in range(STEPS+1)]
    sib=dev(z,x,1-c,y)
    def rows_of(k): return pl.ds(cuts[k]*8,(cuts[k+1]-cuts[k])*8)
    def kept(k): return pltpu.make_async_copy(bias_s.at[:,rows_of(k)],bias_hbm.at[pl.ds(c*half,half),rows_of(k)],bl.at[k])
    def sent(k,cc): return send(bias_s.at[:,rows_of(k)],bias_hbm.at[pl.ds(cc*half,half),rows_of(k)],bs.at[k],br.at[k],sib)
    def look(idx):
        lo=idx&127; hi=idx>>7
        masks=[hi==q for q in range(n)]
        for p in range(npair):
            acc=jnp.zeros((8,128),jnp.int32)
            for q in range(n):
                src=jnp.broadcast_to(tq[p:p+1,q*128:(q+1)*128],(8,128))
                acc=jnp.where(masks[q],jnp.take_along_axis(src,lo,axis=1),acc)
            yield 2*p,(acc>>16).astype(F32)*(SQ/FIX)
            yield 2*p+1,((acc<<16)>>16).astype(F32)*(SQ/FIX)
    slots=lax.broadcasted_iota(jnp.int32,(nr,128),1)//R
    def short_in():
        short_s[...]=jnp.full(short_s.shape,1<<15,jnp.int32)
        short_s[0:WIN,:]=posT_ref[:,Q:Q+128]
        packed=jnp.zeros((nr,128),jnp.int32)
        for u in range(per_row):
            v=short_s[pl.ds(u,nr,stride=per_row),:]
            packed=jnp.where(slots==u,pltpu.roll(v,u*R,1) if u else v,packed)
        for t in range(nr//8):
            for h,v in look(packed[t*8:(t+1)*8]): found_s[h,t*8:(t+1)*8,:]=v
    def short_out():
        for u in range(per_row):
            row=jnp.zeros((nr,128),F32)
            for h in range(half):
                by=((h-u)*R)%128
                v=found_s[h]
                row=jnp.where(slots==h,pltpu.roll(v,by,1) if by else v,row)
            brem_s[pl.ds(u,nr,stride=per_row),:]=row
    def rows(k):
        def row(r,_):
            r8=pl.multiple_of(r*8,8)
            for t in range(tiles):
                for h,v in look(posT_ref[pl.ds(r8,8),t*128:(t+1)*128]):
                    bias_s[h,pl.ds(r8,8),t*128:(t+1)*128]=v
            return 0
        lax.fori_loop(cuts[k],cuts[k+1],row,0)
        kept(k).start(); sent(k,c).start()
    rows(0)
    short_in()
    short_out()
    other.pair()
    rows(1)
    for i in (1,3,2): gather.turn_z(i)
    for i in (0,): gather.turn_a(i); gather.turn_b(i)
    rows(2)
    for i in (1,3,2): other.along(i)
    rows(3)
    for i in (1,3,2): gather.turn_a(i); gather.turn_b(i)
    rows(4)
    for i in (0,1,3,2): gather.turn_ab(i); other.over(i)
    rows(5)
    rows(6)
    edges=[pltpu.make_async_copy(brem_s.at[pl.ds(0,WIN)],brem_hbm.at[c],ed.at[0]),send(brem_s.at[pl.ds(0,WIN)],brem_hbm.at[c],ed.at[1],ed.at[2],sib)]
    for e in edges: e.start()
    gather.last(); other.last()
    for e in edges: e.wait()
    for k in range(STEPS):
        kept(k).wait(); sent(k,c).wait_send(); sent(k,1-c).wait_recv()
    gather.drain(); other.drain()

def call_w(w_qkv,w_proj,w_fc1,w_fc2,pos_index,rel_table):
    rows,cq=w_qkv.shape[1:]; cf=w_fc1.shape[1]; WIN=pos_index.shape[0]; half,T=rel_table.shape; dma=pltpu.SemaphoreType.DMA
    wide=-(-WIN//128)*128; Q=WIN//128*128; n=-(-T//128); mem=pltpu.VMEM
    keys=-(-WIN//(1024//(WIN-Q)))*(1024//(WIN-Q))
    early=4*cq+min(512,cf); late=4*cq+2*cf-early
    sd=jax.ShapeDtypeStruct
    return pl.pallas_call(kernel_w,grid=(1,),
      out_shape=[sd((2,16*rows,early),BF),sd((2*half,WIN,Q),F32),sd((2,WIN,128),F32),sd((rows,late),BF),sd((WIN,wide),jnp.int32)],
      in_specs=[full(v.shape) for v in (w_qkv,w_proj,w_fc1,w_fc2,pos_index,rel_table)],out_specs=[ANY,ANY,ANY,full((rows,late)),full((WIN,wide))],
      scratch_shapes=[mem((half,WIN,Q),F32),mem((keys,128),F32),mem((keys,128),jnp.int32),mem((half,keys*(WIN-Q)//128,128),F32),mem((rows,early),BF),mem((3,half,n*128),F32),mem((half//2,n*128),jnp.int32)]
        +[dma((2,31)),dma((2,31)),dma((2,))]+[dma((STEPS,)),dma((STEPS,)),dma((STEPS,)),dma((2,)),dma((3,))],
      compiler_params=pltpu.CompilerParams(vmem_limit_bytes=63*1024*1024,collective_id=1,has_side_effects=True),name="kernel_w")(w_qkv,w_proj,w_fc1,w_fc2,pos_index,rel_table)

def neighbours(z,x,c,y):
    s=(z*2+x)*2+c
    return [((s+k)%16,yy) for k in (1,15) for yy in (y,1-y)]

def pick(shape,test):
    r=lax.broadcasted_iota(jnp.int32,shape,0); c=lax.broadcasted_iota(jnp.int32,shape,1)
    return jnp.where(test(r,c),1.0,0.0)

def exact(a,b):
    return lax.dot_general(a,b,(((1,),(0,)),((),())),precision=lax.Precision.HIGHEST,preferred_element_type=F32)

def kernel_a2(nheads,in_hbm,og_hbm,wf_hbm,lab_ref,bias_ref,brem_ref,W1,gains_ref,shifts_ref,
              qkv_ref,x_ref,P_hbm,pr_ref,gln2_ref,g_ref,gT_ref,D_ref,ev_hbm,dlast_hbm,dcat_hbm,small_ref,
              x_s,og_s,W2,OT_s,qT_s,vT_s,P_s,kst_s,acc,pst,xn2_s,xn2T_s,tg_s,tgT_s,up_s,gn2_s,dl_s,
              lab_s,psem,xsem,hsem,ss,rs,own,dl,ds,dr,fin):
    i=pl.program_id(0); nw=x_s.shape[0]
    w=i%nw
    z,xc,c,y=place_of()
    s=(z*2+xc)*2+c
    D=x_s.shape[-1]; WIN=qkv_ref.shape[-2]; SLAB=x_s.shape[1]; HALF=SLAB//2
    OFF=(SLAB-WIN)//2
    cq=D//2; lead=W1.shape[2]-4*cq; cf=(W2.shape[2]+lead)//2
    groups=nheads//PER; Q=bias_ref.shape[2]; R=WIN-Q
    gather=Gather(wf_hbm,W2,ss,rs,own)
    mate=dev(z,xc,c,1-y)
    def local(k,half,t):
        hbm,buf=((in_hbm,x_s),(og_hbm,og_s))[t]
        r=pl.multiple_of(y*(nw*WIN)+k*WIN+(WIN//2-OFF)+half*HALF,8)
        return pltpu.make_async_copy(hbm.at[pl.ds(r,HALF)],buf.at[k,pl.ds(half*HALF,HALF)],xsem.at[t,2*k+half])
    def edge(t):
        hbm,buf=((in_hbm,x_s),(og_hbm,og_s))[t]
        return send(hbm.at[pl.ds(0,HALF)],buf.at[nw-1,pl.ds(HALF,HALF)],hsem.at[t,0],hsem.at[t,1],((s+15)%16,1))
    def ready(t):
        local(w,0,t).wait()
        far=jnp.logical_and(w==nw-1,y==1)
        @pl.when(far)
        def _(): edge(t).wait_recv()
        @pl.when(jnp.logical_not(far))
        def _(): local(w,1,t).wait()
    def slab(k,to=None):
        if k is None: return pltpu.make_async_copy(dl_s.at[nw-1],dlast_hbm,dl.at[nw-1])
        at=ev_hbm.at[y*nw+k]
        if to is None: return pltpu.make_async_copy(dl_s.at[k],at,dl.at[k])
        return send(dl_s.at[k],at,ds.at[k],dr.at[k],to)
    everyone=peers_of(z,xc,c,y)+neighbours(z,xc,c,y)
    def met():
        heard(everyone)
        gather.start()
        @pl.when(y==1)
        def _():
            for t in range(2): edge(t).start()
    def first():
        for k in (1,3,2): gather.turn_z(k)
    def second():
        for k in (0,1,3,2): gather.turn_a(k); gather.turn_b(k)
    def third():
        for k in (0,1,3,2): gather.turn_ab(k)
    plan=((0,met),(6,first),(10,second),(14,third))
    @pl.when(i==0)
    def _():
        hail(everyone)
        for k in range(nw):
            for t in range(2):
                local(k,0,t).start()
                if k<nw-1: local(k,1,t).start()
        for t in range(2):
            @pl.when(y==0)
            def _(): local(nw-1,1,t).start()
        lab_s[...]=lab_ref[...].astype(F32).T
        acc[...]=jnp.zeros_like(acc)
        for hh in range(PER): kst_s[(hh+1)*SLAB-16:(hh+1)*SLAB,:]=jnp.zeros((16,2*GROUP),BF)
        small_ref[...]=jnp.zeros_like(small_ref)
        dl_s[:,SLAB-16:,:]=jnp.zeros((nw,16,D),BF)

    @pl.when(i<nw)
    def _():
        ready(0)
        x=x_s[w,OFF:OFF+WIN,:]
        x_ref[0]=x
        xhat,_=norm_stats(x)
        xn=(xhat*gains_ref[0:1,:]+shifts_ref[0:1,:]).astype(BF)
        for k in range(3):
            for m in range(2):
                at=slice(m*cq,(m+1)*cq)
                v=mm(xn,W1[m,:,k*cq:(k+1)*cq]).astype(BF)
                qkv_ref[0,k,:,at]=v
                if k==0: qT_s[at,:]=v.T
                if k==2: vT_s[at,:]=v.T
        mine=y*nw+w
        labr=lab_ref[pl.ds(mine,1),:]
        labc=jnp.sum(jnp.where(lax.broadcasted_iota(jnp.int32,lab_s.shape,1)==mine,lab_s[...],0.0),axis=1,keepdims=True).astype(jnp.int32)
        lane=lax.broadcasted_iota(jnp.int32,(WIN,GROUP),1)
        oh=jnp.where((labc==lane)|((labc+3)==lane),1.0,0.0).astype(BF)
        hi=564.0
        lo=MASK-hi
        sub=lax.broadcasted_iota(jnp.int32,(GROUP,WIN),0)
        nm=jnp.where(sub<3,jnp.where(sub!=labr,-hi,0.0),jnp.where(sub<6,jnp.where(sub-3!=labr,-lo,0.0),0.0)).astype(BF)
        hl=lane//HD
        for hh in range(PER): kst_s[hh*SLAB:hh*SLAB+WIN,GROUP:]=oh
        nmq=nm[:,0:Q]
        def soften(t):
            m=jnp.max(t,axis=0,keepdims=True)
            e=jnp.exp2((t-m)*CEXP)
            l=jnp.sum(e,axis=0,keepdims=True)
            return (e*(1.0/l)).astype(BF)
        def group(gi,_):
            slot=gi%2
            @pl.when(w*groups+gi>=2)
            def _():
                pltpu.make_async_copy(P_s.at[slot],P_hbm.at[0,0],psem.at[slot]).wait()
            o=pl.multiple_of(gi*GROUP,GROUP)
            qTg=jnp.concatenate([qT_s[pl.ds(o,GROUP),0:Q],nmq],axis=0)
            kg=qkv_ref[0,1,:,pl.ds(o,GROUP)]
            for hh in range(PER): kst_s[hh*SLAB:hh*SLAB+WIN,0:GROUP]=jnp.where(hl==hh,kg,jnp.zeros_like(kg))
            t4=mm(kst_s[...],qTg)
            for hh in range(PER):
                p=soften(t4[hh*SLAB:hh*SLAB+WIN]+bias_ref[gi*PER+hh])
                P_s[slot,:,hh*Q:(hh+1)*Q]=p
                OT_s[w,pl.ds(o+hh*HD,HD),0:Q]=mm(vT_s[pl.ds(o+hh*HD,HD),:],p)
            pltpu.make_async_copy(P_s.at[slot],P_hbm.at[w,gi],psem.at[slot]).start()
            for when,what in plan:
                pl.when(w*groups+gi==min(when,nw*groups-1))(what)
            return 0
        lax.fori_loop(0,groups,group,0)
        spread=pick((R,GROUP),lambda r,c: c%R==r).astype(BF)
        own_rows=pick((D,GROUP),lambda r,c: r//HD==c//R)
        qbd=(mm(qT_s[:,Q:WIN],spread)*own_rows).astype(BF)
        nmr=mm(nm[:,Q:WIN],spread).astype(BF)
        brem=jnp.concatenate([brem_ref[0,:,0:GROUP//2],brem_ref[1,:,0:GROUP//2]],axis=1)
        pr=soften(mm(qkv_ref[0,1],qbd)+mm(oh,nmr)+brem)
        pr_ref[0]=pr
        OT_s[w,:,Q:WIN]=exact(mm(vT_s[...],pr)*own_rows,pick((GROUP,R),lambda r,c: r%R==c))

    @pl.when(i==nw-1)
    def _():
        gather.last(); gather.drain()

    @pl.when(i>=nw)
    def _():
        ready(1)
        x=x_s[w,OFF:OFF+WIN,:]
        og=og_s[w,OFF:OFF+WIN,:]
        attn=OT_s[w].astype(BF).T
        branch=shifts_ref[2:3,:]
        for m in range(2):
            branch=branch+mm_nt(attn[:,m*cq:(m+1)*cq],W1[m,:,3*cq:4*cq])
        branch=branch.astype(BF).astype(F32)
        middle=x+branch
        xhat2,rstd2=norm_stats(middle)
        xn2=(xhat2*gains_ref[1:2,:]+shifts_ref[1:2,:]).astype(BF)
        tg=og.astype(BF)
        xn2_s[...]=xn2; xn2T_s[...]=xn2.T; tg_s[...]=tg; tgT_s[...]=tg.T
        up_s[...]=jnp.zeros_like(up_s); gn2_s[...]=jnp.zeros_like(gn2_s)
        CH=lead
        def side(m,_):
            for o in range(0,cf,CH):
                f1=W1[m,:,4*cq:] if o==0 else W2[m,:,o-lead:o-lead+CH]
                f2=W2[m,:,cf-lead+o:cf-lead+o+CH]
                hid=mm(xn2_s[...],f1)
                act,dact=gelu_both(hid)
                a=act.astype(BF)
                up_s[...]+=mm_nt(a,f2)
                gh=(mm(tg_s[...],f2)*dact).astype(BF)
                gn2_s[...]+=mm_nt(gh,f1)
                acc[m,:,cq+o:cq+o+CH]+=mm(xn2T_s[...],gh)
                acc[m,:,cq+cf+o:cq+cf+o+CH]+=mm(tgT_s[...],a)
            return 0
        lax.fori_loop(0,2,side,0)
        dl_s[w,0:WIN,:]=(branch+up_s[...]+shifts_ref[3:4,:]).astype(BF)
        @pl.when(w<nw-1)
        def _():
            slab(w).start(); slab(w,mate).start()
        @pl.when(w==nw-1)
        def _(): slab(None).start()
        gn2=gn2_s[...]
        gln2=norm_back(gn2,xhat2,rstd2,gains_ref[1:2,:])
        gln2_ref[0]=gln2
        gb=(og+gln2).astype(BF)
        gbT=gb.T
        for m in range(2):
            at=slice(m*cq,(m+1)*cq)
            acc[m,:,0:cq]+=mm(gbT,attn[:,at])
            g=mm(gb,W1[m,:,3*cq:4*cq]).astype(BF)
            g_ref[0,:,at]=g
            gT=g.T
            gT_ref[0,at,:]=gT
            prod=gT.astype(F32)*OT_s[w,at,:]
            nh=nheads//2
            D_ref[0,m*nh:(m+1)*nh,:]=jnp.sum(prod.reshape(nh,HD,WIN),axis=1)
        small_ref[1:2,:]+=jnp.sum(gn2*xhat2,axis=0,keepdims=True)
        small_ref[3:4,:]+=jnp.sum(gn2,axis=0,keepdims=True)
        small_ref[4:5,:]+=jnp.sum(gb.astype(F32),axis=0,keepdims=True)
        small_ref[5:6,:]+=jnp.sum(tg.astype(F32),axis=0,keepdims=True)

    @pl.when(i==2*nw-1)
    def _():
        W2[...]=acc[:,:,cq+lead:].astype(BF)
        pst[...]=acc[:,:,:cq+lead].astype(BF)
        a=pltpu.make_async_copy(W2,dcat_hbm.at[:,:,pl.ds(cq+lead,W2.shape[2])],fin.at[0])
        b=pltpu.make_async_copy(pst,dcat_hbm.at[:,:,pl.ds(0,cq+lead)],fin.at[1])
        a.start(); b.start()
        for k in range(2):
            pltpu.make_async_copy(P_s.at[k],P_hbm.at[0,0],psem.at[k]).wait()
        for k in range(nw-1):
            slab(k).wait(); slab(k,mate).wait()
        slab(None).wait()
        @pl.when(y==1)
        def _():
            for t in range(2): edge(t).wait_send()
        a.wait(); b.wait()

def call_a2(inputs,og,wf,lab,bias,brem,W1,gains,shifts):
    nW=lab.shape[0]//2; WIN=lab.shape[1]; D=inputs.shape[1]; NH=bias.shape[0]
    cq=D//2; lead=W1.shape[2]-4*cq; cf=(wf.shape[1]+lead)//2; SLAB=-(-WIN//16)*16
    Q=bias.shape[2]
    sd=jax.ShapeDtypeStruct; dma=pltpu.SemaphoreType.DMA; v=pltpu.VMEM
    early=lambda shape: pl.BlockSpec((1,)+shape,lambda i:(jnp.minimum(i,nW-1),)+(0,)*len(shape))
    late=lambda shape: pl.BlockSpec((1,)+shape,lambda i:(jnp.maximum(i-nW,0),)+(0,)*len(shape))
    outs=[sd((nW,3,WIN,D),BF),sd((nW,WIN,D),F32),sd((nW,NH//PER,WIN,PER*Q),BF),sd((nW,WIN,GROUP),BF),sd((nW,WIN,D),F32),sd((nW,WIN,D),BF),sd((nW,D,WIN),BF),sd((nW,NH,WIN),F32),
          sd((2*nW,SLAB,D),BF),sd((SLAB,D),BF),sd((2,D,cq+2*cf),BF),sd((8,D),F32)]
    return pl.pallas_call(functools.partial(kernel_a2,NH),grid=(2*nW,),
      in_specs=[ANY,ANY,ANY,full(lab.shape),full(bias.shape,pipeline_mode=ONE),full(brem.shape),full(W1.shape,pipeline_mode=ONE),full(gains.shape),full(shifts.shape)],
      out_specs=[early((3,WIN,D)),early((WIN,D)),ANY,early((WIN,GROUP)),late((WIN,D)),late((WIN,D)),late((D,WIN)),late((NH,WIN)),ANY,ANY,ANY,full((8,D))],
      out_shape=outs,
      scratch_shapes=[v((nW,SLAB,D),F32),v((nW,SLAB,D),F32),v((2,D,2*cf-lead),BF),v((nW,D,WIN),F32),v((D,WIN),BF),v((D,WIN),BF),v((2,WIN,PER*Q),BF),v((PER*SLAB,2*GROUP),BF),
        v((2,D,cq+2*cf),F32),v((2,D,cq+lead),BF),v((WIN,D),BF),v((D,WIN),BF),v((WIN,D),BF),v((D,WIN),BF),v((WIN,D),F32),v((WIN,D),F32),v((nW,SLAB,D),BF),
        v((WIN,2*nW),F32),dma((2,)),dma((2,2*nW)),dma((2,2))]+gather_sems()+[dma((nW,)),dma((nW,)),dma((nW,)),dma((2,))],
      compiler_params=pltpu.CompilerParams(vmem_limit_bytes=63*1024*1024,dimension_semantics=("arbitrary",),collective_id=2,has_side_effects=True),
      name="kernel_a2")(inputs,og,wf,lab,bias,brem,W1,gains,shifts)

class Reduce:
    def __init__(self,src,out,own,r1,bufs,ss,rs,ls):
        self.src,self.out,self.own,self.r1,self.bufs=src,out,own,r1,bufs
        self.ss,self.rs,self.ls=ss,rs,ls
        z,x,c,y=place_of()
        self.x,self.c,self.y,self.h,self.l=x,c,y,z//2,z%2
    def to(self,x=None,h=None,l=None,c=None,y=None):
        pick=lambda new,old: old if new is None else new
        return dev(pick(h,self.h)*2+pick(l,self.l),pick(x,self.x),pick(c,self.c),pick(y,self.y))
    def mine(self,k):
        return pltpu.make_async_copy(self.src.at[k%2,:,:,k//2,self.c],self.own.at[k//2,:,:,k%2],self.ls.at[k])
    def theirs(self,k):
        return send(self.src.at[k%2,:,:,k//2,1-self.c],self.r1.at[k//2,:,:,k%2],self.ss.at[k],self.rs.at[k],self.to(c=1-self.c))
    def turns(self,core):
        x,h,l,y=self.x,self.h,self.l,self.y
        s=slice(None)
        if core==0:
            return [((1-x,),dict(x=1-x),lambda a,b,d:(x,a,b,d)),((x,s,1-l),dict(l=1-l),lambda a,d:(x,a,l,d)),
                    ((x,1-h,l),dict(h=1-h),lambda d:(x,h,l,d)),((x,h,l,1-y),dict(y=1-y),None)]
        return [((s,s,1-l),dict(l=1-l),lambda a,b,d:(a,b,l,d)),((s,1-h,l),dict(h=1-h),lambda a,d:(a,h,l,d)),
                ((1-x,h,l),dict(x=1-x),lambda d:(x,h,l,d)),((x,h,l,1-y),dict(y=1-y),None)]
    def give(self,k,core):
        at,where,_=self.turns(core)[k]
        return send(self.own.at[at],self.bufs[k],self.ss.at[4+k],self.rs.at[4+k],self.to(**where))
    def start(self):
        for k in range(4):
            self.theirs(k).start(); self.mine(k).start()
    def add(self,dst,*srcs):
        total=srcs[0][...].astype(F32)
        for s in srcs[1:]: total=total+s[...].astype(F32)
        dst[...]=total.astype(dst.dtype)
    def by_core(self,f):
        for core in range(2):
            @pl.when(self.c==core)
            def _(): f(core)
    def one(self):
        for k in range(4):
            self.mine(k).wait(); self.theirs(k).wait_recv()
        def step(k,_):
            at=(k//8,(k//4)%2,(k//2)%2,k%2)
            self.add(self.own.at[at],self.own.at[at],self.r1.at[at])
            return 0
        lax.fori_loop(0,16,step,0)
        self.by_core(lambda core: self.give(0,core).start())
    def turn(self,k):
        def f(core):
            stay=self.turns(core)[k][2]
            self.give(k,core).wait_recv()
            def step(i,_):
                at=[(i//4,(i//2)%2,i%2),(i//2,i%2),(i,)][k]
                self.add(self.own.at[stay(*at)],self.own.at[stay(*at)],self.bufs[k].at[at])
                return 0
            lax.fori_loop(0,8>>k,step,0)
            self.give(k+1,core).start()
        self.by_core(f)
    def four(self):
        def f(core):
            self.give(3,core).wait_recv()
            self.add(self.out,self.own.at[self.x,self.h,self.l,self.y],self.bufs[3])
            for k in range(4): self.give(k,core).wait_send()
        self.by_core(f)
        for k in range(4): self.theirs(k).wait_send()

def reduce_scratch(rows,cols):
    v=lambda *d: pltpu.VMEM(d+(rows,cols),BF); dma=pltpu.SemaphoreType.DMA
    return [v(2,2,2,2),v(2,2,2,2),v(2,2,2),v(2,2),v(2),v(),dma((8,)),dma((8,)),dma((4,))]

class Sums:
    def __init__(self,slabs,got,res,ss,rs,ts,us):
        self.slabs,self.got,self.res,self.ss,self.rs,self.ts,self.us=slabs,got,res,ss,rs,ts,us
        z,x,c,y=place_of()
        self.s=(z*2+x)*2+c; self.y=y; self.n=slabs.shape[1]
    def part(self,k,yy):
        me=self.y*16+self.s
        return send(self.slabs.at[yy,k],self.got.at[me],self.ss.at[yy*self.n+k],self.rs.at[me],(k,yy))
    def other(self,k,yy):
        return jnp.logical_or(self.s!=k,self.y!=yy)
    def scatter(self):
        for k in range(self.n):
            for yy in range(2):
                @pl.when(self.other(k,yy))
                def _(): self.part(k,yy).start()
    def back(self,to,k):
        return send(self.res.at[k],self.res.at[k],self.ts.at[to],self.us.at[k],(to,self.y))
    def collect(self):
        me=self.y*16+self.s
        @pl.when(self.s<self.n)
        def _():
            self.got[me]=self.slabs[self.y,self.s]
            def wait(i,_):
                @pl.when(i!=me)
                def _():
                    send(self.slabs.at[0,0],self.got.at[i],self.ss.at[0],self.rs.at[i],(self.s,1-self.y)).wait_recv()
                return 0
            lax.fori_loop(0,32,wait,0)
            total=self.got[0]
            for i in range(1,32): total=total+self.got[i]
            self.res[self.s]=total
            for to in range(16):
                @pl.when(self.s!=to)
                def _(): self.back(to,self.s).start()
    def finish(self):
        for k in range(self.n):
            @pl.when(self.s!=k)
            def _(): self.back(k,k).wait_recv()
        @pl.when(self.s<self.n)
        def _():
            for to in range(16):
                @pl.when(self.s!=to)
                def _(): self.back(to,self.s).wait_send()
        for k in range(self.n):
            for yy in range(2):
                @pl.when(self.other(k,yy))
                def _(): self.part(k,yy).wait_send()

def kernel_bc(nheads,x_ref,gln2_ref,qkv_ref,g_ref,gT_ref,D_ref,P_ref,pr_ref,W1,gains_ref,shifts_ref,sm_ref,pos_ref,pose_ref,dcat_hbm,dlast_hbm,
              ev_hbm,hd_hbm,evl_hbm,hdl_hbm,redq_ref,redm_ref,tab_ref,sum_ref,
              G_s,Gx,Gr_s,Gxr,vst_s,dS_s,dsr_s,gbd_s,qbd_s,aq,dq_s,kT_s,gq_s,gqT_s,dd_s,small_ref,acc,slabs,got,res,
              gs,gr_,ge,dl,ds,dr,es,er,us,ss0,rs0,ts0,us0,
              *more):
    w=pl.program_id(0); nw=dd_s.shape[0]
    z,xc,c,y=place_of()
    s=(z*2+xc)*2+c
    mate=dev(z,xc,c,1-y); sib=dev(z,xc,1-c,y)
    D=x_ref.shape[-1]; WIN=x_ref.shape[-2]; SLAB=dd_s.shape[1]
    cq=D//2
    groups=nheads//PER
    tiles=G_s.shape[0]; Q=tiles*128; R=WIN-Q; part=Gx.shape[1]//nheads
    big=Reduce(dcat_hbm,redm_ref,more[9],more[10],more[11:15],*more[15:18])
    red=Reduce(dq_s,redq_ref,more[0],more[1],more[2:6],*more[6:9])
    def slab(k,to=None):
        at=ev_hbm.at[y*nw+k]
        if to is None: return pltpu.make_async_copy(dd_s.at[k],at,dl.at[k])
        return send(dd_s.at[k],at,ds.at[k],dr.at[k],to)
    def tail(k):
        lead=SLAB-hd_hbm.shape[0]
        return send(dd_s.at[nw-1,pl.ds(lead,hd_hbm.shape[0])],hd_hbm,es.at[k],er,((s+1)%16,k))
    def early(k):
        lead=SLAB-hdl_hbm.shape[0]
        if k==0: return pltpu.make_async_copy(dlast_hbm,evl_hbm.at[y],us.at[0])
        if k==1: return send(dlast_hbm,evl_hbm.at[y],us.at[1],us.at[2],mate)
        return send(dlast_hbm.at[pl.ds(lead,hdl_hbm.shape[0])],hdl_hbm,us.at[k+1],us.at[5],((s+1)%16,k-2))
    def edge_trade():
        return send(Gr_s,Gxr,ge.at[0],ge.at[1],sib)
    def trade(h):
        r=pl.multiple_of(h*WIN+(1-c)*(WIN-part),8)
        return send(G_s.at[:,pl.ds(r,part)],Gx.at[:,pl.ds(pl.multiple_of(h*part,8),part)],gs.at[h],gr_.at[h],sib)
    everyone=[((s+t)%16,yy) for t in range(1,16) for yy in (y,1-y)]+[mate]
    @pl.when(w==0)
    def _():
        hail(everyone)
        aq[...]=jnp.zeros_like(aq); G_s[...]=jnp.zeros_like(G_s); Gr_s[...]=jnp.zeros_like(Gr_s); small_ref[...]=sm_ref[...]
        dd_s[:,SLAB-16:,:]=jnp.zeros((nw,16,D),BF)
        for hh in range(PER): vst_s[(hh+1)*SLAB-16:(hh+1)*SLAB,:]=jnp.zeros((16,GROUP),BF)
    def met():
        heard(everyone)
        big.start()
        early(0).start(); early(1).start()
        @pl.when(y==1)
        def _():
            early(2).start(); early(3).start()
    plan=((0,met),(2,big.one),(7,lambda: big.turn(0)),(11,lambda: big.turn(1)),(14,lambda: big.turn(2)))
    kT_s[...]=qkv_ref[0,1].T
    lane=lax.broadcasted_iota(jnp.int32,(WIN,GROUP),1)
    hl=lane//HD
    lift=pick((GROUP,R),lambda r,c: r%R==c).astype(BF)
    own_cols=pick((GROUP,D),lambda r,c: r//R==c//HD)
    gbd_s[...]=(mm(lift,g_ref[0,Q:WIN,:])*own_cols).astype(BF)
    qbd_s[...]=(mm(lift,qkv_ref[0,0,Q:WIN,:])*own_cols).astype(BF)
    Dr=exact(D_ref[0,:,Q:WIN],pick((R,GROUP),lambda r,c: c%R==r))
    Dr=jnp.sum(Dr*pick((nheads,GROUP),lambda r,c: c//R==r),axis=0,keepdims=True)
    dsr=pr_ref[0].astype(F32)*(mm_nt(qkv_ref[0,2],gbd_s[...])-Dr)
    Gr_s[...]+=dsr
    dsr_s[...]=dsr.astype(BF)
    gqT_s[:,Q:WIN]=exact(mm(kT_s[...],dsr_s[...])*pick((D,GROUP),lambda r,c: r//HD==c//R),pick((GROUP,R),lambda r,c: r%R==c))
    def group(gi,_):
        o=pl.multiple_of(gi*GROUP,GROUP)
        gTg=gT_ref[0,pl.ds(o,GROUP),0:Q]
        vg=qkv_ref[0,2,:,pl.ds(o,GROUP)]
        qg=qkv_ref[0,0,0:Q,pl.ds(o,GROUP)]
        gg=g_ref[0,0:Q,pl.ds(o,GROUP)]
        for hh in range(PER): vst_s[hh*SLAB:hh*SLAB+WIN,:]=jnp.where(hl==hh,vg,jnp.zeros_like(vg))
        dp4=mm(vst_s[...],gTg)
        for hh in range(PER):
            h=gi*PER+hh
            dsc=P_ref[0,gi,:,hh*Q:(hh+1)*Q].astype(F32)*(dp4[hh*SLAB:hh*SLAB+WIN]-D_ref[0,pl.ds(h,1),0:Q])
            for k in range(tiles):
                G_s[k,pl.ds(pl.multiple_of(h*WIN,8),WIN),:]+=dsc[:,k*128:(k+1)*128]
            dsl=dsc.astype(BF)
            dS_s[:,hh*Q:(hh+1)*Q]=dsl
            gqT_s[pl.ds(o+hh*HD,HD),0:Q]=mm(kT_s[pl.ds(o+hh*HD,HD),:],dsl)
        zero=jnp.zeros_like(gg); hq=hl[0:Q]
        gst=jnp.concatenate([jnp.where(hq==hh,gg,zero) for hh in range(PER)],axis=0)
        qst=jnp.concatenate([jnp.where(hq==hh,qg,zero) for hh in range(PER)],axis=0)
        dv=mm(P_ref[0,gi],gst)+mm(pr_ref[0],gbd_s[:,pl.ds(o,GROUP)])
        dk=mm(dS_s[...],qst)+mm(dsr_s[...],qbd_s[:,pl.ds(o,GROUP)])
        gq_s[1,:,pl.ds(o,GROUP)]=(dk*(1.0/SQ)).astype(BF)
        gq_s[2,:,pl.ds(o,GROUP)]=dv.astype(BF)
        for when,what in plan:
            pl.when(w*groups+gi==min(when,nw*groups-1))(what)
        @pl.when(w==nw-1)
        def _():
            for hh in range(PER): trade(gi*PER+hh).start()
            @pl.when(gi==0)
            def _(): edge_trade().start()
        return 0
    lax.fori_loop(0,groups,group,0)
    gq_s[0]=(gqT_s[...]*(1.0/SQ)).astype(BF).T
    x=x_ref[0]
    xhat,rstd=norm_stats(x)
    xn=(xhat*gains_ref[0:1,:]+shifts_ref[0:1,:]).astype(BF)
    xnT=xn.T
    gr=jnp.zeros((WIN,D),F32)
    for m in range(2):
        for k in range(3):
            gc=gq_s[k,:,m*cq:(m+1)*cq]
            gr=gr+mm_nt(gc,W1[m,:,k*cq:(k+1)*cq])
            aq[m,:,k*cq:(k+1)*cq]+=mm(xnT,gc)
    @pl.when(w==nw-1)
    def _():
        dq_s[...]=aq[...].astype(BF).reshape(dq_s.shape)
        red.start()
    dd_s[w,0:WIN,:]=(gln2_ref[0]+norm_back(gr,xhat,rstd,gains_ref[0:1,:])).astype(BF)
    slab(w).start(); slab(w,mate).start()
    @pl.when(jnp.logical_and(w==nw-1,y==1))
    def _():
        tail(0).start(); tail(1).start()
    small_ref[0:1,:]+=jnp.sum(gr*xhat,axis=0,keepdims=True)
    small_ref[2:3,:]+=jnp.sum(gr,axis=0,keepdims=True)
    @pl.when(w==nw-1)
    def _():
        for h in range(nheads): trade(h).wait()
        edge_trade().wait()
        acc[...]=jnp.zeros_like(acc)
        nh=acc.shape[0]; LW=tiles*128
        base=c*(WIN-part)
        def one_hots(g,hr,lr,width):
            iota=lax.broadcasted_iota(jnp.int32,(256,width),0).astype(F32).astype(BF)
            A=jnp.concatenate([jnp.where(hr==m,g,0.0) for m in range(nh)],axis=0).astype(BF)
            oh=jnp.where(iota==lr.astype(F32).astype(BF),jnp.ones((),BF),jnp.zeros((),BF))
            return mm_nt(A,oh)
        def rows(r,_):
            r8=pl.multiple_of(r*8,8)
            f8=pl.multiple_of(base+r*8,8)
            pos=pos_ref[pl.ds(f8,8),0:LW]
            hi8=pos>>8; lo8=pos&255
            tot=jnp.zeros((nh*nheads,256),F32)
            for k in range(8):
                g=jnp.concatenate([G_s[q,pl.ds(f8+k,nheads,stride=WIN),:]+Gx[q,pl.ds(r8+k,nheads,stride=part),:] for q in range(tiles)],axis=1)
                tot=tot+one_hots(g,hi8[k:k+1,:],lo8[k:k+1,:],LW)
            acc[...]+=tot.reshape(acc.shape)
            return 0
        turned=mm_nt(pick((GROUP,GROUP),lambda r,c: c==(r%nheads)*R+r//nheads).astype(BF),(Gr_s[...]+Gxr[...]).astype(BF))
        tot=jnp.zeros((nh*nheads,256),F32)
        for k in range(R):
            pos=pose_ref[k:k+1,:]
            hi=jnp.where(c==k//(R//2),pos>>8,-1)
            tot=tot+one_hots(turned[k*nheads:(k+1)*nheads],hi,pos&255,WIN)
        acc[...]+=tot.reshape(acc.shape)
        n=part//8
        cuts=[c,n*5//25,n*15//25,n]
        for f,after in enumerate((red.one,lambda: red.turn(0),None)):
            lax.fori_loop(cuts[f],cuts[f+1],rows,0)
            if after: after()
        half=nheads//2
        for yy in range(2):
            for k in range(nh): slabs[yy,k]=acc[k,yy*half:(yy+1)*half]
            for k in range(2): slabs[yy,nh+k]=small_ref[:,k*256:(k+1)*256]
        sums=Sums(slabs,got,res,ss0,rs0,ts0,us0)
        sums.scatter()
        red.turn(1)
        sums.collect()
        red.turn(2)
        big.four()
        sums.finish()
        red.four()
        for m in range(nh):
            tab_ref[:,m*256:(m+1)*256]=res[m]
        for k in range(2): sum_ref[:,k*256:(k+1)*256]=res[nh+k]
        for k in range(nw):
            slab(k).wait(); slab(k,mate).wait()
        @pl.when(y==1)
        def _():
            tail(0).wait_send(); tail(1).wait_send(); early(2).wait_send(); early(3).wait_send()
        tail(0).wait_recv(); early(2).wait_recv()
        early(0).wait(); early(1).wait()

def call_bc(x,gln2,qkv,g,gT,Dd,Pp,Pr,W1,gains,shifts,sm,pp,pos_index,dcat,dlast,T):
    nW,WIN,D=x.shape; NH=Dd.shape[1]
    cq=D//2; tiles=WIN//128; Q=tiles*128; SLAB=-(-WIN//16)*16; EDGE=-(-(SLAB-WIN//2)//16)*16
    part=-(-WIN//16)*8
    nh=-(-T//256)
    rows,more=dcat.shape[-2:]; cols=3*cq
    sd=jax.ShapeDtypeStruct; dma=pltpu.SemaphoreType.DMA; v=pltpu.VMEM
    return pl.pallas_call(functools.partial(kernel_bc,NH),grid=(nW,),
      in_specs=[per((WIN,D)),per((WIN,D)),per((3,WIN,D)),per((WIN,D)),per((D,WIN)),per((NH,WIN)),per(Pp.shape[1:]),per((WIN,GROUP)),
        full((2,D,cols),pipeline_mode=ONE),full(gains.shape),full(shifts.shape),full(sm.shape),full(pp.shape,pipeline_mode=ONE),pl.BlockSpec((WIN-Q,WIN),lambda w:(Q//(WIN-Q),0)),ANY,ANY],
      out_specs=[ANY,ANY,ANY,ANY,full((rows,cols),pipeline_mode=ONE),full((rows,more),pipeline_mode=ONE),full((NH//2,nh*256),pipeline_mode=ONE),full(sm.shape)],
      out_shape=[sd((2*nW,SLAB,D),BF),sd((EDGE,D),BF),sd((2,SLAB,D),BF),sd((EDGE,D),BF),sd((rows,cols),F32),sd((rows,more),F32),sd((NH//2,nh*256),F32),sd(sm.shape,F32)],
      scratch_shapes=[v((tiles,NH*WIN,128),F32),v((tiles,NH*part,128),F32),v((WIN,GROUP),F32),v((WIN,GROUP),F32),v((PER*SLAB,GROUP),BF),v((WIN,PER*Q),BF),v((WIN,GROUP),BF),v((GROUP,D),BF),v((GROUP,D),BF),v((2,D,cols),F32),v((2,2,2,2,2,rows,cols),BF),v((D,WIN),BF),v((3,WIN,D),BF),v((D,WIN),F32),
        v((nW,SLAB,D),BF),v(sm.shape,F32),v((nh,NH,256),F32),v((2,nh+2,8,256),F32),v((32,8,256),F32),v((nh+2,8,256),F32),
        dma((NH,)),dma((NH,)),dma((2,)),dma((nW,)),dma((nW,)),dma((nW,)),dma((2,)),dma,dma((6,)),dma((2*nh+4,)),dma((32,)),dma((16,)),dma((nh+2,))]+reduce_scratch(rows,cols)+reduce_scratch(rows,more),
      compiler_params=pltpu.CompilerParams(vmem_limit_bytes=63*1024*1024,dimension_semantics=("arbitrary",),collective_id=3,has_side_effects=True),
      name="kernel_bc")(x,gln2,qkv,g,gT,Dd,Pp,Pr,W1,gains,shifts,sm,pp,pos_index,dcat,dlast)


def kernel_f(in_ref,og_ref,ev_ref,evl_ref,ev2_ref,hd_ref,hd2_ref,redq_ref,redm_ref,tab_ref,sum_ref,
             out_ref,din_ref,dqkv_ref,dproj_ref,dfc1_ref,dfc2_ref,dgain_ref,dshift_ref,dtab_ref,end_s):
    j=pl.program_id(0); nw=pl.num_programs(0)//2
    shift=in_ref.shape[0]//2; WIN=2*shift
    edge,SLAB=hd_ref.shape[0],ev_ref.shape[1]
    off=edge-(SLAB-shift)
    @pl.when(j==0)
    def _():
        end_s[0]=hd_ref[...].astype(F32); end_s[1]=hd2_ref[...].astype(F32)
        cq=dqkv_ref.shape[2]; cf=dfc1_ref.shape[1]
        for k in range(3): dqkv_ref[k]=redq_ref[:,k*cq:(k+1)*cq]
        dproj_ref[...]=redm_ref[:,0:cq]
        dfc1_ref[...]=redm_ref[:,cq:cq+cf]
        dfc2_ref[...]=redm_ref[:,cq+cf:]
        dgain_ref[...]=sum_ref[0:2,:]; dshift_ref[...]=sum_ref[2:6,:]
        dtab_ref[...]=tab_ref[:,0:dtab_ref.shape[1]]
    e=jnp.where(j%nw==nw-1,evl_ref[0],ev_ref[0]).astype(F32)
    for k,(base,res,v) in enumerate(((in_ref,out_ref,e),(og_ref,din_ref,ev2_ref[0].astype(F32)))):
        res[0:shift,:]=base[0:shift,:]+end_s[k,off:off+shift,:]
        res[shift:WIN,:]=base[shift:WIN,:]+v[0:shift,:]
        end_s[k]=v[SLAB-edge:,:]

def call_f(inputs,og,ev,evl,ev2,hd,hd2,redq,redm,tab,small,cq,cf,T):
    tok,D=inputs.shape; n,SLAB,_=ev.shape; WIN=tok//n; rows=redq.shape[0]
    sd=jax.ShapeDtypeStruct
    blk=pl.BlockSpec((WIN,D),lambda j:(j,0)); slab=pl.BlockSpec((1,SLAB,D),lambda j:(j,0,0))
    shapes=[(3,rows,cq),(rows,cq),(rows,cf),(rows,cf),(2,D),(4,D),(tab.shape[0],T)]
    return pl.pallas_call(kernel_f,grid=(n,),
      in_specs=[blk,blk,slab,pl.BlockSpec((1,SLAB,D),lambda j:(j//(n//2),0,0)),slab]+[full(v.shape) for v in (hd,hd2,redq,redm,tab,small)],
      out_specs=[blk,blk]+[full(v) for v in shapes],
      out_shape=[sd((tok,D),F32),sd((tok,D),F32)]+[sd(v,F32) for v in shapes],
      scratch_shapes=[pltpu.VMEM((2,)+hd.shape,F32)],
      compiler_params=pltpu.CompilerParams(vmem_limit_bytes=63*1024*1024,dimension_semantics=("arbitrary",)),
      name="kernel_f")(inputs,og,ev,evl,ev2,hd,hd2,redq,redm,tab,small)

def gathered(piece,names,nseq,nheads):
    full=lax.all_gather(piece,names,axis=0,tiled=False)
    return full.reshape((nseq,nheads)+piece.shape)

def natural(block):
    s,h,r,c=block.shape
    return block.transpose(0,2,1,3).reshape(s*r,h*c)

def owners(grad,nseq,nheads):
    r,c=grad.shape
    return grad.reshape(nseq,r//nseq,nheads,c//nheads).transpose(0,2,1,3).reshape(nseq*nheads,r//nseq,c//nheads)

def from_next(rows):
    n=lax.axis_size("seq")
    return lax.ppermute(rows,"seq",[(i,(i-1)%n) for i in range(n)])

def to_next(rows):
    n=lax.axis_size("seq")
    return lax.ppermute(rows,"seq",[(i,(i+1)%n) for i in range(n)])

def spread(rows):
    n=lax.axis_size("heads")
    flat=rows.reshape(-1,rows.shape[-1])
    if n==2:
        other=lax.ppermute(flat,"heads",[(0,1),(1,0)])
        me=lax.axis_index("heads")
        return jnp.where(me==0,jnp.concatenate([flat,other]),jnp.concatenate([other,flat]))
    return lax.all_gather(flat,"heads",axis=0,tiled=True)

def place(rows,base,shift):
    every=spread(rows)
    keep=every.shape[0]-shift
    return base+jnp.concatenate([to_next(every[keep:]),every[:keep]]).astype(F32)

def body(inputs,w_qkv,w_proj,w_fc1,w_fc2,gains,shifts,rel_table,region,pos_index,out_grad):
    nseq=lax.axis_size("seq"); nheads=lax.axis_size("heads"); me=lax.axis_index("heads")
    linked=nseq==16 and nheads==2
    names=("seq","heads")
    tok,D=inputs.shape; WIN=pos_index.shape[0]; shift=WIN//2; T=rel_table.shape[1]
    nW=tok//WIN//nheads
    rows=w_qkv.shape[1]; cq=w_qkv.shape[2]; cf=w_fc1.shape[1]
    lab=region.reshape(-1,WIN)
    if linked:
        W1,bias,brem,wf,posT=call_w(w_qkv,w_proj.T,w_fc1,w_fc2.T,pos_index,rel_table)
        qkv,x,Pp,Pr,gln2,g,gT,Dd,ev,dlast,dcat,sm=call_a2(inputs,out_grad,wf,lab,bias,brem,W1,gains,shifts)
        ev2,hd2,evl,hd,redq,redm,d_table,small=call_bc(x,gln2,qkv,g,gT,Dd,Pp,Pr,W1,gains,shifts,sm,posT,pos_index,dcat.reshape(2,2,2,2,2,rows,-1),dlast,T)
        out,din,dq,dp,d1,d2,dg,dsh,dt=call_f(inputs,out_grad,ev,evl,ev2,hd,hd2,redq,redm,d_table,small,cq,cf,T)
        return (out,din,dq,dp.T,d1,d2.T,dg,dsh,dt)
    posT=pos_index.T
    wide=-(-WIN//128)*128
    posP=jnp.pad(posT,((0,0),(0,wide-WIN)))
    start=me*nW*WIN
    lab=lax.dynamic_slice_in_dim(lab,me*nW,nW,0)
    labc=lab[:,:,None]; labr=lab[:,None,:]
    wq=jnp.concatenate([w_qkv[0],w_qkv[1],w_qkv[2],w_proj.T],axis=1).astype(BF)
    wf=jnp.concatenate([w_fc1,w_fc2.T],axis=1).astype(BF)
    table=lax.all_gather(rel_table,"heads",axis=0,tiled=True)
    NH=table.shape[0]
    every=gathered(jnp.concatenate([wq,wf],axis=1),names,nseq,nheads)
    ends=[i*cq for i in range(5)]+[4*cq+cf,4*cq+2*cf]
    W=jnp.concatenate([natural(every[...,a:b]) for a,b in zip(ends[:-1],ends[1:])],axis=1)[None]
    bias=call_p(posP,pack_table(table),WIN)
    def mine(v):
        ext=jnp.concatenate([v,from_next(v[:shift])])
        return lax.dynamic_slice_in_dim(ext,start+shift,nW*WIN,0).reshape(nW,WIN,-1)
    x=mine(inputs); og=mine(out_grad)
    delta,gln2,qkv,g,gT,Dd,Pp,dcat,sm_a=call_a(x,og,labc,labr,bias,W,gains,shifts)
    dd,dqkv,G,sm_b=call_b(x,gln2,qkv,g,gT,Dd,Pp,W,gains,shifts)
    grads=[dqkv[0,:,c*D:(c+1)*D] for c in range(3)]+[dcat[0,:,:D],dcat[0,:,D:D+cf*nheads],dcat[0,:,D+cf*nheads:]]
    red=lax.psum_scatter(jnp.concatenate([owners(v,nseq,nheads) for v in grads],axis=2),names,scatter_dimension=0,tiled=False).astype(F32)
    redq,redm=red[:,:3*cq],red[:,3*cq:]
    d_table,small=lax.psum((call_t(G,posT,T,NH),sm_a+sm_b),names)
    nl=rel_table.shape[0]
    d_table=lax.dynamic_slice_in_dim(d_table,me*nl,nl,0)
    output=place(delta,inputs,shift)
    d_inputs=place(dd,out_grad,shift)
    d_qkv=redq.reshape(rows,3,cq).transpose(1,0,2)
    d_proj=redm[:,:cq].T; d_fc1=redm[:,cq:cq+cf]; d_fc2=redm[:,cq+cf:].T
    return (output,d_inputs,d_qkv,d_proj,d_fc1,d_fc2,small[0:2],small[2:6],d_table)

def solution(mesh):
    placed=(P("seq",None),P(None,"seq","heads"),P("heads","seq"),P("seq","heads"),P("heads","seq"),P(),P(),P("heads",None),P("seq"),P(),P("seq",None))
    return jax.shard_map(body,mesh=mesh,in_specs=placed,
    out_specs=(P("seq",None),P("seq",None),P(None,"seq","heads"),P("heads","seq"),P("seq","heads"),P("heads","seq"),P(),P(),P("heads",None)),
    check_vma=False)
```

```python
import functools
import math

import jax, jax.numpy as jnp
from jax import lax
from jax.experimental import pallas as pl
from jax.experimental.pallas import tpu as pltpu
from jax.sharding import PartitionSpec as P

BF=jnp.bfloat16; F32=jnp.float32
HD=32; GROUP=128; PER=4
EPS=1e-5
SQ=math.sqrt(32.0)
CEXP=math.log2(math.e)/SQ
MASK=100.0*SQ

def mm(a,b):
    return lax.dot_general(a,b,(((1,),(0,)),((),())),preferred_element_type=F32)
def mm_nt(a,b):
    return lax.dot_general(a,b,(((1,),(1,)),((),())),preferred_element_type=F32)

def norm_stats(v):
    mean=jnp.mean(v,axis=-1,keepdims=True)
    c=v-mean
    var=jnp.mean(c*c,axis=-1,keepdims=True)
    rstd=lax.rsqrt(var+EPS)
    return c*rstd, rstd

def norm_back(gy,xhat,rstd,gain):
    gx=gy*gain
    m1=jnp.mean(gx,axis=-1,keepdims=True)
    m2=jnp.mean(gx*xhat,axis=-1,keepdims=True)
    return rstd*(gx-m1-xhat*m2)

P0=0.3275911
A1,A2,A3,A4,A5=0.254829592,-0.284496736,1.421413741,-1.453152027,1.061405429
def gelu_both(x):
    e=jnp.exp2(x*x*(-0.5*math.log2(math.e)))
    t=1.0/(1.0+(P0/math.sqrt(2.0))*jnp.abs(x))
    poly=t*(0.5*A1+t*(0.5*A2+t*(0.5*A3+t*(0.5*A4+t*(0.5*A5)))))
    half=poly*e
    phi=jnp.where(x>=0,1.0-half,half)
    return x*phi, phi+x*e*(1.0/math.sqrt(2.0*math.pi))

def kernel_a(nheads,x_ref,og_ref,labc_ref,labr_ref,bias_ref,W_ref,gains_ref,shifts_ref,
             delta_ref,gln2_ref,qkv_ref,g_ref,gT_ref,D_ref,P_hbm,dcat_ref,small_ref,
             qT_s,vT_s,OT_s,P_s,acc,sem,xn2_s,xn2T_s,tg_s,tgT_s,up_s,gn2_s):
    w=pl.program_id(0); nw=pl.num_programs(0)
    D=x_ref.shape[-1]; WIN=x_ref.shape[-2]
    parts=W_ref.shape[0]; cq=D//parts; cf=(W_ref.shape[2]-4*cq)//2
    groups=nheads//PER
    x=x_ref[0]
    xhat,_=norm_stats(x)
    xn=(xhat*gains_ref[0:1,:]+shifts_ref[0:1,:]).astype(BF)
    for c in range(3):
        for m in range(parts):
            at=slice(m*cq,(m+1)*cq)
            y=mm(xn,W_ref[m,:,c*cq:(c+1)*cq]).astype(BF)
            qkv_ref[0,c,:,at]=y
            if c==0: qT_s[at,:]=y.T
            if c==2: vT_s[at,:]=y.T
    labc=labc_ref[0]; labr=labr_ref[0]
    lane=lax.broadcasted_iota(jnp.int32,(WIN,GROUP),1)
    oh=jnp.where((labc==lane)|((labc+3)==lane),1.0,0.0).astype(BF)
    hi=564.0
    lo=MASK-hi
    sub=lax.broadcasted_iota(jnp.int32,(GROUP,WIN),0)
    nm=jnp.where(sub<3,jnp.where(sub!=labr,-hi,0.0),jnp.where(sub<6,jnp.where(sub-3!=labr,-lo,0.0),0.0)).astype(BF)
    hl=lane//HD

    def group(gi,_):
        slot=gi%2
        step=w*groups+gi
        @pl.when(step>=2)
        def _():
            pltpu.make_async_copy(P_s.at[slot],P_hbm.at[0,pl.ds(0,PER)],sem.at[slot]).wait()
        o=pl.multiple_of(gi*GROUP,GROUP)
        qTg=jnp.concatenate([qT_s[pl.ds(o,GROUP),:],nm],axis=0)
        kg=qkv_ref[0,1,:,pl.ds(o,GROUP)]
        for hh in range(PER):
            kh=jnp.concatenate([jnp.where(hl==hh,kg,jnp.zeros_like(kg)),oh],axis=1)
            t=mm(kh,qTg)+bias_ref[gi*PER+hh]
            m=jnp.max(t,axis=0,keepdims=True)
            e=jnp.exp2((t-m)*CEXP)
            l=jnp.sum(e,axis=0,keepdims=True)
            p=(e*(1.0/l)).astype(BF)
            P_s[slot,hh]=p
            OT_s[pl.ds(o+hh*HD,HD),:]=mm(vT_s[pl.ds(o+hh*HD,HD),:],p)
        pltpu.make_async_copy(P_s.at[slot],P_hbm.at[w,pl.ds(gi*PER,PER)],sem.at[slot]).start()
        return 0
    lax.fori_loop(0,groups,group,0)

    attn=OT_s[...].astype(BF).T
    branch=shifts_ref[2:3,:]
    for m in range(parts):
        branch=branch+mm_nt(attn[:,m*cq:(m+1)*cq],W_ref[m,:,3*cq:4*cq])
    branch=branch.astype(BF).astype(F32)
    middle=x+branch
    xhat2,rstd2=norm_stats(middle)
    xn2=(xhat2*gains_ref[1:2,:]+shifts_ref[1:2,:]).astype(BF)
    og=og_ref[0]
    tg=og.astype(BF)
    xn2_s[...]=xn2; xn2T_s[...]=xn2.T; tg_s[...]=tg; tgT_s[...]=tg.T
    up_s[...]=jnp.zeros_like(up_s); gn2_s[...]=jnp.zeros_like(gn2_s)
    CH=min(512,cf); each=cf//CH
    @pl.when(w==0)
    def _():
        acc[...]=jnp.zeros_like(acc)
        small_ref[...]=jnp.zeros_like(small_ref)
    def chunk(c,_):
        m=c//each
        o=pl.multiple_of((c%each)*CH,CH)
        f1=W_ref[m,:,pl.ds(4*cq+o,CH)]; f2=W_ref[m,:,pl.ds(4*cq+cf+o,CH)]
        hid=mm(xn2_s[...],f1)
        act,dact=gelu_both(hid)
        a=act.astype(BF)
        up_s[...]+=mm_nt(a,f2)
        gh=(mm(tg_s[...],f2)*dact).astype(BF)
        gn2_s[...]+=mm_nt(gh,f1)
        acc[m,:,pl.ds(cq+o,CH)]+=mm(xn2T_s[...],gh)
        acc[m,:,pl.ds(cq+cf+o,CH)]+=mm(tgT_s[...],a)
        return 0
    lax.fori_loop(0,parts*each,chunk,0)
    delta_ref[0]=(branch+up_s[...]+shifts_ref[3:4,:]).astype(BF)
    gn2=gn2_s[...]
    gln2=norm_back(gn2,xhat2,rstd2,gains_ref[1:2,:])
    gln2_ref[0]=gln2
    gb=(og+gln2).astype(BF)
    gbT=gb.T
    for m in range(parts):
        at=slice(m*cq,(m+1)*cq)
        acc[m,:,0:cq]+=mm(gbT,attn[:,at])
        g=mm(gb,W_ref[m,:,3*cq:4*cq]).astype(BF)
        g_ref[0,:,at]=g
        gT=g.T
        gT_ref[0,at,:]=gT
        prod=gT.astype(F32)*OT_s[at,:]
        nh=nheads//parts
        D_ref[0,m*nh:(m+1)*nh,:]=jnp.sum(prod.reshape(nh,HD,WIN),axis=1)
    small_ref[1:2,:]+=jnp.sum(gn2*xhat2,axis=0,keepdims=True)
    small_ref[3:4,:]+=jnp.sum(gn2,axis=0,keepdims=True)
    small_ref[4:5,:]+=jnp.sum(gb.astype(F32),axis=0,keepdims=True)
    small_ref[5:6,:]+=jnp.sum(tg.astype(F32),axis=0,keepdims=True)
    @pl.when(w==nw-1)
    def _():
        dcat_ref[...]=acc[...].astype(BF)
        for s in range(2):
            pltpu.make_async_copy(P_s.at[s],P_hbm.at[0,pl.ds(0,PER)],sem.at[s]).wait()

def full(shape,**kw):
    return pl.BlockSpec(shape,lambda w:(0,)*len(shape),**kw)
def per(shape,**kw):
    return pl.BlockSpec((1,)+shape,lambda w:(w,)+(0,)*len(shape),**kw)
ONE=pl.Buffered(1)
ANY=pl.BlockSpec(memory_space=pl.ANY)

def call_a(x,og,labc,labr,bias,W,gains,shifts):
    nW,WIN,D=x.shape; NH=bias.shape[0]
    parts,_,Ct=W.shape; Cg=Ct-3*(D//parts)
    sd=jax.ShapeDtypeStruct
    outs=[sd((nW,WIN,D),BF),sd((nW,WIN,D),F32),sd((nW,3,WIN,D),BF),sd((nW,WIN,D),BF),sd((nW,D,WIN),BF),sd((nW,NH,WIN),F32),
          sd((nW,NH,WIN,WIN),BF),sd((parts,D,Cg),BF),sd((8,D),F32)]
    return pl.pallas_call(functools.partial(kernel_a,NH),grid=(nW,),
      in_specs=[per((WIN,D)),per((WIN,D)),per((WIN,1)),per((1,WIN)),full((NH,WIN,WIN),pipeline_mode=ONE),
        full((parts,D,Ct),pipeline_mode=ONE),full(gains.shape),full(shifts.shape)],
      out_specs=[per((WIN,D)),per((WIN,D)),per((3,WIN,D)),per((WIN,D)),per((D,WIN)),per((NH,WIN)),ANY,full((parts,D,Cg)),full((8,D))],
      out_shape=outs,
      scratch_shapes=[pltpu.VMEM((D,WIN),BF),pltpu.VMEM((D,WIN),BF),pltpu.VMEM((D,WIN),F32),pltpu.VMEM((2,PER,WIN,WIN),BF),
        pltpu.VMEM((parts,D,Cg),F32),pltpu.SemaphoreType.DMA((2,)),
        pltpu.VMEM((WIN,D),BF),pltpu.VMEM((D,WIN),BF),pltpu.VMEM((WIN,D),BF),pltpu.VMEM((D,WIN),BF),pltpu.VMEM((WIN,D),F32),pltpu.VMEM((WIN,D),F32)],
      compiler_params=pltpu.CompilerParams(vmem_limit_bytes=62*1024*1024,dimension_semantics=("arbitrary",)),
      name="kernel_a")(x,og,labc,labr,bias,W,gains,shifts)

def kernel_b(nheads,x_ref,gln2_ref,qkv_ref,g_ref,gT_ref,D_ref,P_ref,W_ref,gains_ref,shifts_ref,
             dd_ref,dqkv_ref,G_hbm,small_ref,G_s,aq,kT_s,gq_s,gqT_s,sem):
    w=pl.program_id(0); nw=pl.num_programs(0)
    D=x_ref.shape[-1]; WIN=x_ref.shape[-2]
    parts=W_ref.shape[0]; cq=D//parts
    groups=nheads//PER
    @pl.when(w==0)
    def _():
        aq[...]=jnp.zeros_like(aq); G_s[...]=jnp.zeros_like(G_s); small_ref[...]=jnp.zeros_like(small_ref)
    kT_s[...]=qkv_ref[0,1].T
    lane=lax.broadcasted_iota(jnp.int32,(WIN,GROUP),1)
    hl=lane//HD
    def group(gi,_):
        o=pl.multiple_of(gi*GROUP,GROUP)
        gTg=gT_ref[0,pl.ds(o,GROUP),:]
        vg=qkv_ref[0,2,:,pl.ds(o,GROUP)]
        qg=qkv_ref[0,0,:,pl.ds(o,GROUP)]
        gg=g_ref[0,:,pl.ds(o,GROUP)]
        dv=jnp.zeros((WIN,GROUP),F32); dk=jnp.zeros((WIN,GROUP),F32)
        zero=jnp.zeros_like(vg)
        for hh in range(PER):
            h=gi*PER+hh
            p=P_ref[0,h]
            dp=mm(jnp.where(hl==hh,vg,zero),gTg)
            ds_=p.astype(F32)*(dp-D_ref[0,pl.ds(h,1),:])
            for c in range(G_s.shape[0]):
                wd=min(128,WIN-c*128)
                G_s[c,pl.ds(pl.multiple_of(h*WIN,8),WIN),:wd]+=ds_[:,c*128:c*128+wd]
            dsl=ds_.astype(BF)
            dv+=mm(p,jnp.where(hl==hh,gg,zero))
            dk+=mm(dsl,jnp.where(hl==hh,qg,zero))
            gqT_s[pl.ds(o+hh*HD,HD),:]=mm(kT_s[pl.ds(o+hh*HD,HD),:],dsl)
        gq_s[1,:,pl.ds(o,GROUP)]=(dk*(1.0/SQ)).astype(BF)
        gq_s[2,:,pl.ds(o,GROUP)]=dv.astype(BF)
        return 0
    lax.fori_loop(0,groups,group,0)
    gq_s[0]=(gqT_s[...]*(1.0/SQ)).astype(BF).T
    x=x_ref[0]
    xhat,rstd=norm_stats(x)
    xn=(xhat*gains_ref[0:1,:]+shifts_ref[0:1,:]).astype(BF)
    xnT=xn.T
    gr=jnp.zeros((WIN,D),F32)
    for m in range(parts):
        for c in range(3):
            gc=gq_s[c,:,m*cq:(m+1)*cq]
            gr=gr+mm_nt(gc,W_ref[m,:,c*cq:(c+1)*cq])
            aq[m,:,c*cq:(c+1)*cq]+=mm(xnT,gc)
    dd_ref[0]=(gln2_ref[0]+norm_back(gr,xhat,rstd,gains_ref[0:1,:])).astype(BF)
    small_ref[0:1,:]+=jnp.sum(gr*xhat,axis=0,keepdims=True)
    small_ref[2:3,:]+=jnp.sum(gr,axis=0,keepdims=True)
    @pl.when(w==nw-1)
    def _():
        dqkv_ref[...]=aq[...].astype(BF)
        cp=pltpu.make_async_copy(G_s,G_hbm,sem); cp.start(); cp.wait()

def call_b(x,gln2,qkv,g,gT,Dd,Pp,W,gains,shifts):
    nW,WIN,D=x.shape; NH=Dd.shape[1]
    parts=W.shape[0]; cq=D//parts; tiles=-(-WIN//128)
    sd=jax.ShapeDtypeStruct
    return pl.pallas_call(functools.partial(kernel_b,NH),grid=(nW,),
      in_specs=[per((WIN,D)),per((WIN,D)),per((3,WIN,D)),per((WIN,D)),per((D,WIN)),per((NH,WIN)),per((NH,WIN,WIN)),
        full((parts,D,3*cq),pipeline_mode=ONE),full(gains.shape),full(shifts.shape)],
      out_specs=[per((WIN,D)),full((parts,D,3*cq)),ANY,full((8,D))],
      out_shape=[sd((nW,WIN,D),BF),sd((parts,D,3*cq),BF),sd((tiles,NH*WIN,128),F32),sd((8,D),F32)],
      scratch_shapes=[pltpu.VMEM((tiles,NH*WIN,128),F32),pltpu.VMEM((parts,D,3*cq),F32),pltpu.VMEM((D,WIN),BF),pltpu.VMEM((3,WIN,D),BF),pltpu.VMEM((D,WIN),F32),
        pltpu.SemaphoreType.DMA],
      compiler_params=pltpu.CompilerParams(vmem_limit_bytes=62*1024*1024,dimension_semantics=("arbitrary",)),
      name="kernel_b")(x,gln2,qkv,g,gT,Dd,Pp,W,gains,shifts)

FIX=8191.0

def pack_table(table):
    NH,T=table.shape
    n=-(-T//128)
    q=jnp.round(jnp.clip(table,-4.0,4.0)*FIX).astype(jnp.int32)
    q=jnp.pad(q,((0,0),(0,n*128-T)))
    q=q.reshape(NH//2,2,n,128)
    return (q[:,0]*65536)|(q[:,1]&65535)

def kernel_p(pos_ref,tab_ref,bias_ref):
    npair,n,_=tab_ref.shape
    WIN=bias_ref.shape[-1]
    tiles=-(-WIN//128)
    def row(r,_):
        r8=pl.multiple_of(r*8,8)
        for c in range(tiles):
            width=min(128,WIN-c*128)
            idx=pos_ref[pl.ds(r8,8),c*128:(c+1)*128]
            lo=idx&127; hi=idx>>7
            masks=[hi==k for k in range(n)]
            for p in range(npair):
                acc=jnp.zeros((8,128),jnp.int32)
                for k in range(n):
                    src=jnp.broadcast_to(tab_ref[p,k:k+1,:],(8,128))
                    acc=jnp.where(masks[k],jnp.take_along_axis(src,lo,axis=1),acc)
                a=(acc>>16).astype(F32)*(SQ/FIX)
                b=((acc<<16)>>16).astype(F32)*(SQ/FIX)
                bias_ref[2*p,pl.ds(r8,8),c*128:c*128+width]=a[:,:width]
                bias_ref[2*p+1,pl.ds(r8,8),c*128:c*128+width]=b[:,:width]
        return 0
    lax.fori_loop(0,bias_ref.shape[1]//8,row,0)

def call_p(posT_pad,tab,WIN):
    NH=tab.shape[0]*2
    return pl.pallas_call(kernel_p,out_shape=jax.ShapeDtypeStruct((NH,WIN,WIN),F32),
      compiler_params=pltpu.CompilerParams(vmem_limit_bytes=40*1024*1024),name="kernel_p")(posT_pad,tab)

def kernel_t(NH,G_ref,hi_ref,lo_ref,out_ref):
    WIN=hi_ref.shape[0]; LW=G_ref.shape[0]*128
    nh=out_ref.shape[0]//NH
    out_ref[...]=jnp.zeros_like(out_ref)
    def rows(r,_):
        r8=pl.multiple_of(r*8,8)
        hi8=hi_ref[pl.ds(r8,8),:]; lo8=lo_ref[pl.ds(r8,8),:]
        tot=jnp.zeros(out_ref.shape,F32)
        iota=lax.broadcasted_iota(jnp.int32,(256,LW),0).astype(F32).astype(BF)
        for k in range(8):
            g=jnp.concatenate([G_ref[c,pl.ds(r8+k,NH,stride=WIN),:] for c in range(LW//128)],axis=1)
            hr=hi8[k:k+1,:]; lr=lo8[k:k+1,:].astype(F32).astype(BF)
            A=jnp.concatenate([jnp.where(hr==m,g,0.0) for m in range(nh)],axis=0).astype(BF)
            oh=jnp.where(iota==lr,jnp.ones((),BF),jnp.zeros((),BF))
            tot=tot+lax.dot_general(A,oh,(((1,),(1,)),((),())),preferred_element_type=F32)
        out_ref[...]+=tot
        return 0
    lax.fori_loop(0,WIN//8,rows,0)

def call_t(G,posT,T,NH):
    WIN=posT.shape[0]; nt=G.shape[0]
    nh=-(-T//256)
    pp=jnp.pad(posT,((0,0),(0,nt*128-WIN)),constant_values=nh*256)
    hi=pp>>8; lo=pp&255
    o=pl.pallas_call(functools.partial(kernel_t,NH),out_shape=jax.ShapeDtypeStruct((nh*NH,256),F32),
      compiler_params=pltpu.CompilerParams(vmem_limit_bytes=40*1024*1024),name="kernel_t")(G,hi,lo)
    return o.reshape(nh,NH,256).transpose(1,0,2).reshape(NH,nh*256)[:,:T]


MESHID=pl.DeviceIdType.MESH

def place_of():
    s=lax.axis_index("seq"); y=lax.axis_index("heads")
    return s//4,(s//2)%2,s%2,y

def dev(z,x,c,y):
    return ((z*2+x)*2+c,y)

def peers_of(z,x,c,y):
    return [dev(z,x,1-c,y),dev(z,1-x,c,y),dev(z,x,c,1-y)]+[dev((z+i)%4,x,c,y) for i in (1,2,3)]

def hail(devices):
    bar=pltpu.get_barrier_semaphore()
    for d in devices:
        pl.semaphore_signal(bar,inc=1,device_id=d,device_id_type=MESHID)

def heard(devices):
    pl.semaphore_wait(pltpu.get_barrier_semaphore(),len(devices))

def greet(devices):
    hail(devices)
    heard(devices)

def send(src,dst,ss,rs,to):
    return pltpu.make_async_remote_copy(src_ref=src,dst_ref=dst,send_sem=ss,recv_sem=rs,device_id=to,device_id_type=MESHID)


class Gather:
    def __init__(self,src,dst,ss,rs,own,cols=None):
        self.src,self.dst,self.ss,self.rs,self.own=src,dst,ss,rs,own
        self.cols=pl.ds(0,dst.shape[2]) if cols is None else cols
        z,x,c,y=self.at=place_of()
        self.xa=x+(1-2*x)*(1-c); self.ya=y+(1-2*y)*c
        self.xb=x+(1-2*x)*c; self.yb=y+(1-2*y)*(1-c)
        self.sib=dev(z,x,1-c,y); self.pa=dev(z,self.xa,c,self.ya); self.pb=dev(z,self.xb,c,self.yb)
    def slot(self,zz,xx,cc,yy):
        n=self.src.shape[0]
        return self.dst.at[yy,pl.ds(pl.multiple_of(((zz*2+xx)*2+cc)*n,n),n),self.cols]
    def copy(self,src,where,k,to):
        return send(src,self.slot(*where),self.ss.at[k],self.rs.at[k],to)
    def go(self,where,k,to,src=None):
        self.copy(self.slot(*where) if src is None else src,where,k,to).start()
    def came(self,where,k):
        self.copy(self.src,where,k,self.sib).wait_recv()
    def keep(self):
        z,x,c,y=self.at
        return pltpu.make_async_copy(self.src,self.slot(z,x,c,y),self.own)
    def start(self):
        z,x,c,y=self.at
        me=(z,x,c,y)
        self.keep().start()
        for i in (1,2,3):
            self.go(me,i-1,dev((z+i)%4,x,c,y),self.src)
        self.go(me,3,self.pa,self.src); self.go(me,7,self.pb,self.src); self.go(me,15,self.sib,self.src)
    def z(self,i):
        return (self.at[0]+4-i)%4
    def turn_z(self,i):
        z,x,c,y=self.at
        at=(self.z(i),x,c,y); self.came(at,i-1)
        self.go(at,3+i,self.pa); self.go(at,7+i,self.pb); self.go(at,15+i,self.sib)
    def turn_a(self,i):
        at=(self.z(i),self.xa,self.at[2],self.ya); self.came(at,3+i)
        self.go(at,11+i,self.pb); self.go(at,19+i,self.sib)
    def turn_b(self,i):
        at=(self.z(i),self.xb,self.at[2],self.yb); self.came(at,7+i)
        self.go(at,23+i,self.sib)
    def turn_ab(self,i):
        z,x,c,y=self.at
        at=(self.z(i),1-x,c,1-y); self.came(at,11+i)
        self.go(at,27+i,self.sib)
    def last(self):
        z,x,c,y=self.at
        for i in range(4):
            zz=self.z(i)
            self.came((zz,x,1-c,y),15+i); self.came((zz,self.xb,1-c,self.yb),19+i)
            self.came((zz,self.xa,1-c,self.ya),23+i); self.came((zz,1-x,1-c,1-y),27+i)
    def drain(self):
        z,x,c,y=self.at
        for k in range(31):
            self.copy(self.src,(z,x,c,y),k,self.sib).wait_send()
        self.keep().wait()

class GatherLate(Gather):
    def start(self):
        z,x,c,y=self.at
        me=(z,x,c,y)
        self.keep().start()
        self.go(me,0,self.pa,self.src)
        for i in (1,2,3):
            self.go(me,i,dev((z+i)%4,x,c,y),self.src)
        self.go(me,7,self.pb,self.src); self.go(me,15,self.sib,self.src)
    def pair(self):
        z,x,c,y=self.at
        at=(z,self.xa,c,self.ya); self.came(at,0)
        for i in (1,2,3):
            self.go(at,3+i,dev((z+i)%4,x,c,y))
        self.go(at,11,self.pb); self.go(at,19,self.sib)
    def along(self,i):
        z,x,c,y=self.at
        at=(self.z(i),x,c,y); self.came(at,i)
        self.go(at,7+i,self.pb); self.go(at,15+i,self.sib)
        at=(self.z(i),self.xa,c,self.ya); self.came(at,3+i)
        self.go(at,11+i,self.pb); self.go(at,19+i,self.sib)
    def over(self,i):
        z,x,c,y=self.at
        at=(self.z(i),self.xb,c,self.yb); self.came(at,7+i)
        self.go(at,23+i,self.sib)
        at=(self.z(i),1-x,c,1-y); self.came(at,11+i)
        self.go(at,27+i,self.sib)

def gather_sems():
    return [pltpu.SemaphoreType.DMA((31,)),pltpu.SemaphoreType.DMA((31,)),pltpu.SemaphoreType.DMA]

STEPS=7
def kernel_w(qkv_ref,proj_ref,fc1_ref,fc2_ref,pos_ref,tab_ref,W_hbm,bias_hbm,brem_hbm,wf_ref,posT_ref,
             bias_s,brem_s,short_s,found_s,wq_s,tb,tq,ss,rs,own,bs,br,bl,tsem,ed):
    z,x,c,y=place_of()
    cq=qkv_ref.shape[2]; cf=fc1_ref.shape[1]
    for k in range(3): wq_s[:,k*cq:(k+1)*cq]=qkv_ref[k].astype(BF)
    wq_s[:,3*cq:4*cq]=proj_ref[...].astype(BF)
    lead=wq_s.shape[1]-4*cq
    wq_s[:,4*cq:]=fc1_ref[:,0:lead].astype(BF)
    half,T=tab_ref.shape
    tb[2]=jnp.zeros(tb.shape[1:],F32)
    tb[2,:,0:T]=tab_ref[...]
    greet(peers_of(z,x,c,y))
    mid=wq_s.shape[1]//2
    gather=Gather(wq_s.at[:,pl.ds(0,mid)],W_hbm,ss.at[0],rs.at[0],own.at[0],pl.ds(0,mid))
    other=GatherLate(wq_s.at[:,pl.ds(mid,mid)],W_hbm,ss.at[1],rs.at[1],own.at[1],pl.ds(mid,mid))
    swap=send(tb.at[2],tb.at[y],tsem.at[0],tsem.at[1],dev(z,x,c,1-y))
    swap.start()
    gather.start(); other.start()
    tb[y]=tb[2]
    wf_ref[:,0:cf-lead]=fc1_ref[:,lead:].astype(BF)
    wf_ref[:,cf-lead:]=fc2_ref[...].astype(BF)
    WIN,Q=bias_s.shape[-2:]; tiles=Q//128; n=tb.shape[2]//128; R=WIN-Q; per_row=128//R; nr=found_s.shape[1]
    posT_ref[...]=jnp.full(posT_ref.shape,1<<15,jnp.int32)
    posT_ref[:,0:WIN]=pos_ref[...].astype(F32).T.astype(jnp.int32)
    swap.wait()
    npair=half//2
    for p in range(npair):
        a,b=[jnp.floor(jnp.clip(tb[c,2*p+k:2*p+k+1,:],-4.0,4.0)*FIX+0.5).astype(jnp.int32) for k in range(2)]
        tq[p:p+1,:]=(a*65536)|(b&65535)
    nrow=WIN//8
    cuts=[nrow*k//STEPS for k in range(STEPS+1)]
    sib=dev(z,x,1-c,y)
    def rows_of(k): return pl.ds(cuts[k]*8,(cuts[k+1]-cuts[k])*8)
    def kept(k): return pltpu.make_async_copy(bias_s.at[:,rows_of(k)],bias_hbm.at[pl.ds(c*half,half),rows_of(k)],bl.at[k])
    def sent(k,cc): return send(bias_s.at[:,rows_of(k)],bias_hbm.at[pl.ds(cc*half,half),rows_of(k)],bs.at[k],br.at[k],sib)
    def look(idx):
        lo=idx&127; hi=idx>>7
        masks=[hi==q for q in range(n)]
        for p in range(npair):
            acc=jnp.zeros((8,128),jnp.int32)
            for q in range(n):
                src=jnp.broadcast_to(tq[p:p+1,q*128:(q+1)*128],(8,128))
                acc=jnp.where(masks[q],jnp.take_along_axis(src,lo,axis=1),acc)
            yield 2*p,(acc>>16).astype(F32)*(SQ/FIX)
            yield 2*p+1,((acc<<16)>>16).astype(F32)*(SQ/FIX)
    slots=lax.broadcasted_iota(jnp.int32,(nr,128),1)//R
    def short_in():
        short_s[...]=jnp.full(short_s.shape,1<<15,jnp.int32)
        short_s[0:WIN,:]=posT_ref[:,Q:Q+128]
        packed=jnp.zeros((nr,128),jnp.int32)
        for u in range(per_row):
            v=short_s[pl.ds(u,nr,stride=per_row),:]
            packed=jnp.where(slots==u,pltpu.roll(v,u*R,1) if u else v,packed)
        for t in range(nr//8):
            for h,v in look(packed[t*8:(t+1)*8]): found_s[h,t*8:(t+1)*8,:]=v
    def short_out():
        for u in range(per_row):
            row=jnp.zeros((nr,128),F32)
            for h in range(half):
                by=((h-u)*R)%128
                v=found_s[h]
                row=jnp.where(slots==h,pltpu.roll(v,by,1) if by else v,row)
            brem_s[pl.ds(u,nr,stride=per_row),:]=row
    def rows(k):
        def row(r,_):
            r8=pl.multiple_of(r*8,8)
            for t in range(tiles):
                for h,v in look(posT_ref[pl.ds(r8,8),t*128:(t+1)*128]):
                    bias_s[h,pl.ds(r8,8),t*128:(t+1)*128]=v
            return 0
        lax.fori_loop(cuts[k],cuts[k+1],row,0)
        kept(k).start(); sent(k,c).start()
    rows(0)
    short_in()
    short_out()
    other.pair()
    rows(1)
    for i in (1,3,2): gather.turn_z(i)
    for i in (0,): gather.turn_a(i); gather.turn_b(i)
    rows(2)
    for i in (1,3,2): other.along(i)
    rows(3)
    for i in (1,3,2): gather.turn_a(i); gather.turn_b(i)
    rows(4)
    for i in (0,1,3,2): gather.turn_ab(i); other.over(i)
    rows(5)
    rows(6)
    edges=[pltpu.make_async_copy(brem_s.at[pl.ds(0,WIN)],brem_hbm.at[c],ed.at[0]),send(brem_s.at[pl.ds(0,WIN)],brem_hbm.at[c],ed.at[1],ed.at[2],sib)]
    for e in edges: e.start()
    gather.last(); other.last()
    for e in edges: e.wait()
    for k in range(STEPS):
        kept(k).wait(); sent(k,c).wait_send(); sent(k,1-c).wait_recv()
    gather.drain(); other.drain()

def call_w(w_qkv,w_proj,w_fc1,w_fc2,pos_index,rel_table):
    rows,cq=w_qkv.shape[1:]; cf=w_fc1.shape[1]; WIN=pos_index.shape[0]; half,T=rel_table.shape; dma=pltpu.SemaphoreType.DMA
    wide=-(-WIN//128)*128; Q=WIN//128*128; n=-(-T//128); mem=pltpu.VMEM
    keys=-(-WIN//(1024//(WIN-Q)))*(1024//(WIN-Q))
    early=4*cq+min(512,cf); late=4*cq+2*cf-early
    sd=jax.ShapeDtypeStruct
    return pl.pallas_call(kernel_w,grid=(1,),
      out_shape=[sd((2,16*rows,early),BF),sd((2*half,WIN,Q),F32),sd((2,WIN,128),F32),sd((rows,late),BF),sd((WIN,wide),jnp.int32)],
      in_specs=[full(v.shape) for v in (w_qkv,w_proj,w_fc1,w_fc2,pos_index,rel_table)],out_specs=[ANY,ANY,ANY,full((rows,late)),full((WIN,wide))],
      scratch_shapes=[mem((half,WIN,Q),F32),mem((keys,128),F32),mem((keys,128),jnp.int32),mem((half,keys*(WIN-Q)//128,128),F32),mem((rows,early),BF),mem((3,half,n*128),F32),mem((half//2,n*128),jnp.int32)]
        +[dma((2,31)),dma((2,31)),dma((2,))]+[dma((STEPS,)),dma((STEPS,)),dma((STEPS,)),dma((2,)),dma((3,))],
      compiler_params=pltpu.CompilerParams(vmem_limit_bytes=63*1024*1024,collective_id=1,has_side_effects=True),name="kernel_w")(w_qkv,w_proj,w_fc1,w_fc2,pos_index,rel_table)

def neighbours(z,x,c,y):
    s=(z*2+x)*2+c
    return [((s+k)%16,yy) for k in (1,15) for yy in (y,1-y)]

def pick(shape,test):
    r=lax.broadcasted_iota(jnp.int32,shape,0); c=lax.broadcasted_iota(jnp.int32,shape,1)
    return jnp.where(test(r,c),1.0,0.0)

def exact(a,b):
    return lax.dot_general(a,b,(((1,),(0,)),((),())),precision=lax.Precision.HIGHEST,preferred_element_type=F32)

def kernel_a2(nheads,in_hbm,og_hbm,wf_hbm,lab_ref,bias_ref,brem_ref,W1,gains_ref,shifts_ref,
              qkv_ref,x_ref,P_hbm,pr_ref,gln2_ref,g_ref,gT_ref,D_ref,ev_hbm,dlast_hbm,dcat_hbm,small_ref,
              x_s,og_s,W2,OT_s,qT_s,vT_s,P_s,kst_s,acc,pst,xn2_s,xn2T_s,tg_s,tgT_s,up_s,gn2_s,dl_s,
              lab_s,psem,xsem,hsem,ss,rs,own,dl,ds,dr,fin):
    i=pl.program_id(0); nw=x_s.shape[0]
    w=i%nw
    z,xc,c,y=place_of()
    s=(z*2+xc)*2+c
    D=x_s.shape[-1]; WIN=qkv_ref.shape[-2]; SLAB=x_s.shape[1]; HALF=SLAB//2
    OFF=(SLAB-WIN)//2
    cq=D//2; lead=W1.shape[2]-4*cq; cf=(W2.shape[2]+lead)//2
    groups=nheads//PER; Q=bias_ref.shape[2]; R=WIN-Q
    gather=Gather(wf_hbm,W2,ss,rs,own)
    mate=dev(z,xc,c,1-y)
    def local(k,half,t):
        hbm,buf=((in_hbm,x_s),(og_hbm,og_s))[t]
        r=pl.multiple_of(y*(nw*WIN)+k*WIN+(WIN//2-OFF)+half*HALF,8)
        return pltpu.make_async_copy(hbm.at[pl.ds(r,HALF)],buf.at[k,pl.ds(half*HALF,HALF)],xsem.at[t,2*k+half])
    def edge(t):
        hbm,buf=((in_hbm,x_s),(og_hbm,og_s))[t]
        return send(hbm.at[pl.ds(0,HALF)],buf.at[nw-1,pl.ds(HALF,HALF)],hsem.at[t,0],hsem.at[t,1],((s+15)%16,1))
    def ready(t):
        local(w,0,t).wait()
        far=jnp.logical_and(w==nw-1,y==1)
        @pl.when(far)
        def _(): edge(t).wait_recv()
        @pl.when(jnp.logical_not(far))
        def _(): local(w,1,t).wait()
    def slab(k,to=None):
        if k is None: return pltpu.make_async_copy(dl_s.at[nw-1],dlast_hbm,dl.at[nw-1])
        at=ev_hbm.at[y*nw+k]
        if to is None: return pltpu.make_async_copy(dl_s.at[k],at,dl.at[k])
        return send(dl_s.at[k],at,ds.at[k],dr.at[k],to)
    everyone=peers_of(z,xc,c,y)+neighbours(z,xc,c,y)
    def met():
        heard(everyone)
        gather.start()
        @pl.when(y==1)
        def _():
            for t in range(2): edge(t).start()
    def first():
        for k in (1,3,2): gather.turn_z(k)
    def second():
        for k in (0,1,3,2): gather.turn_a(k); gather.turn_b(k)
    def third():
        for k in (0,1,3,2): gather.turn_ab(k)
    plan=((0,met),(6,first),(10,second),(14,third))
    @pl.when(i==0)
    def _():
        hail(everyone)
        for k in range(nw):
            for t in range(2):
                local(k,0,t).start()
                if k<nw-1: local(k,1,t).start()
        for t in range(2):
            @pl.when(y==0)
            def _(): local(nw-1,1,t).start()
        lab_s[...]=lab_ref[...].astype(F32).T
        acc[...]=jnp.zeros_like(acc)
        for hh in range(PER): kst_s[(hh+1)*SLAB-16:(hh+1)*SLAB,:]=jnp.zeros((16,2*GROUP),BF)
        small_ref[...]=jnp.zeros_like(small_ref)
        dl_s[:,SLAB-16:,:]=jnp.zeros((nw,16,D),BF)

    @pl.when(i<nw)
    def _():
        ready(0)
        x=x_s[w,OFF:OFF+WIN,:]
        x_ref[0]=x
        xhat,_=norm_stats(x)
        xn=(xhat*gains_ref[0:1,:]+shifts_ref[0:1,:]).astype(BF)
        for k in range(3):
            for m in range(2):
                at=slice(m*cq,(m+1)*cq)
                v=mm(xn,W1[m,:,k*cq:(k+1)*cq]).astype(BF)
                qkv_ref[0,k,:,at]=v
                if k==0: qT_s[at,:]=v.T
                if k==2: vT_s[at,:]=v.T
        mine=y*nw+w
        labr=lab_ref[pl.ds(mine,1),:]
        labc=jnp.sum(jnp.where(lax.broadcasted_iota(jnp.int32,lab_s.shape,1)==mine,lab_s[...],0.0),axis=1,keepdims=True).astype(jnp.int32)
        lane=lax.broadcasted_iota(jnp.int32,(WIN,GROUP),1)
        oh=jnp.where((labc==lane)|((labc+3)==lane),1.0,0.0).astype(BF)
        hi=564.0
        lo=MASK-hi
        sub=lax.broadcasted_iota(jnp.int32,(GROUP,WIN),0)
        nm=jnp.where(sub<3,jnp.where(sub!=labr,-hi,0.0),jnp.where(sub<6,jnp.where(sub-3!=labr,-lo,0.0),0.0)).astype(BF)
        hl=lane//HD
        for hh in range(PER): kst_s[hh*SLAB:hh*SLAB+WIN,GROUP:]=oh
        nmq=nm[:,0:Q]
        def soften(t):
            m=jnp.max(t,axis=0,keepdims=True)
            e=jnp.exp2((t-m)*CEXP)
            l=jnp.sum(e,axis=0,keepdims=True)
            return (e*(1.0/l)).astype(BF)
        def group(gi,_):
            slot=gi%2
            @pl.when(w*groups+gi>=2)
            def _():
                pltpu.make_async_copy(P_s.at[slot],P_hbm.at[0,0],psem.at[slot]).wait()
            o=pl.multiple_of(gi*GROUP,GROUP)
            qTg=jnp.concatenate([qT_s[pl.ds(o,GROUP),0:Q],nmq],axis=0)
            kg=qkv_ref[0,1,:,pl.ds(o,GROUP)]
            for hh in range(PER): kst_s[hh*SLAB:hh*SLAB+WIN,0:GROUP]=jnp.where(hl==hh,kg,jnp.zeros_like(kg))
            t4=mm(kst_s[...],qTg)
            for hh in range(PER):
                p=soften(t4[hh*SLAB:hh*SLAB+WIN]+bias_ref[gi*PER+hh])
                P_s[slot,:,hh*Q:(hh+1)*Q]=p
                OT_s[w,pl.ds(o+hh*HD,HD),0:Q]=mm(vT_s[pl.ds(o+hh*HD,HD),:],p)
            pltpu.make_async_copy(P_s.at[slot],P_hbm.at[w,gi],psem.at[slot]).start()
            for when,what in plan:
                pl.when(w*groups+gi==min(when,nw*groups-1))(what)
            return 0
        lax.fori_loop(0,groups,group,0)
        spread=pick((R,GROUP),lambda r,c: c%R==r).astype(BF)
        own_rows=pick((D,GROUP),lambda r,c: r//HD==c//R)
        qbd=(mm(qT_s[:,Q:WIN],spread)*own_rows).astype(BF)
        nmr=mm(nm[:,Q:WIN],spread).astype(BF)
        brem=jnp.concatenate([brem_ref[0,:,0:GROUP//2],brem_ref[1,:,0:GROUP//2]],axis=1)
        pr=soften(mm(qkv_ref[0,1],qbd)+mm(oh,nmr)+brem)
        pr_ref[0]=pr
        OT_s[w,:,Q:WIN]=exact(mm(vT_s[...],pr)*own_rows,pick((GROUP,R),lambda r,c: r%R==c))

    @pl.when(i==nw-1)
    def _():
        gather.last(); gather.drain()

    @pl.when(i>=nw)
    def _():
        ready(1)
        x=x_s[w,OFF:OFF+WIN,:]
        og=og_s[w,OFF:OFF+WIN,:]
        attn=OT_s[w].astype(BF).T
        branch=shifts_ref[2:3,:]
        for m in range(2):
            branch=branch+mm_nt(attn[:,m*cq:(m+1)*cq],W1[m,:,3*cq:4*cq])
        branch=branch.astype(BF).astype(F32)
        middle=x+branch
        xhat2,rstd2=norm_stats(middle)
        xn2=(xhat2*gains_ref[1:2,:]+shifts_ref[1:2,:]).astype(BF)
        tg=og.astype(BF)
        xn2_s[...]=xn2; xn2T_s[...]=xn2.T; tg_s[...]=tg; tgT_s[...]=tg.T
        up_s[...]=jnp.zeros_like(up_s); gn2_s[...]=jnp.zeros_like(gn2_s)
        CH=lead
        def side(m,_):
            for o in range(0,cf,CH):
                f1=W1[m,:,4*cq:] if o==0 else W2[m,:,o-lead:o-lead+CH]
                f2=W2[m,:,cf-lead+o:cf-lead+o+CH]
                hid=mm(xn2_s[...],f1)
                act,dact=gelu_both(hid)
                a=act.astype(BF)
                up_s[...]+=mm_nt(a,f2)
                gh=(mm(tg_s[...],f2)*dact).astype(BF)
                gn2_s[...]+=mm_nt(gh,f1)
                acc[m,:,cq+o:cq+o+CH]+=mm(xn2T_s[...],gh)
                acc[m,:,cq+cf+o:cq+cf+o+CH]+=mm(tgT_s[...],a)
            return 0
        lax.fori_loop(0,2,side,0)
        dl_s[w,0:WIN,:]=(branch+up_s[...]+shifts_ref[3:4,:]).astype(BF)
        @pl.when(w<nw-1)
        def _():
            slab(w).start(); slab(w,mate).start()
        @pl.when(w==nw-1)
        def _(): slab(None).start()
        gn2=gn2_s[...]
        gln2=norm_back(gn2,xhat2,rstd2,gains_ref[1:2,:])
        gln2_ref[0]=gln2
        gb=(og+gln2).astype(BF)
        gbT=gb.T
        for m in range(2):
            at=slice(m*cq,(m+1)*cq)
            acc[m,:,0:cq]+=mm(gbT,attn[:,at])
            g=mm(gb,W1[m,:,3*cq:4*cq]).astype(BF)
            g_ref[0,:,at]=g
            gT=g.T
            gT_ref[0,at,:]=gT
            prod=gT.astype(F32)*OT_s[w,at,:]
            nh=nheads//2
            D_ref[0,m*nh:(m+1)*nh,:]=jnp.sum(prod.reshape(nh,HD,WIN),axis=1)
        small_ref[1:2,:]+=jnp.sum(gn2*xhat2,axis=0,keepdims=True)
        small_ref[3:4,:]+=jnp.sum(gn2,axis=0,keepdims=True)
        small_ref[4:5,:]+=jnp.sum(gb.astype(F32),axis=0,keepdims=True)
        small_ref[5:6,:]+=jnp.sum(tg.astype(F32),axis=0,keepdims=True)

    @pl.when(i==2*nw-1)
    def _():
        W2[...]=acc[:,:,cq+lead:].astype(BF)
        pst[...]=acc[:,:,:cq+lead].astype(BF)
        a=pltpu.make_async_copy(W2,dcat_hbm.at[:,:,pl.ds(cq+lead,W2.shape[2])],fin.at[0])
        b=pltpu.make_async_copy(pst,dcat_hbm.at[:,:,pl.ds(0,cq+lead)],fin.at[1])
        a.start(); b.start()
        for k in range(2):
            pltpu.make_async_copy(P_s.at[k],P_hbm.at[0,0],psem.at[k]).wait()
        for k in range(nw-1):
            slab(k).wait(); slab(k,mate).wait()
        slab(None).wait()
        @pl.when(y==1)
        def _():
            for t in range(2): edge(t).wait_send()
        a.wait(); b.wait()

def call_a2(inputs,og,wf,lab,bias,brem,W1,gains,shifts):
    nW=lab.shape[0]//2; WIN=lab.shape[1]; D=inputs.shape[1]; NH=bias.shape[0]
    cq=D//2; lead=W1.shape[2]-4*cq; cf=(wf.shape[1]+lead)//2; SLAB=-(-WIN//16)*16
    Q=bias.shape[2]
    sd=jax.ShapeDtypeStruct; dma=pltpu.SemaphoreType.DMA; v=pltpu.VMEM
    early=lambda shape: pl.BlockSpec((1,)+shape,lambda i:(jnp.minimum(i,nW-1),)+(0,)*len(shape))
    late=lambda shape: pl.BlockSpec((1,)+shape,lambda i:(jnp.maximum(i-nW,0),)+(0,)*len(shape))
    outs=[sd((nW,3,WIN,D),BF),sd((nW,WIN,D),F32),sd((nW,NH//PER,WIN,PER*Q),BF),sd((nW,WIN,GROUP),BF),sd((nW,WIN,D),F32),sd((nW,WIN,D),BF),sd((nW,D,WIN),BF),sd((nW,NH,WIN),F32),
          sd((2*nW,SLAB,D),BF),sd((SLAB,D),BF),sd((2,D,cq+2*cf),BF),sd((8,D),F32)]
    return pl.pallas_call(functools.partial(kernel_a2,NH),grid=(2*nW,),
      in_specs=[ANY,ANY,ANY,full(lab.shape),full(bias.shape,pipeline_mode=ONE),full(brem.shape),full(W1.shape,pipeline_mode=ONE),full(gains.shape),full(shifts.shape)],
      out_specs=[early((3,WIN,D)),early((WIN,D)),ANY,early((WIN,GROUP)),late((WIN,D)),late((WIN,D)),late((D,WIN)),late((NH,WIN)),ANY,ANY,ANY,full((8,D))],
      out_shape=outs,
      scratch_shapes=[v((nW,SLAB,D),F32),v((nW,SLAB,D),F32),v((2,D,2*cf-lead),BF),v((nW,D,WIN),F32),v((D,WIN),BF),v((D,WIN),BF),v((2,WIN,PER*Q),BF),v((PER*SLAB,2*GROUP),BF),
        v((2,D,cq+2*cf),F32),v((2,D,cq+lead),BF),v((WIN,D),BF),v((D,WIN),BF),v((WIN,D),BF),v((D,WIN),BF),v((WIN,D),F32),v((WIN,D),F32),v((nW,SLAB,D),BF),
        v((WIN,2*nW),F32),dma((2,)),dma((2,2*nW)),dma((2,2))]+gather_sems()+[dma((nW,)),dma((nW,)),dma((nW,)),dma((2,))],
      compiler_params=pltpu.CompilerParams(vmem_limit_bytes=63*1024*1024,dimension_semantics=("arbitrary",),collective_id=2,has_side_effects=True),
      name="kernel_a2")(inputs,og,wf,lab,bias,brem,W1,gains,shifts)

class Reduce:
    def __init__(self,src,out,own,r1,bufs,ss,rs,ls):
        self.src,self.out,self.own,self.r1,self.bufs=src,out,own,r1,bufs
        self.ss,self.rs,self.ls=ss,rs,ls
        z,x,c,y=place_of()
        self.x,self.c,self.y,self.h,self.l=x,c,y,z//2,z%2
    def to(self,x=None,h=None,l=None,c=None,y=None):
        pick=lambda new,old: old if new is None else new
        return dev(pick(h,self.h)*2+pick(l,self.l),pick(x,self.x),pick(c,self.c),pick(y,self.y))
    def mine(self,k):
        return pltpu.make_async_copy(self.src.at[k%2,:,:,k//2,self.c],self.own.at[k//2,:,:,k%2],self.ls.at[k])
    def theirs(self,k):
        return send(self.src.at[k%2,:,:,k//2,1-self.c],self.r1.at[k//2,:,:,k%2],self.ss.at[k],self.rs.at[k],self.to(c=1-self.c))
    def turns(self,core):
        x,h,l,y=self.x,self.h,self.l,self.y
        s=slice(None)
        if core==0:
            return [((1-x,),dict(x=1-x),lambda a,b,d:(x,a,b,d)),((x,s,1-l),dict(l=1-l),lambda a,d:(x,a,l,d)),
                    ((x,1-h,l),dict(h=1-h),lambda d:(x,h,l,d)),((x,h,l,1-y),dict(y=1-y),None)]
        return [((s,s,1-l),dict(l=1-l),lambda a,b,d:(a,b,l,d)),((s,1-h,l),dict(h=1-h),lambda a,d:(a,h,l,d)),
                ((1-x,h,l),dict(x=1-x),lambda d:(x,h,l,d)),((x,h,l,1-y),dict(y=1-y),None)]
    def give(self,k,core):
        at,where,_=self.turns(core)[k]
        return send(self.own.at[at],self.bufs[k],self.ss.at[4+k],self.rs.at[4+k],self.to(**where))
    def start(self):
        for k in range(4):
            self.theirs(k).start(); self.mine(k).start()
    def add(self,dst,*srcs):
        total=srcs[0][...].astype(F32)
        for s in srcs[1:]: total=total+s[...].astype(F32)
        dst[...]=total.astype(dst.dtype)
    def by_core(self,f):
        for core in range(2):
            @pl.when(self.c==core)
            def _(): f(core)
    def one(self):
        for k in range(4):
            self.mine(k).wait(); self.theirs(k).wait_recv()
        def step(k,_):
            at=(k//8,(k//4)%2,(k//2)%2,k%2)
            self.add(self.own.at[at],self.own.at[at],self.r1.at[at])
            return 0
        lax.fori_loop(0,16,step,0)
        self.by_core(lambda core: self.give(0,core).start())
    def turn(self,k):
        def f(core):
            stay=self.turns(core)[k][2]
            self.give(k,core).wait_recv()
            def step(i,_):
                at=[(i//4,(i//2)%2,i%2),(i//2,i%2),(i,)][k]
                self.add(self.own.at[stay(*at)],self.own.at[stay(*at)],self.bufs[k].at[at])
                return 0
            lax.fori_loop(0,8>>k,step,0)
            self.give(k+1,core).start()
        self.by_core(f)
    def four(self):
        def f(core):
            self.give(3,core).wait_recv()
            self.add(self.out,self.own.at[self.x,self.h,self.l,self.y],self.bufs[3])
            for k in range(4): self.give(k,core).wait_send()
        self.by_core(f)
        for k in range(4): self.theirs(k).wait_send()

def reduce_scratch(rows,cols):
    v=lambda *d: pltpu.VMEM(d+(rows,cols),BF); dma=pltpu.SemaphoreType.DMA
    return [v(2,2,2,2),v(2,2,2,2),v(2,2,2),v(2,2),v(2),v(),dma((8,)),dma((8,)),dma((4,))]

class Sums:
    def __init__(self,slabs,got,res,ss,rs,ts,us):
        self.slabs,self.got,self.res,self.ss,self.rs,self.ts,self.us=slabs,got,res,ss,rs,ts,us
        z,x,c,y=place_of()
        self.s=(z*2+x)*2+c; self.y=y; self.n=slabs.shape[1]
    def part(self,k,yy):
        me=self.y*16+self.s
        return send(self.slabs.at[yy,k],self.got.at[me],self.ss.at[yy*self.n+k],self.rs.at[me],(k,yy))
    def other(self,k,yy):
        return jnp.logical_or(self.s!=k,self.y!=yy)
    def scatter(self):
        for k in range(self.n):
            for yy in range(2):
                @pl.when(self.other(k,yy))
                def _(): self.part(k,yy).start()
    def back(self,to,k):
        return send(self.res.at[k],self.res.at[k],self.ts.at[to],self.us.at[k],(to,self.y))
    def collect(self):
        me=self.y*16+self.s
        @pl.when(self.s<self.n)
        def _():
            self.got[me]=self.slabs[self.y,self.s]
            def wait(i,_):
                @pl.when(i!=me)
                def _():
                    send(self.slabs.at[0,0],self.got.at[i],self.ss.at[0],self.rs.at[i],(self.s,1-self.y)).wait_recv()
                return 0
            lax.fori_loop(0,32,wait,0)
            total=self.got[0]
            for i in range(1,32): total=total+self.got[i]
            self.res[self.s]=total
            for to in range(16):
                @pl.when(self.s!=to)
                def _(): self.back(to,self.s).start()
    def finish(self):
        for k in range(self.n):
            @pl.when(self.s!=k)
            def _(): self.back(k,k).wait_recv()
        @pl.when(self.s<self.n)
        def _():
            for to in range(16):
                @pl.when(self.s!=to)
                def _(): self.back(to,self.s).wait_send()
        for k in range(self.n):
            for yy in range(2):
                @pl.when(self.other(k,yy))
                def _(): self.part(k,yy).wait_send()

def kernel_bc(nheads,x_ref,gln2_ref,qkv_ref,g_ref,gT_ref,D_ref,P_ref,pr_ref,W1,gains_ref,shifts_ref,sm_ref,pos_ref,pose_ref,dcat_hbm,dlast_hbm,
              ev_hbm,hd_hbm,evl_hbm,hdl_hbm,redq_ref,redm_ref,tab_ref,sum_ref,
              G_s,Gx,Gr_s,Gxr,vst_s,dS_s,dsr_s,gbd_s,qbd_s,aq,dq_s,kT_s,gq_s,gqT_s,dd_s,small_ref,acc,slabs,got,res,
              gs,gr_,ge,dl,ds,dr,es,er,us,ss0,rs0,ts0,us0,
              *more):
    w=pl.program_id(0); nw=dd_s.shape[0]
    z,xc,c,y=place_of()
    s=(z*2+xc)*2+c
    mate=dev(z,xc,c,1-y); sib=dev(z,xc,1-c,y)
    D=x_ref.shape[-1]; WIN=x_ref.shape[-2]; SLAB=dd_s.shape[1]
    cq=D//2
    groups=nheads//PER
    tiles=G_s.shape[0]; Q=tiles*128; R=WIN-Q; part=Gx.shape[1]//nheads
    big=Reduce(dcat_hbm,redm_ref,more[9],more[10],more[11:15],*more[15:18])
    red=Reduce(dq_s,redq_ref,more[0],more[1],more[2:6],*more[6:9])
    def slab(k,to=None):
        at=ev_hbm.at[y*nw+k]
        if to is None: return pltpu.make_async_copy(dd_s.at[k],at,dl.at[k])
        return send(dd_s.at[k],at,ds.at[k],dr.at[k],to)
    def tail(k):
        lead=SLAB-hd_hbm.shape[0]
        return send(dd_s.at[nw-1,pl.ds(lead,hd_hbm.shape[0])],hd_hbm,es.at[k],er,((s+1)%16,k))
    def early(k):
        lead=SLAB-hdl_hbm.shape[0]
        if k==0: return pltpu.make_async_copy(dlast_hbm,evl_hbm.at[y],us.at[0])
        if k==1: return send(dlast_hbm,evl_hbm.at[y],us.at[1],us.at[2],mate)
        return send(dlast_hbm.at[pl.ds(lead,hdl_hbm.shape[0])],hdl_hbm,us.at[k+1],us.at[5],((s+1)%16,k-2))
    def edge_trade():
        return send(Gr_s,Gxr,ge.at[0],ge.at[1],sib)
    def trade(h):
        r=pl.multiple_of(h*WIN+(1-c)*(WIN-part),8)
        return send(G_s.at[:,pl.ds(r,part)],Gx.at[:,pl.ds(pl.multiple_of(h*part,8),part)],gs.at[h],gr_.at[h],sib)
    everyone=[((s+t)%16,yy) for t in range(1,16) for yy in (y,1-y)]+[mate]
    @pl.when(w==0)
    def _():
        hail(everyone)
        aq[...]=jnp.zeros_like(aq); G_s[...]=jnp.zeros_like(G_s); Gr_s[...]=jnp.zeros_like(Gr_s); small_ref[...]=sm_ref[...]
        dd_s[:,SLAB-16:,:]=jnp.zeros((nw,16,D),BF)
        for hh in range(PER): vst_s[(hh+1)*SLAB-16:(hh+1)*SLAB,:]=jnp.zeros((16,GROUP),BF)
    def met():
        heard(everyone)
        big.start()
        early(0).start(); early(1).start()
        @pl.when(y==1)
        def _():
            early(2).start(); early(3).start()
    plan=((0,met),(2,big.one),(8,lambda: big.turn(0)),(11,lambda: big.turn(1)),(14,lambda: big.turn(2)))
    kT_s[...]=qkv_ref[0,1].T
    lane=lax.broadcasted_iota(jnp.int32,(WIN,GROUP),1)
    hl=lane//HD
    lift=pick((GROUP,R),lambda r,c: r%R==c).astype(BF)
    own_cols=pick((GROUP,D),lambda r,c: r//R==c//HD)
    gbd_s[...]=(mm(lift,g_ref[0,Q:WIN,:])*own_cols).astype(BF)
    qbd_s[...]=(mm(lift,qkv_ref[0,0,Q:WIN,:])*own_cols).astype(BF)
    Dr=exact(D_ref[0,:,Q:WIN],pick((R,GROUP),lambda r,c: c%R==r))
    Dr=jnp.sum(Dr*pick((nheads,GROUP),lambda r,c: c//R==r),axis=0,keepdims=True)
    dsr=pr_ref[0].astype(F32)*(mm_nt(qkv_ref[0,2],gbd_s[...])-Dr)
    Gr_s[...]+=dsr
    dsr_s[...]=dsr.astype(BF)
    gqT_s[:,Q:WIN]=exact(mm(kT_s[...],dsr_s[...])*pick((D,GROUP),lambda r,c: r//HD==c//R),pick((GROUP,R),lambda r,c: r%R==c))
    def group(gi,_):
        o=pl.multiple_of(gi*GROUP,GROUP)
        gTg=gT_ref[0,pl.ds(o,GROUP),0:Q]
        vg=qkv_ref[0,2,:,pl.ds(o,GROUP)]
        qg=qkv_ref[0,0,0:Q,pl.ds(o,GROUP)]
        gg=g_ref[0,0:Q,pl.ds(o,GROUP)]
        for hh in range(PER): vst_s[hh*SLAB:hh*SLAB+WIN,:]=jnp.where(hl==hh,vg,jnp.zeros_like(vg))
        dp4=mm(vst_s[...],gTg)
        for hh in range(PER):
            h=gi*PER+hh
            dsc=P_ref[0,gi,:,hh*Q:(hh+1)*Q].astype(F32)*(dp4[hh*SLAB:hh*SLAB+WIN]-D_ref[0,pl.ds(h,1),0:Q])
            for k in range(tiles):
                G_s[k,pl.ds(pl.multiple_of(h*WIN,8),WIN),:]+=dsc[:,k*128:(k+1)*128]
            dsl=dsc.astype(BF)
            dS_s[:,hh*Q:(hh+1)*Q]=dsl
            gqT_s[pl.ds(o+hh*HD,HD),0:Q]=mm(kT_s[pl.ds(o+hh*HD,HD),:],dsl)
        zero=jnp.zeros_like(gg); hq=hl[0:Q]
        gst=jnp.concatenate([jnp.where(hq==hh,gg,zero) for hh in range(PER)],axis=0)
        qst=jnp.concatenate([jnp.where(hq==hh,qg,zero) for hh in range(PER)],axis=0)
        dv=mm(P_ref[0,gi],gst)+mm(pr_ref[0],gbd_s[:,pl.ds(o,GROUP)])
        dk=mm(dS_s[...],qst)+mm(dsr_s[...],qbd_s[:,pl.ds(o,GROUP)])
        gq_s[1,:,pl.ds(o,GROUP)]=(dk*(1.0/SQ)).astype(BF)
        gq_s[2,:,pl.ds(o,GROUP)]=dv.astype(BF)
        for when,what in plan:
            pl.when(w*groups+gi==min(when,nw*groups-1))(what)
        @pl.when(w==nw-1)
        def _():
            for hh in range(PER): trade(gi*PER+hh).start()
            @pl.when(gi==0)
            def _(): edge_trade().start()
        return 0
    lax.fori_loop(0,groups,group,0)
    gq_s[0]=(gqT_s[...]*(1.0/SQ)).astype(BF).T
    x=x_ref[0]
    xhat,rstd=norm_stats(x)
    xn=(xhat*gains_ref[0:1,:]+shifts_ref[0:1,:]).astype(BF)
    xnT=xn.T
    gr=jnp.zeros((WIN,D),F32)
    for m in range(2):
        for k in range(3):
            gc=gq_s[k,:,m*cq:(m+1)*cq]
            gr=gr+mm_nt(gc,W1[m,:,k*cq:(k+1)*cq])
            aq[m,:,k*cq:(k+1)*cq]+=mm(xnT,gc)
    @pl.when(w==nw-1)
    def _():
        dq_s[...]=aq[...].astype(BF).reshape(dq_s.shape)
        red.start()
    dd_s[w,0:WIN,:]=(gln2_ref[0]+norm_back(gr,xhat,rstd,gains_ref[0:1,:])).astype(BF)
    slab(w).start(); slab(w,mate).start()
    @pl.when(jnp.logical_and(w==nw-1,y==1))
    def _():
        tail(0).start(); tail(1).start()
    small_ref[0:1,:]+=jnp.sum(gr*xhat,axis=0,keepdims=True)
    small_ref[2:3,:]+=jnp.sum(gr,axis=0,keepdims=True)
    @pl.when(w==nw-1)
    def _():
        for h in range(nheads): trade(h).wait()
        edge_trade().wait()
        acc[...]=jnp.zeros_like(acc)
        nh=acc.shape[0]; LW=tiles*128
        base=c*(WIN-part)
        def one_hots(g,hr,lr,width):
            iota=lax.broadcasted_iota(jnp.int32,(256,width),0).astype(F32).astype(BF)
            A=jnp.concatenate([jnp.where(hr==m,g,0.0) for m in range(nh)],axis=0).astype(BF)
            oh=jnp.where(iota==lr.astype(F32).astype(BF),jnp.ones((),BF),jnp.zeros((),BF))
            return mm_nt(A,oh)
        def rows(r,_):
            r8=pl.multiple_of(r*8,8)
            f8=pl.multiple_of(base+r*8,8)
            pos=pos_ref[pl.ds(f8,8),0:LW]
            hi8=pos>>8; lo8=pos&255
            tot=jnp.zeros((nh*nheads,256),F32)
            for k in range(8):
                g=jnp.concatenate([G_s[q,pl.ds(f8+k,nheads,stride=WIN),:]+Gx[q,pl.ds(r8+k,nheads,stride=part),:] for q in range(tiles)],axis=1)
                tot=tot+one_hots(g,hi8[k:k+1,:],lo8[k:k+1,:],LW)
            acc[...]+=tot.reshape(acc.shape)
            return 0
        turned=mm_nt(pick((GROUP,GROUP),lambda r,c: c==(r%nheads)*R+r//nheads).astype(BF),(Gr_s[...]+Gxr[...]).astype(BF))
        tot=jnp.zeros((nh*nheads,256),F32)
        for k in range(R):
            pos=pose_ref[k:k+1,:]
            hi=jnp.where(c==k//(R//2),pos>>8,-1)
            tot=tot+one_hots(turned[k*nheads:(k+1)*nheads],hi,pos&255,WIN)
        acc[...]+=tot.reshape(acc.shape)
        n=part//8
        cuts=[c,n*5//25,n*15//25,n]
        for f,after in enumerate((red.one,lambda: red.turn(0),None)):
            lax.fori_loop(cuts[f],cuts[f+1],rows,0)
            if after: after()
        half=nheads//2
        for yy in range(2):
            for k in range(nh): slabs[yy,k]=acc[k,yy*half:(yy+1)*half]
            for k in range(2): slabs[yy,nh+k]=small_ref[:,k*256:(k+1)*256]
        sums=Sums(slabs,got,res,ss0,rs0,ts0,us0)
        sums.scatter()
        red.turn(1)
        sums.collect()
        red.turn(2)
        big.four()
        sums.finish()
        red.four()
        for m in range(nh):
            tab_ref[:,m*256:(m+1)*256]=res[m]
        for k in range(2): sum_ref[:,k*256:(k+1)*256]=res[nh+k]
        for k in range(nw):
            slab(k).wait(); slab(k,mate).wait()
        @pl.when(y==1)
        def _():
            tail(0).wait_send(); tail(1).wait_send(); early(2).wait_send(); early(3).wait_send()
        tail(0).wait_recv(); early(2).wait_recv()
        early(0).wait(); early(1).wait()

def call_bc(x,gln2,qkv,g,gT,Dd,Pp,Pr,W1,gains,shifts,sm,pp,pos_index,dcat,dlast,T):
    nW,WIN,D=x.shape; NH=Dd.shape[1]
    cq=D//2; tiles=WIN//128; Q=tiles*128; SLAB=-(-WIN//16)*16; EDGE=-(-(SLAB-WIN//2)//16)*16
    part=-(-WIN//16)*8
    nh=-(-T//256)
    rows,more=dcat.shape[-2:]; cols=3*cq
    sd=jax.ShapeDtypeStruct; dma=pltpu.SemaphoreType.DMA; v=pltpu.VMEM
    return pl.pallas_call(functools.partial(kernel_bc,NH),grid=(nW,),
      in_specs=[per((WIN,D)),per((WIN,D)),per((3,WIN,D)),per((WIN,D)),per((D,WIN)),per((NH,WIN)),per(Pp.shape[1:]),per((WIN,GROUP)),
        full((2,D,cols),pipeline_mode=ONE),full(gains.shape),full(shifts.shape),full(sm.shape),full(pp.shape,pipeline_mode=ONE),pl.BlockSpec((WIN-Q,WIN),lambda w:(Q//(WIN-Q),0)),ANY,ANY],
      out_specs=[ANY,ANY,ANY,ANY,full((rows,cols),pipeline_mode=ONE),full((rows,more),pipeline_mode=ONE),full((NH//2,nh*256),pipeline_mode=ONE),full(sm.shape)],
      out_shape=[sd((2*nW,SLAB,D),BF),sd((EDGE,D),BF),sd((2,SLAB,D),BF),sd((EDGE,D),BF),sd((rows,cols),F32),sd((rows,more),F32),sd((NH//2,nh*256),F32),sd(sm.shape,F32)],
      scratch_shapes=[v((tiles,NH*WIN,128),F32),v((tiles,NH*part,128),F32),v((WIN,GROUP),F32),v((WIN,GROUP),F32),v((PER*SLAB,GROUP),BF),v((WIN,PER*Q),BF),v((WIN,GROUP),BF),v((GROUP,D),BF),v((GROUP,D),BF),v((2,D,cols),F32),v((2,2,2,2,2,rows,cols),BF),v((D,WIN),BF),v((3,WIN,D),BF),v((D,WIN),F32),
        v((nW,SLAB,D),BF),v(sm.shape,F32),v((nh,NH,256),F32),v((2,nh+2,8,256),F32),v((32,8,256),F32),v((nh+2,8,256),F32),
        dma((NH,)),dma((NH,)),dma((2,)),dma((nW,)),dma((nW,)),dma((nW,)),dma((2,)),dma,dma((6,)),dma((2*nh+4,)),dma((32,)),dma((16,)),dma((nh+2,))]+reduce_scratch(rows,cols)+reduce_scratch(rows,more),
      compiler_params=pltpu.CompilerParams(vmem_limit_bytes=63*1024*1024,dimension_semantics=("arbitrary",),collective_id=3,has_side_effects=True),
      name="kernel_bc")(x,gln2,qkv,g,gT,Dd,Pp,Pr,W1,gains,shifts,sm,pp,pos_index,dcat,dlast)


def kernel_f(in_ref,og_ref,ev_ref,evl_ref,ev2_ref,hd_ref,hd2_ref,redq_ref,redm_ref,tab_ref,sum_ref,
             out_ref,din_ref,dqkv_ref,dproj_ref,dfc1_ref,dfc2_ref,dgain_ref,dshift_ref,dtab_ref,end_s):
    j=pl.program_id(0); nw=pl.num_programs(0)//2
    shift=in_ref.shape[0]//2; WIN=2*shift
    edge,SLAB=hd_ref.shape[0],ev_ref.shape[1]
    off=edge-(SLAB-shift)
    @pl.when(j==0)
    def _():
        end_s[0]=hd_ref[...].astype(F32); end_s[1]=hd2_ref[...].astype(F32)
        cq=dqkv_ref.shape[2]; cf=dfc1_ref.shape[1]
        for k in range(3): dqkv_ref[k]=redq_ref[:,k*cq:(k+1)*cq]
        dproj_ref[...]=redm_ref[:,0:cq]
        dfc1_ref[...]=redm_ref[:,cq:cq+cf]
        dfc2_ref[...]=redm_ref[:,cq+cf:]
        dgain_ref[...]=sum_ref[0:2,:]; dshift_ref[...]=sum_ref[2:6,:]
        dtab_ref[...]=tab_ref[:,0:dtab_ref.shape[1]]
    e=jnp.where(j%nw==nw-1,evl_ref[0],ev_ref[0]).astype(F32)
    for k,(base,res,v) in enumerate(((in_ref,out_ref,e),(og_ref,din_ref,ev2_ref[0].astype(F32)))):
        res[0:shift,:]=base[0:shift,:]+end_s[k,off:off+shift,:]
        res[shift:WIN,:]=base[shift:WIN,:]+v[0:shift,:]
        end_s[k]=v[SLAB-edge:,:]

def call_f(inputs,og,ev,evl,ev2,hd,hd2,redq,redm,tab,small,cq,cf,T):
    tok,D=inputs.shape; n,SLAB,_=ev.shape; WIN=tok//n; rows=redq.shape[0]
    sd=jax.ShapeDtypeStruct
    blk=pl.BlockSpec((WIN,D),lambda j:(j,0)); slab=pl.BlockSpec((1,SLAB,D),lambda j:(j,0,0))
    shapes=[(3,rows,cq),(rows,cq),(rows,cf),(rows,cf),(2,D),(4,D),(tab.shape[0],T)]
    return pl.pallas_call(kernel_f,grid=(n,),
      in_specs=[blk,blk,slab,pl.BlockSpec((1,SLAB,D),lambda j:(j//(n//2),0,0)),slab]+[full(v.shape) for v in (hd,hd2,redq,redm,tab,small)],
      out_specs=[blk,blk]+[full(v) for v in shapes],
      out_shape=[sd((tok,D),F32),sd((tok,D),F32)]+[sd(v,F32) for v in shapes],
      scratch_shapes=[pltpu.VMEM((2,)+hd.shape,F32)],
      compiler_params=pltpu.CompilerParams(vmem_limit_bytes=63*1024*1024,dimension_semantics=("arbitrary",)),
      name="kernel_f")(inputs,og,ev,evl,ev2,hd,hd2,redq,redm,tab,small)

def gathered(piece,names,nseq,nheads):
    full=lax.all_gather(piece,names,axis=0,tiled=False)
    return full.reshape((nseq,nheads)+piece.shape)

def natural(block):
    s,h,r,c=block.shape
    return block.transpose(0,2,1,3).reshape(s*r,h*c)

def owners(grad,nseq,nheads):
    r,c=grad.shape
    return grad.reshape(nseq,r//nseq,nheads,c//nheads).transpose(0,2,1,3).reshape(nseq*nheads,r//nseq,c//nheads)

def from_next(rows):
    n=lax.axis_size("seq")
    return lax.ppermute(rows,"seq",[(i,(i-1)%n) for i in range(n)])

def to_next(rows):
    n=lax.axis_size("seq")
    return lax.ppermute(rows,"seq",[(i,(i+1)%n) for i in range(n)])

def spread(rows):
    n=lax.axis_size("heads")
    flat=rows.reshape(-1,rows.shape[-1])
    if n==2:
        other=lax.ppermute(flat,"heads",[(0,1),(1,0)])
        me=lax.axis_index("heads")
        return jnp.where(me==0,jnp.concatenate([flat,other]),jnp.concatenate([other,flat]))
    return lax.all_gather(flat,"heads",axis=0,tiled=True)

def place(rows,base,shift):
    every=spread(rows)
    keep=every.shape[0]-shift
    return base+jnp.concatenate([to_next(every[keep:]),every[:keep]]).astype(F32)

def body(inputs,w_qkv,w_proj,w_fc1,w_fc2,gains,shifts,rel_table,region,pos_index,out_grad):
    nseq=lax.axis_size("seq"); nheads=lax.axis_size("heads"); me=lax.axis_index("heads")
    linked=nseq==16 and nheads==2
    names=("seq","heads")
    tok,D=inputs.shape; WIN=pos_index.shape[0]; shift=WIN//2; T=rel_table.shape[1]
    nW=tok//WIN//nheads
    rows=w_qkv.shape[1]; cq=w_qkv.shape[2]; cf=w_fc1.shape[1]
    lab=region.reshape(-1,WIN)
    if linked:
        W1,bias,brem,wf,posT=call_w(w_qkv,w_proj.T,w_fc1,w_fc2.T,pos_index,rel_table)
        qkv,x,Pp,Pr,gln2,g,gT,Dd,ev,dlast,dcat,sm=call_a2(inputs,out_grad,wf,lab,bias,brem,W1,gains,shifts)
        ev2,hd2,evl,hd,redq,redm,d_table,small=call_bc(x,gln2,qkv,g,gT,Dd,Pp,Pr,W1,gains,shifts,sm,posT,pos_index,dcat.reshape(2,2,2,2,2,rows,-1),dlast,T)
        out,din,dq,dp,d1,d2,dg,dsh,dt=call_f(inputs,out_grad,ev,evl,ev2,hd,hd2,redq,redm,d_table,small,cq,cf,T)
        return (out,din,dq,dp.T,d1,d2.T,dg,dsh,dt)
    posT=pos_index.T
    wide=-(-WIN//128)*128
    posP=jnp.pad(posT,((0,0),(0,wide-WIN)))
    start=me*nW*WIN
    lab=lax.dynamic_slice_in_dim(lab,me*nW,nW,0)
    labc=lab[:,:,None]; labr=lab[:,None,:]
    wq=jnp.concatenate([w_qkv[0],w_qkv[1],w_qkv[2],w_proj.T],axis=1).astype(BF)
    wf=jnp.concatenate([w_fc1,w_fc2.T],axis=1).astype(BF)
    table=lax.all_gather(rel_table,"heads",axis=0,tiled=True)
    NH=table.shape[0]
    every=gathered(jnp.concatenate([wq,wf],axis=1),names,nseq,nheads)
    ends=[i*cq for i in range(5)]+[4*cq+cf,4*cq+2*cf]
    W=jnp.concatenate([natural(every[...,a:b]) for a,b in zip(ends[:-1],ends[1:])],axis=1)[None]
    bias=call_p(posP,pack_table(table),WIN)
    def mine(v):
        ext=jnp.concatenate([v,from_next(v[:shift])])
        return lax.dynamic_slice_in_dim(ext,start+shift,nW*WIN,0).reshape(nW,WIN,-1)
    x=mine(inputs); og=mine(out_grad)
    delta,gln2,qkv,g,gT,Dd,Pp,dcat,sm_a=call_a(x,og,labc,labr,bias,W,gains,shifts)
    dd,dqkv,G,sm_b=call_b(x,gln2,qkv,g,gT,Dd,Pp,W,gains,shifts)
    grads=[dqkv[0,:,c*D:(c+1)*D] for c in range(3)]+[dcat[0,:,:D],dcat[0,:,D:D+cf*nheads],dcat[0,:,D+cf*nheads:]]
    red=lax.psum_scatter(jnp.concatenate([owners(v,nseq,nheads) for v in grads],axis=2),names,scatter_dimension=0,tiled=False).astype(F32)
    redq,redm=red[:,:3*cq],red[:,3*cq:]
    d_table,small=lax.psum((call_t(G,posT,T,NH),sm_a+sm_b),names)
    nl=rel_table.shape[0]
    d_table=lax.dynamic_slice_in_dim(d_table,me*nl,nl,0)
    output=place(delta,inputs,shift)
    d_inputs=place(dd,out_grad,shift)
    d_qkv=redq.reshape(rows,3,cq).transpose(1,0,2)
    d_proj=redm[:,:cq].T; d_fc1=redm[:,cq:cq+cf]; d_fc2=redm[:,cq+cf:].T
    return (output,d_inputs,d_qkv,d_proj,d_fc1,d_fc2,small[0:2],small[2:6],d_table)

def solution(mesh):
    placed=(P("seq",None),P(None,"seq","heads"),P("heads","seq"),P("seq","heads"),P("heads","seq"),P(),P(),P("heads",None),P("seq"),P(),P("seq",None))
    return jax.shard_map(body,mesh=mesh,in_specs=placed,
    out_specs=(P("seq",None),P("seq",None),P(None,"seq","heads"),P("heads","seq"),P("seq","heads"),P("heads","seq"),P(),P(),P("heads",None)),
    check_vma=False)
```
